256 devices in a mesh: gx: 16 (over y, z_hi, core), gy: 16 (over x, z_lo).
Axes of the slice: x: 4, y: 4, z: 8 (z_hi: 2, z_lo: 4; z = z_hi * 4 + z_lo), core: 2. Of those that a mesh axis runs over, the one named last changes fastest.
Arguments:
- right_side: float32 [2, 16, 256, 2048], P(None, None, 'gx', 'gy'), may hold values from -12 to 12
- classes: int32 [16, 256, 2048], P(None, 'gx', 'gy'), may hold values from 0 to 15
- sea_mask: int32 [16, 256, 2048], P(None, 'gx', 'gy'), may hold values from 0 to 1, as said below
- kappa_table: float32 [16], replicated, may hold values from 0.002 to 0.2
- cross_table: float32 [16], replicated, may hold values from 0.5 to 4
- vertical_table: float32 [16], replicated, may hold values from 0.05 to 0.5
Outputs:
- solution_field: float32 [2, 16, 256, 2048], P(None, None, 'gx', 'gy')
- residual: float32 [2, 16, 256, 2048], P(None, None, 'gx', 'gy')
The draws below stay inside these ranges and needn't reach their ends.
Inputs may be any that keep to these rules, and one draw needn't show every extreme that they name: `sea_mask`: land cells (value 0) occur only where both horizontal indices of the cell are even.
All inputs are finite; a program needn't handle non-finite values.
Results may differ from the reference program's by a relative error of at most 0.0055.
Values sent between devices are 32-bit elements; how exact they have to be, the bound alone decides.
No kernel may reach another device: no remote copies, remote signals or barrier semaphores. Data moves between devices by JAX's collectives and lax.ppermute only.
A program may use at most 128 MiB of HBM per device.

```python
import math
import jax
import jax.numpy as jnp
from jax import lax

NZ = 16
LEVELS = 3
CLASSES = 16
RHS = 2
NX = 256
NY = 2048


def draw_right_side(key, part):
    key = jax.random.fold_in(key, 11)
    across = jnp.arange(NX, dtype=jnp.float32) / NX
    rising = (1.0 + 2.0 * across)[None, None, :, None]
    values = jnp.clip(jax.random.normal(key, (RHS, NZ, NX, NY), jnp.float32), -4.0, 4.0)
    return values * rising


def draw_sea_mask(key, part):
    key = jax.random.fold_in(key, 23)
    candidate = jax.random.randint(key, (NZ, NX, NY), 0, 5) < 3
    even_first = (jnp.arange(NX) % 2 == 0)[None, :, None]
    even_second = (jnp.arange(NY) % 2 == 0)[None, None, :]
    land = candidate & even_first & even_second
    return jnp.where(land, 0, 1).astype(jnp.int32)


def plant(drawn, key, least, high):
    longest = drawn.shape.index(max(drawn.shape))
    spots = []
    for shift in (0, 1):
        where = [jax.random.randint(jax.random.fold_in(key, axis), (), 0, length) for axis, length in enumerate(drawn.shape)]
        where[longest] = (where[longest] + shift) % drawn.shape[longest]
        spots.append(tuple(where))
    return drawn.at[spots[0]].set(least).at[spots[1]].set(high)


def setup_inputs(seed: int = 0) -> dict:
    key_of = jax.random.split(jax.random.key(seed), 7)
    right_side = draw_right_side(jax.random.fold_in(key_of[6], 71), 0)
    classes = plant(jax.random.randint(key_of[1], (NZ, NX, NY), 0, CLASSES), jax.random.fold_in(key_of[1], 1), 0, CLASSES - 1).astype(jnp.int32)
    sea_mask = draw_sea_mask(jax.random.fold_in(key_of[6], 71), 0)
    kappa_table = jnp.clip(jnp.exp(jax.random.uniform(key_of[3], (CLASSES,), jnp.float32, math.log(0.002), math.log(0.2))), 0.002, 0.2)
    cross_table = jnp.clip(jnp.exp(jax.random.uniform(key_of[4], (CLASSES,), jnp.float32, math.log(0.5), math.log(4.0))), 0.5, 4.0)
    vertical_table = jnp.clip(jnp.exp(jax.random.uniform(key_of[5], (CLASSES,), jnp.float32, math.log(0.05), math.log(0.5))), 0.05, 0.5)
    return {"right_side": right_side, "classes": classes, "sea_mask": sea_mask, "kappa_table": kappa_table, "cross_table": cross_table, "vertical_table": vertical_table}


def cheb_weights(degree, lower_end, upper_end):
    middle = 0.5 * (upper_end + lower_end)
    radius = 0.5 * (upper_end - lower_end)
    return [1.0 / (middle + radius * math.cos(math.pi * (2 * index_k + 1) / (2 * degree))) for index_k in range(degree)]

def look_up(classes, values_table):
    result = jnp.zeros(classes.shape, jnp.float32)
    for entry in range(values_table.shape[0]):
        result = jnp.where(classes == entry, values_table[entry], result)
    return result

def coarsen_sum(vector):
    shape = vector.shape
    blocks = vector.reshape(shape[:-3] + (shape[-3] // 2, 2, shape[-2] // 2, 2, shape[-1] // 2, 2))
    return lax.optimization_barrier(jnp.sum(blocks, axis=(-5, -3, -1)))

def coarsen_mean(vector):
    return 0.125 * coarsen_sum(vector)

def spread_up(vector):
    return jnp.repeat(jnp.repeat(jnp.repeat(vector, 2, axis=-3), 2, axis=-2), 2, axis=-1)

def build_coeffs(padded_w, vertical, mass_term, factor):
    face_x = factor * jnp.sqrt(padded_w[:, :-1, 1:-1] * padded_w[:, 1:, 1:-1])
    face_y = factor * jnp.sqrt(padded_w[:, 1:-1, :-1] * padded_w[:, 1:-1, 1:])
    face_z = jnp.pad(factor * jnp.sqrt(vertical[:-1] * vertical[1:]), ((1, 1), (0, 0), (0, 0)))
    diagonal = mass_term + face_x[:, :-1] + face_x[:, 1:] + face_y[:, :, :-1] + face_y[:, :, 1:] + face_z[:-1] + face_z[1:]
    return (face_x, face_y, face_z, diagonal)

def apply_operator(vector, coeffs, padded):
    face_x, face_y, face_z, diagonal = coeffs
    padded_z = jnp.pad(vector, ((0, 0), (1, 1), (0, 0), (0, 0)))
    neighbours = face_x[:, :-1] * padded[:, :, :-2, 1:-1] + face_x[:, 1:] * padded[:, :, 2:, 1:-1]
    neighbours = neighbours + face_y[:, :, :-1] * padded[:, :, 1:-1, :-2] + face_y[:, :, 1:] * padded[:, :, 1:-1, 2:]
    neighbours = neighbours + face_z[:-1] * padded_z[:, :-2] + face_z[1:] * padded_z[:, 2:]
    return diagonal * vector - neighbours

def smooth_pass(approx, source, coeffs, weights, operator):
    for step_index, weight in enumerate(weights):
        if approx is None:
            approx = weight * source / coeffs[3]
        else:
            approx = approx + weight * (source - operator(approx)) / coeffs[3]
    return approx

def pad_sides(vector):
    return jnp.pad(vector, ((0, 0), (0, 0), (1, 1), (1, 1)))

def cycle_down(source, coeff_list, tier_index):
    coeffs = coeff_list[tier_index]

    def operator(vector):
        return apply_operator(vector, coeffs, pad_sides(vector))
    if tier_index == len(coeff_list) - 1:
        return smooth_pass(None, source, coeffs, cheb_weights(4, 0.1, 2.0), operator)
    smooth_weights = cheb_weights(2, 0.3, 2.0)
    approx = smooth_pass(None, source, coeffs, smooth_weights, operator)
    defect = source - operator(approx)
    approx = approx + spread_up(cycle_down(coarsen_sum(defect), coeff_list, tier_index + 1))
    return smooth_pass(approx, source, coeffs, smooth_weights, operator)

def reference(right_side, classes, sea_mask, kappa_table, cross_table, vertical_table):
    sea = sea_mask.astype(jnp.float32)
    crosswise = look_up(classes, cross_table) * sea
    vertical = look_up(classes, vertical_table) * sea
    mass_term = look_up(classes, kappa_table) * sea + (1.0 - sea)
    coeff_list = []
    factor = 1.0
    for tier_index in range(LEVELS):
        padded_w = jnp.pad(crosswise, ((0, 0), (1, 1), (1, 1)))
        coeff_list.append(build_coeffs(padded_w, vertical, mass_term, factor))
        if tier_index < LEVELS - 1:
            crosswise = coarsen_mean(crosswise)
            vertical = coarsen_mean(vertical)
            mass_term = coarsen_sum(mass_term)
            factor = 4.0

    def fine_operator(vector):
        return apply_operator(vector, coeff_list[0], pad_sides(vector))
    direction = cycle_down(cycle_down(right_side, coeff_list, 0), coeff_list, 0)
    image = fine_operator(fine_operator(direction))
    step_length = lax.optimization_barrier(jnp.sum(right_side * direction, axis=(1, 2, 3))) / lax.optimization_barrier(jnp.sum(direction * image, axis=(1, 2, 3)))
    step_length = step_length[:, None, None, None]
    return (step_length * direction, right_side - step_length * image)
```

```python
import functools
import math

import jax
import jax.numpy as jnp
from jax import lax
from jax.experimental import pallas as pl
from jax.experimental.pallas import tpu as pltpu
from jax.sharding import PartitionSpec as P

F32 = jnp.float32
NZ = 16
ROWS = 16
COLS = 128
WIDE = 256
HALF = 64
EXT0 = 32
EXT1 = 40
EXT2 = 24


def cheb_weights(degree, lower_end, upper_end):
    middle = 0.5 * (upper_end + lower_end)
    radius = 0.5 * (upper_end - lower_end)
    return [
        1.0 / (middle + radius * math.cos(math.pi * (2 * index_k + 1) / (2 * degree)))
        for index_k in range(degree)
    ]


FINE = cheb_weights(2, 0.3, 2.0)
COARSE = cheb_weights(4, 0.1, 2.0)


def loop(count, body):
    def step(index, carry):
        body(index)
        return carry

    lax.fori_loop(0, count, step, 0)


def lanes(rows, width):
    return lax.broadcasted_iota(jnp.int32, (rows, width), 1)


def sublanes(rows, width):
    return lax.broadcasted_iota(jnp.int32, (rows, width), 0)


def lane_sum(value, step):
    width = value.shape[1]
    first = (lanes(*value.shape) // step) % 2 == 0
    return value + jnp.where(first, pltpu.roll(value, width - step, 1), pltpu.roll(value, step, 1))


def across(value, step):
    rows, width = value.shape
    return (
        pltpu.roll(value, 1, 0)
        + pltpu.roll(value, rows - 1, 0)
        + pltpu.roll(value, step, 1)
        + pltpu.roll(value, width - step, 1)
    )


def row_pairs(buffer, value):
    rows = value.shape[0]
    parts = []
    for half in range(2):
        buffer[half, 0:rows, :] = value[:, half * COLS : (half + 1) * COLS]
        parts.append(
            buffer[half, pl.ds(0, rows // 2, stride=2), :] + buffer[half, pl.ds(1, rows // 2, stride=2), :]
        )
    return jnp.concatenate(parts, axis=1)


def row_repeat(buffer, value):
    rows = value.shape[0]
    parts = []
    for half in range(2):
        part = value[:, half * COLS : (half + 1) * COLS]
        buffer[half, pl.ds(0, rows, stride=2), :] = part
        buffer[half, pl.ds(1, rows, stride=2), :] = part
        parts.append(buffer[half, 0 : 2 * rows, :])
    return jnp.concatenate(parts, axis=1)


def pick(table_row, index):
    rows, width = index.shape
    table = jnp.broadcast_to(table_row, (rows, COLS))
    parts = [
        jnp.take_along_axis(table, index[:, start : start + COLS], axis=1)
        for start in range(0, width, COLS)
    ]
    return parts[0] if len(parts) == 1 else jnp.concatenate(parts, axis=1)


def pack_halves(first, second):
    left = lanes(*first.shape) < HALF
    low = jnp.where(left, first, pltpu.roll(second, HALF, 1))
    high = jnp.where(left, pltpu.roll(first, HALF, 1), second)
    return low, high


def unpack_halves(from_right, from_left):
    left = lanes(*from_right.shape) < HALF
    first = jnp.where(left, from_right, pltpu.roll(from_left, HALF, 1))
    second = jnp.where(left, pltpu.roll(from_right, HALF, 1), from_left)
    return first, second


def pack_sea(fields):
    rows, width = fields[0].shape
    even_lane = lanes(rows, width) % 2 == 0
    even_row = sublanes(rows, width) % 2 == 0
    pairs = [
        jnp.where(even_lane, fields[i], pltpu.roll(fields[i + 1], 1, 1)) for i in (0, 2)
    ]
    return jnp.where(even_row, pairs[0], pltpu.roll(pairs[1], 1, 0))


def unpack_sea(packed):
    rows, width = packed.shape
    spot = (lanes(rows, width) % 2 == 0) & (sublanes(rows, width) % 2 == 0)
    fields = []
    for pair in (packed, pltpu.roll(packed, rows - 1, 0)):
        for field in (pair, pltpu.roll(pair, width - 1, 1)):
            fields.append(jnp.where(spot, field, 1.0))
    return fields


def columns_kernel(rhs, classes, sea, to_left, to_right):
    def pair(z):
        low, high = pack_halves(rhs[0, z], rhs[1, z])
        to_left[z] = low
        to_right[z] = high

    loop(NZ, pair)

    def class_pair(z):
        low, high = pack_halves(classes[z].astype(F32), classes[z + 8].astype(F32))
        to_left[16 + z] = low
        to_right[16 + z] = high

    loop(8, class_pair)
    for j in range(2):
        quads = [
            pack_sea([sea[8 * j + 4 * q + i].astype(F32) for i in range(4)]) for q in range(2)
        ]
        low, high = pack_halves(quads[0], quads[1])
        to_left[24 + j] = low
        to_right[24 + j] = high


MSG_Y = 26
MSG_X = 54


def rows_kernel(place, rhs, classes, sea, from_left, from_right, table, r_out, c_out, s_out, msg_x, msg_o, row_c, row_s):
    core = place[0]
    gy = place[2]
    left = lanes(ROWS, COLS) < HALF
    inside = jnp.where(
        left,
        jnp.where(gy < place[4] - 1, 1.0, 0.0),
        jnp.where(gy > 0, 1.0, 0.0),
    )

    def rhs_step(z):
        halo = unpack_halves(from_right[z], from_left[z])
        for i in range(2):
            r_out[z, i] = jnp.concatenate([rhs[i, z], halo[i]], axis=1)

    loop(NZ, rhs_step)

    def class_step(z):
        first, second = unpack_halves(from_right[16 + z], from_left[16 + z])
        c_out[z] = jnp.concatenate([classes[z].astype(F32), first], axis=1)
        c_out[z + 8] = jnp.concatenate([classes[z + 8].astype(F32), second], axis=1)

    loop(8, class_step)
    for j in range(2):
        quads = unpack_halves(from_right[24 + j], from_left[24 + j])
        for q in range(2):
            for i, field in enumerate(unpack_sea(quads[q])):
                z = 8 * j + 4 * q + i
                s_out[z] = jnp.concatenate([sea[z].astype(F32), field * inside], axis=1)

    for message, start, edge in (
        (msg_x, 8 * (1 - core), 8 - (1 - core)),
        (msg_o, 8 * core, 8 - core),
    ):
        start = pl.multiple_of(start, 8)

        def copy(z, message=message, start=start, edge=edge):
            for i in range(2):
                message[2 * z + i] = r_out[z, i, pl.ds(start, 8), :]
            message[32 + z] = c_out[z, pl.ds(start, 8), :]
            row_c[pl.ds(z, 1), :] = c_out[z, pl.ds(edge, 1), :]
            row_s[pl.ds(z, 1), :] = s_out[z, pl.ds(edge, 1), :]

        loop(NZ, copy)

        def copy_sea(j, message=message, start=start):
            message[48 + j] = pack_sea([s_out[4 * j + i, pl.ds(start, 8), :] for i in range(4)])

        loop(4, copy_sea)
        edge_g = pick(table[0:1], row_c[...].astype(jnp.int32)) * row_s[...]
        message[52] = edge_g[0:8]
        message[53] = edge_g[8:16]


def material_kernel(c_in, s_in, table, g_out, h_out, k_out, packed, buffer):
    def fields(z):
        index = c_in[z].astype(jnp.int32)
        sea = s_in[z]
        g = pick(table[0:1], index) * sea
        h = pick(table[1:2], index) * sea
        k = pick(table[2:3], index) * sea + (1.0 - sea)
        g_out[z] = g
        h_out[z] = h
        k_out[z] = k
        return g * g, h * h, k

    even = lanes(8, WIDE) % 2 == 0

    def coarse(pair):
        first = fields(2 * pair)
        second = fields(2 * pair + 1)
        return [
            lane_sum(row_pairs(buffer.at[i], first[i] + second[i]), 1) for i in range(3)
        ]

    def step(j):
        near = coarse(j)
        far = coarse(j + 4)
        packed[j] = jnp.where(even, 0.125 * near[0], 0.125 * near[1])
        packed[j + 4] = jnp.where(even, 0.125 * far[0], 0.125 * far[1])
        packed[j + 8] = jnp.where(even, near[2], far[2])

    loop(4, step)


def unpack_lanes(packed):
    even = lanes(*packed.shape) % 2 == 0
    width = packed.shape[1]
    return (
        jnp.where(even, packed, pltpu.roll(packed, 1, 1)),
        jnp.where(even, pltpu.roll(packed, width - 1, 1), packed),
    )


class Level:
    def __init__(self, depth, step, g, h, inverse, diagonal=None):
        self.depth, self.step = depth, step
        self.g, self.h, self.inverse, self.diagonal = g, h, inverse, diagonal

    def couple(self, x, z, i):
        horizontal = self.g[z] * across(self.g[z] * x[z + 1, i], self.step)
        vertical = self.h[z + 1] * (self.h[z] * x[z, i] + self.h[z + 2] * x[z + 2, i])
        return horizontal + vertical

    def first(self, x, r, weight):
        def body(z):
            scaled = weight * self.inverse[z]
            for i in range(2):
                x[z + 1, i] = scaled * r[z, i]

        loop(self.depth, body)

    def update(self, new, x, r, weight):
        def body(z):
            scaled = weight * self.inverse[z]
            for i in range(2):
                new[z + 1, i] = (1.0 - weight) * x[z + 1, i] + scaled * (r[z, i] + self.couple(x, z, i))

        loop(self.depth, body)

    def defect(self, x, r, z, i):
        return r[z, i] - self.diagonal[z] * x[z + 1, i] + self.couple(x, z, i)

    def diagonal_of(self, k, z):
        horizontal = self.g[z] * across(self.g[z], self.step)
        vertical = self.h[z + 1] * (self.h[z] + self.h[z + 2])
        return k + horizontal + vertical


def clear_ends(*refs):
    for ref in refs:
        ref[0] = jnp.zeros(ref.shape[1:], ref.dtype)
        ref[ref.shape[0] - 1] = jnp.zeros(ref.shape[1:], ref.dtype)


def fine_restrict(level, x, r, buffer, out):
    even = lanes(8, WIDE) % 2 == 0

    def body(pair):
        sums = []
        for i in range(2):
            total = level.defect(x, r, 2 * pair, i) + level.defect(x, r, 2 * pair + 1, i)
            sums.append(lane_sum(row_pairs(buffer.at[i], total[8:24]), 1))
        out[pair] = jnp.where(even, sums[0], sums[1])

    loop(NZ // 2, body)


def down_kernel(place, r_own, g_own, h_own, k_own, from_x, from_o, table, r, g, h, d, inverse, xp, r1, xa, ka, edges, buffer):
    core = place[0]
    gx = place[1]
    gy = place[2]
    open_side = jnp.where((gx > 0) & (gx < place[3] - 1), 1.0, 0.0)
    lane = lanes(8, WIDE)
    ends = jnp.where(
        lane < COLS,
        1.0,
        jnp.where(lane < COLS + HALF, jnp.where(gy < place[4] - 1, 1.0, 0.0), jnp.where(gy > 0, 1.0, 0.0)),
    )
    clear_ends(h, xp, xa)

    def own(z):
        for i in range(2):
            r[z, i, 8:24, :] = r_own[z, i]
        g[z, 8:24, :] = g_own[z]
        h[z + 1, 8:24, :] = h_own[z]
        ka[z, 8:24, :] = k_own[z]

    loop(NZ, own)
    for message, start, scale, slot in ((from_x, 24 * (1 - core), 1.0, 1 - core), (from_o, 24 * core, open_side, core)):
        start = pl.multiple_of(start, 8)

        def halo(j, message=message, start=start, scale=scale):
            for q, sea in enumerate(unpack_sea(message[48 + j])):
                z = 4 * j + q
                sea = sea * (scale * ends)
                index = message[32 + z].astype(jnp.int32)
                g[z, pl.ds(start, 8), :] = pick(table[0:1], index) * sea
                h[z + 1, pl.ds(start, 8), :] = pick(table[1:2], index) * sea
                ka[z, pl.ds(start, 8), :] = pick(table[2:3], index) * sea + (1.0 - sea)
                for i in range(2):
                    r[z, i, pl.ds(start, 8), :] = message[2 * z + i]

        loop(4, halo)
        edges[slot, 0:8, :] = message[52] * scale
        edges[slot, 8:16, :] = message[53] * scale

    level = Level(NZ, 1, g, h, inverse, d)
    row = sublanes(EXT0, WIDE)

    def diagonals(z):
        here = g[z]
        below = jnp.where(row == 0, edges[0, pl.ds(z, 1), :], pltpu.roll(here, 1, 0))
        above = jnp.where(row == EXT0 - 1, edges[1, pl.ds(z, 1), :], pltpu.roll(here, EXT0 - 1, 0))
        beside = pltpu.roll(here, 1, 1) + pltpu.roll(here, WIDE - 1, 1)
        total = ka[z] + here * (below + above + beside) + h[z + 1] * (h[z] + h[z + 2])
        d[z] = total
        inverse[z] = 1.0 / total

    loop(NZ, diagonals)
    level.first(xa, r, FINE[0])
    level.update(xp, xa, r, FINE[1])
    fine_restrict(level, xp, r, buffer, r1)


def gather_rows(core, out_store, own, partner, odd, second, count):
    starts = (16, 24 - 16 * core, 8 + 16 * core, 32 * core, 32 - 32 * core)

    def body(j):
        tiles = (own[j], partner[j], odd[j], odd[count + j], second[j])
        for start, tile in zip(starts, tiles):
            start = start if isinstance(start, int) else pl.multiple_of(start, 8)
            out_store(j, start, tile)

    return body


def coarse_coefficients(core, pieces, g1, h1, d1, i1, g2, h2, i2, w1, k1, u1, k2, buffer):
    clear_ends(h1, h2)

    def store(j, start, tile):
        first, second = unpack_lanes(tile)
        w1[j, pl.ds(start, 8), :] = first
        u1[j, pl.ds(start, 8), :] = second

    def store_k(j, start, tile):
        first, second = unpack_lanes(tile)
        k1[j, pl.ds(start, 8), :] = jnp.where(first == 0.0, 1.0, first)
        k1[j + 4, pl.ds(start, 8), :] = jnp.where(second == 0.0, 1.0, second)

    own, partner, odd, far = pieces
    starts = (16, 24 - 16 * core, 8 + 16 * core, 32 * core, 32 - 32 * core)
    starts = [s if isinstance(s, int) else pl.multiple_of(s, 8) for s in starts]

    def crosswise(j):
        for start, tile in zip(starts, (own[j], partner[j], odd[j], odd[12 + j], far[j])):
            store(j, start, tile)

    loop(8, crosswise)

    def masses(j):
        tiles = (own[8 + j], partner[8 + j], odd[8 + j], odd[20 + j], far[8 + j])
        for start, tile in zip(starts, tiles):
            store_k(j, start, tile)

    loop(4, masses)

    def roots(z):
        g1[z] = 2.0 * jnp.sqrt(w1[z])
        h1[z + 1] = 2.0 * jnp.sqrt(u1[z])

    loop(8, roots)
    one = Level(8, 2, g1, h1, i1, d1)

    def diagonals(z):
        total = one.diagonal_of(k1[z], z)
        d1[z] = total
        i1[z] = 1.0 / total

    loop(8, diagonals)

    def coarser(z):
        sums = [
            lane_sum(row_pairs(buffer.at[i], field[2 * z] + field[2 * z + 1]), 2)
            for i, field in enumerate((w1, u1, k1))
        ]
        blank = jnp.zeros((4, WIDE), F32)
        g2[z] = jnp.concatenate([2.0 * jnp.sqrt(0.125 * sums[0]), blank], axis=0)
        h2[z + 1] = jnp.concatenate([2.0 * jnp.sqrt(0.125 * sums[1]), blank], axis=0)
        k2[z] = jnp.concatenate([sums[2], blank + 1.0], axis=0)

    loop(4, coarser)
    two = Level(4, 4, g2, h2, i2)

    def diagonals_two(z):
        i2[z] = 1.0 / two.diagonal_of(k2[z], z)

    loop(4, diagonals_two)


def coarse_solve(core, one, two, pieces, r1, xa1, xb1, r2, xa2, xb2, buffer):
    own, partner, odd, far = pieces
    clear_ends(xa1, xb1, xa2, xb2)
    starts = (16, 24 - 16 * core, 8 + 16 * core, 32 * core, 32 - 32 * core)
    starts = [s if isinstance(s, int) else pl.multiple_of(s, 8) for s in starts]

    def assemble(z):
        tiles = (own[z], partner[z], odd[z], odd[8 + z], far[z])
        for start, tile in zip(starts, tiles):
            for i, field in enumerate(unpack_lanes(tile)):
                r1[z, i, pl.ds(start, 8), :] = field

    loop(8, assemble)
    one.first(xa1, r1, FINE[0])
    one.update(xb1, xa1, r1, FINE[1])

    def restrict(z):
        for i in range(2):
            total = one.defect(xb1, r1, 2 * z, i) + one.defect(xb1, r1, 2 * z + 1, i)
            sums = lane_sum(row_pairs(buffer.at[i], total), 2)
            r2[z, i] = jnp.concatenate([sums, jnp.zeros((4, WIDE), F32)], axis=0)

    loop(4, restrict)
    two.first(xa2, r2, COARSE[0])
    two.update(xb2, xa2, r2, COARSE[1])
    two.update(xa2, xb2, r2, COARSE[2])
    two.update(xb2, xa2, r2, COARSE[3])

    def prolong(z):
        for i in range(2):
            fine = row_repeat(buffer.at[i], xb2[z + 1, i, 0:20, :])
            for half in range(2):
                xa1[2 * z + half + 1, i] = xb1[2 * z + half + 1, i] + fine

    loop(4, prolong)
    one.update(xb1, xa1, r1, FINE[0])
    one.update(xa1, xb1, r1, FINE[1])


def fine_correct(level, out, xp, c1, buffer):
    def body(pair):
        for i in range(2):
            fine = row_repeat(buffer.at[i], c1[pair + 1, i, 12:28, :])
            for half in range(2):
                out[2 * pair + half + 1, i] = xp[2 * pair + half + 1, i] + fine

    loop(NZ // 2, body)


def middle_kernel(
    place, r, g, h, d, inverse, xp, own, partner, odd, far, m_own, m_partner, m_odd, m_far,
    z_out, xp_out, r1_out, g1, h1, d1, i1, g2, h2, i2,
    xa, xb, r1, xa1, xb1, r2, xa2, xb2, w1, k1, u1, k2, buffer,
):
    core = place[0]
    coarse_coefficients(
        core, (m_own, m_partner, m_odd, m_far), g1, h1, d1, i1, g2, h2, i2, w1, k1, u1, k2, buffer
    )
    zero = Level(NZ, 1, g, h, inverse, d)
    one = Level(8, 2, g1, h1, i1, d1)
    two = Level(4, 4, g2, h2, i2)
    coarse_solve(core, one, two, (own, partner, odd, far), r1, xa1, xb1, r2, xa2, xb2, buffer)
    clear_ends(xa, xb, xp_out)
    fine_correct(zero, xa, xp, xa1, buffer)
    zero.update(xb, xa, r, FINE[0])

    def last(z):
        scaled = FINE[1] * inverse[z]
        for i in range(2):
            z_out[z, i] = (1.0 - FINE[1]) * xb[z + 1, i] + scaled * (r[z, i] + zero.couple(xb, z, i))

    loop(NZ, last)
    zero.first(xa, z_out, FINE[0])
    zero.update(xp_out, xa, z_out, FINE[1])
    fine_restrict(zero, xp_out, z_out, buffer, r1_out)


def last_kernel(
    place, rhs, r, g, h, d, inverse, xp, own, partner, odd, far, g1, h1, d1, i1, g2, h2, i2,
    direction, image, sums,
    xa, xb, r1, xa1, xb1, r2, xa2, xb2, totals, buffer,
):
    core = place[0]
    zero = Level(NZ, 1, g, h, inverse, d)
    one = Level(8, 2, g1, h1, i1, d1)
    two = Level(4, 4, g2, h2, i2)
    coarse_solve(core, one, two, (own, partner, odd, far), r1, xa1, xb1, r2, xa2, xb2, buffer)
    clear_ends(xa, xb)
    fine_correct(zero, xa, xp, xa1, buffer)
    zero.update(xb, xa, r, FINE[0])
    zero.update(xa, xb, r, FINE[1])

    def first_image(z):
        for i in range(2):
            xb[z + 1, i] = d[z] * xa[z + 1, i] - zero.couple(xa, z, i)

    loop(NZ, first_image)
    totals[...] = jnp.zeros(totals.shape, F32)

    def second_image(z):
        for i in range(2):
            field = xa[z + 1, i, 8:24, 0:COLS]
            value = (d[z] * xb[z + 1, i] - zero.couple(xb, z, i))[8:24, 0:COLS]
            direction[i, z] = field
            image[i, z] = value
            totals[i] += rhs[i, z] * field
            totals[2 + i] += field * value

    loop(NZ, second_image)
    row = sublanes(8, COLS)
    lane = lanes(8, COLS)
    line = jnp.zeros((8, COLS), F32)
    for i in range(4):
        line = jnp.where(lane == i, jnp.sum(totals[i]), line)

    def spread(j):
        sums[pl.ds(pl.multiple_of(8 * j, 8), 8), :] = line

    loop(sums.shape[0] // 8, spread)


def scale_kernel(rhs, direction, image, sums, solution_field, residual):
    total = jnp.sum(sums[...], axis=0, keepdims=True)
    lane = lanes(1, COLS)
    parts = [jnp.sum(jnp.where(lane == i, total, 0.0), axis=1, keepdims=True) for i in range(4)]
    for i in range(2):
        alpha = parts[i] / parts[2 + i]

        def body(z, i=i, alpha=alpha):
            solution_field[i, z] = alpha * direction[i, z]
            residual[i, z] = rhs[i, z] - alpha * image[i, z]

        loop(NZ, body)


def call(kernel, operands, outs, scratch=(), place=True):
    vmem = pl.BlockSpec(memory_space=pltpu.VMEM)
    specs = [vmem] * len(operands)
    if place:
        specs[0] = pl.BlockSpec(memory_space=pltpu.SMEM)
    return pl.pallas_call(
        kernel,
        out_shape=[jax.ShapeDtypeStruct(shape, F32) for shape in outs],
        in_specs=specs,
        out_specs=[vmem] * len(outs),
        scratch_shapes=[pltpu.VMEM(shape, F32) for shape in scratch],
        compiler_params=pltpu.CompilerParams(vmem_limit_bytes=48 * 1024 * 1024),
    )(*operands)


FIELD0 = (NZ, 2, EXT0, WIDE)
PADDED0 = (NZ + 2, 2, EXT0, WIDE)
PADDED1 = (10, 2, EXT1, WIDE)
PADDED2 = (6, 2, EXT2, WIDE)
BUFFER = (3, 2, EXT1, COLS)
COARSE_SCRATCH = [(8, 2, EXT1, WIDE), PADDED1, PADDED1, (4, 2, EXT2, WIDE), PADDED2, PADDED2]


def shards(count_x, count_y, right_side, classes, sea_mask, kappa_table, cross_table, vertical_table):
    gx = lax.axis_index("gx")
    gy = lax.axis_index("gy")
    place = jnp.stack([gx % 2, gx, gy, jnp.int32(count_x), jnp.int32(count_y)]).astype(jnp.int32)
    table = jnp.stack([jnp.sqrt(cross_table), jnp.sqrt(vertical_table), kappa_table])
    table = jnp.pad(table, ((0, 5), (0, COLS - table.shape[1])))

    pairs_on_chip = [(i, i ^ 1) for i in range(count_x)]
    pairs_across = [(i, i + 1 if i % 2 else i - 1) for i in range(1, count_x - 1)]

    def on_chip(value):
        return lax.ppermute(value, "gx", pairs_on_chip)

    def across_chips(value):
        return lax.ppermute(value, "gx", pairs_across)

    def three_steps(own):
        partner = on_chip(own)
        odd = across_chips(jnp.concatenate([own, partner], axis=0))
        far = on_chip(odd[: own.shape[0]])
        return own, partner, odd, far

    to_left, to_right = call(
        columns_kernel, (right_side, classes, sea_mask), [(MSG_Y, ROWS, COLS)] * 2, place=False
    )
    forward = [(i, i + 1) for i in range(count_y - 1)]
    backward = [(i + 1, i) for i in range(count_y - 1)]
    from_left = lax.ppermute(to_right, "gy", forward)
    from_right = lax.ppermute(to_left, "gy", backward)

    r_own, c_own, s_own, msg_x, msg_o = call(
        rows_kernel,
        (place, right_side, classes, sea_mask, from_left, from_right, table),
        [(NZ, 2, ROWS, WIDE), (NZ, ROWS, WIDE), (NZ, ROWS, WIDE), (MSG_X, 8, WIDE), (MSG_X, 8, WIDE)],
        [(NZ, WIDE), (NZ, WIDE)],
    )
    from_o = across_chips(msg_o)
    from_x = on_chip(msg_x)
    g_own, h_own, k_own, packed = call(
        material_kernel,
        (c_own, s_own, table),
        [(NZ, ROWS, WIDE)] * 3 + [(12, 8, WIDE)],
        [BUFFER],
        place=False,
    )
    material = three_steps(packed)
    r, g, h, d, inverse, xp, r1 = call(
        down_kernel,
        (place, r_own, g_own, h_own, k_own, from_x, from_o, table),
        [FIELD0, (NZ, EXT0, WIDE), (NZ + 2, EXT0, WIDE), (NZ, EXT0, WIDE), (NZ, EXT0, WIDE), PADDED0, (8, 8, WIDE)],
        [PADDED0, (NZ, EXT0, WIDE), (2, NZ, WIDE), BUFFER],
    )
    one = [(8, EXT1, WIDE), (10, EXT1, WIDE), (8, EXT1, WIDE), (8, EXT1, WIDE)]
    two = [(4, EXT2, WIDE), (6, EXT2, WIDE), (4, EXT2, WIDE)]
    r, xp, r1, *coarse = call(
        middle_kernel,
        (place, r, g, h, d, inverse, xp, *three_steps(r1), *material),
        [FIELD0, PADDED0, (8, 8, WIDE), *one, *two],
        [PADDED0, PADDED0, *COARSE_SCRATCH, one[0], one[0], one[0], two[0], BUFFER],
    )
    count = count_x * count_y
    direction, image, sums = call(
        last_kernel,
        (place, right_side, r, g, h, d, inverse, xp, *three_steps(r1), *coarse),
        [(2, NZ, ROWS, COLS)] * 2 + [(count, COLS)],
        [PADDED0, PADDED0, *COARSE_SCRATCH, (4, ROWS, COLS), BUFFER],
    )
    sums = lax.all_to_all(sums.reshape(count, 1, COLS), ("gx", "gy"), 0, 0).reshape(count, COLS)
    return tuple(
        call(
            scale_kernel,
            (right_side, direction, image, sums),
            [(2, NZ, ROWS, COLS)] * 2,
            place=False,
        )
    )


def solution(mesh):
    return jax.shard_map(
        functools.partial(shards, mesh.shape["gx"], mesh.shape["gy"]),
        mesh=mesh,
        in_specs=(
            P(None, None, "gx", "gy"),
            P(None, "gx", "gy"),
            P(None, "gx", "gy"),
            P(),
            P(),
            P(),
        ),
        out_specs=(P(None, None, "gx", "gy"), P(None, None, "gx", "gy")),
        check_vma=False,
    )
```

```python
import functools
import math

import jax
import jax.numpy as jnp
from jax import lax
from jax.experimental import pallas as pl
from jax.experimental.pallas import tpu as pltpu
from jax.sharding import PartitionSpec as P

F32 = jnp.float32
NZ = 16
ROWS = 16
COLS = 128
WIDE = 256
HALF = 64
UNROLL = 8
EXT0 = 32
EXT1 = 40
EXT2 = 24


def cheb_weights(degree, lower_end, upper_end):
    middle = 0.5 * (upper_end + lower_end)
    radius = 0.5 * (upper_end - lower_end)
    return [
        1.0 / (middle + radius * math.cos(math.pi * (2 * index_k + 1) / (2 * degree)))
        for index_k in range(degree)
    ]


FINE = cheb_weights(2, 0.3, 2.0)
COARSE = cheb_weights(4, 0.1, 2.0)


def loop(count, body):
    def step(index, carry):
        body(index)
        return carry

    lax.fori_loop(0, count, step, 0, unroll=min(count, UNROLL))


def lanes(rows, width):
    return lax.broadcasted_iota(jnp.int32, (rows, width), 1)


def sublanes(rows, width):
    return lax.broadcasted_iota(jnp.int32, (rows, width), 0)


def lane_sum(value, step):
    width = value.shape[1]
    first = (lanes(*value.shape) // step) % 2 == 0
    return value + jnp.where(first, pltpu.roll(value, width - step, 1), pltpu.roll(value, step, 1))


def across(value, step):
    rows, width = value.shape
    return (
        pltpu.roll(value, 1, 0)
        + pltpu.roll(value, rows - 1, 0)
        + pltpu.roll(value, step, 1)
        + pltpu.roll(value, width - step, 1)
    )


def row_pairs(buffer, value):
    rows = value.shape[0]
    parts = []
    for half in range(2):
        buffer[half, 0:rows, :] = value[:, half * COLS : (half + 1) * COLS]
        parts.append(
            buffer[half, pl.ds(0, rows // 2, stride=2), :] + buffer[half, pl.ds(1, rows // 2, stride=2), :]
        )
    return jnp.concatenate(parts, axis=1)


def row_repeat(buffer, value):
    rows = value.shape[0]
    parts = []
    for half in range(2):
        part = value[:, half * COLS : (half + 1) * COLS]
        buffer[half, pl.ds(0, rows, stride=2), :] = part
        buffer[half, pl.ds(1, rows, stride=2), :] = part
        parts.append(buffer[half, 0 : 2 * rows, :])
    return jnp.concatenate(parts, axis=1)


def pick(table_row, index):
    rows, width = index.shape
    table = jnp.broadcast_to(table_row, (rows, COLS))
    parts = [
        jnp.take_along_axis(table, index[:, start : start + COLS], axis=1)
        for start in range(0, width, COLS)
    ]
    return parts[0] if len(parts) == 1 else jnp.concatenate(parts, axis=1)


def pack_halves(first, second):
    left = lanes(*first.shape) < HALF
    low = jnp.where(left, first, pltpu.roll(second, HALF, 1))
    high = jnp.where(left, pltpu.roll(first, HALF, 1), second)
    return low, high


def unpack_halves(from_right, from_left):
    left = lanes(*from_right.shape) < HALF
    first = jnp.where(left, from_right, pltpu.roll(from_left, HALF, 1))
    second = jnp.where(left, pltpu.roll(from_right, HALF, 1), from_left)
    return first, second


def pack_sea(fields):
    rows, width = fields[0].shape
    even_lane = lanes(rows, width) % 2 == 0
    even_row = sublanes(rows, width) % 2 == 0
    pairs = [
        jnp.where(even_lane, fields[i], pltpu.roll(fields[i + 1], 1, 1)) for i in (0, 2)
    ]
    return jnp.where(even_row, pairs[0], pltpu.roll(pairs[1], 1, 0))


def unpack_sea(packed):
    rows, width = packed.shape
    spot = (lanes(rows, width) % 2 == 0) & (sublanes(rows, width) % 2 == 0)
    fields = []
    for pair in (packed, pltpu.roll(packed, rows - 1, 0)):
        for field in (pair, pltpu.roll(pair, width - 1, 1)):
            fields.append(jnp.where(spot, field, 1.0))
    return fields


def fill_message(message, rhs, classes, sea, start, edge):
    def fields(z):
        for i in range(2):
            message[2 * z + i] = rhs(z, i)[pl.ds(start, 8), :]
        message[32 + z] = classes.at[z][pl.ds(start, 8), :]
        message.at[52 + z // 8][pl.ds(z % 8, 1), :] = classes.at[z][pl.ds(edge, 1), :]
        message.at[54 + z // 8][pl.ds(z % 8, 1), :] = sea.at[z][pl.ds(edge, 1), :]

    loop(NZ, fields)

    def quads(j):
        message[48 + j] = pack_sea([sea[4 * j + i, pl.ds(start, 8), :] for i in range(4)])

    loop(4, quads)


MSG_Y = 26
MSG_X = 56


def start_kernel(place, rhs_in, classes_in, sea_in, rhs, classes, sea, to_left, to_right, message, classes_int, sea_int, sems):
    core = place[0]
    copies = [
        pltpu.make_async_copy(source, target, sems.at[i])
        for i, (source, target) in enumerate(((classes_in, classes_int), (sea_in, sea_int), (rhs_in, rhs)))
    ]
    for copy in copies:
        copy.start()
    copies[0].wait()
    copies[1].wait()

    def convert(pair):
        for z in (2 * pair, 2 * pair + 1):
            classes[z] = classes_int[z].astype(F32)
            sea[z] = sea_int[z].astype(F32)
        to_left[16 + pair], to_right[16 + pair] = pack_halves(classes[2 * pair], classes[2 * pair + 1])

    loop(8, convert)
    for j in range(2):
        quads = [pack_sea([sea[8 * j + 4 * q + i] for i in range(4)]) for q in range(2)]
        to_left[24 + j], to_right[24 + j] = pack_halves(quads[0], quads[1])
    copies[2].wait()

    def pair(z):
        to_left[z], to_right[z] = pack_halves(rhs[0, z], rhs[1, z])

    loop(NZ, pair)
    start = pl.multiple_of(8 * core, 8)
    fill_message(message, lambda z, i: rhs.at[i, z], classes, sea, start, 8 - core)


def corner_kernel(message, to_left, to_right):
    def pair(p):
        to_left[p], to_right[p] = pack_halves(message[2 * p], message[2 * p + 1])

    loop(MSG_X // 2, pair)


def rows_kernel(place, rhs, classes, sea, from_left, from_right, after, r_out, c_out, s_out, message):
    core = place[0]
    gy = place[2]
    left = lanes(ROWS, COLS) < HALF
    inside = jnp.where(
        left,
        jnp.where(gy < place[4] - 1, 1.0, 0.0),
        jnp.where(gy > 0, 1.0, 0.0),
    )

    def rhs_step(z):
        halo = unpack_halves(from_right[z], from_left[z])
        for i in range(2):
            r_out[z, i] = jnp.concatenate([rhs[i, z], halo[i]], axis=1)

    loop(NZ, rhs_step)

    def class_step(pair):
        for i, halo in enumerate(unpack_halves(from_right[16 + pair], from_left[16 + pair])):
            c_out[2 * pair + i] = jnp.concatenate([classes[2 * pair + i], halo], axis=1)

    loop(8, class_step)
    for j in range(2):
        quads = unpack_halves(from_right[24 + j], from_left[24 + j])
        for q in range(2):
            for i, field in enumerate(unpack_sea(quads[q])):
                z = 8 * j + 4 * q + i
                s_out[z] = jnp.concatenate([sea[z], field * inside], axis=1)
    start = pl.multiple_of(8 * (1 - core), 8)
    fill_message(message, lambda z, i: r_out.at[z, i], c_out, s_out, start, 7 + core)


def material_kernel(c_in, s_in, table, g_out, h_out, k_out, packed, buffer):
    def fields(z):
        index = c_in[z].astype(jnp.int32)
        sea = s_in[z]
        g = pick(table[0:1], index) * sea
        h = pick(table[1:2], index) * sea
        k = pick(table[2:3], index) * sea + (1.0 - sea)
        g_out[z] = g
        h_out[z] = h
        k_out[z] = k
        return g * g, h * h, k

    even = lanes(8, WIDE) % 2 == 0

    def coarse(pair):
        first = fields(2 * pair)
        second = fields(2 * pair + 1)
        return [
            lane_sum(row_pairs(buffer.at[i], first[i] + second[i]), 1) for i in range(3)
        ]

    def step(j):
        near = coarse(j)
        far = coarse(j + 4)
        packed[j] = jnp.where(even, 0.125 * near[0], 0.125 * near[1])
        packed[j + 4] = jnp.where(even, 0.125 * far[0], 0.125 * far[1])
        packed[j + 8] = jnp.where(even, near[2], far[2])

    loop(4, step)


def unpack_lanes(packed):
    even = lanes(*packed.shape) % 2 == 0
    width = packed.shape[1]
    return (
        jnp.where(even, packed, pltpu.roll(packed, 1, 1)),
        jnp.where(even, pltpu.roll(packed, width - 1, 1), packed),
    )


class Level:
    def __init__(self, depth, step, g, h, inverse, diagonal=None):
        self.depth, self.step = depth, step
        self.g, self.h, self.inverse, self.diagonal = g, h, inverse, diagonal

    def couple(self, x, z, i):
        horizontal = self.g[z] * across(self.g[z] * x[z + 1, i], self.step)
        vertical = self.h[z + 1] * (self.h[z] * x[z, i] + self.h[z + 2] * x[z + 2, i])
        return horizontal + vertical

    def first(self, x, r, weight):
        def body(z):
            scaled = weight * self.inverse[z]
            for i in range(2):
                x[z + 1, i] = scaled * r[z, i]

        loop(self.depth, body)

    def update(self, new, x, r, weight):
        def body(z):
            scaled = weight * self.inverse[z]
            for i in range(2):
                new[z + 1, i] = (1.0 - weight) * x[z + 1, i] + scaled * (r[z, i] + self.couple(x, z, i))

        loop(self.depth, body)

    def defect(self, x, r, z, i):
        return r[z, i] - self.diagonal[z] * x[z + 1, i] + self.couple(x, z, i)

    def diagonal_of(self, k, z):
        horizontal = self.g[z] * across(self.g[z], self.step)
        vertical = self.h[z + 1] * (self.h[z] + self.h[z + 2])
        return k + horizontal + vertical


def clear_ends(*refs):
    for ref in refs:
        ref[0] = jnp.zeros(ref.shape[1:], ref.dtype)
        ref[ref.shape[0] - 1] = jnp.zeros(ref.shape[1:], ref.dtype)


def fine_restrict(level, x, r, buffer, out):
    even = lanes(8, WIDE) % 2 == 0

    def body(pair):
        sums = []
        for i in range(2):
            total = level.defect(x, r, 2 * pair, i) + level.defect(x, r, 2 * pair + 1, i)
            sums.append(lane_sum(row_pairs(buffer.at[i], total[8:24]), 1))
        out[pair] = jnp.where(even, sums[0], sums[1])

    loop(NZ // 2, body)


def down_kernel(
    place, r_own, g_own, h_own, k_own, from_x, from_o, corner_left, corner_right, table, after,
    r, g, h, d, inverse, xp, r1, xa, ka, wide, edges, buffer,
):
    core = place[0]
    gx = place[1]
    gy = place[2]
    open_side = jnp.where((gx > 0) & (gx < place[3] - 1), 1.0, 0.0)
    lane = lanes(8, WIDE)
    ends = jnp.where(
        lane < COLS,
        1.0,
        jnp.where(lane < COLS + HALF, jnp.where(gy < place[4] - 1, 1.0, 0.0), jnp.where(gy > 0, 1.0, 0.0)),
    )
    clear_ends(h, xp, xa)

    def own(z):
        for i in range(2):
            r[z, i, 8:24, :] = r_own[z, i]
        g[z, 8:24, :] = g_own[z]
        h[z + 1, 8:24, :] = h_own[z]
        ka[z, 8:24, :] = k_own[z]

    loop(NZ, own)

    def widen(p):
        for i, halo in enumerate(unpack_halves(corner_right[p], corner_left[p])):
            wide[2 * p + i] = jnp.concatenate([from_o[2 * p + i], halo], axis=1)

    loop(MSG_X // 2, widen)
    for message, start, scale, slot in ((from_x, 24 * (1 - core), 1.0, 1 - core), (wide, 24 * core, open_side, core)):
        start = pl.multiple_of(start, 8)
        valid = scale * ends

        def halo(j, message=message, start=start, valid=valid):
            for q, sea in enumerate(unpack_sea(message[48 + j])):
                z = 4 * j + q
                sea = sea * valid
                index = message[32 + z].astype(jnp.int32)
                g[z, pl.ds(start, 8), :] = pick(table[0:1], index) * sea
                h[z + 1, pl.ds(start, 8), :] = pick(table[1:2], index) * sea
                ka[z, pl.ds(start, 8), :] = pick(table[2:3], index) * sea + (1.0 - sea)
                for i in range(2):
                    r[z, i, pl.ds(start, 8), :] = message[2 * z + i]

        loop(4, halo)
        for j in range(2):
            index = message[52 + j].astype(jnp.int32)
            edges[slot, 8 * j : 8 * j + 8, :] = pick(table[0:1], index) * (message[54 + j] * valid)

    level = Level(NZ, 1, g, h, inverse, d)
    row = sublanes(EXT0, WIDE)

    def diagonals(z):
        here = g[z]
        below = jnp.where(row == 0, edges[0, pl.ds(z, 1), :], pltpu.roll(here, 1, 0))
        above = jnp.where(row == EXT0 - 1, edges[1, pl.ds(z, 1), :], pltpu.roll(here, EXT0 - 1, 0))
        beside = pltpu.roll(here, 1, 1) + pltpu.roll(here, WIDE - 1, 1)
        total = ka[z] + here * (below + above + beside) + h[z + 1] * (h[z] + h[z + 2])
        d[z] = total
        inverse[z] = 1.0 / total

    loop(NZ, diagonals)
    level.first(xa, r, FINE[0])
    level.update(xp, xa, r, FINE[1])
    fine_restrict(level, xp, r, buffer, r1)


def coarse_coefficients(core, pieces, g1, h1, d1, i1, g2, h2, i2, w1, k1, u1, k2, buffer):
    clear_ends(h1, h2)

    def store(j, start, tile):
        first, second = unpack_lanes(tile)
        w1[j, pl.ds(start, 8), :] = first
        u1[j, pl.ds(start, 8), :] = second

    def store_k(j, start, tile):
        first, second = unpack_lanes(tile)
        k1[j, pl.ds(start, 8), :] = jnp.where(first == 0.0, 1.0, first)
        k1[j + 4, pl.ds(start, 8), :] = jnp.where(second == 0.0, 1.0, second)

    own, partner, odd, far = pieces
    starts = (16, 24 - 16 * core, 8 + 16 * core, 32 * core, 32 - 32 * core)
    starts = [s if isinstance(s, int) else pl.multiple_of(s, 8) for s in starts]

    def crosswise(j):
        for start, tile in zip(starts, (own[j], partner[j], odd[j], odd[12 + j], far[j])):
            store(j, start, tile)

    loop(8, crosswise)

    def masses(j):
        tiles = (own[8 + j], partner[8 + j], odd[8 + j], odd[20 + j], far[8 + j])
        for start, tile in zip(starts, tiles):
            store_k(j, start, tile)

    loop(4, masses)

    def roots(z):
        g1[z] = 2.0 * jnp.sqrt(w1[z])
        h1[z + 1] = 2.0 * jnp.sqrt(u1[z])

    loop(8, roots)
    one = Level(8, 2, g1, h1, i1, d1)

    def diagonals(z):
        total = one.diagonal_of(k1[z], z)
        d1[z] = total
        i1[z] = 1.0 / total

    loop(8, diagonals)

    def coarser(z):
        sums = [
            lane_sum(row_pairs(buffer.at[i], field[2 * z] + field[2 * z + 1]), 2)
            for i, field in enumerate((w1, u1, k1))
        ]
        blank = jnp.zeros((4, WIDE), F32)
        g2[z] = jnp.concatenate([2.0 * jnp.sqrt(0.125 * sums[0]), blank], axis=0)
        h2[z + 1] = jnp.concatenate([2.0 * jnp.sqrt(0.125 * sums[1]), blank], axis=0)
        k2[z] = jnp.concatenate([sums[2], blank + 1.0], axis=0)

    loop(4, coarser)
    two = Level(4, 4, g2, h2, i2)

    def diagonals_two(z):
        i2[z] = 1.0 / two.diagonal_of(k2[z], z)

    loop(4, diagonals_two)


def coarse_solve(core, one, two, pieces, r1, xa1, xb1, r2, xa2, xb2, buffer):
    own, partner, odd, far = pieces
    clear_ends(xa1, xb1, xa2, xb2)
    starts = (16, 24 - 16 * core, 8 + 16 * core, 32 * core, 32 - 32 * core)
    starts = [s if isinstance(s, int) else pl.multiple_of(s, 8) for s in starts]

    def assemble(z):
        tiles = (own[z], partner[z], odd[z], odd[8 + z], far[z])
        for start, tile in zip(starts, tiles):
            for i, field in enumerate(unpack_lanes(tile)):
                r1[z, i, pl.ds(start, 8), :] = field

    loop(8, assemble)
    one.first(xa1, r1, FINE[0])
    one.update(xb1, xa1, r1, FINE[1])

    def restrict(z):
        for i in range(2):
            total = one.defect(xb1, r1, 2 * z, i) + one.defect(xb1, r1, 2 * z + 1, i)
            sums = lane_sum(row_pairs(buffer.at[i], total), 2)
            r2[z, i] = jnp.concatenate([sums, jnp.zeros((4, WIDE), F32)], axis=0)

    loop(4, restrict)
    two.first(xa2, r2, COARSE[0])
    two.update(xb2, xa2, r2, COARSE[1])
    two.update(xa2, xb2, r2, COARSE[2])
    two.update(xb2, xa2, r2, COARSE[3])

    def prolong(z):
        for i in range(2):
            fine = row_repeat(buffer.at[i], xb2[z + 1, i, 0:20, :])
            for half in range(2):
                xa1[2 * z + half + 1, i] = xb1[2 * z + half + 1, i] + fine

    loop(4, prolong)
    one.update(xb1, xa1, r1, FINE[0])
    one.update(xa1, xb1, r1, FINE[1])


def fine_correct(level, out, xp, c1, buffer):
    def body(pair):
        for i in range(2):
            fine = row_repeat(buffer.at[i], c1[pair + 1, i, 12:28, :])
            for half in range(2):
                out[2 * pair + half + 1, i] = xp[2 * pair + half + 1, i] + fine

    loop(NZ // 2, body)


def coarse_kernel(
    place, own, partner, odd, far, g1, h1, d1, i1, g2, h2, i2, w1, k1, u1, k2, buffer
):
    coarse_coefficients(
        place[0], (own, partner, odd, far), g1, h1, d1, i1, g2, h2, i2, w1, k1, u1, k2, buffer
    )


def middle_kernel(
    place, r, g, h, d, inverse, xp, own, partner, odd, far, g1, h1, d1, i1, g2, h2, i2,
    z_out, xp_out, r1_out,
    xa, xb, r1, xa1, xb1, r2, xa2, xb2, buffer,
):
    core = place[0]
    zero = Level(NZ, 1, g, h, inverse, d)
    one = Level(8, 2, g1, h1, i1, d1)
    two = Level(4, 4, g2, h2, i2)
    coarse_solve(core, one, two, (own, partner, odd, far), r1, xa1, xb1, r2, xa2, xb2, buffer)
    clear_ends(xa, xb, xp_out)
    fine_correct(zero, xa, xp, xa1, buffer)
    zero.update(xb, xa, r, FINE[0])

    def last(z):
        scaled = FINE[1] * inverse[z]
        for i in range(2):
            z_out[z, i] = (1.0 - FINE[1]) * xb[z + 1, i] + scaled * (r[z, i] + zero.couple(xb, z, i))

    loop(NZ, last)
    zero.first(xa, z_out, FINE[0])
    zero.update(xp_out, xa, z_out, FINE[1])
    fine_restrict(zero, xp_out, z_out, buffer, r1_out)


def last_kernel(
    place, rhs, r, g, h, d, inverse, xp, own, partner, odd, far, g1, h1, d1, i1, g2, h2, i2,
    direction, image, sums,
    xa, xb, r1, xa1, xb1, r2, xa2, xb2, totals, buffer,
):
    core = place[0]
    zero = Level(NZ, 1, g, h, inverse, d)
    one = Level(8, 2, g1, h1, i1, d1)
    two = Level(4, 4, g2, h2, i2)
    coarse_solve(core, one, two, (own, partner, odd, far), r1, xa1, xb1, r2, xa2, xb2, buffer)
    clear_ends(xa, xb)
    fine_correct(zero, xa, xp, xa1, buffer)
    zero.update(xb, xa, r, FINE[0])
    zero.update(xa, xb, r, FINE[1])

    def first_image(z):
        for i in range(2):
            xb[z + 1, i] = d[z] * xa[z + 1, i] - zero.couple(xa, z, i)

    loop(NZ, first_image)
    totals[...] = jnp.zeros(totals.shape, F32)

    def second_image(z):
        for i in range(2):
            field = xa[z + 1, i, 8:24, 0:COLS]
            value = (d[z] * xb[z + 1, i] - zero.couple(xb, z, i))[8:24, 0:COLS]
            direction[i, z] = field
            image[i, z] = value
            totals[i] += rhs[i, z] * field
            totals[2 + i] += field * value

    loop(NZ, second_image)
    row = sublanes(8, COLS)
    lane = lanes(8, COLS)
    line = jnp.zeros((8, COLS), F32)
    for i in range(4):
        line = jnp.where(lane == i, jnp.sum(totals[i]), line)

    def spread(j):
        sums[pl.ds(pl.multiple_of(8 * j, 8), 8), :] = line

    loop(sums.shape[0] // 8, spread)


def scale_kernel(rhs, direction, image, sums, solution_field, residual):
    total = jnp.sum(sums[...], axis=0, keepdims=True)
    lane = lanes(1, COLS)
    parts = [jnp.sum(jnp.where(lane == i, total, 0.0), axis=1, keepdims=True) for i in range(4)]
    for i in range(2):
        alpha = parts[i] / parts[2 + i]

        def body(z, i=i, alpha=alpha):
            solution_field[i, z] = alpha * direction[i, z]
            residual[i, z] = rhs[i, z] - alpha * image[i, z]

        loop(NZ, body)


COSTS = {
    "start_kernel": 3,
    "corner_kernel": 1,
    "rows_kernel": 3,
    "material_kernel": 2,
    "down_kernel": 5,
    "coarse_kernel": 3,
    "middle_kernel": 9,
    "last_kernel": 9,
    "scale_kernel": 1,
}


def call(kernel, operands, outs, scratch=(), place=True, far=None):
    far = far or {}
    vmem = pl.BlockSpec(memory_space=pltpu.VMEM)
    specs = [pl.BlockSpec(memory_space=far[i]) if i in far else vmem for i in range(len(operands))]
    if place:
        specs[0] = pl.BlockSpec(memory_space=pltpu.SMEM)
    return pl.pallas_call(
        kernel,
        out_shape=[jax.ShapeDtypeStruct(shape, F32) for shape in outs],
        in_specs=specs,
        out_specs=[vmem] * len(outs),
        scratch_shapes=[pltpu.VMEM(shape, F32) if isinstance(shape, tuple) else shape for shape in scratch],
        cost_estimate=pl.CostEstimate(
            flops=COSTS[kernel.__name__] * 1_000_000_000, bytes_accessed=COSTS[kernel.__name__] * 3_000_000, transcendentals=0
        ),
        compiler_params=pltpu.CompilerParams(vmem_limit_bytes=16 * 1024 * 1024),
    )(*operands)


FIELD0 = (NZ, 2, EXT0, WIDE)
PADDED0 = (NZ + 2, 2, EXT0, WIDE)
PADDED1 = (10, 2, EXT1, WIDE)
PADDED2 = (6, 2, EXT2, WIDE)
BUFFER = (3, 2, EXT1, COLS)
COARSE_SCRATCH = [(8, 2, EXT1, WIDE), PADDED1, PADDED1, (4, 2, EXT2, WIDE), PADDED2, PADDED2]


def shards(count_x, count_y, right_side, classes, sea_mask, kappa_table, cross_table, vertical_table):
    gx = lax.axis_index("gx")
    gy = lax.axis_index("gy")
    place = jnp.stack([gx % 2, gx, gy, jnp.int32(count_x), jnp.int32(count_y)]).astype(jnp.int32)
    table = jnp.stack([jnp.sqrt(cross_table), jnp.sqrt(vertical_table), kappa_table])
    table = jnp.pad(table, ((0, 5), (0, COLS - table.shape[1])))

    pairs_on_chip = [(i, i ^ 1) for i in range(count_x)]
    pairs_across = [(i, i + 1 if i % 2 else i - 1) for i in range(1, count_x - 1)]

    def on_chip(value):
        return lax.ppermute(value, "gx", pairs_on_chip)

    def across_chips(value):
        return lax.ppermute(value, "gx", pairs_across)

    def with_partner(own):
        partner = on_chip(own)
        return own, partner, jnp.concatenate([own, partner], axis=0)

    def with_neighbours(own, partner, both):
        odd = across_chips(both)
        return own, partner, odd, on_chip(odd[: own.shape[0]])

    def three_steps(own):
        return with_neighbours(*with_partner(own))

    forward = [(i, i + 1) for i in range(count_y - 1)]
    backward = [(i + 1, i) for i in range(count_y - 1)]

    def both_sides(to_left, to_right):
        return lax.ppermute(to_right, "gy", forward), lax.ppermute(to_left, "gy", backward)

    block = (NZ, ROWS, COLS)
    rhs, classes, sea, to_left, to_right, msg_o = call(
        start_kernel,
        (place, right_side, classes, sea_mask),
        [(2, *block), block, block, (MSG_Y, ROWS, COLS), (MSG_Y, ROWS, COLS), (MSG_X, 8, COLS)],
        [pltpu.VMEM(block, jnp.int32), pltpu.VMEM(block, jnp.int32), pltpu.SemaphoreType.DMA((3,))],
        far={1: pltpu.HBM, 2: pltpu.HBM, 3: pltpu.HBM},
    )
    from_o = across_chips(msg_o)
    from_left, from_right = both_sides(to_left, to_right)
    corner_tiles = call(corner_kernel, (from_o,), [(MSG_X // 2, 8, COLS)] * 2, place=False)
    corners = both_sides(*corner_tiles)
    r_own, c_own, s_own, msg_x = call(
        rows_kernel,
        (place, rhs, classes, sea, from_left, from_right, corner_tiles[0]),
        [(NZ, 2, ROWS, WIDE), (NZ, ROWS, WIDE), (NZ, ROWS, WIDE), (MSG_X, 8, WIDE)],
        far={6: pl.ANY},
    )
    from_x = on_chip(msg_x)
    g_own, h_own, k_own, packed = call(
        material_kernel,
        (c_own, s_own, table),
        [(NZ, ROWS, WIDE)] * 3 + [(12, 8, WIDE)],
        [BUFFER],
        place=False,
    )
    material = with_partner(packed)
    r, g, h, d, inverse, xp, r1 = call(
        down_kernel,
        (place, r_own, g_own, h_own, k_own, from_x, from_o, *corners, table, material[2]),
        [FIELD0, (NZ, EXT0, WIDE), (NZ + 2, EXT0, WIDE), (NZ, EXT0, WIDE), (NZ, EXT0, WIDE), PADDED0, (8, 8, WIDE)],
        [PADDED0, (NZ, EXT0, WIDE), (MSG_X, 8, WIDE), (2, NZ, WIDE), BUFFER],
        far={10: pl.ANY},
    )
    material = with_neighbours(*material)
    one = [(8, EXT1, WIDE), (10, EXT1, WIDE), (8, EXT1, WIDE), (8, EXT1, WIDE)]
    two = [(4, EXT2, WIDE), (6, EXT2, WIDE), (4, EXT2, WIDE)]
    coarse = call(
        coarse_kernel, (place, *material), [*one, *two], [one[0], one[0], one[0], two[0], BUFFER]
    )
    r, xp, r1 = call(
        middle_kernel,
        (place, r, g, h, d, inverse, xp, *three_steps(r1), *coarse),
        [FIELD0, PADDED0, (8, 8, WIDE)],
        [PADDED0, PADDED0, *COARSE_SCRATCH, BUFFER],
    )
    count = count_x * count_y
    direction, image, sums = call(
        last_kernel,
        (place, rhs, r, g, h, d, inverse, xp, *three_steps(r1), *coarse),
        [(2, NZ, ROWS, COLS)] * 2 + [(count, COLS)],
        [PADDED0, PADDED0, *COARSE_SCRATCH, (4, ROWS, COLS), BUFFER],
    )
    sums = lax.all_to_all(sums.reshape(count, 1, COLS), ("gx", "gy"), 0, 0).reshape(count, COLS)
    return tuple(
        call(
            scale_kernel,
            (rhs, direction, image, sums),
            [(2, NZ, ROWS, COLS)] * 2,
            place=False,
        )
    )


def solution(mesh):
    return jax.shard_map(
        functools.partial(shards, mesh.shape["gx"], mesh.shape["gy"]),
        mesh=mesh,
        in_specs=(
            P(None, None, "gx", "gy"),
            P(None, "gx", "gy"),
            P(None, "gx", "gy"),
            P(),
            P(),
            P(),
        ),
        out_specs=(P(None, None, "gx", "gy"), P(None, None, "gx", "gy")),
        check_vma=False,
    )
```

```python
import functools
import math

import jax
import jax.numpy as jnp
from jax import lax
from jax.experimental import pallas as pl
from jax.experimental.pallas import tpu as pltpu
from jax.sharding import PartitionSpec as P

F32 = jnp.float32
NZ = 16
ROWS = 16
COLS = 128
WIDE = 256
HALF = 64
UNROLL = 8
EXT0 = 32
EXT1 = 40
EXT2 = 24


def cheb_weights(degree, lower_end, upper_end):
    middle = 0.5 * (upper_end + lower_end)
    radius = 0.5 * (upper_end - lower_end)
    return [
        1.0 / (middle + radius * math.cos(math.pi * (2 * index_k + 1) / (2 * degree)))
        for index_k in range(degree)
    ]


FINE = cheb_weights(2, 0.3, 2.0)
COARSE = cheb_weights(4, 0.1, 2.0)


def loop(count, body):
    def step(index, carry):
        body(index)
        return carry

    lax.fori_loop(0, count, step, 0, unroll=min(count, UNROLL))


def lanes(rows, width):
    return lax.broadcasted_iota(jnp.int32, (rows, width), 1)


def sublanes(rows, width):
    return lax.broadcasted_iota(jnp.int32, (rows, width), 0)


def lane_sum(value, step):
    width = value.shape[1]
    first = (lanes(*value.shape) // step) % 2 == 0
    return value + jnp.where(first, pltpu.roll(value, width - step, 1), pltpu.roll(value, step, 1))


def across(value, step):
    rows, width = value.shape
    return (
        pltpu.roll(value, 1, 0)
        + pltpu.roll(value, rows - 1, 0)
        + pltpu.roll(value, step, 1)
        + pltpu.roll(value, width - step, 1)
    )


def row_pairs(buffer, value):
    rows = value.shape[0]
    parts = []
    for half in range(2):
        buffer[half, 0:rows, :] = value[:, half * COLS : (half + 1) * COLS]
        parts.append(
            buffer[half, pl.ds(0, rows // 2, stride=2), :] + buffer[half, pl.ds(1, rows // 2, stride=2), :]
        )
    return jnp.concatenate(parts, axis=1)


def row_repeat(buffer, value):
    rows = value.shape[0]
    parts = []
    for half in range(2):
        part = value[:, half * COLS : (half + 1) * COLS]
        buffer[half, pl.ds(0, rows, stride=2), :] = part
        buffer[half, pl.ds(1, rows, stride=2), :] = part
        parts.append(buffer[half, 0 : 2 * rows, :])
    return jnp.concatenate(parts, axis=1)


def pick(table_row, index):
    rows, width = index.shape
    table = jnp.broadcast_to(table_row, (rows, COLS))
    parts = [
        jnp.take_along_axis(table, index[:, start : start + COLS], axis=1)
        for start in range(0, width, COLS)
    ]
    return parts[0] if len(parts) == 1 else jnp.concatenate(parts, axis=1)


def pack_halves(first, second):
    left = lanes(*first.shape) < HALF
    low = jnp.where(left, first, pltpu.roll(second, HALF, 1))
    high = jnp.where(left, pltpu.roll(first, HALF, 1), second)
    return low, high


def unpack_halves(from_right, from_left):
    left = lanes(*from_right.shape) < HALF
    first = jnp.where(left, from_right, pltpu.roll(from_left, HALF, 1))
    second = jnp.where(left, pltpu.roll(from_right, HALF, 1), from_left)
    return first, second


def pack_sea(fields):
    rows, width = fields[0].shape
    even_lane = lanes(rows, width) % 2 == 0
    even_row = sublanes(rows, width) % 2 == 0
    pairs = [
        jnp.where(even_lane, fields[i], pltpu.roll(fields[i + 1], 1, 1)) for i in (0, 2)
    ]
    return jnp.where(even_row, pairs[0], pltpu.roll(pairs[1], 1, 0))


def unpack_sea(packed):
    rows, width = packed.shape
    spot = (lanes(rows, width) % 2 == 0) & (sublanes(rows, width) % 2 == 0)
    fields = []
    for pair in (packed, pltpu.roll(packed, rows - 1, 0)):
        for field in (pair, pltpu.roll(pair, width - 1, 1)):
            fields.append(jnp.where(spot, field, 1.0))
    return fields


def fill_message(message, rhs, classes, sea, start, edge):
    def fields(z):
        for i in range(2):
            message[2 * z + i] = rhs(z, i)[pl.ds(start, 8), :]
        message[32 + z] = classes.at[z][pl.ds(start, 8), :]
        message.at[52 + z // 8][pl.ds(z % 8, 1), :] = classes.at[z][pl.ds(edge, 1), :]
        message.at[54 + z // 8][pl.ds(z % 8, 1), :] = sea.at[z][pl.ds(edge, 1), :]

    loop(NZ, fields)

    def quads(j):
        message[48 + j] = pack_sea([sea[4 * j + i, pl.ds(start, 8), :] for i in range(4)])

    loop(4, quads)


MSG_Y = 26
MSG_X = 56


def start_kernel(place, fields, to_left, to_right, message):
    core = place[0]
    classes, sea = fields.at[2], fields.at[3]

    def convert(pair):
        to_left[16 + pair], to_right[16 + pair] = pack_halves(classes[2 * pair], classes[2 * pair + 1])

    loop(8, convert)
    for j in range(2):
        quads = [pack_sea([sea[8 * j + 4 * q + i] for i in range(4)]) for q in range(2)]
        to_left[24 + j], to_right[24 + j] = pack_halves(quads[0], quads[1])

    def pair(z):
        to_left[z], to_right[z] = pack_halves(fields[0, z], fields[1, z])

    loop(NZ, pair)
    start = pl.multiple_of(8 * core, 8)
    fill_message(message, lambda z, i: fields.at[i, z], classes, sea, start, 8 - core)


def corner_kernel(message, to_left, to_right):
    def pair(p):
        to_left[p], to_right[p] = pack_halves(message[2 * p], message[2 * p + 1])

    loop(MSG_X // 2, pair)


def rows_kernel(place, fields, from_left, from_right, after, r_out, c_out, s_out, message):
    core = place[0]
    gy = place[2]
    left = lanes(ROWS, COLS) < HALF
    inside = jnp.where(
        left,
        jnp.where(gy < place[4] - 1, 1.0, 0.0),
        jnp.where(gy > 0, 1.0, 0.0),
    )

    def rhs_step(z):
        halo = unpack_halves(from_right[z], from_left[z])
        for i in range(2):
            r_out[z, i] = jnp.concatenate([fields[i, z], halo[i]], axis=1)

    loop(NZ, rhs_step)

    def class_step(pair):
        for i, halo in enumerate(unpack_halves(from_right[16 + pair], from_left[16 + pair])):
            c_out[2 * pair + i] = jnp.concatenate([fields[2, 2 * pair + i], halo], axis=1)

    loop(8, class_step)
    for j in range(2):
        quads = unpack_halves(from_right[24 + j], from_left[24 + j])
        for q in range(2):
            for i, field in enumerate(unpack_sea(quads[q])):
                z = 8 * j + 4 * q + i
                s_out[z] = jnp.concatenate([fields[3, z], field * inside], axis=1)
    start = pl.multiple_of(8 * (1 - core), 8)
    fill_message(message, lambda z, i: r_out.at[z, i], c_out, s_out, start, 7 + core)


def material_kernel(c_in, s_in, table, g_out, h_out, k_out, packed, buffer):
    def fields(z):
        index = c_in[z].astype(jnp.int32)
        sea = s_in[z]
        g = pick(table[0:1], index) * sea
        h = pick(table[1:2], index) * sea
        k = pick(table[2:3], index) * sea + (1.0 - sea)
        g_out[z] = g
        h_out[z] = h
        k_out[z] = k
        return g * g, h * h, k

    even = lanes(8, WIDE) % 2 == 0

    def coarse(pair):
        first = fields(2 * pair)
        second = fields(2 * pair + 1)
        return [
            lane_sum(row_pairs(buffer.at[i], first[i] + second[i]), 1) for i in range(3)
        ]

    def step(j):
        near = coarse(j)
        far = coarse(j + 4)
        packed[j] = jnp.where(even, 0.125 * near[0], 0.125 * near[1])
        packed[j + 4] = jnp.where(even, 0.125 * far[0], 0.125 * far[1])
        packed[j + 8] = jnp.where(even, near[2], far[2])

    loop(4, step)


def unpack_lanes(packed):
    even = lanes(*packed.shape) % 2 == 0
    width = packed.shape[1]
    return (
        jnp.where(even, packed, pltpu.roll(packed, 1, 1)),
        jnp.where(even, pltpu.roll(packed, width - 1, 1), packed),
    )


class Level:
    def __init__(self, depth, step, g, h, inverse, diagonal=None):
        self.depth, self.step = depth, step
        self.g, self.h, self.inverse, self.diagonal = g, h, inverse, diagonal

    def couple(self, x, z, i):
        horizontal = self.g[z] * across(self.g[z] * x[z + 1, i], self.step)
        vertical = self.h[z + 1] * (self.h[z] * x[z, i] + self.h[z + 2] * x[z + 2, i])
        return horizontal + vertical

    def first(self, x, r, weight):
        def body(z):
            scaled = weight * self.inverse[z]
            for i in range(2):
                x[z + 1, i] = scaled * r[z, i]

        loop(self.depth, body)

    def update(self, new, x, r, weight):
        def body(z):
            scaled = weight * self.inverse[z]
            for i in range(2):
                new[z + 1, i] = (1.0 - weight) * x[z + 1, i] + scaled * (r[z, i] + self.couple(x, z, i))

        loop(self.depth, body)

    def defect(self, x, r, z, i):
        return r[z, i] - self.diagonal[z] * x[z + 1, i] + self.couple(x, z, i)

    def diagonal_of(self, k, z):
        horizontal = self.g[z] * across(self.g[z], self.step)
        vertical = self.h[z + 1] * (self.h[z] + self.h[z + 2])
        return k + horizontal + vertical


def clear_ends(*refs):
    for ref in refs:
        ref[0] = jnp.zeros(ref.shape[1:], ref.dtype)
        ref[ref.shape[0] - 1] = jnp.zeros(ref.shape[1:], ref.dtype)


def fine_restrict(level, x, r, buffer, out):
    even = lanes(8, WIDE) % 2 == 0

    def body(pair):
        sums = []
        for i in range(2):
            total = level.defect(x, r, 2 * pair, i) + level.defect(x, r, 2 * pair + 1, i)
            sums.append(lane_sum(row_pairs(buffer.at[i], total[8:24]), 1))
        out[pair] = jnp.where(even, sums[0], sums[1])

    loop(NZ // 2, body)


def down_kernel(
    place, r_own, g_own, h_own, k_own, from_x, from_o, corner_left, corner_right, table,
    r, g, h, d, inverse, xp, r1, xa, ka, wide, edges, buffer,
):
    core = place[0]
    gx = place[1]
    gy = place[2]
    open_side = jnp.where((gx > 0) & (gx < place[3] - 1), 1.0, 0.0)
    lane = lanes(8, WIDE)
    ends = jnp.where(
        lane < COLS,
        1.0,
        jnp.where(lane < COLS + HALF, jnp.where(gy < place[4] - 1, 1.0, 0.0), jnp.where(gy > 0, 1.0, 0.0)),
    )
    clear_ends(h, xp, xa)

    def own(z):
        for i in range(2):
            r[z, i, 8:24, :] = r_own[z, i]
        g[z, 8:24, :] = g_own[z]
        h[z + 1, 8:24, :] = h_own[z]
        ka[z, 8:24, :] = k_own[z]

    loop(NZ, own)

    def widen(p):
        for i, halo in enumerate(unpack_halves(corner_right[p], corner_left[p])):
            wide[2 * p + i] = jnp.concatenate([from_o[2 * p + i], halo], axis=1)

    loop(MSG_X // 2, widen)
    for message, start, scale, slot in ((from_x, 24 * (1 - core), 1.0, 1 - core), (wide, 24 * core, open_side, core)):
        start = pl.multiple_of(start, 8)
        valid = scale * ends

        def halo(j, message=message, start=start, valid=valid):
            for q, sea in enumerate(unpack_sea(message[48 + j])):
                z = 4 * j + q
                sea = sea * valid
                index = message[32 + z].astype(jnp.int32)
                g[z, pl.ds(start, 8), :] = pick(table[0:1], index) * sea
                h[z + 1, pl.ds(start, 8), :] = pick(table[1:2], index) * sea
                ka[z, pl.ds(start, 8), :] = pick(table[2:3], index) * sea + (1.0 - sea)
                for i in range(2):
                    r[z, i, pl.ds(start, 8), :] = message[2 * z + i]

        loop(4, halo)
        for j in range(2):
            index = message[52 + j].astype(jnp.int32)
            edges[slot, 8 * j : 8 * j + 8, :] = pick(table[0:1], index) * (message[54 + j] * valid)

    level = Level(NZ, 1, g, h, inverse, d)
    row = sublanes(EXT0, WIDE)

    def diagonals(z):
        here = g[z]
        below = jnp.where(row == 0, edges[0, pl.ds(z, 1), :], pltpu.roll(here, 1, 0))
        above = jnp.where(row == EXT0 - 1, edges[1, pl.ds(z, 1), :], pltpu.roll(here, EXT0 - 1, 0))
        beside = pltpu.roll(here, 1, 1) + pltpu.roll(here, WIDE - 1, 1)
        total = ka[z] + here * (below + above + beside) + h[z + 1] * (h[z] + h[z + 2])
        d[z] = total
        inverse[z] = 1.0 / total

    loop(NZ, diagonals)
    level.first(xa, r, FINE[0])
    level.update(xp, xa, r, FINE[1])
    fine_restrict(level, xp, r, buffer, r1)


def coarse_coefficients(place, pieces, g1, h1, d1, i1, g2, h2, i2, w1, k1, u1, k2, buffer):
    core = place[0]
    clear_ends(h1, h2)
    own, partner, odd, far = pieces
    low = jnp.where(place[1] >= 2, 1.0, 0.0)
    high = jnp.where(place[1] < place[3] - 2, 1.0, 0.0)
    near_side = jnp.where(core == 0, low, high)
    far_side = jnp.where(core == 0, high, low)
    scales = (1.0, 1.0, near_side, near_side, far_side)
    starts = (16, 24 - 16 * core, 8 + 16 * core, 32 * core, 32 - 32 * core)
    starts = [s if isinstance(s, int) else pl.multiple_of(s, 8) for s in starts]

    def crosswise(j):
        tiles = (own[j], partner[j], odd[j], odd[12 + j], far[j])
        for start, tile, scale in zip(starts, tiles, scales):
            first, second = unpack_lanes(tile)
            w1[j, pl.ds(start, 8), :] = first * scale
            u1[j, pl.ds(start, 8), :] = second * scale

    loop(8, crosswise)

    def masses(j):
        tiles = (own[8 + j], partner[8 + j], odd[8 + j], odd[20 + j], far[8 + j])
        for start, tile in zip(starts, tiles):
            k1[j, pl.ds(start, 8), :], k1[j + 4, pl.ds(start, 8), :] = unpack_lanes(tile)

    loop(4, masses)

    def roots(z):
        g1[z] = 2.0 * jnp.sqrt(w1[z])
        h1[z + 1] = 2.0 * jnp.sqrt(u1[z])

    loop(8, roots)
    one = Level(8, 2, g1, h1, i1, d1)

    def diagonals(z):
        total = one.diagonal_of(k1[z], z)
        d1[z] = total
        i1[z] = 1.0 / total

    loop(8, diagonals)

    def coarser(z):
        sums = [
            lane_sum(row_pairs(buffer.at[i], field[2 * z] + field[2 * z + 1]), 2)
            for i, field in enumerate((w1, u1, k1))
        ]
        blank = jnp.zeros((4, WIDE), F32)
        g2[z] = jnp.concatenate([2.0 * jnp.sqrt(0.125 * sums[0]), blank], axis=0)
        h2[z + 1] = jnp.concatenate([2.0 * jnp.sqrt(0.125 * sums[1]), blank], axis=0)
        k2[z] = jnp.concatenate([sums[2], blank + 1.0], axis=0)

    loop(4, coarser)
    two = Level(4, 4, g2, h2, i2)

    def diagonals_two(z):
        i2[z] = 1.0 / two.diagonal_of(k2[z], z)

    loop(4, diagonals_two)


def coarse_solve(core, one, two, pieces, r1, xa1, xb1, r2, xa2, xb2, buffer):
    own, partner, odd, far = pieces
    clear_ends(xa1, xb1, xa2, xb2)
    starts = (16, 24 - 16 * core, 8 + 16 * core, 32 * core, 32 - 32 * core)
    starts = [s if isinstance(s, int) else pl.multiple_of(s, 8) for s in starts]

    def assemble(z):
        tiles = (own[z], partner[z], odd[z], odd[8 + z], far[z])
        for start, tile in zip(starts, tiles):
            for i, field in enumerate(unpack_lanes(tile)):
                r1[z, i, pl.ds(start, 8), :] = field

    loop(8, assemble)
    one.first(xa1, r1, FINE[0])
    one.update(xb1, xa1, r1, FINE[1])

    def restrict(z):
        for i in range(2):
            total = one.defect(xb1, r1, 2 * z, i) + one.defect(xb1, r1, 2 * z + 1, i)
            sums = lane_sum(row_pairs(buffer.at[i], total), 2)
            r2[z, i] = jnp.concatenate([sums, jnp.zeros((4, WIDE), F32)], axis=0)

    loop(4, restrict)
    two.first(xa2, r2, COARSE[0])
    two.update(xb2, xa2, r2, COARSE[1])
    two.update(xa2, xb2, r2, COARSE[2])
    two.update(xb2, xa2, r2, COARSE[3])

    def prolong(z):
        for i in range(2):
            fine = row_repeat(buffer.at[i], xb2[z + 1, i, 0:20, :])
            for half in range(2):
                xa1[2 * z + half + 1, i] = xb1[2 * z + half + 1, i] + fine

    loop(4, prolong)
    one.update(xb1, xa1, r1, FINE[0])
    one.update(xa1, xb1, r1, FINE[1])


def fine_correct(level, out, xp, c1, buffer):
    def body(pair):
        for i in range(2):
            fine = row_repeat(buffer.at[i], c1[pair + 1, i, 12:28, :])
            for half in range(2):
                out[2 * pair + half + 1, i] = xp[2 * pair + half + 1, i] + fine

    loop(NZ // 2, body)


def coarse_kernel(
    place, own, partner, odd, far, g1, h1, d1, i1, g2, h2, i2, w1, k1, u1, k2, buffer
):
    coarse_coefficients(
        place, (own, partner, odd, far), g1, h1, d1, i1, g2, h2, i2, w1, k1, u1, k2, buffer
    )


def middle_kernel(
    place, r, g, h, d, inverse, xp, own, partner, odd, far, g1, h1, d1, i1, g2, h2, i2,
    z_out, xp_out, r1_out,
    xa, xb, r1, xa1, xb1, r2, xa2, xb2, buffer,
):
    core = place[0]
    zero = Level(NZ, 1, g, h, inverse, d)
    one = Level(8, 2, g1, h1, i1, d1)
    two = Level(4, 4, g2, h2, i2)
    coarse_solve(core, one, two, (own, partner, odd, far), r1, xa1, xb1, r2, xa2, xb2, buffer)
    clear_ends(xa, xb, xp_out)
    fine_correct(zero, xa, xp, xa1, buffer)
    zero.update(xb, xa, r, FINE[0])

    def last(z):
        scaled = FINE[1] * inverse[z]
        for i in range(2):
            z_out[z, i] = (1.0 - FINE[1]) * xb[z + 1, i] + scaled * (r[z, i] + zero.couple(xb, z, i))

    loop(NZ, last)
    zero.first(xa, z_out, FINE[0])
    zero.update(xp_out, xa, z_out, FINE[1])
    fine_restrict(zero, xp_out, z_out, buffer, r1_out)


def last_kernel(
    place, rhs, r, g, h, d, inverse, xp, own, partner, odd, far, g1, h1, d1, i1, g2, h2, i2,
    direction, image, sums,
    xa, xb, r1, xa1, xb1, r2, xa2, xb2, totals, buffer,
):
    core = place[0]
    zero = Level(NZ, 1, g, h, inverse, d)
    one = Level(8, 2, g1, h1, i1, d1)
    two = Level(4, 4, g2, h2, i2)
    coarse_solve(core, one, two, (own, partner, odd, far), r1, xa1, xb1, r2, xa2, xb2, buffer)
    clear_ends(xa, xb)
    fine_correct(zero, xa, xp, xa1, buffer)
    zero.update(xb, xa, r, FINE[0])
    zero.update(xa, xb, r, FINE[1])

    def first_image(z):
        for i in range(2):
            xb[z + 1, i] = d[z] * xa[z + 1, i] - zero.couple(xa, z, i)

    loop(NZ, first_image)
    totals[...] = jnp.zeros(totals.shape, F32)

    def second_image(z):
        for i in range(2):
            field = xa[z + 1, i, 8:24, 0:COLS]
            value = (d[z] * xb[z + 1, i] - zero.couple(xb, z, i))[8:24, 0:COLS]
            direction[i, z] = field
            image[i, z] = value
            totals[i] += rhs[i, z] * field
            totals[2 + i] += field * value

    loop(NZ, second_image)
    row = sublanes(8, COLS)
    lane = lanes(8, COLS)
    line = jnp.zeros((8, COLS), F32)
    for i in range(4):
        line = jnp.where(lane == i, jnp.sum(totals[i]), line)

    def spread(j):
        sums[pl.ds(pl.multiple_of(8 * j, 8), 8), :] = line

    loop(sums.shape[0] // 8, spread)


def scale_kernel(rhs, direction, image, sums, solution_field, residual):
    total = jnp.sum(sums[...], axis=0, keepdims=True)
    lane = lanes(1, COLS)
    parts = [jnp.sum(jnp.where(lane == i, total, 0.0), axis=1, keepdims=True) for i in range(4)]
    for i in range(2):
        alpha = parts[i] / parts[2 + i]

        def body(z, i=i, alpha=alpha):
            solution_field[i, z] = alpha * direction[i, z]
            residual[i, z] = rhs[i, z] - alpha * image[i, z]

        loop(NZ, body)


COSTS = {
    "start_kernel": 3,
    "corner_kernel": 1,
    "rows_kernel": 3,
    "material_kernel": 2,
    "down_kernel": 5,
    "coarse_kernel": 3,
    "middle_kernel": 9,
    "last_kernel": 9,
    "scale_kernel": 1,
}


def call(kernel, operands, outs, scratch=(), place=True, far=None):
    far = far or {}
    vmem = pl.BlockSpec(memory_space=pltpu.VMEM)
    specs = [pl.BlockSpec(memory_space=far[i]) if i in far else vmem for i in range(len(operands))]
    if place:
        specs[0] = pl.BlockSpec(memory_space=pltpu.SMEM)
    return pl.pallas_call(
        kernel,
        out_shape=[jax.ShapeDtypeStruct(shape, F32) for shape in outs],
        in_specs=specs,
        out_specs=[vmem] * len(outs),
        scratch_shapes=[pltpu.VMEM(shape, F32) if isinstance(shape, tuple) else shape for shape in scratch],
        cost_estimate=pl.CostEstimate(
            flops=COSTS[kernel.__name__] * 1_000_000_000, bytes_accessed=COSTS[kernel.__name__] * 3_000_000, transcendentals=0
        ),
        compiler_params=pltpu.CompilerParams(vmem_limit_bytes=16 * 1024 * 1024),
    )(*operands)


FIELD0 = (NZ, 2, EXT0, WIDE)
PADDED0 = (NZ + 2, 2, EXT0, WIDE)
PADDED1 = (10, 2, EXT1, WIDE)
PADDED2 = (6, 2, EXT2, WIDE)
BUFFER = (3, 2, EXT1, COLS)
COARSE_SCRATCH = [(8, 2, EXT1, WIDE), PADDED1, PADDED1, (4, 2, EXT2, WIDE), PADDED2, PADDED2]


def shards(count_x, count_y, right_side, classes, sea_mask, kappa_table, cross_table, vertical_table):
    gx = lax.axis_index("gx")
    gy = lax.axis_index("gy")
    place = jnp.stack([gx % 2, gx, gy, jnp.int32(count_x), jnp.int32(count_y)]).astype(jnp.int32)
    table = jnp.stack([jnp.sqrt(cross_table), jnp.sqrt(vertical_table), kappa_table])
    table = jnp.pad(table, ((0, 5), (0, COLS - table.shape[1])))

    pairs_on_chip = [(i, i ^ 1) for i in range(count_x)]
    pairs_across = [(i, (i + 1 if i % 2 else i - 1) % count_x) for i in range(count_x)]

    def on_chip(value):
        return lax.ppermute(value, "gx", pairs_on_chip)

    def across_chips(value):
        return lax.ppermute(value, "gx", pairs_across)

    def neighbours(own, partner):
        return across_chips(jnp.concatenate([own, partner], axis=0))

    def rows_of(own, partner):
        odd = neighbours(own, partner)
        return own, partner, odd, on_chip(odd[: own.shape[0]])

    forward = [(i, (i + 1) % count_y) for i in range(count_y)]
    backward = [(target, source) for source, target in forward]

    def both_sides(to_left, to_right):
        return lax.ppermute(to_right, "gy", forward), lax.ppermute(to_left, "gy", backward)

    fields = jnp.concatenate(
        [right_side, classes.astype(F32)[None], sea_mask.astype(F32)[None]], axis=0
    )
    to_left, to_right, msg_o = call(
        start_kernel, (place, fields), [(MSG_Y, ROWS, COLS), (MSG_Y, ROWS, COLS), (MSG_X, 8, COLS)]
    )
    from_o = across_chips(msg_o)
    from_left, from_right = both_sides(to_left, to_right)
    corner_tiles = call(corner_kernel, (from_o,), [(MSG_X // 2, 8, COLS)] * 2, place=False)
    corners = both_sides(*corner_tiles)
    r_own, c_own, s_own, msg_x = call(
        rows_kernel,
        (place, fields, from_left, from_right, corner_tiles[0]),
        [(NZ, 2, ROWS, WIDE), (NZ, ROWS, WIDE), (NZ, ROWS, WIDE), (MSG_X, 8, WIDE)],
        far={4: pl.ANY},
    )
    from_x = on_chip(msg_x)
    g_own, h_own, k_own, packed = call(
        material_kernel,
        (c_own, s_own, table),
        [(NZ, ROWS, WIDE)] * 3 + [(12, 8, WIDE)],
        [BUFFER],
        place=False,
    )
    packed_partner = on_chip(packed)
    packed_odd = neighbours(packed, packed_partner)
    r, g, h, d, inverse, xp, r1 = call(
        down_kernel,
        (place, r_own, g_own, h_own, k_own, from_x, from_o, *corners, table),
        [FIELD0, (NZ, EXT0, WIDE), (NZ + 2, EXT0, WIDE), (NZ, EXT0, WIDE), (NZ, EXT0, WIDE), PADDED0, (8, 8, WIDE)],
        [PADDED0, (NZ, EXT0, WIDE), (MSG_X, 8, WIDE), (2, NZ, WIDE), BUFFER],
    )
    received = on_chip(jnp.concatenate([r1, packed_odd[:12]], axis=0))
    material = (packed, packed_partner, packed_odd, received[8:])
    one = [(8, EXT1, WIDE), (10, EXT1, WIDE), (8, EXT1, WIDE), (8, EXT1, WIDE)]
    two = [(4, EXT2, WIDE), (6, EXT2, WIDE), (4, EXT2, WIDE)]
    coarse = call(
        coarse_kernel, (place, *material), [*one, *two], [one[0], one[0], one[0], two[0], BUFFER]
    )
    r, xp, r1 = call(
        middle_kernel,
        (place, r, g, h, d, inverse, xp, *rows_of(r1, received[:8]), *coarse),
        [FIELD0, PADDED0, (8, 8, WIDE)],
        [PADDED0, PADDED0, *COARSE_SCRATCH, BUFFER],
    )
    count = count_x * count_y
    direction, image, sums = call(
        last_kernel,
        (place, fields, r, g, h, d, inverse, xp, *rows_of(r1, on_chip(r1)), *coarse),
        [(2, NZ, ROWS, COLS)] * 2 + [(count, COLS)],
        [PADDED0, PADDED0, *COARSE_SCRATCH, (4, ROWS, COLS), BUFFER],
    )
    sums = lax.all_to_all(sums.reshape(count, 1, COLS), ("gx", "gy"), 0, 0).reshape(count, COLS)
    return tuple(
        call(
            scale_kernel,
            (fields, direction, image, sums),
            [(2, NZ, ROWS, COLS)] * 2,
            place=False,
        )
    )


def solution(mesh):
    return jax.shard_map(
        functools.partial(shards, mesh.shape["gx"], mesh.shape["gy"]),
        mesh=mesh,
        in_specs=(
            P(None, None, "gx", "gy"),
            P(None, "gx", "gy"),
            P(None, "gx", "gy"),
            P(),
            P(),
            P(),
        ),
        out_specs=(P(None, None, "gx", "gy"), P(None, None, "gx", "gy")),
        check_vma=False,
    )
```

```python
import functools
import math

import jax
import jax.numpy as jnp
from jax import lax
from jax.experimental import pallas as pl
from jax.experimental.pallas import tpu as pltpu
from jax.sharding import PartitionSpec as P

F32 = jnp.float32
NZ = 16
ROWS = 16
COLS = 128
WIDE = 256
HALF = 64
UNROLL = 8
EXT0 = 32
EXT1 = 40
EXT2 = 24


def cheb_weights(degree, lower_end, upper_end):
    middle = 0.5 * (upper_end + lower_end)
    radius = 0.5 * (upper_end - lower_end)
    return [
        1.0 / (middle + radius * math.cos(math.pi * (2 * index_k + 1) / (2 * degree)))
        for index_k in range(degree)
    ]


FINE = cheb_weights(2, 0.3, 2.0)
COARSE = cheb_weights(4, 0.1, 2.0)


def loop(count, body):
    def step(index, carry):
        body(index)
        return carry

    lax.fori_loop(0, count, step, 0, unroll=min(count, UNROLL))


def lanes(rows, width):
    return lax.broadcasted_iota(jnp.int32, (rows, width), 1)


def sublanes(rows, width):
    return lax.broadcasted_iota(jnp.int32, (rows, width), 0)


def lane_sum(value, step):
    width = value.shape[1]
    first = (lanes(*value.shape) // step) % 2 == 0
    return value + jnp.where(first, pltpu.roll(value, width - step, 1), pltpu.roll(value, step, 1))


def across(value, step):
    rows, width = value.shape
    return (
        pltpu.roll(value, 1, 0)
        + pltpu.roll(value, rows - 1, 0)
        + pltpu.roll(value, step, 1)
        + pltpu.roll(value, width - step, 1)
    )


def row_pairs(buffer, value):
    rows, width = value.shape
    parts = []
    for half in range(width // COLS):
        buffer[half, 0:rows, :] = value[:, half * COLS : (half + 1) * COLS]
        parts.append(
            buffer[half, pl.ds(0, rows // 2, stride=2), :] + buffer[half, pl.ds(1, rows // 2, stride=2), :]
        )
    return parts[0] if len(parts) == 1 else jnp.concatenate(parts, axis=1)


def row_repeat(buffer, value):
    rows, width = value.shape
    parts = []
    for half in range(width // COLS):
        part = value[:, half * COLS : (half + 1) * COLS]
        buffer[half, pl.ds(0, rows, stride=2), :] = part
        buffer[half, pl.ds(1, rows, stride=2), :] = part
        parts.append(buffer[half, 0 : 2 * rows, :])
    return parts[0] if len(parts) == 1 else jnp.concatenate(parts, axis=1)


def column_pairs(value):
    row = lax.broadcasted_iota(jnp.int32, (WIDE, COLS), 0)
    column = lax.broadcasted_iota(jnp.int32, (WIDE, COLS), 1)
    matrix = jnp.where(row // 2 == column, 1.0, 0.0)
    return jnp.dot(value, matrix, precision=lax.Precision.HIGHEST, preferred_element_type=F32)


def column_repeat(value):
    row = lax.broadcasted_iota(jnp.int32, (COLS, WIDE), 0)
    column = lax.broadcasted_iota(jnp.int32, (COLS, WIDE), 1)
    matrix = jnp.where(column // 2 == row, 1.0, 0.0)
    return jnp.dot(value, matrix, precision=lax.Precision.HIGHEST, preferred_element_type=F32)


def pick(table_row, index):
    rows, width = index.shape
    table = jnp.broadcast_to(table_row, (rows, COLS))
    parts = [
        jnp.take_along_axis(table, index[:, start : start + COLS], axis=1)
        for start in range(0, width, COLS)
    ]
    return parts[0] if len(parts) == 1 else jnp.concatenate(parts, axis=1)


def pack_halves(first, second):
    left = lanes(*first.shape) < HALF
    low = jnp.where(left, first, pltpu.roll(second, HALF, 1))
    high = jnp.where(left, pltpu.roll(first, HALF, 1), second)
    return low, high


def unpack_halves(from_right, from_left):
    left = lanes(*from_right.shape) < HALF
    first = jnp.where(left, from_right, pltpu.roll(from_left, HALF, 1))
    second = jnp.where(left, pltpu.roll(from_right, HALF, 1), from_left)
    return first, second


def pack_sea(fields):
    rows, width = fields[0].shape
    even_lane = lanes(rows, width) % 2 == 0
    even_row = sublanes(rows, width) % 2 == 0
    pairs = [
        jnp.where(even_lane, fields[i], pltpu.roll(fields[i + 1], 1, 1)) for i in (0, 2)
    ]
    return jnp.where(even_row, pairs[0], pltpu.roll(pairs[1], 1, 0))


def unpack_sea(packed):
    rows, width = packed.shape
    spot = (lanes(rows, width) % 2 == 0) & (sublanes(rows, width) % 2 == 0)
    fields = []
    for pair in (packed, pltpu.roll(packed, rows - 1, 0)):
        for field in (pair, pltpu.roll(pair, width - 1, 1)):
            fields.append(jnp.where(spot, field, 1.0))
    return fields


def fill_message(message, rhs, classes, sea, start, edge):
    def fields(z):
        for i in range(2):
            message[2 * z + i] = rhs(z, i)[pl.ds(start, 8), :]
        message[32 + z] = classes.at[z][pl.ds(start, 8), :]
        message.at[52 + z // 8][pl.ds(z % 8, 1), :] = classes.at[z][pl.ds(edge, 1), :]
        message.at[54 + z // 8][pl.ds(z % 8, 1), :] = sea.at[z][pl.ds(edge, 1), :]

    loop(NZ, fields)

    def quads(j):
        message[48 + j] = pack_sea([sea[4 * j + i, pl.ds(start, 8), :] for i in range(4)])

    loop(4, quads)


MSG_Y = 26
MSG_X = 56
R_TILES = 16
M_TILES = 24


def start_kernel(place, fields, to_left, to_right, message):
    core = place[0]
    classes, sea = fields.at[2], fields.at[3]

    def convert(pair):
        to_left[16 + pair], to_right[16 + pair] = pack_halves(classes[2 * pair], classes[2 * pair + 1])

    loop(8, convert)
    for j in range(2):
        quads = [pack_sea([sea[8 * j + 4 * q + i] for i in range(4)]) for q in range(2)]
        to_left[24 + j], to_right[24 + j] = pack_halves(quads[0], quads[1])

    def pair(z):
        to_left[z], to_right[z] = pack_halves(fields[0, z], fields[1, z])

    loop(NZ, pair)
    start = pl.multiple_of(8 * core, 8)
    fill_message(message, lambda z, i: fields.at[i, z], classes, sea, start, 8 - core)


def corner_kernel(message, to_left, to_right):
    def pair(p):
        to_left[p], to_right[p] = pack_halves(message[2 * p], message[2 * p + 1])

    loop(MSG_X // 2, pair)


def rows_kernel(place, fields, from_left, from_right, after, r_out, c_out, s_out, message):
    core = place[0]
    gy = place[2]
    left = lanes(ROWS, COLS) < HALF
    inside = jnp.where(
        left,
        jnp.where(gy < place[4] - 1, 1.0, 0.0),
        jnp.where(gy > 0, 1.0, 0.0),
    )

    def rhs_step(z):
        halo = unpack_halves(from_right[z], from_left[z])
        for i in range(2):
            r_out[z, i] = jnp.concatenate([fields[i, z], halo[i]], axis=1)

    loop(NZ, rhs_step)

    def class_step(pair):
        for i, halo in enumerate(unpack_halves(from_right[16 + pair], from_left[16 + pair])):
            c_out[2 * pair + i] = jnp.concatenate([fields[2, 2 * pair + i], halo], axis=1)

    loop(8, class_step)
    for j in range(2):
        quads = unpack_halves(from_right[24 + j], from_left[24 + j])
        for q in range(2):
            for i, field in enumerate(unpack_sea(quads[q])):
                z = 8 * j + 4 * q + i
                s_out[z] = jnp.concatenate([fields[3, z], field * inside], axis=1)
    start = pl.multiple_of(8 * (1 - core), 8)
    fill_message(message, lambda z, i: r_out.at[z, i], c_out, s_out, start, 7 + core)


def material_kernel(c_in, s_in, table, g_out, h_out, k_out, coarse, sums, buffer):
    def fields(z):
        index = c_in[z].astype(jnp.int32)
        sea = s_in[z]
        g = pick(table[0:1], index) * sea
        h = pick(table[1:2], index) * sea
        k = pick(table[2:3], index) * sea + (1.0 - sea)
        g_out[z] = g
        h_out[z] = h
        k_out[z] = k
        return 0.125 * g * g, 0.125 * h * h, k

    def step(pair):
        first = fields(2 * pair)
        second = fields(2 * pair + 1)
        for i in range(3):
            sums[8 * i + pair] = row_pairs(buffer.at[i], first[i] + second[i])

    loop(8, step)
    coarse[...] = column_pairs(sums[...].reshape(M_TILES * 8, WIDE)).reshape(M_TILES, 8, COLS)


class Level:
    def __init__(self, depth, step, g, h, inverse, diagonal=None):
        self.depth, self.step = depth, step
        self.g, self.h, self.inverse, self.diagonal = g, h, inverse, diagonal

    def couple(self, x, z, i):
        horizontal = self.g[z] * across(self.g[z] * x[z + 1, i], self.step)
        vertical = self.h[z + 1] * (self.h[z] * x[z, i] + self.h[z + 2] * x[z + 2, i])
        return horizontal + vertical

    def first(self, x, r, weight):
        def body(z):
            scaled = weight * self.inverse[z]
            for i in range(2):
                x[z + 1, i] = scaled * r[z, i]

        loop(self.depth, body)

    def update(self, new, x, r, weight):
        def body(z):
            scaled = weight * self.inverse[z]
            for i in range(2):
                new[z + 1, i] = (1.0 - weight) * x[z + 1, i] + scaled * (r[z, i] + self.couple(x, z, i))

        loop(self.depth, body)

    def defect(self, x, r, z, i):
        return r[z, i] - self.diagonal[z] * x[z + 1, i] + self.couple(x, z, i)

    def diagonal_of(self, k, z):
        horizontal = self.g[z] * across(self.g[z], self.step)
        vertical = self.h[z + 1] * (self.h[z] + self.h[z + 2])
        return k + horizontal + vertical


def clear_ends(*refs):
    for ref in refs:
        ref[0] = jnp.zeros(ref.shape[1:], ref.dtype)
        ref[ref.shape[0] - 1] = jnp.zeros(ref.shape[1:], ref.dtype)


def fine_restrict(level, x, r, sums, buffer, out):
    def body(pair):
        for i in range(2):
            total = level.defect(x, r, 2 * pair, i) + level.defect(x, r, 2 * pair + 1, i)
            sums[2 * pair + i] = row_pairs(buffer.at[i], total[8:24])

    loop(NZ // 2, body)
    out[...] = column_pairs(sums[...].reshape(R_TILES * 8, WIDE)).reshape(R_TILES, 8, COLS)


def down_kernel(
    place, r_own, g_own, h_own, k_own, from_x, from_o, corner_left, corner_right, table,
    r, g, h, d, inverse, xp, r1, xa, ka, wide, edges, sums, buffer,
):
    core = place[0]
    gx = place[1]
    gy = place[2]
    open_side = jnp.where((gx > 0) & (gx < place[3] - 1), 1.0, 0.0)
    lane = lanes(8, WIDE)
    ends = jnp.where(
        lane < COLS,
        1.0,
        jnp.where(lane < COLS + HALF, jnp.where(gy < place[4] - 1, 1.0, 0.0), jnp.where(gy > 0, 1.0, 0.0)),
    )
    clear_ends(h, xp, xa)

    def own(z):
        for i in range(2):
            r[z, i, 8:24, :] = r_own[z, i]
        g[z, 8:24, :] = g_own[z]
        h[z + 1, 8:24, :] = h_own[z]
        ka[z, 8:24, :] = k_own[z]

    loop(NZ, own)

    def widen(p):
        for i, halo in enumerate(unpack_halves(corner_right[p], corner_left[p])):
            wide[2 * p + i] = jnp.concatenate([from_o[2 * p + i], halo], axis=1)

    loop(MSG_X // 2, widen)
    for message, start, scale, slot in ((from_x, 24 * (1 - core), 1.0, 1 - core), (wide, 24 * core, open_side, core)):
        start = pl.multiple_of(start, 8)
        valid = scale * ends

        def halo(j, message=message, start=start, valid=valid):
            for q, sea in enumerate(unpack_sea(message[48 + j])):
                z = 4 * j + q
                sea = sea * valid
                index = message[32 + z].astype(jnp.int32)
                g[z, pl.ds(start, 8), :] = pick(table[0:1], index) * sea
                h[z + 1, pl.ds(start, 8), :] = pick(table[1:2], index) * sea
                ka[z, pl.ds(start, 8), :] = pick(table[2:3], index) * sea + (1.0 - sea)
                for i in range(2):
                    r[z, i, pl.ds(start, 8), :] = message[2 * z + i]

        loop(4, halo)
        for j in range(2):
            index = message[52 + j].astype(jnp.int32)
            edges[slot, 8 * j : 8 * j + 8, :] = pick(table[0:1], index) * (message[54 + j] * valid)

    level = Level(NZ, 1, g, h, inverse, d)
    row = sublanes(EXT0, WIDE)

    def diagonals(z):
        here = g[z]
        below = jnp.where(row == 0, edges[0, pl.ds(z, 1), :], pltpu.roll(here, 1, 0))
        above = jnp.where(row == EXT0 - 1, edges[1, pl.ds(z, 1), :], pltpu.roll(here, EXT0 - 1, 0))
        beside = pltpu.roll(here, 1, 1) + pltpu.roll(here, WIDE - 1, 1)
        total = ka[z] + here * (below + above + beside) + h[z + 1] * (h[z] + h[z + 2])
        d[z] = total
        inverse[z] = 1.0 / total

    loop(NZ, diagonals)
    level.first(xa, r, FINE[0])
    level.update(xp, xa, r, FINE[1])
    fine_restrict(level, xp, r, sums, buffer, r1)


def coarse_coefficients(place, pieces, g1, h1, d1, i1, g2, h2, i2, w1, k1, u1, k2, buffer):
    core = place[0]
    clear_ends(h1, h2)
    own, partner, odd, far = pieces
    low = jnp.where(place[1] >= 2, 1.0, 0.0)
    high = jnp.where(place[1] < place[3] - 2, 1.0, 0.0)
    near_side = jnp.where(core == 0, low, high)
    far_side = jnp.where(core == 0, high, low)
    scales = (1.0, 1.0, near_side, near_side, far_side)
    starts = (16, 24 - 16 * core, 8 + 16 * core, 32 * core, 32 - 32 * core)
    starts = [s if isinstance(s, int) else pl.multiple_of(s, 8) for s in starts]

    def assemble(z):
        for i, field in enumerate((w1, u1, k1)):
            j = 8 * i + z
            tiles = (own[j], partner[j], odd[j], odd[M_TILES + j], far[j])
            for start, tile, scale in zip(starts, tiles, scales):
                field[z, pl.ds(start, 8), :] = tile * scale if i < 2 else tile

    loop(8, assemble)

    def roots(z):
        g1[z] = 2.0 * jnp.sqrt(w1[z])
        h1[z + 1] = 2.0 * jnp.sqrt(u1[z])

    loop(8, roots)
    one = Level(8, 1, g1, h1, i1, d1)

    def diagonals(z):
        total = one.diagonal_of(k1[z], z)
        d1[z] = total
        i1[z] = 1.0 / total

    loop(8, diagonals)

    def coarser(z):
        sums = [
            lane_sum(row_pairs(buffer.at[i], field[2 * z] + field[2 * z + 1]), 1)
            for i, field in enumerate((w1, u1, k1))
        ]
        blank = jnp.zeros((4, COLS), F32)
        g2[z] = jnp.concatenate([2.0 * jnp.sqrt(0.125 * sums[0]), blank], axis=0)
        h2[z + 1] = jnp.concatenate([2.0 * jnp.sqrt(0.125 * sums[1]), blank], axis=0)
        k2[z] = jnp.concatenate([sums[2], blank + 1.0], axis=0)

    loop(4, coarser)
    two = Level(4, 2, g2, h2, i2)

    def diagonals_two(z):
        i2[z] = 1.0 / two.diagonal_of(k2[z], z)

    loop(4, diagonals_two)


def coarse_solve(core, one, two, pieces, r1, xa1, xb1, r2, xa2, xb2, buffer):
    own, partner, odd, far = pieces
    clear_ends(xa1, xb1, xa2, xb2)
    starts = (16, 24 - 16 * core, 8 + 16 * core, 32 * core, 32 - 32 * core)
    starts = [s if isinstance(s, int) else pl.multiple_of(s, 8) for s in starts]

    def assemble(z):
        for i in range(2):
            j = 2 * z + i
            tiles = (own[j], partner[j], odd[j], odd[R_TILES + j], far[j])
            for start, tile in zip(starts, tiles):
                r1[z, i, pl.ds(start, 8), :] = tile

    loop(8, assemble)
    one.first(xa1, r1, FINE[0])
    one.update(xb1, xa1, r1, FINE[1])

    def restrict(z):
        for i in range(2):
            total = one.defect(xb1, r1, 2 * z, i) + one.defect(xb1, r1, 2 * z + 1, i)
            sums = lane_sum(row_pairs(buffer.at[i], total), 1)
            r2[z, i] = jnp.concatenate([sums, jnp.zeros((4, COLS), F32)], axis=0)

    loop(4, restrict)
    two.first(xa2, r2, COARSE[0])
    two.update(xb2, xa2, r2, COARSE[1])
    two.update(xa2, xb2, r2, COARSE[2])
    two.update(xb2, xa2, r2, COARSE[3])

    inner = [ref.at[:, :, 8:32, :] for ref in (xa1, xb1, r1)]
    inner_one = Level(8, 1, *(ref.at[:, 8:32, :] for ref in (one.g, one.h, one.inverse)))

    def prolong(z):
        for i in range(2):
            fine = row_repeat(buffer.at[i], xb2[z + 1, i, 4:16, :])
            for half in range(2):
                inner[0][2 * z + half + 1, i] = inner[1][2 * z + half + 1, i] + fine

    loop(4, prolong)
    inner_one.update(inner[1], inner[0], inner[2], FINE[0])
    inner_one.update(inner[0], inner[1], inner[2], FINE[1])


def fine_correct(level, out, xp, c1, wide, buffer):
    rows = c1[1:9, :, 12:28, :].reshape(R_TILES * 16, COLS)
    wide[...] = column_repeat(rows).reshape(R_TILES, 16, WIDE)

    def body(pair):
        for i in range(2):
            fine = row_repeat(buffer.at[i], wide[2 * pair + i])
            for half in range(2):
                out[2 * pair + half + 1, i] = xp[2 * pair + half + 1, i] + fine

    loop(NZ // 2, body)


def join_kernel(r1, odd, message):
    message[0:R_TILES] = r1[...]
    message[R_TILES:] = odd[0:M_TILES]


def near_kernel(odd, after, near):
    near[...] = odd[0:R_TILES]


def coarse_kernel(
    place, own, partner, odd, far, g1, h1, d1, i1, g2, h2, i2, w1, k1, u1, k2, buffer
):
    coarse_coefficients(
        place, (own, partner, odd, far), g1, h1, d1, i1, g2, h2, i2, w1, k1, u1, k2, buffer
    )


def middle_kernel(
    place, r, g, h, d, inverse, xp, own, partner, odd, far, g1, h1, d1, i1, g2, h2, i2,
    z_out, xp_out, r1_out,
    xa, xb, r1, xa1, xb1, r2, xa2, xb2, wide, sums, buffer,
):
    core = place[0]
    zero = Level(NZ, 1, g, h, inverse, d)
    one = Level(8, 1, g1, h1, i1, d1)
    two = Level(4, 2, g2, h2, i2)
    coarse_solve(core, one, two, (own, partner, odd, far), r1, xa1, xb1, r2, xa2, xb2, buffer)
    clear_ends(xa, xb, xp_out)
    fine_correct(zero, xa, xp, xa1, wide, buffer)
    zero.update(xb, xa, r, FINE[0])

    def last(z):
        scaled = FINE[1] * inverse[z]
        for i in range(2):
            z_out[z, i] = (1.0 - FINE[1]) * xb[z + 1, i] + scaled * (r[z, i] + zero.couple(xb, z, i))

    loop(NZ, last)
    zero.first(xa, z_out, FINE[0])
    zero.update(xp_out, xa, z_out, FINE[1])
    fine_restrict(zero, xp_out, z_out, sums, buffer, r1_out)


def last_kernel(
    place, rhs, r, g, h, d, inverse, xp, own, partner, odd, far, g1, h1, d1, i1, g2, h2, i2,
    direction, image, sums,
    xa, xb, r1, xa1, xb1, r2, xa2, xb2, wide, totals, buffer,
):
    core = place[0]
    zero = Level(NZ, 1, g, h, inverse, d)
    one = Level(8, 1, g1, h1, i1, d1)
    two = Level(4, 2, g2, h2, i2)
    coarse_solve(core, one, two, (own, partner, odd, far), r1, xa1, xb1, r2, xa2, xb2, buffer)
    clear_ends(xa, xb)
    fine_correct(zero, xa, xp, xa1, wide, buffer)
    zero.update(xb, xa, r, FINE[0])
    zero.update(xa, xb, r, FINE[1])

    def first_image(z):
        for i in range(2):
            xb[z + 1, i] = d[z] * xa[z + 1, i] - zero.couple(xa, z, i)

    loop(NZ, first_image)
    totals[...] = jnp.zeros(totals.shape, F32)

    def second_image(z):
        for i in range(2):
            field = xa[z + 1, i, 8:24, 0:COLS]
            value = (d[z] * xb[z + 1, i] - zero.couple(xb, z, i))[8:24, 0:COLS]
            direction[i, z] = field
            image[i, z] = value
            totals[i] += rhs[i, z] * field
            totals[2 + i] += field * value

    loop(NZ, second_image)
    row = sublanes(8, COLS)
    lane = lanes(8, COLS)
    line = jnp.zeros((8, COLS), F32)
    for i in range(4):
        line = jnp.where(lane == i, jnp.sum(totals[i]), line)

    def spread(j):
        sums[pl.ds(pl.multiple_of(8 * j, 8), 8), :] = line

    loop(sums.shape[0] // 8, spread)


def scale_kernel(rhs, direction, image, sums, solution_field, residual):
    total = jnp.sum(sums[...], axis=0, keepdims=True)
    lane = lanes(1, COLS)
    parts = [jnp.sum(jnp.where(lane == i, total, 0.0), axis=1, keepdims=True) for i in range(4)]
    for i in range(2):
        alpha = parts[i] / parts[2 + i]

        def body(z, i=i, alpha=alpha):
            solution_field[i, z] = alpha * direction[i, z]
            residual[i, z] = rhs[i, z] - alpha * image[i, z]

        loop(NZ, body)


COSTS = {
    "start_kernel": 3,
    "corner_kernel": 1,
    "rows_kernel": 3,
    "material_kernel": 2,
    "down_kernel": 5,
    "join_kernel": 1,
    "near_kernel": 1,
    "coarse_kernel": 3,
    "middle_kernel": 9,
    "last_kernel": 9,
    "scale_kernel": 1,
}


def call(kernel, operands, outs, scratch=(), place=True, far=None):
    far = far or {}
    vmem = pl.BlockSpec(memory_space=pltpu.VMEM)
    specs = [pl.BlockSpec(memory_space=far[i]) if i in far else vmem for i in range(len(operands))]
    if place:
        specs[0] = pl.BlockSpec(memory_space=pltpu.SMEM)
    return pl.pallas_call(
        kernel,
        out_shape=[jax.ShapeDtypeStruct(shape, F32) for shape in outs],
        in_specs=specs,
        out_specs=[vmem] * len(outs),
        scratch_shapes=[pltpu.VMEM(shape, F32) if isinstance(shape, tuple) else shape for shape in scratch],
        cost_estimate=pl.CostEstimate(
            flops=COSTS[kernel.__name__] * 1_000_000_000, bytes_accessed=COSTS[kernel.__name__] * 3_000_000, transcendentals=0
        ),
        compiler_params=pltpu.CompilerParams(vmem_limit_bytes=16 * 1024 * 1024),
    )(*operands)


FIELD0 = (NZ, 2, EXT0, WIDE)
PADDED0 = (NZ + 2, 2, EXT0, WIDE)
PADDED1 = (10, 2, EXT1, COLS)
PADDED2 = (6, 2, EXT2, COLS)
BUFFER = (3, 2, EXT1, COLS)
SUMS = (R_TILES, 8, WIDE)
SPREAD = (R_TILES, 16, WIDE)
COARSE_SCRATCH = [(8, 2, EXT1, COLS), PADDED1, PADDED1, (4, 2, EXT2, COLS), PADDED2, PADDED2, SPREAD]


def shards(count_x, count_y, right_side, classes, sea_mask, kappa_table, cross_table, vertical_table):
    gx = lax.axis_index("gx")
    gy = lax.axis_index("gy")
    place = jnp.stack([gx % 2, gx, gy, jnp.int32(count_x), jnp.int32(count_y)]).astype(jnp.int32)
    table = jnp.stack([jnp.sqrt(cross_table), jnp.sqrt(vertical_table), kappa_table])
    table = jnp.pad(table, ((0, 5), (0, COLS - table.shape[1])))

    pairs_on_chip = [(i, i ^ 1) for i in range(count_x)]
    pairs_across = [(i, (i + 1 if i % 2 else i - 1) % count_x) for i in range(count_x)]

    def on_chip(value):
        return lax.ppermute(value, "gx", pairs_on_chip)

    def across_chips(value):
        return lax.ppermute(value, "gx", pairs_across)

    def neighbours(own, partner):
        return across_chips(jnp.concatenate([own, partner], axis=0))

    def rows_of(own, partner):
        odd = neighbours(own, partner)
        return own, partner, odd, on_chip(odd[: own.shape[0]])

    forward = [(i, (i + 1) % count_y) for i in range(count_y)]
    backward = [(target, source) for source, target in forward]

    def both_sides(to_left, to_right):
        return lax.ppermute(to_right, "gy", forward), lax.ppermute(to_left, "gy", backward)

    part = lax.broadcasted_iota(jnp.int32, (4, *classes.shape), 0)
    materials = jnp.where(part == 2, classes[None], sea_mask[None]).astype(F32)
    fields = jnp.where(part == 0, right_side[0:1], jnp.where(part == 1, right_side[1:2], materials))
    to_left, to_right, msg_o = call(
        start_kernel, (place, fields), [(MSG_Y, ROWS, COLS), (MSG_Y, ROWS, COLS), (MSG_X, 8, COLS)]
    )
    from_o = across_chips(msg_o)
    from_left, from_right = both_sides(to_left, to_right)
    corner_tiles = call(corner_kernel, (from_o,), [(MSG_X // 2, 8, COLS)] * 2, place=False)
    corners = both_sides(*corner_tiles)
    r_own, c_own, s_own, msg_x = call(
        rows_kernel,
        (place, fields, from_left, from_right, corner_tiles[0]),
        [(NZ, 2, ROWS, WIDE), (NZ, ROWS, WIDE), (NZ, ROWS, WIDE), (MSG_X, 8, WIDE)],
        far={4: pl.ANY},
    )
    from_x = on_chip(msg_x)
    g_own, h_own, k_own, packed = call(
        material_kernel,
        (c_own, s_own, table),
        [(NZ, ROWS, WIDE)] * 3 + [(M_TILES, 8, COLS)],
        [(M_TILES, 8, WIDE), BUFFER],
        place=False,
    )
    packed_partner = on_chip(packed)
    packed_odd = neighbours(packed, packed_partner)
    r, g, h, d, inverse, xp, r1 = call(
        down_kernel,
        (place, r_own, g_own, h_own, k_own, from_x, from_o, *corners, table),
        [FIELD0, (NZ, EXT0, WIDE), (NZ + 2, EXT0, WIDE), (NZ, EXT0, WIDE), (NZ, EXT0, WIDE), PADDED0, (R_TILES, 8, COLS)],
        [PADDED0, (NZ, EXT0, WIDE), (MSG_X, 8, WIDE), (2, NZ, WIDE), SUMS, BUFFER],
    )
    received = on_chip(call(join_kernel, (r1, packed_odd), [(R_TILES + M_TILES, 8, COLS)], place=False)[0])
    material = (packed, packed_partner, packed_odd, received[R_TILES:])
    one = [(8, EXT1, COLS), (10, EXT1, COLS), (8, EXT1, COLS), (8, EXT1, COLS)]
    two = [(4, EXT2, COLS), (6, EXT2, COLS), (4, EXT2, COLS)]
    coarse = call(
        coarse_kernel, (place, *material), [*one, *two], [one[0], one[0], one[0], two[0], BUFFER]
    )
    partner = received[:R_TILES]
    odd = neighbours(r1, partner)
    near = call(near_kernel, (odd, coarse[0]), [(R_TILES, 8, COLS)], place=False, far={1: pl.ANY})[0]
    r, xp, r1 = call(
        middle_kernel,
        (place, r, g, h, d, inverse, xp, r1, partner, odd, on_chip(near), *coarse),
        [FIELD0, PADDED0, (R_TILES, 8, COLS)],
        [PADDED0, PADDED0, *COARSE_SCRATCH, SUMS, BUFFER],
    )
    count = count_x * count_y
    direction, image, sums = call(
        last_kernel,
        (place, fields, r, g, h, d, inverse, xp, *rows_of(r1, on_chip(r1)), *coarse),
        [(2, NZ, ROWS, COLS)] * 2 + [(count, COLS)],
        [PADDED0, PADDED0, *COARSE_SCRATCH, (4, ROWS, COLS), BUFFER],
    )
    sums = lax.all_to_all(sums.reshape(count, 1, COLS), ("gx", "gy"), 0, 0).reshape(count, COLS)
    return tuple(
        call(
            scale_kernel,
            (fields, direction, image, sums),
            [(2, NZ, ROWS, COLS)] * 2,
            place=False,
        )
    )


def solution(mesh):
    return jax.shard_map(
        functools.partial(shards, mesh.shape["gx"], mesh.shape["gy"]),
        mesh=mesh,
        in_specs=(
            P(None, None, "gx", "gy"),
            P(None, "gx", "gy"),
            P(None, "gx", "gy"),
            P(),
            P(),
            P(),
        ),
        out_specs=(P(None, None, "gx", "gy"), P(None, None, "gx", "gy")),
        check_vma=False,
    )
```

```python
import functools
import math

import jax
import jax.numpy as jnp
from jax import lax
from jax.experimental import pallas as pl
from jax.experimental.pallas import tpu as pltpu
from jax.sharding import PartitionSpec as P

F32 = jnp.float32
NZ = 16
ROWS = 16
COLS = 128
WIDE = 256
HALF = 64
UNROLL = 8
EXT0 = 32
EXT1 = 40
EXT2 = 24


def cheb_weights(degree, lower_end, upper_end):
    middle = 0.5 * (upper_end + lower_end)
    radius = 0.5 * (upper_end - lower_end)
    return [
        1.0 / (middle + radius * math.cos(math.pi * (2 * index_k + 1) / (2 * degree)))
        for index_k in range(degree)
    ]


FINE = cheb_weights(2, 0.3, 2.0)
COARSE = cheb_weights(4, 0.1, 2.0)


def loop(count, body):
    def step(index, carry):
        body(index)
        return carry

    lax.fori_loop(0, count, step, 0, unroll=min(count, UNROLL))


def lanes(rows, width):
    return lax.broadcasted_iota(jnp.int32, (rows, width), 1)


def sublanes(rows, width):
    return lax.broadcasted_iota(jnp.int32, (rows, width), 0)


def lane_sum(value, step):
    width = value.shape[1]
    first = (lanes(*value.shape) // step) % 2 == 0
    return value + jnp.where(first, pltpu.roll(value, width - step, 1), pltpu.roll(value, step, 1))


def across(value, step):
    rows, width = value.shape
    return (
        pltpu.roll(value, 1, 0)
        + pltpu.roll(value, rows - 1, 0)
        + pltpu.roll(value, step, 1)
        + pltpu.roll(value, width - step, 1)
    )


def row_pairs(buffer, value):
    rows, width = value.shape
    parts = []
    for half in range(width // COLS):
        buffer[half, 0:rows, :] = value[:, half * COLS : (half + 1) * COLS]
        parts.append(
            buffer[half, pl.ds(0, rows // 2, stride=2), :] + buffer[half, pl.ds(1, rows // 2, stride=2), :]
        )
    return parts[0] if len(parts) == 1 else jnp.concatenate(parts, axis=1)


def row_repeat(buffer, value):
    rows, width = value.shape
    parts = []
    for half in range(width // COLS):
        part = value[:, half * COLS : (half + 1) * COLS]
        buffer[half, pl.ds(0, rows, stride=2), :] = part
        buffer[half, pl.ds(1, rows, stride=2), :] = part
        parts.append(buffer[half, 0 : 2 * rows, :])
    return parts[0] if len(parts) == 1 else jnp.concatenate(parts, axis=1)


def column_pairs(value):
    row = lax.broadcasted_iota(jnp.int32, (WIDE, COLS), 0)
    column = lax.broadcasted_iota(jnp.int32, (WIDE, COLS), 1)
    matrix = jnp.where(row // 2 == column, 1.0, 0.0)
    return jnp.dot(value, matrix, precision=lax.Precision.HIGHEST, preferred_element_type=F32)


def column_repeat(value):
    row = lax.broadcasted_iota(jnp.int32, (COLS, WIDE), 0)
    column = lax.broadcasted_iota(jnp.int32, (COLS, WIDE), 1)
    matrix = jnp.where(column // 2 == row, 1.0, 0.0)
    return jnp.dot(value, matrix, precision=lax.Precision.HIGHEST, preferred_element_type=F32)


def pick(table_row, index):
    rows, width = index.shape
    table = jnp.broadcast_to(table_row, (rows, COLS))
    parts = [
        jnp.take_along_axis(table, index[:, start : start + COLS], axis=1)
        for start in range(0, width, COLS)
    ]
    return parts[0] if len(parts) == 1 else jnp.concatenate(parts, axis=1)


def pack_halves(first, second):
    left = lanes(*first.shape) < HALF
    low = jnp.where(left, first, pltpu.roll(second, HALF, 1))
    high = jnp.where(left, pltpu.roll(first, HALF, 1), second)
    return low, high


def unpack_halves(from_right, from_left):
    left = lanes(*from_right.shape) < HALF
    first = jnp.where(left, from_right, pltpu.roll(from_left, HALF, 1))
    second = jnp.where(left, pltpu.roll(from_right, HALF, 1), from_left)
    return first, second


def pack_sea(fields):
    rows, width = fields[0].shape
    even_lane = lanes(rows, width) % 2 == 0
    even_row = sublanes(rows, width) % 2 == 0
    pairs = [
        jnp.where(even_lane, fields[i], pltpu.roll(fields[i + 1], 1, 1)) for i in (0, 2)
    ]
    return jnp.where(even_row, pairs[0], pltpu.roll(pairs[1], 1, 0))


def unpack_sea(packed):
    rows, width = packed.shape
    spot = (lanes(rows, width) % 2 == 0) & (sublanes(rows, width) % 2 == 0)
    fields = []
    for pair in (packed, pltpu.roll(packed, rows - 1, 0)):
        for field in (pair, pltpu.roll(pair, width - 1, 1)):
            fields.append(jnp.where(spot, field, 1.0))
    return fields


MSG_Y = 26
MSG_X = 54
R_TILES = 16
M_TILES = 24


def start_kernel(fields, to_left, to_right):
    def pair(z):
        to_left[z], to_right[z] = pack_halves(fields[0, z], fields[1, z])

    loop(NZ, pair)

    def class_pair(p):
        to_left[16 + p], to_right[16 + p] = pack_halves(fields[2, 2 * p], fields[2, 2 * p + 1])

    loop(8, class_pair)
    for j in range(2):
        quads = [pack_sea([fields[3, 8 * j + 4 * q + i] for i in range(4)]) for q in range(2)]
        to_left[24 + j], to_right[24 + j] = pack_halves(quads[0], quads[1])


def rows_kernel(place, fields, from_left, from_right, table, r_out, c_out, s_out, msg_x, msg_o, row_c, row_s):
    core = place[0]
    gy = place[2]
    left = lanes(ROWS, COLS) < HALF
    inside = jnp.where(
        left,
        jnp.where(gy < place[4] - 1, 1.0, 0.0),
        jnp.where(gy > 0, 1.0, 0.0),
    )

    def rhs_step(z):
        halo = unpack_halves(from_right[z], from_left[z])
        for i in range(2):
            r_out[z, i] = jnp.concatenate([fields[i, z], halo[i]], axis=1)

    loop(NZ, rhs_step)

    def class_step(pair):
        for i, halo in enumerate(unpack_halves(from_right[16 + pair], from_left[16 + pair])):
            c_out[2 * pair + i] = jnp.concatenate([fields[2, 2 * pair + i], halo], axis=1)

    loop(8, class_step)
    for j in range(2):
        quads = unpack_halves(from_right[24 + j], from_left[24 + j])
        for q in range(2):
            for i, field in enumerate(unpack_sea(quads[q])):
                z = 8 * j + 4 * q + i
                s_out[z] = jnp.concatenate([fields[3, z], field * inside], axis=1)
    near = pl.multiple_of(8 * (1 - core), 8)
    far = pl.multiple_of(8 * core, 8)
    sides = ((msg_o, far, 8 - core, 0), (msg_x, near, 7 + core, 1))

    def copy(z):
        for message, start, edge, slot in sides:
            for i in range(2):
                message[2 * z + i] = r_out[z, i, pl.ds(start, 8), :]
            message[32 + z] = c_out[z, pl.ds(start, 8), :]
            row_c[slot, pl.ds(z, 1), :] = c_out[z, pl.ds(edge, 1), :]
            row_s[slot, pl.ds(z, 1), :] = s_out[z, pl.ds(edge, 1), :]

    loop(NZ, copy)

    def copy_sea(j):
        for message, start, edge, slot in sides:
            message[48 + j] = pack_sea([s_out[4 * j + i, pl.ds(start, 8), :] for i in range(4)])

    loop(4, copy_sea)
    for message, start, edge, slot in sides:
        root = pick(table[0:1], row_c[slot].astype(jnp.int32)) * row_s[slot]
        message[52] = root[0:8]
        message[53] = root[8:16]


def material_kernel(c_in, s_in, table, g_out, h_out, k_out, coarse, sums, buffer):
    def fields(z):
        index = c_in[z].astype(jnp.int32)
        sea = s_in[z]
        g = pick(table[0:1], index) * sea
        h = pick(table[1:2], index) * sea
        k = pick(table[2:3], index) * sea + (1.0 - sea)
        g_out[z] = g
        h_out[z] = h
        k_out[z] = k
        return 0.125 * g * g, 0.125 * h * h, k

    def step(pair):
        first = fields(2 * pair)
        second = fields(2 * pair + 1)
        for i in range(3):
            sums[8 * i + pair] = row_pairs(buffer.at[i], first[i] + second[i])

    loop(8, step)
    coarse[...] = column_pairs(sums[...].reshape(M_TILES * 8, WIDE)).reshape(M_TILES, 8, COLS)


class Level:
    def __init__(self, depth, step, g, h, inverse, diagonal=None):
        self.depth, self.step = depth, step
        self.g, self.h, self.inverse, self.diagonal = g, h, inverse, diagonal

    def couple(self, x, z, i):
        horizontal = self.g[z] * across(self.g[z] * x[z + 1, i], self.step)
        vertical = self.h[z + 1] * (self.h[z] * x[z, i] + self.h[z + 2] * x[z + 2, i])
        return horizontal + vertical

    def first(self, x, r, weight):
        def body(z):
            scaled = weight * self.inverse[z]
            for i in range(2):
                x[z + 1, i] = scaled * r[z, i]

        loop(self.depth, body)

    def update(self, new, x, r, weight):
        def body(z):
            scaled = weight * self.inverse[z]
            for i in range(2):
                new[z + 1, i] = (1.0 - weight) * x[z + 1, i] + scaled * (r[z, i] + self.couple(x, z, i))

        loop(self.depth, body)

    def defect(self, x, r, z, i):
        return r[z, i] - self.diagonal[z] * x[z + 1, i] + self.couple(x, z, i)

    def diagonal_of(self, k, z):
        horizontal = self.g[z] * across(self.g[z], self.step)
        vertical = self.h[z + 1] * (self.h[z] + self.h[z + 2])
        return k + horizontal + vertical


def clear_ends(*refs):
    for ref in refs:
        ref[0] = jnp.zeros(ref.shape[1:], ref.dtype)
        ref[ref.shape[0] - 1] = jnp.zeros(ref.shape[1:], ref.dtype)


def fine_restrict(level, x, r, sums, buffer, out):
    def body(pair):
        for i in range(2):
            total = level.defect(x, r, 2 * pair, i) + level.defect(x, r, 2 * pair + 1, i)
            sums[2 * pair + i] = row_pairs(buffer.at[i], total[8:24])

    loop(NZ // 2, body)
    out[...] = column_pairs(sums[...].reshape(R_TILES * 8, WIDE)).reshape(R_TILES, 8, COLS)


def down_kernel(
    place, r_own, g_own, h_own, k_own, from_x, from_o, table,
    r, g, h, d, inverse, xp, r1, xa, ka, edges, sums, buffer,
):
    core = place[0]
    gx = place[1]
    gy = place[2]
    open_side = jnp.where((gx > 0) & (gx < place[3] - 1), 1.0, 0.0)
    lane = lanes(8, WIDE)
    ends = jnp.where(
        lane < COLS,
        1.0,
        jnp.where(lane < COLS + HALF, jnp.where(gy < place[4] - 1, 1.0, 0.0), jnp.where(gy > 0, 1.0, 0.0)),
    )
    clear_ends(h, xp, xa)

    def own(z):
        for i in range(2):
            r[z, i, 8:24, :] = r_own[z, i]
        g[z, 8:24, :] = g_own[z]
        h[z + 1, 8:24, :] = h_own[z]
        ka[z, 8:24, :] = k_own[z]

    loop(NZ, own)

    for message, start, scale, slot in ((from_x, 24 * (1 - core), 1.0, 1 - core), (from_o, 24 * core, open_side, core)):
        start = pl.multiple_of(start, 8)
        valid = scale * ends

        def halo(j, message=message, start=start, valid=valid):
            for q, sea in enumerate(unpack_sea(message[48 + j])):
                z = 4 * j + q
                sea = sea * valid
                index = message[32 + z].astype(jnp.int32)
                g[z, pl.ds(start, 8), :] = pick(table[0:1], index) * sea
                h[z + 1, pl.ds(start, 8), :] = pick(table[1:2], index) * sea
                ka[z, pl.ds(start, 8), :] = pick(table[2:3], index) * sea + (1.0 - sea)
                for i in range(2):
                    r[z, i, pl.ds(start, 8), :] = message[2 * z + i]

        loop(4, halo)
        for j in range(2):
            edges[slot, 8 * j : 8 * j + 8, :] = message[52 + j] * scale

    level = Level(NZ, 1, g, h, inverse, d)
    row = sublanes(EXT0, WIDE)

    def diagonals(z):
        here = g[z]
        below = jnp.where(row == 0, edges[0, pl.ds(z, 1), :], pltpu.roll(here, 1, 0))
        above = jnp.where(row == EXT0 - 1, edges[1, pl.ds(z, 1), :], pltpu.roll(here, EXT0 - 1, 0))
        beside = pltpu.roll(here, 1, 1) + pltpu.roll(here, WIDE - 1, 1)
        total = ka[z] + here * (below + above + beside) + h[z + 1] * (h[z] + h[z + 2])
        d[z] = total
        inverse[z] = 1.0 / total

    loop(NZ, diagonals)
    level.first(xa, r, FINE[0])
    level.update(xp, xa, r, FINE[1])
    fine_restrict(level, xp, r, sums, buffer, r1)


def coarse_coefficients(place, pieces, g1, h1, d1, i1, g2, h2, i2, w1, k1, u1, k2, buffer):
    core = place[0]
    clear_ends(h1, h2)
    own, partner, odd, far = pieces
    low = jnp.where(place[1] >= 2, 1.0, 0.0)
    high = jnp.where(place[1] < place[3] - 2, 1.0, 0.0)
    near_side = jnp.where(core == 0, low, high)
    far_side = jnp.where(core == 0, high, low)
    scales = (1.0, 1.0, near_side, near_side, far_side)
    starts = (16, 24 - 16 * core, 8 + 16 * core, 32 * core, 32 - 32 * core)
    starts = [s if isinstance(s, int) else pl.multiple_of(s, 8) for s in starts]

    def assemble(z):
        for i, field in enumerate((w1, u1, k1)):
            j = 8 * i + z
            tiles = (own[j], partner[j], odd[j], odd[M_TILES + j], far[j])
            for start, tile, scale in zip(starts, tiles, scales):
                field[z, pl.ds(start, 8), :] = tile * scale if i < 2 else tile

    loop(8, assemble)

    def roots(z):
        g1[z] = 2.0 * jnp.sqrt(w1[z])
        h1[z + 1] = 2.0 * jnp.sqrt(u1[z])

    loop(8, roots)
    one = Level(8, 1, g1, h1, i1, d1)

    def diagonals(z):
        total = one.diagonal_of(k1[z], z)
        d1[z] = total
        i1[z] = 1.0 / total

    loop(8, diagonals)

    def coarser(z):
        sums = [
            lane_sum(row_pairs(buffer.at[i], field[2 * z] + field[2 * z + 1]), 1)
            for i, field in enumerate((w1, u1, k1))
        ]
        blank = jnp.zeros((4, COLS), F32)
        g2[z] = jnp.concatenate([2.0 * jnp.sqrt(0.125 * sums[0]), blank], axis=0)
        h2[z + 1] = jnp.concatenate([2.0 * jnp.sqrt(0.125 * sums[1]), blank], axis=0)
        k2[z] = jnp.concatenate([sums[2], blank + 1.0], axis=0)

    loop(4, coarser)
    two = Level(4, 2, g2, h2, i2)

    def diagonals_two(z):
        i2[z] = 1.0 / two.diagonal_of(k2[z], z)

    loop(4, diagonals_two)


def coarse_solve(core, one, two, pieces, r1, xa1, xb1, r2, xa2, xb2, buffer):
    own, partner, odd, far = pieces
    clear_ends(xa1, xb1, xa2, xb2)
    starts = (16, 24 - 16 * core, 8 + 16 * core, 32 * core, 32 - 32 * core)
    starts = [s if isinstance(s, int) else pl.multiple_of(s, 8) for s in starts]

    def assemble(z):
        for i in range(2):
            j = 2 * z + i
            tiles = (own[j], partner[j], odd[j], odd[R_TILES + j], far[j])
            for start, tile in zip(starts, tiles):
                r1[z, i, pl.ds(start, 8), :] = tile

    loop(8, assemble)
    one.first(xa1, r1, FINE[0])
    one.update(xb1, xa1, r1, FINE[1])

    def restrict(z):
        for i in range(2):
            total = one.defect(xb1, r1, 2 * z, i) + one.defect(xb1, r1, 2 * z + 1, i)
            sums = lane_sum(row_pairs(buffer.at[i], total), 1)
            r2[z, i] = jnp.concatenate([sums, jnp.zeros((4, COLS), F32)], axis=0)

    loop(4, restrict)
    two.first(xa2, r2, COARSE[0])
    two.update(xb2, xa2, r2, COARSE[1])
    two.update(xa2, xb2, r2, COARSE[2])
    two.update(xb2, xa2, r2, COARSE[3])

    inner = [ref.at[:, :, 8:32, :] for ref in (xa1, xb1, r1)]
    inner_one = Level(8, 1, *(ref.at[:, 8:32, :] for ref in (one.g, one.h, one.inverse)))

    def prolong(z):
        for i in range(2):
            fine = row_repeat(buffer.at[i], xb2[z + 1, i, 4:16, :])
            for half in range(2):
                inner[0][2 * z + half + 1, i] = inner[1][2 * z + half + 1, i] + fine

    loop(4, prolong)
    inner_one.update(inner[1], inner[0], inner[2], FINE[0])
    inner_one.update(inner[0], inner[1], inner[2], FINE[1])


def fine_correct(level, out, xp, c1, wide, buffer):
    rows = c1[1:9, :, 12:28, :].reshape(R_TILES * 16, COLS)
    wide[...] = column_repeat(rows).reshape(R_TILES, 16, WIDE)

    def body(pair):
        for i in range(2):
            fine = row_repeat(buffer.at[i], wide[2 * pair + i])
            for half in range(2):
                out[2 * pair + half + 1, i] = xp[2 * pair + half + 1, i] + fine

    loop(NZ // 2, body)


def join_kernel(r1, odd, message):
    message[0:R_TILES] = r1[...]
    message[R_TILES:] = odd[0:M_TILES]


def near_kernel(odd, after, near):
    near[...] = odd[0:R_TILES]


def coarse_kernel(
    place, own, partner, odd, far, g1, h1, d1, i1, g2, h2, i2, w1, k1, u1, k2, buffer
):
    coarse_coefficients(
        place, (own, partner, odd, far), g1, h1, d1, i1, g2, h2, i2, w1, k1, u1, k2, buffer
    )


def middle_kernel(
    place, r, g, h, d, inverse, xp, own, partner, odd, far, g1, h1, d1, i1, g2, h2, i2,
    z_out, xp_out, r1_out,
    xa, xb, r1, xa1, xb1, r2, xa2, xb2, wide, sums, buffer,
):
    core = place[0]
    zero = Level(NZ, 1, g, h, inverse, d)
    one = Level(8, 1, g1, h1, i1, d1)
    two = Level(4, 2, g2, h2, i2)
    coarse_solve(core, one, two, (own, partner, odd, far), r1, xa1, xb1, r2, xa2, xb2, buffer)
    clear_ends(xa, xb, xp_out)
    fine_correct(zero, xa, xp, xa1, wide, buffer)
    zero.update(xb, xa, r, FINE[0])

    def last(z):
        scaled = FINE[1] * inverse[z]
        for i in range(2):
            z_out[z, i] = (1.0 - FINE[1]) * xb[z + 1, i] + scaled * (r[z, i] + zero.couple(xb, z, i))

    loop(NZ, last)
    zero.first(xa, z_out, FINE[0])
    zero.update(xp_out, xa, z_out, FINE[1])
    fine_restrict(zero, xp_out, z_out, sums, buffer, r1_out)


def last_kernel(
    place, rhs, r, g, h, d, inverse, xp, own, partner, odd, far, g1, h1, d1, i1, g2, h2, i2,
    direction, image, sums,
    xa, xb, r1, xa1, xb1, r2, xa2, xb2, wide, totals, buffer,
):
    core = place[0]
    zero = Level(NZ, 1, g, h, inverse, d)
    one = Level(8, 1, g1, h1, i1, d1)
    two = Level(4, 2, g2, h2, i2)
    coarse_solve(core, one, two, (own, partner, odd, far), r1, xa1, xb1, r2, xa2, xb2, buffer)
    clear_ends(xa, xb)
    fine_correct(zero, xa, xp, xa1, wide, buffer)
    zero.update(xb, xa, r, FINE[0])
    zero.update(xa, xb, r, FINE[1])

    def first_image(z):
        for i in range(2):
            xb[z + 1, i] = d[z] * xa[z + 1, i] - zero.couple(xa, z, i)

    loop(NZ, first_image)
    totals[...] = jnp.zeros(totals.shape, F32)

    def second_image(z):
        for i in range(2):
            field = xa[z + 1, i, 8:24, 0:COLS]
            value = (d[z] * xb[z + 1, i] - zero.couple(xb, z, i))[8:24, 0:COLS]
            direction[i, z] = field
            image[i, z] = value
            totals[i] += rhs[i, z] * field
            totals[2 + i] += field * value

    loop(NZ, second_image)
    row = sublanes(8, COLS)
    lane = lanes(8, COLS)
    line = jnp.zeros((8, COLS), F32)
    for i in range(4):
        line = jnp.where(lane == i, jnp.sum(totals[i]), line)

    def spread(j):
        sums[pl.ds(pl.multiple_of(8 * j, 8), 8), :] = line

    loop(sums.shape[0] // 8, spread)


def scale_kernel(rhs, direction, image, sums, solution_field, residual):
    total = jnp.sum(sums[...], axis=0, keepdims=True)
    lane = lanes(1, COLS)
    parts = [jnp.sum(jnp.where(lane == i, total, 0.0), axis=1, keepdims=True) for i in range(4)]
    for i in range(2):
        alpha = parts[i] / parts[2 + i]

        def body(z, i=i, alpha=alpha):
            solution_field[i, z] = alpha * direction[i, z]
            residual[i, z] = rhs[i, z] - alpha * image[i, z]

        loop(NZ, body)


COSTS = {
    "start_kernel": 3,
    "rows_kernel": 3,
    "material_kernel": 2,
    "down_kernel": 5,
    "join_kernel": 1,
    "near_kernel": 1,
    "coarse_kernel": 3,
    "middle_kernel": 9,
    "last_kernel": 9,
    "scale_kernel": 1,
}


def call(kernel, operands, outs, scratch=(), place=True, far=None):
    far = far or {}
    vmem = pl.BlockSpec(memory_space=pltpu.VMEM)
    specs = [pl.BlockSpec(memory_space=far[i]) if i in far else vmem for i in range(len(operands))]
    if place:
        specs[0] = pl.BlockSpec(memory_space=pltpu.SMEM)
    return pl.pallas_call(
        kernel,
        out_shape=[jax.ShapeDtypeStruct(shape, F32) for shape in outs],
        in_specs=specs,
        out_specs=[vmem] * len(outs),
        scratch_shapes=[pltpu.VMEM(shape, F32) if isinstance(shape, tuple) else shape for shape in scratch],
        cost_estimate=pl.CostEstimate(
            flops=COSTS[kernel.__name__] * 1_000_000_000, bytes_accessed=COSTS[kernel.__name__] * 3_000_000, transcendentals=0
        ),
        compiler_params=pltpu.CompilerParams(vmem_limit_bytes=16 * 1024 * 1024),
    )(*operands)


FIELD0 = (NZ, 2, EXT0, WIDE)
PADDED0 = (NZ + 2, 2, EXT0, WIDE)
PADDED1 = (10, 2, EXT1, COLS)
PADDED2 = (6, 2, EXT2, COLS)
BUFFER = (3, 2, EXT1, COLS)
SUMS = (R_TILES, 8, WIDE)
SPREAD = (R_TILES, 16, WIDE)
COARSE_SCRATCH = [(8, 2, EXT1, COLS), PADDED1, PADDED1, (4, 2, EXT2, COLS), PADDED2, PADDED2, SPREAD]


def shards(count_x, count_y, right_side, classes, sea_mask, kappa_table, cross_table, vertical_table):
    gx = lax.axis_index("gx")
    gy = lax.axis_index("gy")
    place = jnp.stack([gx % 2, gx, gy, jnp.int32(count_x), jnp.int32(count_y)]).astype(jnp.int32)
    table = jnp.stack([jnp.sqrt(cross_table), jnp.sqrt(vertical_table), kappa_table])
    table = jnp.pad(table, ((0, 5), (0, COLS - table.shape[1])))

    pairs_on_chip = [(i, i ^ 1) for i in range(count_x)]
    pairs_across = [(i, (i + 1 if i % 2 else i - 1) % count_x) for i in range(count_x)]

    def on_chip(value):
        return lax.ppermute(value, "gx", pairs_on_chip)

    def across_chips(value):
        return lax.ppermute(value, "gx", pairs_across)

    def neighbours(own, partner):
        return across_chips(jnp.concatenate([own, partner], axis=0))

    def rows_of(own, partner):
        odd = neighbours(own, partner)
        return own, partner, odd, on_chip(odd[: own.shape[0]])

    forward = [(i, (i + 1) % count_y) for i in range(count_y)]
    backward = [(target, source) for source, target in forward]

    def both_sides(to_left, to_right):
        return lax.ppermute(to_right, "gy", forward), lax.ppermute(to_left, "gy", backward)

    part = lax.broadcasted_iota(jnp.int32, (4, *classes.shape), 0)
    materials = jnp.where(part == 2, classes[None], sea_mask[None]).astype(F32)
    twice = jnp.broadcast_to(right_side[None], (2, *right_side.shape)).reshape(part.shape)
    fields = jnp.where(part < 2, twice, materials)
    to_left, to_right = call(start_kernel, (fields,), [(MSG_Y, ROWS, COLS)] * 2, place=False)
    r_own, c_own, s_own, msg_x, msg_o = call(
        rows_kernel,
        (place, fields, *both_sides(to_left, to_right), table),
        [(NZ, 2, ROWS, WIDE), (NZ, ROWS, WIDE), (NZ, ROWS, WIDE), (MSG_X, 8, WIDE), (MSG_X, 8, WIDE)],
        [(2, NZ, WIDE), (2, NZ, WIDE)],
    )
    from_o = across_chips(msg_o)
    from_x = on_chip(msg_x)
    g_own, h_own, k_own, packed = call(
        material_kernel,
        (c_own, s_own, table),
        [(NZ, ROWS, WIDE)] * 3 + [(M_TILES, 8, COLS)],
        [(M_TILES, 8, WIDE), BUFFER],
        place=False,
    )
    packed_partner = on_chip(packed)
    packed_odd = neighbours(packed, packed_partner)
    r, g, h, d, inverse, xp, r1 = call(
        down_kernel,
        (place, r_own, g_own, h_own, k_own, from_x, from_o, table),
        [FIELD0, (NZ, EXT0, WIDE), (NZ + 2, EXT0, WIDE), (NZ, EXT0, WIDE), (NZ, EXT0, WIDE), PADDED0, (R_TILES, 8, COLS)],
        [PADDED0, (NZ, EXT0, WIDE), (2, NZ, WIDE), SUMS, BUFFER],
    )
    received = on_chip(call(join_kernel, (r1, packed_odd), [(R_TILES + M_TILES, 8, COLS)], place=False)[0])
    material = (packed, packed_partner, packed_odd, received[R_TILES:])
    one = [(8, EXT1, COLS), (10, EXT1, COLS), (8, EXT1, COLS), (8, EXT1, COLS)]
    two = [(4, EXT2, COLS), (6, EXT2, COLS), (4, EXT2, COLS)]
    coarse = call(
        coarse_kernel, (place, *material), [*one, *two], [one[0], one[0], one[0], two[0], BUFFER]
    )
    partner = received[:R_TILES]
    odd = neighbours(r1, partner)
    near = call(near_kernel, (odd, coarse[0]), [(R_TILES, 8, COLS)], place=False, far={1: pl.ANY})[0]
    r, xp, r1 = call(
        middle_kernel,
        (place, r, g, h, d, inverse, xp, r1, partner, odd, on_chip(near), *coarse),
        [FIELD0, PADDED0, (R_TILES, 8, COLS)],
        [PADDED0, PADDED0, *COARSE_SCRATCH, SUMS, BUFFER],
    )
    count = count_x * count_y
    direction, image, sums = call(
        last_kernel,
        (place, fields, r, g, h, d, inverse, xp, *rows_of(r1, on_chip(r1)), *coarse),
        [(2, NZ, ROWS, COLS)] * 2 + [(count, COLS)],
        [PADDED0, PADDED0, *COARSE_SCRATCH, (4, ROWS, COLS), BUFFER],
    )
    sums = lax.all_to_all(sums.reshape(count, 1, COLS), ("gx", "gy"), 0, 0).reshape(count, COLS)
    return tuple(
        call(
            scale_kernel,
            (fields, direction, image, sums),
            [(2, NZ, ROWS, COLS)] * 2,
            place=False,
        )
    )


def solution(mesh):
    return jax.shard_map(
        functools.partial(shards, mesh.shape["gx"], mesh.shape["gy"]),
        mesh=mesh,
        in_specs=(
            P(None, None, "gx", "gy"),
            P(None, "gx", "gy"),
            P(None, "gx", "gy"),
            P(),
            P(),
            P(),
        ),
        out_specs=(P(None, None, "gx", "gy"), P(None, None, "gx", "gy")),
        check_vma=False,
    )
```

```python
import functools
import math

import jax
import jax.numpy as jnp
from jax import lax
from jax.experimental import pallas as pl
from jax.experimental.pallas import tpu as pltpu
from jax.sharding import PartitionSpec as P

F32 = jnp.float32
NZ = 16
ROWS = 16
COLS = 128
WIDE = 256
HALF = 64
UNROLL = 8
EXT0 = 32
EXT1 = 40
EXT2 = 24


def cheb_weights(degree, lower_end, upper_end):
    middle = 0.5 * (upper_end + lower_end)
    radius = 0.5 * (upper_end - lower_end)
    return [
        1.0 / (middle + radius * math.cos(math.pi * (2 * index_k + 1) / (2 * degree)))
        for index_k in range(degree)
    ]


FINE = cheb_weights(2, 0.3, 2.0)
COARSE = cheb_weights(4, 0.1, 2.0)


def loop(count, body):
    def step(index, carry):
        body(index)
        return carry

    lax.fori_loop(0, count, step, 0, unroll=min(count, UNROLL))


def lanes(rows, width):
    return lax.broadcasted_iota(jnp.int32, (rows, width), 1)


def sublanes(rows, width):
    return lax.broadcasted_iota(jnp.int32, (rows, width), 0)


def lane_sum(value, step):
    width = value.shape[1]
    first = (lanes(*value.shape) // step) % 2 == 0
    return value + jnp.where(first, pltpu.roll(value, width - step, 1), pltpu.roll(value, step, 1))


def across(value, step):
    rows, width = value.shape
    return (
        pltpu.roll(value, 1, 0)
        + pltpu.roll(value, rows - 1, 0)
        + pltpu.roll(value, step, 1)
        + pltpu.roll(value, width - step, 1)
    )


def row_pairs(buffer, value):
    rows, width = value.shape
    parts = []
    for half in range(width // COLS):
        buffer[half, 0:rows, :] = value[:, half * COLS : (half + 1) * COLS]
        parts.append(
            buffer[half, pl.ds(0, rows // 2, stride=2), :] + buffer[half, pl.ds(1, rows // 2, stride=2), :]
        )
    return parts[0] if len(parts) == 1 else jnp.concatenate(parts, axis=1)


def row_repeat(buffer, value):
    rows, width = value.shape
    parts = []
    for half in range(width // COLS):
        part = value[:, half * COLS : (half + 1) * COLS]
        buffer[half, pl.ds(0, rows, stride=2), :] = part
        buffer[half, pl.ds(1, rows, stride=2), :] = part
        parts.append(buffer[half, 0 : 2 * rows, :])
    return parts[0] if len(parts) == 1 else jnp.concatenate(parts, axis=1)


def column_pairs(value):
    row = lax.broadcasted_iota(jnp.int32, (WIDE, COLS), 0)
    column = lax.broadcasted_iota(jnp.int32, (WIDE, COLS), 1)
    matrix = jnp.where(row // 2 == column, 1.0, 0.0)
    return jnp.dot(value, matrix, precision=lax.Precision.HIGHEST, preferred_element_type=F32)


def column_repeat(value):
    row = lax.broadcasted_iota(jnp.int32, (COLS, WIDE), 0)
    column = lax.broadcasted_iota(jnp.int32, (COLS, WIDE), 1)
    matrix = jnp.where(column // 2 == row, 1.0, 0.0)
    return jnp.dot(value, matrix, precision=lax.Precision.HIGHEST, preferred_element_type=F32)


def pick(table_row, index):
    rows, width = index.shape
    table = jnp.broadcast_to(table_row, (rows, COLS))
    parts = [
        jnp.take_along_axis(table, index[:, start : start + COLS], axis=1)
        for start in range(0, width, COLS)
    ]
    return parts[0] if len(parts) == 1 else jnp.concatenate(parts, axis=1)


def pack_halves(first, second):
    left = lanes(*first.shape) < HALF
    low = jnp.where(left, first, pltpu.roll(second, HALF, 1))
    high = jnp.where(left, pltpu.roll(first, HALF, 1), second)
    return low, high


def unpack_halves(from_right, from_left):
    left = lanes(*from_right.shape) < HALF
    first = jnp.where(left, from_right, pltpu.roll(from_left, HALF, 1))
    second = jnp.where(left, pltpu.roll(from_right, HALF, 1), from_left)
    return first, second


def pack_sea(fields):
    rows, width = fields[0].shape
    even_lane = lanes(rows, width) % 2 == 0
    even_row = sublanes(rows, width) % 2 == 0
    pairs = [
        jnp.where(even_lane, fields[i], pltpu.roll(fields[i + 1], 1, 1)) for i in (0, 2)
    ]
    return jnp.where(even_row, pairs[0], pltpu.roll(pairs[1], 1, 0))


def unpack_sea(packed):
    rows, width = packed.shape
    spot = (lanes(rows, width) % 2 == 0) & (sublanes(rows, width) % 2 == 0)
    fields = []
    for pair in (packed, pltpu.roll(packed, rows - 1, 0)):
        for field in (pair, pltpu.roll(pair, width - 1, 1)):
            fields.append(jnp.where(spot, field, 1.0))
    return fields


MSG_Y = 26
MSG_X = 54
R_TILES = 16
M_TILES = 24


def start_kernel(fields, to_left, to_right):
    def pair(z):
        to_left[z], to_right[z] = pack_halves(fields[0, z], fields[1, z])

    loop(NZ, pair)

    def class_pair(p):
        to_left[16 + p], to_right[16 + p] = pack_halves(fields[2, 2 * p], fields[2, 2 * p + 1])

    loop(8, class_pair)
    for j in range(2):
        quads = [pack_sea([fields[3, 8 * j + 4 * q + i] for i in range(4)]) for q in range(2)]
        to_left[24 + j], to_right[24 + j] = pack_halves(quads[0], quads[1])


def rows_kernel(place, fields, from_left, from_right, table, r_out, c_out, s_out, msg_x, msg_o, row_c, row_s):
    core = place[0]
    gy = place[2]
    left = lanes(ROWS, COLS) < HALF
    inside = jnp.where(
        left,
        jnp.where(gy < place[4] - 1, 1.0, 0.0),
        jnp.where(gy > 0, 1.0, 0.0),
    )

    def rhs_step(z):
        halo = unpack_halves(from_right[z], from_left[z])
        for i in range(2):
            r_out[z, i] = jnp.concatenate([fields[i, z], halo[i]], axis=1)

    loop(NZ, rhs_step)

    def class_step(pair):
        for i, halo in enumerate(unpack_halves(from_right[16 + pair], from_left[16 + pair])):
            c_out[2 * pair + i] = jnp.concatenate([fields[2, 2 * pair + i], halo], axis=1)

    loop(8, class_step)
    for j in range(2):
        quads = unpack_halves(from_right[24 + j], from_left[24 + j])
        for q in range(2):
            for i, field in enumerate(unpack_sea(quads[q])):
                z = 8 * j + 4 * q + i
                s_out[z] = jnp.concatenate([fields[3, z], field * inside], axis=1)
    near = pl.multiple_of(8 * (1 - core), 8)
    far = pl.multiple_of(8 * core, 8)
    sides = ((msg_o, far, 8 - core, 0), (msg_x, near, 7 + core, 1))

    def copy(z):
        for message, start, edge, slot in sides:
            for i in range(2):
                message[2 * z + i] = r_out[z, i, pl.ds(start, 8), :]
            message[32 + z] = c_out[z, pl.ds(start, 8), :]
            row_c[slot, pl.ds(z, 1), :] = c_out[z, pl.ds(edge, 1), :]
            row_s[slot, pl.ds(z, 1), :] = s_out[z, pl.ds(edge, 1), :]

    loop(NZ, copy)

    def copy_sea(j):
        for message, start, edge, slot in sides:
            message[48 + j] = pack_sea([s_out[4 * j + i, pl.ds(start, 8), :] for i in range(4)])

    loop(4, copy_sea)
    for message, start, edge, slot in sides:
        root = pick(table[0:1], row_c[slot].astype(jnp.int32)) * row_s[slot]
        message[52] = root[0:8]
        message[53] = root[8:16]


def material_kernel(c_in, s_in, table, g_out, h_out, k_out, coarse, sums, buffer):
    def fields(z):
        index = c_in[z].astype(jnp.int32)
        sea = s_in[z]
        g = pick(table[0:1], index) * sea
        h = pick(table[1:2], index) * sea
        k = pick(table[2:3], index) * sea + (1.0 - sea)
        g_out[z] = g
        h_out[z] = h
        k_out[z] = k
        return 0.125 * g * g, 0.125 * h * h, k

    def step(pair):
        first = fields(2 * pair)
        second = fields(2 * pair + 1)
        for i in range(3):
            sums[8 * i + pair] = row_pairs(buffer.at[i], first[i] + second[i])

    loop(8, step)
    coarse[...] = column_pairs(sums[...].reshape(M_TILES * 8, WIDE)).reshape(M_TILES, 8, COLS)


class Level:
    def __init__(self, depth, step, g, h, inverse, diagonal=None):
        self.depth, self.step = depth, step
        self.g, self.h, self.inverse, self.diagonal = g, h, inverse, diagonal

    def couple(self, x, z, i):
        horizontal = self.g[z] * across(self.g[z] * x[z + 1, i], self.step)
        vertical = self.h[z + 1] * (self.h[z] * x[z, i] + self.h[z + 2] * x[z + 2, i])
        return horizontal + vertical

    def first(self, x, r, weight):
        def body(z):
            scaled = weight * self.inverse[z]
            for i in range(2):
                x[z + 1, i] = scaled * r[z, i]

        loop(self.depth, body)

    def update(self, new, x, r, weight):
        def body(z):
            scaled = weight * self.inverse[z]
            for i in range(2):
                new[z + 1, i] = (1.0 - weight) * x[z + 1, i] + scaled * (r[z, i] + self.couple(x, z, i))

        loop(self.depth, body)

    def defect(self, x, r, z, i):
        return r[z, i] - self.diagonal[z] * x[z + 1, i] + self.couple(x, z, i)

    def diagonal_of(self, k, z):
        horizontal = self.g[z] * across(self.g[z], self.step)
        vertical = self.h[z + 1] * (self.h[z] + self.h[z + 2])
        return k + horizontal + vertical


def clear_ends(*refs):
    for ref in refs:
        ref[0] = jnp.zeros(ref.shape[1:], ref.dtype)
        ref[ref.shape[0] - 1] = jnp.zeros(ref.shape[1:], ref.dtype)


def fine_restrict(level, x, r, sums, buffer, out):
    def body(pair):
        for i in range(2):
            total = level.defect(x, r, 2 * pair, i) + level.defect(x, r, 2 * pair + 1, i)
            sums[2 * pair + i] = row_pairs(buffer.at[i], total[8:24])

    loop(NZ // 2, body)
    out[...] = column_pairs(sums[...].reshape(R_TILES * 8, WIDE)).reshape(R_TILES, 8, COLS)


def down_kernel(
    place, r_own, g_own, h_own, k_own, from_x, from_o, table,
    r, g, h, d, inverse, xp, r1, xa, ka, edges, sums, buffer,
):
    core = place[0]
    gx = place[1]
    gy = place[2]
    open_side = jnp.where((gx > 0) & (gx < place[3] - 1), 1.0, 0.0)
    lane = lanes(8, WIDE)
    ends = jnp.where(
        lane < COLS,
        1.0,
        jnp.where(lane < COLS + HALF, jnp.where(gy < place[4] - 1, 1.0, 0.0), jnp.where(gy > 0, 1.0, 0.0)),
    )
    clear_ends(h, xp, xa)

    def own(z):
        for i in range(2):
            r[z, i, 8:24, :] = r_own[z, i]
        g[z, 8:24, :] = g_own[z]
        h[z + 1, 8:24, :] = h_own[z]
        ka[z, 8:24, :] = k_own[z]

    loop(NZ, own)

    for message, start, scale, slot in ((from_x, 24 * (1 - core), 1.0, 1 - core), (from_o, 24 * core, open_side, core)):
        start = pl.multiple_of(start, 8)
        valid = scale * ends

        def halo(j, message=message, start=start, valid=valid):
            for q, sea in enumerate(unpack_sea(message[48 + j])):
                z = 4 * j + q
                sea = sea * valid
                index = message[32 + z].astype(jnp.int32)
                g[z, pl.ds(start, 8), :] = pick(table[0:1], index) * sea
                h[z + 1, pl.ds(start, 8), :] = pick(table[1:2], index) * sea
                ka[z, pl.ds(start, 8), :] = pick(table[2:3], index) * sea + (1.0 - sea)
                for i in range(2):
                    r[z, i, pl.ds(start, 8), :] = message[2 * z + i]

        loop(4, halo)
        for j in range(2):
            edges[slot, 8 * j : 8 * j + 8, :] = message[52 + j] * scale

    level = Level(NZ, 1, g, h, inverse, d)
    row = sublanes(EXT0, WIDE)

    def diagonals(z):
        here = g[z]
        below = jnp.where(row == 0, edges[0, pl.ds(z, 1), :], pltpu.roll(here, 1, 0))
        above = jnp.where(row == EXT0 - 1, edges[1, pl.ds(z, 1), :], pltpu.roll(here, EXT0 - 1, 0))
        beside = pltpu.roll(here, 1, 1) + pltpu.roll(here, WIDE - 1, 1)
        total = ka[z] + here * (below + above + beside) + h[z + 1] * (h[z] + h[z + 2])
        d[z] = total
        inverse[z] = 1.0 / total

    loop(NZ, diagonals)
    level.first(xa, r, FINE[0])
    level.update(xp, xa, r, FINE[1])
    fine_restrict(level, xp, r, sums, buffer, r1)


def coarse_coefficients(place, pieces, g1, h1, d1, i1, g2, h2, i2, w1, k1, u1, k2, buffer):
    core = place[0]
    clear_ends(h1, h2)
    own, partner, near, far, second = pieces
    low = jnp.where(place[1] >= 2, 1.0, 0.0)
    high = jnp.where(place[1] < place[3] - 2, 1.0, 0.0)
    near_side = jnp.where(core == 0, low, high)
    far_side = jnp.where(core == 0, high, low)
    scales = (1.0, 1.0, near_side, near_side, far_side)
    starts = (16, 24 - 16 * core, 8 + 16 * core, 32 * core, 32 - 32 * core)
    starts = [s if isinstance(s, int) else pl.multiple_of(s, 8) for s in starts]

    def assemble(z):
        for i, field in enumerate((w1, u1, k1)):
            j = 8 * i + z
            tiles = (own[j], partner[j], near[j], far[j], second[j])
            for start, tile, scale in zip(starts, tiles, scales):
                field[z, pl.ds(start, 8), :] = tile * scale if i < 2 else tile

    loop(8, assemble)

    def roots(z):
        g1[z] = 2.0 * jnp.sqrt(w1[z])
        h1[z + 1] = 2.0 * jnp.sqrt(u1[z])

    loop(8, roots)
    one = Level(8, 1, g1, h1, i1, d1)

    def diagonals(z):
        total = one.diagonal_of(k1[z], z)
        d1[z] = total
        i1[z] = 1.0 / total

    loop(8, diagonals)

    def coarser(z):
        sums = [
            lane_sum(row_pairs(buffer.at[i], field[2 * z] + field[2 * z + 1]), 1)
            for i, field in enumerate((w1, u1, k1))
        ]
        blank = jnp.zeros((4, COLS), F32)
        g2[z] = jnp.concatenate([2.0 * jnp.sqrt(0.125 * sums[0]), blank], axis=0)
        h2[z + 1] = jnp.concatenate([2.0 * jnp.sqrt(0.125 * sums[1]), blank], axis=0)
        k2[z] = jnp.concatenate([sums[2], blank + 1.0], axis=0)

    loop(4, coarser)
    two = Level(4, 2, g2, h2, i2)

    def diagonals_two(z):
        i2[z] = 1.0 / two.diagonal_of(k2[z], z)

    loop(4, diagonals_two)


def coarse_solve(core, one, two, pieces, r1, xa1, xb1, r2, xa2, xb2, buffer):
    own, partner, near, far, second = pieces
    clear_ends(xa1, xb1, xa2, xb2)
    starts = (16, 24 - 16 * core, 8 + 16 * core, 32 * core, 32 - 32 * core)
    starts = [s if isinstance(s, int) else pl.multiple_of(s, 8) for s in starts]

    def assemble(z):
        for i in range(2):
            j = 2 * z + i
            tiles = (own[j], partner[j], near[j], far[j], second[j])
            for start, tile in zip(starts, tiles):
                r1[z, i, pl.ds(start, 8), :] = tile

    loop(8, assemble)
    one.first(xa1, r1, FINE[0])
    one.update(xb1, xa1, r1, FINE[1])

    def restrict(z):
        for i in range(2):
            total = one.defect(xb1, r1, 2 * z, i) + one.defect(xb1, r1, 2 * z + 1, i)
            sums = lane_sum(row_pairs(buffer.at[i], total), 1)
            r2[z, i] = jnp.concatenate([sums, jnp.zeros((4, COLS), F32)], axis=0)

    loop(4, restrict)
    two.first(xa2, r2, COARSE[0])
    two.update(xb2, xa2, r2, COARSE[1])
    two.update(xa2, xb2, r2, COARSE[2])
    two.update(xb2, xa2, r2, COARSE[3])

    inner = [ref.at[:, :, 8:32, :] for ref in (xa1, xb1, r1)]
    inner_one = Level(8, 1, *(ref.at[:, 8:32, :] for ref in (one.g, one.h, one.inverse)))

    def prolong(z):
        for i in range(2):
            fine = row_repeat(buffer.at[i], xb2[z + 1, i, 4:16, :])
            for half in range(2):
                inner[0][2 * z + half + 1, i] = inner[1][2 * z + half + 1, i] + fine

    loop(4, prolong)
    inner_one.update(inner[1], inner[0], inner[2], FINE[0])
    inner_one.update(inner[0], inner[1], inner[2], FINE[1])


def fine_correct(level, out, xp, c1, wide, buffer):
    rows = c1[1:9, :, 12:28, :].reshape(R_TILES * 16, COLS)
    wide[...] = column_repeat(rows).reshape(R_TILES, 16, WIDE)

    def body(pair):
        for i in range(2):
            fine = row_repeat(buffer.at[i], wide[2 * pair + i])
            for half in range(2):
                out[2 * pair + half + 1, i] = xp[2 * pair + half + 1, i] + fine

    loop(NZ // 2, body)


def after_kernel(value, after, out):
    out[...] = value[...]


def near_kernel(value, out):
    out[...] = value[...]


def coarse_kernel(
    place, own, partner, near, far, second, g1, h1, d1, i1, g2, h2, i2, w1, k1, u1, k2, buffer
):
    coarse_coefficients(
        place, (own, partner, near, far, second), g1, h1, d1, i1, g2, h2, i2, w1, k1, u1, k2, buffer
    )


def middle_kernel(
    place, r, g, h, d, inverse, xp, own, partner, near, far, second, g1, h1, d1, i1, g2, h2, i2,
    z_out, xp_out, r1_out,
    xa, xb, r1, xa1, xb1, r2, xa2, xb2, wide, sums, buffer,
):
    core = place[0]
    zero = Level(NZ, 1, g, h, inverse, d)
    one = Level(8, 1, g1, h1, i1, d1)
    two = Level(4, 2, g2, h2, i2)
    coarse_solve(core, one, two, (own, partner, near, far, second), r1, xa1, xb1, r2, xa2, xb2, buffer)
    clear_ends(xa, xb, xp_out)
    fine_correct(zero, xa, xp, xa1, wide, buffer)
    zero.update(xb, xa, r, FINE[0])

    def last(z):
        scaled = FINE[1] * inverse[z]
        for i in range(2):
            z_out[z, i] = (1.0 - FINE[1]) * xb[z + 1, i] + scaled * (r[z, i] + zero.couple(xb, z, i))

    loop(NZ, last)
    zero.first(xa, z_out, FINE[0])
    zero.update(xp_out, xa, z_out, FINE[1])
    fine_restrict(zero, xp_out, z_out, sums, buffer, r1_out)


def last_kernel(
    place, rhs, r, g, h, d, inverse, xp, own, partner, near, far, second, g1, h1, d1, i1, g2, h2, i2,
    direction, image, sums,
    xa, xb, r1, xa1, xb1, r2, xa2, xb2, wide, totals, buffer,
):
    core = place[0]
    zero = Level(NZ, 1, g, h, inverse, d)
    one = Level(8, 1, g1, h1, i1, d1)
    two = Level(4, 2, g2, h2, i2)
    coarse_solve(core, one, two, (own, partner, near, far, second), r1, xa1, xb1, r2, xa2, xb2, buffer)
    clear_ends(xa, xb)
    fine_correct(zero, xa, xp, xa1, wide, buffer)
    zero.update(xb, xa, r, FINE[0])
    zero.update(xa, xb, r, FINE[1])

    def first_image(z):
        for i in range(2):
            xb[z + 1, i] = d[z] * xa[z + 1, i] - zero.couple(xa, z, i)

    loop(NZ, first_image)
    totals[...] = jnp.zeros(totals.shape, F32)

    def second_image(z):
        for i in range(2):
            field = xa[z + 1, i, 8:24, 0:COLS]
            value = (d[z] * xb[z + 1, i] - zero.couple(xb, z, i))[8:24, 0:COLS]
            direction[i, z] = field
            image[i, z] = value
            totals[i] += rhs[i, z] * field
            totals[2 + i] += field * value

    loop(NZ, second_image)
    row = sublanes(8, COLS)
    lane = lanes(8, COLS)
    line = jnp.zeros((8, COLS), F32)
    for i in range(4):
        line = jnp.where(lane == i, jnp.sum(totals[i]), line)

    def spread(j):
        sums[pl.ds(pl.multiple_of(8 * j, 8), 8), :] = line

    loop(sums.shape[0] // 8, spread)


def scale_kernel(rhs, direction, image, sums, solution_field, residual):
    total = jnp.sum(sums[...], axis=0, keepdims=True)
    lane = lanes(1, COLS)
    parts = [jnp.sum(jnp.where(lane == i, total, 0.0), axis=1, keepdims=True) for i in range(4)]
    for i in range(2):
        alpha = parts[i] / parts[2 + i]

        def body(z, i=i, alpha=alpha):
            solution_field[i, z] = alpha * direction[i, z]
            residual[i, z] = rhs[i, z] - alpha * image[i, z]

        loop(NZ, body)


COSTS = {
    "start_kernel": 3,
    "rows_kernel": 3,
    "material_kernel": 2,
    "down_kernel": 5,
    "after_kernel": 1,
    "near_kernel": 30,
    "coarse_kernel": 3,
    "middle_kernel": 9,
    "last_kernel": 9,
    "scale_kernel": 1,
}


def call(kernel, operands, outs, scratch=(), place=True, far=None):
    far = far or {}
    vmem = pl.BlockSpec(memory_space=pltpu.VMEM)
    specs = [pl.BlockSpec(memory_space=far[i]) if i in far else vmem for i in range(len(operands))]
    if place:
        specs[0] = pl.BlockSpec(memory_space=pltpu.SMEM)
    return pl.pallas_call(
        kernel,
        out_shape=[jax.ShapeDtypeStruct(shape, F32) for shape in outs],
        in_specs=specs,
        out_specs=[vmem] * len(outs),
        scratch_shapes=[pltpu.VMEM(shape, F32) if isinstance(shape, tuple) else shape for shape in scratch],
        cost_estimate=pl.CostEstimate(
            flops=COSTS[kernel.__name__] * 1_000_000_000, bytes_accessed=COSTS[kernel.__name__] * 3_000_000, transcendentals=0
        ),
        compiler_params=pltpu.CompilerParams(vmem_limit_bytes=16 * 1024 * 1024),
    )(*operands)


FIELD0 = (NZ, 2, EXT0, WIDE)
PADDED0 = (NZ + 2, 2, EXT0, WIDE)
PADDED1 = (10, 2, EXT1, COLS)
PADDED2 = (6, 2, EXT2, COLS)
BUFFER = (3, 2, EXT1, COLS)
SUMS = (R_TILES, 8, WIDE)
SPREAD = (R_TILES, 16, WIDE)
COARSE_SCRATCH = [(8, 2, EXT1, COLS), PADDED1, PADDED1, (4, 2, EXT2, COLS), PADDED2, PADDED2, SPREAD]


def shards(count_x, count_y, right_side, classes, sea_mask, kappa_table, cross_table, vertical_table):
    gx = lax.axis_index("gx")
    gy = lax.axis_index("gy")
    place = jnp.stack([gx % 2, gx, gy, jnp.int32(count_x), jnp.int32(count_y)]).astype(jnp.int32)
    table = jnp.stack([jnp.sqrt(cross_table), jnp.sqrt(vertical_table), kappa_table])
    table = jnp.pad(table, ((0, 5), (0, COLS - table.shape[1])))

    pairs_on_chip = [(i, i ^ 1) for i in range(count_x)]
    pairs_across = [(i, (i + 1 if i % 2 else i - 1) % count_x) for i in range(count_x)]

    pairs_beyond = [(i, (i - 2 if i % 2 else i + 2) % count_x) for i in range(count_x)]

    def on_chip(value):
        return lax.ppermute(value, "gx", pairs_on_chip)

    def across_chips(value):
        return lax.ppermute(value, "gx", pairs_across)

    def after(value, other):
        return call(after_kernel, (value, other), [value.shape], place=False, far={1: pl.ANY})[0]

    def rows_of(own):
        near = across_chips(own)
        far = lax.ppermute(own, "gx", pairs_beyond)
        near_copy = call(near_kernel, (near,), [near.shape], place=False)[0]
        return own, on_chip(own), near, far, on_chip(near_copy)

    forward = [(i, (i + 1) % count_y) for i in range(count_y)]
    backward = [(target, source) for source, target in forward]

    def both_sides(to_left, to_right):
        return lax.ppermute(to_right, "gy", forward), lax.ppermute(to_left, "gy", backward)

    part = lax.broadcasted_iota(jnp.int32, (4, *classes.shape), 0)
    materials = jnp.where(part == 2, classes[None], sea_mask[None]).astype(F32)
    twice = jnp.broadcast_to(right_side[None], (2, *right_side.shape)).reshape(part.shape)
    fields = jnp.where(part < 2, twice, materials)
    to_left, to_right = call(start_kernel, (fields,), [(MSG_Y, ROWS, COLS)] * 2, place=False)
    r_own, c_own, s_own, msg_x, msg_o = call(
        rows_kernel,
        (place, fields, *both_sides(to_left, to_right), table),
        [(NZ, 2, ROWS, WIDE), (NZ, ROWS, WIDE), (NZ, ROWS, WIDE), (MSG_X, 8, WIDE), (MSG_X, 8, WIDE)],
        [(2, NZ, WIDE), (2, NZ, WIDE)],
    )
    from_o = across_chips(msg_o)
    from_x = on_chip(msg_x)
    g_own, h_own, k_own, packed = call(
        material_kernel,
        (c_own, s_own, table),
        [(NZ, ROWS, WIDE)] * 3 + [(M_TILES, 8, COLS)],
        [(M_TILES, 8, WIDE), BUFFER],
        place=False,
    )
    material = after(packed, from_o)
    r, g, h, d, inverse, xp, r1 = call(
        down_kernel,
        (place, r_own, g_own, h_own, k_own, from_x, from_o, table),
        [FIELD0, (NZ, EXT0, WIDE), (NZ + 2, EXT0, WIDE), (NZ, EXT0, WIDE), (NZ, EXT0, WIDE), PADDED0, (R_TILES, 8, COLS)],
        [PADDED0, (NZ, EXT0, WIDE), (2, NZ, WIDE), SUMS, BUFFER],
    )
    near = lax.ppermute(material, "gx", pairs_across)
    material = (material, on_chip(material), near, lax.ppermute(material, "gx", pairs_beyond), on_chip(after(near, r1)))
    one = [(8, EXT1, COLS), (10, EXT1, COLS), (8, EXT1, COLS), (8, EXT1, COLS)]
    two = [(4, EXT2, COLS), (6, EXT2, COLS), (4, EXT2, COLS)]
    coarse = call(
        coarse_kernel, (place, *material), [*one, *two], [one[0], one[0], one[0], two[0], BUFFER]
    )
    r, xp, r1 = call(
        middle_kernel,
        (place, r, g, h, d, inverse, xp, *rows_of(r1), *coarse),
        [FIELD0, PADDED0, (R_TILES, 8, COLS)],
        [PADDED0, PADDED0, *COARSE_SCRATCH, SUMS, BUFFER],
    )
    count = count_x * count_y
    direction, image, sums = call(
        last_kernel,
        (place, fields, r, g, h, d, inverse, xp, *rows_of(r1), *coarse),
        [(2, NZ, ROWS, COLS)] * 2 + [(count, COLS)],
        [PADDED0, PADDED0, *COARSE_SCRATCH, (4, ROWS, COLS), BUFFER],
    )
    sums = lax.all_to_all(sums.reshape(count, 1, COLS), ("gx", "gy"), 0, 0).reshape(count, COLS)
    return tuple(
        call(
            scale_kernel,
            (fields, direction, image, sums),
            [(2, NZ, ROWS, COLS)] * 2,
            place=False,
        )
    )


def solution(mesh):
    return jax.shard_map(
        functools.partial(shards, mesh.shape["gx"], mesh.shape["gy"]),
        mesh=mesh,
        in_specs=(
            P(None, None, "gx", "gy"),
            P(None, "gx", "gy"),
            P(None, "gx", "gy"),
            P(),
            P(),
            P(),
        ),
        out_specs=(P(None, None, "gx", "gy"), P(None, None, "gx", "gy")),
        check_vma=False,
    )
```

```python
import functools
import math

import jax
import jax.numpy as jnp
from jax import lax
from jax.experimental import pallas as pl
from jax.experimental.pallas import tpu as pltpu
from jax.sharding import PartitionSpec as P

F32 = jnp.float32
NZ = 16
ROWS = 16
COLS = 128
WIDE = 256
HALF = 64
UNROLL = 8
EXT0 = 32
EXT1 = 40
EXT2 = 24


def cheb_weights(degree, lower_end, upper_end):
    middle = 0.5 * (upper_end + lower_end)
    radius = 0.5 * (upper_end - lower_end)
    return [
        1.0 / (middle + radius * math.cos(math.pi * (2 * index_k + 1) / (2 * degree)))
        for index_k in range(degree)
    ]


FINE = cheb_weights(2, 0.3, 2.0)
COARSE = cheb_weights(4, 0.1, 2.0)


def loop(count, body):
    def step(index, carry):
        body(index)
        return carry

    lax.fori_loop(0, count, step, 0, unroll=min(count, UNROLL))


def lanes(rows, width):
    return lax.broadcasted_iota(jnp.int32, (rows, width), 1)


def sublanes(rows, width):
    return lax.broadcasted_iota(jnp.int32, (rows, width), 0)


def lane_sum(value, step):
    width = value.shape[1]
    first = (lanes(*value.shape) // step) % 2 == 0
    return value + jnp.where(first, pltpu.roll(value, width - step, 1), pltpu.roll(value, step, 1))


def across(value, step):
    rows, width = value.shape
    return (
        pltpu.roll(value, 1, 0)
        + pltpu.roll(value, rows - 1, 0)
        + pltpu.roll(value, step, 1)
        + pltpu.roll(value, width - step, 1)
    )


def row_pairs(buffer, value):
    rows, width = value.shape
    parts = []
    for half in range(width // COLS):
        buffer[half, 0:rows, :] = value[:, half * COLS : (half + 1) * COLS]
        parts.append(
            buffer[half, pl.ds(0, rows // 2, stride=2), :] + buffer[half, pl.ds(1, rows // 2, stride=2), :]
        )
    return parts[0] if len(parts) == 1 else jnp.concatenate(parts, axis=1)


def row_repeat(buffer, value):
    rows, width = value.shape
    parts = []
    for half in range(width // COLS):
        part = value[:, half * COLS : (half + 1) * COLS]
        buffer[half, pl.ds(0, rows, stride=2), :] = part
        buffer[half, pl.ds(1, rows, stride=2), :] = part
        parts.append(buffer[half, 0 : 2 * rows, :])
    return parts[0] if len(parts) == 1 else jnp.concatenate(parts, axis=1)


def column_pairs(value):
    row = lax.broadcasted_iota(jnp.int32, (WIDE, COLS), 0)
    column = lax.broadcasted_iota(jnp.int32, (WIDE, COLS), 1)
    matrix = jnp.where(row // 2 == column, 1.0, 0.0)
    return jnp.dot(value, matrix, precision=lax.Precision.HIGHEST, preferred_element_type=F32)


def column_repeat(value):
    row = lax.broadcasted_iota(jnp.int32, (COLS, WIDE), 0)
    column = lax.broadcasted_iota(jnp.int32, (COLS, WIDE), 1)
    matrix = jnp.where(column // 2 == row, 1.0, 0.0)
    return jnp.dot(value, matrix, precision=lax.Precision.HIGHEST, preferred_element_type=F32)


def pick(table_row, index):
    rows, width = index.shape
    table = jnp.broadcast_to(table_row, (rows, COLS))
    parts = [
        jnp.take_along_axis(table, index[:, start : start + COLS], axis=1)
        for start in range(0, width, COLS)
    ]
    return parts[0] if len(parts) == 1 else jnp.concatenate(parts, axis=1)


def pack_halves(first, second):
    left = lanes(*first.shape) < HALF
    low = jnp.where(left, first, pltpu.roll(second, HALF, 1))
    high = jnp.where(left, pltpu.roll(first, HALF, 1), second)
    return low, high


def unpack_halves(from_right, from_left):
    left = lanes(*from_right.shape) < HALF
    first = jnp.where(left, from_right, pltpu.roll(from_left, HALF, 1))
    second = jnp.where(left, pltpu.roll(from_right, HALF, 1), from_left)
    return first, second


def pack_sea(fields):
    rows, width = fields[0].shape
    even_lane = lanes(rows, width) % 2 == 0
    even_row = sublanes(rows, width) % 2 == 0
    pairs = [
        jnp.where(even_lane, fields[i], pltpu.roll(fields[i + 1], 1, 1)) for i in (0, 2)
    ]
    return jnp.where(even_row, pairs[0], pltpu.roll(pairs[1], 1, 0))


def unpack_sea(packed):
    rows, width = packed.shape
    spot = (lanes(rows, width) % 2 == 0) & (sublanes(rows, width) % 2 == 0)
    fields = []
    for pair in (packed, pltpu.roll(packed, rows - 1, 0)):
        for field in (pair, pltpu.roll(pair, width - 1, 1)):
            fields.append(jnp.where(spot, field, 1.0))
    return fields


def fill_message(message, rhs, classes, sea, start, edge):
    def fields(z):
        for i in range(2):
            message[2 * z + i] = rhs(z, i)[pl.ds(start, 8), :]
        message[32 + z] = classes.at[z][pl.ds(start, 8), :]
        message.at[52 + z // 8][pl.ds(z % 8, 1), :] = classes.at[z][pl.ds(edge, 1), :]
        message.at[54 + z // 8][pl.ds(z % 8, 1), :] = sea.at[z][pl.ds(edge, 1), :]

    loop(NZ, fields)

    def quads(j):
        message[48 + j] = pack_sea([sea[4 * j + i, pl.ds(start, 8), :] for i in range(4)])

    loop(4, quads)


MSG_Y = 26
MSG_X = 56
R_TILES = 16
M_TILES = 24


def start_kernel(place, fields, to_left, to_right, message):
    core = place[0]
    classes, sea = fields.at[2], fields.at[3]

    def convert(pair):
        to_left[16 + pair], to_right[16 + pair] = pack_halves(classes[2 * pair], classes[2 * pair + 1])

    loop(8, convert)
    for j in range(2):
        quads = [pack_sea([sea[8 * j + 4 * q + i] for i in range(4)]) for q in range(2)]
        to_left[24 + j], to_right[24 + j] = pack_halves(quads[0], quads[1])

    def pair(z):
        to_left[z], to_right[z] = pack_halves(fields[0, z], fields[1, z])

    loop(NZ, pair)
    start = pl.multiple_of(8 * core, 8)
    fill_message(message, lambda z, i: fields.at[i, z], classes, sea, start, 8 - core)


def corner_kernel(message, after, to_left, to_right):
    def pair(p):
        to_left[p], to_right[p] = pack_halves(message[2 * p], message[2 * p + 1])

    loop(MSG_X // 2, pair)


def widen_kernel(message, corner_left, corner_right, wide):
    def pair(p):
        for i, halo in enumerate(unpack_halves(corner_right[p], corner_left[p])):
            wide[2 * p + i] = jnp.concatenate([message[2 * p + i], halo], axis=1)

    loop(MSG_X // 2, pair)


def rows_kernel(place, fields, from_left, from_right, r_out, c_out, s_out, message):
    core = place[0]
    gy = place[2]
    left = lanes(ROWS, COLS) < HALF
    inside = jnp.where(
        left,
        jnp.where(gy < place[4] - 1, 1.0, 0.0),
        jnp.where(gy > 0, 1.0, 0.0),
    )

    def rhs_step(z):
        halo = unpack_halves(from_right[z], from_left[z])
        for i in range(2):
            r_out[z, i] = jnp.concatenate([fields[i, z], halo[i]], axis=1)

    loop(NZ, rhs_step)

    def class_step(pair):
        for i, halo in enumerate(unpack_halves(from_right[16 + pair], from_left[16 + pair])):
            c_out[2 * pair + i] = jnp.concatenate([fields[2, 2 * pair + i], halo], axis=1)

    loop(8, class_step)
    for j in range(2):
        quads = unpack_halves(from_right[24 + j], from_left[24 + j])
        for q in range(2):
            for i, field in enumerate(unpack_sea(quads[q])):
                z = 8 * j + 4 * q + i
                s_out[z] = jnp.concatenate([fields[3, z], field * inside], axis=1)
    start = pl.multiple_of(8 * (1 - core), 8)
    fill_message(message, lambda z, i: r_out.at[z, i], c_out, s_out, start, 7 + core)


def material_kernel(c_in, s_in, table, g_out, h_out, k_out, coarse, sums, buffer):
    def fields(z):
        index = c_in[z].astype(jnp.int32)
        sea = s_in[z]
        g = pick(table[0:1], index) * sea
        h = pick(table[1:2], index) * sea
        k = pick(table[2:3], index) * sea + (1.0 - sea)
        g_out[z] = g
        h_out[z] = h
        k_out[z] = k
        return 0.125 * g * g, 0.125 * h * h, k

    def step(pair):
        first = fields(2 * pair)
        second = fields(2 * pair + 1)
        for i in range(3):
            sums[8 * i + pair] = row_pairs(buffer.at[i], first[i] + second[i])

    loop(8, step)
    coarse[...] = column_pairs(sums[...].reshape(M_TILES * 8, WIDE)).reshape(M_TILES, 8, COLS)


class Level:
    def __init__(self, depth, step, g, h, inverse, diagonal=None):
        self.depth, self.step = depth, step
        self.g, self.h, self.inverse, self.diagonal = g, h, inverse, diagonal

    def couple(self, x, z, i):
        horizontal = self.g[z] * across(self.g[z] * x[z + 1, i], self.step)
        vertical = self.h[z + 1] * (self.h[z] * x[z, i] + self.h[z + 2] * x[z + 2, i])
        return horizontal + vertical

    def first(self, x, r, weight):
        def body(z):
            scaled = weight * self.inverse[z]
            for i in range(2):
                x[z + 1, i] = scaled * r[z, i]

        loop(self.depth, body)

    def update(self, new, x, r, weight):
        def body(z):
            scaled = weight * self.inverse[z]
            for i in range(2):
                new[z + 1, i] = (1.0 - weight) * x[z + 1, i] + scaled * (r[z, i] + self.couple(x, z, i))

        loop(self.depth, body)

    def defect(self, x, r, z, i):
        return r[z, i] - self.diagonal[z] * x[z + 1, i] + self.couple(x, z, i)

    def diagonal_of(self, k, z):
        horizontal = self.g[z] * across(self.g[z], self.step)
        vertical = self.h[z + 1] * (self.h[z] + self.h[z + 2])
        return k + horizontal + vertical


def clear_ends(*refs):
    for ref in refs:
        ref[0] = jnp.zeros(ref.shape[1:], ref.dtype)
        ref[ref.shape[0] - 1] = jnp.zeros(ref.shape[1:], ref.dtype)


def fine_restrict(level, x, r, sums, buffer, out):
    def body(pair):
        for i in range(2):
            total = level.defect(x, r, 2 * pair, i) + level.defect(x, r, 2 * pair + 1, i)
            sums[2 * pair + i] = row_pairs(buffer.at[i], total[8:24])

    loop(NZ // 2, body)
    out[...] = column_pairs(sums[...].reshape(R_TILES * 8, WIDE)).reshape(R_TILES, 8, COLS)


def down_kernel(
    place, r_own, g_own, h_own, k_own, from_x, wide, table,
    r, g, h, d, inverse, xp, r1, xa, ka, edges, sums, buffer,
):
    core = place[0]
    gx = place[1]
    gy = place[2]
    open_side = jnp.where((gx > 0) & (gx < place[3] - 1), 1.0, 0.0)
    lane = lanes(8, WIDE)
    ends = jnp.where(
        lane < COLS,
        1.0,
        jnp.where(lane < COLS + HALF, jnp.where(gy < place[4] - 1, 1.0, 0.0), jnp.where(gy > 0, 1.0, 0.0)),
    )
    clear_ends(h, xp, xa)

    def own(z):
        for i in range(2):
            r[z, i, 8:24, :] = r_own[z, i]
        g[z, 8:24, :] = g_own[z]
        h[z + 1, 8:24, :] = h_own[z]
        ka[z, 8:24, :] = k_own[z]

    loop(NZ, own)

    for message, start, scale, slot in ((from_x, 24 * (1 - core), 1.0, 1 - core), (wide, 24 * core, open_side, core)):
        start = pl.multiple_of(start, 8)
        valid = scale * ends

        def halo(j, message=message, start=start, valid=valid):
            for q, sea in enumerate(unpack_sea(message[48 + j])):
                z = 4 * j + q
                sea = sea * valid
                index = message[32 + z].astype(jnp.int32)
                g[z, pl.ds(start, 8), :] = pick(table[0:1], index) * sea
                h[z + 1, pl.ds(start, 8), :] = pick(table[1:2], index) * sea
                ka[z, pl.ds(start, 8), :] = pick(table[2:3], index) * sea + (1.0 - sea)
                for i in range(2):
                    r[z, i, pl.ds(start, 8), :] = message[2 * z + i]

        loop(4, halo)
        for j in range(2):
            index = message[52 + j].astype(jnp.int32)
            edges[slot, 8 * j : 8 * j + 8, :] = pick(table[0:1], index) * (message[54 + j] * valid)

    level = Level(NZ, 1, g, h, inverse, d)
    row = sublanes(EXT0, WIDE)

    def diagonals(z):
        here = g[z]
        below = jnp.where(row == 0, edges[0, pl.ds(z, 1), :], pltpu.roll(here, 1, 0))
        above = jnp.where(row == EXT0 - 1, edges[1, pl.ds(z, 1), :], pltpu.roll(here, EXT0 - 1, 0))
        beside = pltpu.roll(here, 1, 1) + pltpu.roll(here, WIDE - 1, 1)
        total = ka[z] + here * (below + above + beside) + h[z + 1] * (h[z] + h[z + 2])
        d[z] = total
        inverse[z] = 1.0 / total

    loop(NZ, diagonals)
    level.first(xa, r, FINE[0])
    level.update(xp, xa, r, FINE[1])
    fine_restrict(level, xp, r, sums, buffer, r1)


def coarse_coefficients(place, pieces, g1, h1, d1, i1, g2, h2, i2, w1, k1, u1, k2, buffer):
    core = place[0]
    clear_ends(h1, h2)
    own, partner, odd, far = pieces
    low = jnp.where(place[1] >= 2, 1.0, 0.0)
    high = jnp.where(place[1] < place[3] - 2, 1.0, 0.0)
    near_side = jnp.where(core == 0, low, high)
    far_side = jnp.where(core == 0, high, low)
    scales = (1.0, 1.0, near_side, near_side, far_side)
    starts = (16, 24 - 16 * core, 8 + 16 * core, 32 * core, 32 - 32 * core)
    starts = [s if isinstance(s, int) else pl.multiple_of(s, 8) for s in starts]

    def assemble(z):
        for i, field in enumerate((w1, u1, k1)):
            j = 8 * i + z
            tiles = (own[j], partner[j], odd[j], odd[M_TILES + j], far[j])
            for start, tile, scale in zip(starts, tiles, scales):
                field[z, pl.ds(start, 8), :] = tile * scale if i < 2 else tile

    loop(8, assemble)

    def roots(z):
        g1[z] = 2.0 * jnp.sqrt(w1[z])
        h1[z + 1] = 2.0 * jnp.sqrt(u1[z])

    loop(8, roots)
    one = Level(8, 1, g1, h1, i1, d1)

    def diagonals(z):
        total = one.diagonal_of(k1[z], z)
        d1[z] = total
        i1[z] = 1.0 / total

    loop(8, diagonals)

    def coarser(z):
        sums = [
            lane_sum(row_pairs(buffer.at[i], field[2 * z] + field[2 * z + 1]), 1)
            for i, field in enumerate((w1, u1, k1))
        ]
        blank = jnp.zeros((4, COLS), F32)
        g2[z] = jnp.concatenate([2.0 * jnp.sqrt(0.125 * sums[0]), blank], axis=0)
        h2[z + 1] = jnp.concatenate([2.0 * jnp.sqrt(0.125 * sums[1]), blank], axis=0)
        k2[z] = jnp.concatenate([sums[2], blank + 1.0], axis=0)

    loop(4, coarser)
    two = Level(4, 2, g2, h2, i2)

    def diagonals_two(z):
        i2[z] = 1.0 / two.diagonal_of(k2[z], z)

    loop(4, diagonals_two)


def coarse_solve(core, one, two, pieces, r1, xa1, xb1, r2, xa2, xb2, buffer):
    own, partner, odd, far = pieces
    clear_ends(xa1, xb1, xa2, xb2)
    starts = (16, 24 - 16 * core, 8 + 16 * core, 32 * core, 32 - 32 * core)
    starts = [s if isinstance(s, int) else pl.multiple_of(s, 8) for s in starts]

    def assemble(z):
        for i in range(2):
            j = 2 * z + i
            tiles = (own[j], partner[j], odd[j], odd[R_TILES + j], far[j])
            for start, tile in zip(starts, tiles):
                r1[z, i, pl.ds(start, 8), :] = tile

    loop(8, assemble)
    one.first(xa1, r1, FINE[0])
    one.update(xb1, xa1, r1, FINE[1])

    def restrict(z):
        for i in range(2):
            total = one.defect(xb1, r1, 2 * z, i) + one.defect(xb1, r1, 2 * z + 1, i)
            sums = lane_sum(row_pairs(buffer.at[i], total), 1)
            r2[z, i] = jnp.concatenate([sums, jnp.zeros((4, COLS), F32)], axis=0)

    loop(4, restrict)
    two.first(xa2, r2, COARSE[0])
    two.update(xb2, xa2, r2, COARSE[1])
    two.update(xa2, xb2, r2, COARSE[2])
    two.update(xb2, xa2, r2, COARSE[3])

    inner = [ref.at[:, :, 8:32, :] for ref in (xa1, xb1, r1)]
    inner_one = Level(8, 1, *(ref.at[:, 8:32, :] for ref in (one.g, one.h, one.inverse)))

    def prolong(z):
        for i in range(2):
            fine = row_repeat(buffer.at[i], xb2[z + 1, i, 4:16, :])
            for half in range(2):
                inner[0][2 * z + half + 1, i] = inner[1][2 * z + half + 1, i] + fine

    loop(4, prolong)
    inner_one.update(inner[1], inner[0], inner[2], FINE[0])
    inner_one.update(inner[0], inner[1], inner[2], FINE[1])


def fine_correct(level, out, xp, c1, wide, buffer):
    rows = c1[1:9, :, 12:28, :].reshape(R_TILES * 16, COLS)
    wide[...] = column_repeat(rows).reshape(R_TILES, 16, WIDE)

    def body(pair):
        for i in range(2):
            fine = row_repeat(buffer.at[i], wide[2 * pair + i])
            for half in range(2):
                out[2 * pair + half + 1, i] = xp[2 * pair + half + 1, i] + fine

    loop(NZ // 2, body)


def near_kernel(odd, near):
    near[...] = odd[0:R_TILES]


def after_kernel(odd, after, near):
    near[...] = odd[0:M_TILES]


def coarse_kernel(
    place, own, partner, odd, far, g1, h1, d1, i1, g2, h2, i2, w1, k1, u1, k2, buffer
):
    coarse_coefficients(
        place, (own, partner, odd, far), g1, h1, d1, i1, g2, h2, i2, w1, k1, u1, k2, buffer
    )


def middle_kernel(
    place, r, g, h, d, inverse, xp, own, partner, odd, far, g1, h1, d1, i1, g2, h2, i2,
    z_out, xp_out, r1_out,
    xa, xb, r1, xa1, xb1, r2, xa2, xb2, wide, sums, buffer,
):
    core = place[0]
    zero = Level(NZ, 1, g, h, inverse, d)
    one = Level(8, 1, g1, h1, i1, d1)
    two = Level(4, 2, g2, h2, i2)
    coarse_solve(core, one, two, (own, partner, odd, far), r1, xa1, xb1, r2, xa2, xb2, buffer)
    clear_ends(xa, xb, xp_out)
    fine_correct(zero, xa, xp, xa1, wide, buffer)
    zero.update(xb, xa, r, FINE[0])

    def last(z):
        scaled = FINE[1] * inverse[z]
        for i in range(2):
            z_out[z, i] = (1.0 - FINE[1]) * xb[z + 1, i] + scaled * (r[z, i] + zero.couple(xb, z, i))

    loop(NZ, last)
    zero.first(xa, z_out, FINE[0])
    zero.update(xp_out, xa, z_out, FINE[1])
    fine_restrict(zero, xp_out, z_out, sums, buffer, r1_out)


def last_kernel(
    place, rhs, r, g, h, d, inverse, xp, own, partner, odd, far, g1, h1, d1, i1, g2, h2, i2,
    direction, image, sums,
    xa, xb, r1, xa1, xb1, r2, xa2, xb2, wide, totals, buffer,
):
    core = place[0]
    zero = Level(NZ, 1, g, h, inverse, d)
    one = Level(8, 1, g1, h1, i1, d1)
    two = Level(4, 2, g2, h2, i2)
    coarse_solve(core, one, two, (own, partner, odd, far), r1, xa1, xb1, r2, xa2, xb2, buffer)
    clear_ends(xa, xb)
    fine_correct(zero, xa, xp, xa1, wide, buffer)
    zero.update(xb, xa, r, FINE[0])
    zero.update(xa, xb, r, FINE[1])

    def first_image(z):
        for i in range(2):
            xb[z + 1, i] = d[z] * xa[z + 1, i] - zero.couple(xa, z, i)

    loop(NZ, first_image)
    totals[...] = jnp.zeros(totals.shape, F32)

    def second_image(z):
        for i in range(2):
            field = xa[z + 1, i, 8:24, 0:COLS]
            value = (d[z] * xb[z + 1, i] - zero.couple(xb, z, i))[8:24, 0:COLS]
            direction[i, z] = field
            image[i, z] = value
            totals[i] += rhs[i, z] * field
            totals[2 + i] += field * value

    loop(NZ, second_image)
    row = sublanes(8, COLS)
    lane = lanes(8, COLS)
    line = jnp.zeros((8, COLS), F32)
    for i in range(4):
        line = jnp.where(lane == i, jnp.sum(totals[i]), line)

    def spread(j):
        sums[pl.ds(pl.multiple_of(8 * j, 8), 8), :] = line

    loop(sums.shape[0] // 8, spread)


def scale_kernel(rhs, direction, image, sums, solution_field, residual):
    total = jnp.sum(sums[...], axis=0, keepdims=True)
    lane = lanes(1, COLS)
    parts = [jnp.sum(jnp.where(lane == i, total, 0.0), axis=1, keepdims=True) for i in range(4)]
    for i in range(2):
        alpha = parts[i] / parts[2 + i]

        def body(z, i=i, alpha=alpha):
            solution_field[i, z] = alpha * direction[i, z]
            residual[i, z] = rhs[i, z] - alpha * image[i, z]

        loop(NZ, body)


COSTS = {
    "start_kernel": 1,
    "corner_kernel": 1,
    "widen_kernel": 30,
    "rows_kernel": 1,
    "material_kernel": 1,
    "down_kernel": 4,
    "near_kernel": 30,
    "after_kernel": 30,
    "coarse_kernel": 1,
    "middle_kernel": 6,
    "last_kernel": 6,
    "scale_kernel": 1,
}


def call(kernel, operands, outs, scratch=(), place=True, far=None):
    far = far or {}
    vmem = pl.BlockSpec(memory_space=pltpu.VMEM)
    specs = [pl.BlockSpec(memory_space=far[i]) if i in far else vmem for i in range(len(operands))]
    if place:
        specs[0] = pl.BlockSpec(memory_space=pltpu.SMEM)
    return pl.pallas_call(
        kernel,
        out_shape=[jax.ShapeDtypeStruct(shape, F32) for shape in outs],
        in_specs=specs,
        out_specs=[vmem] * len(outs),
        scratch_shapes=[pltpu.VMEM(shape, F32) if isinstance(shape, tuple) else shape for shape in scratch],
        cost_estimate=pl.CostEstimate(
            flops=COSTS[kernel.__name__] * 1_000_000_000, bytes_accessed=COSTS[kernel.__name__] * 3_000_000, transcendentals=0
        ),
        compiler_params=pltpu.CompilerParams(vmem_limit_bytes=16 * 1024 * 1024),
    )(*operands)


FIELD0 = (NZ, 2, EXT0, WIDE)
PADDED0 = (NZ + 2, 2, EXT0, WIDE)
PADDED1 = (10, 2, EXT1, COLS)
PADDED2 = (6, 2, EXT2, COLS)
BUFFER = (3, 2, EXT1, COLS)
SUMS = (R_TILES, 8, WIDE)
SPREAD = (R_TILES, 16, WIDE)
COARSE_SCRATCH = [(8, 2, EXT1, COLS), PADDED1, PADDED1, (4, 2, EXT2, COLS), PADDED2, PADDED2, SPREAD]


def shards(count_x, count_y, right_side, classes, sea_mask, kappa_table, cross_table, vertical_table):
    gx = lax.axis_index("gx")
    gy = lax.axis_index("gy")
    place = jnp.stack([gx % 2, gx, gy, jnp.int32(count_x), jnp.int32(count_y)]).astype(jnp.int32)
    table = jnp.stack([jnp.sqrt(cross_table), jnp.sqrt(vertical_table), kappa_table])
    table = jnp.pad(table, ((0, 5), (0, COLS - table.shape[1])))

    pairs_on_chip = [(i, i ^ 1) for i in range(count_x)]
    pairs_across = [(i, (i + 1 if i % 2 else i - 1) % count_x) for i in range(count_x)]

    def on_chip(value):
        return lax.ppermute(value, "gx", pairs_on_chip)

    def across_chips(value):
        return lax.ppermute(value, "gx", pairs_across)

    def rows_of(own, partner):
        odd = across_chips(jnp.concatenate([own, partner], axis=0))
        near = call(near_kernel, (odd,), [own.shape], place=False)[0]
        return own, partner, odd, on_chip(near)

    forward = [(i, (i + 1) % count_y) for i in range(count_y)]
    backward = [(target, source) for source, target in forward]

    def both_sides(to_left, to_right):
        return lax.ppermute(to_right, "gy", forward), lax.ppermute(to_left, "gy", backward)

    part = lax.broadcasted_iota(jnp.int32, (4, *classes.shape), 0)
    materials = jnp.where(part == 2, classes[None], sea_mask[None]).astype(F32)
    twice = jnp.broadcast_to(right_side[None], (2, *right_side.shape)).reshape(part.shape)
    fields = jnp.where(part < 2, twice, materials)
    to_left, to_right, msg_o = call(
        start_kernel, (place, fields), [(MSG_Y, ROWS, COLS), (MSG_Y, ROWS, COLS), (MSG_X, 8, COLS)]
    )
    from_o = across_chips(msg_o)
    from_left, from_right = both_sides(to_left, to_right)
    r_own, c_own, s_own, msg_x = call(
        rows_kernel,
        (place, fields, from_left, from_right),
        [(NZ, 2, ROWS, WIDE), (NZ, ROWS, WIDE), (NZ, ROWS, WIDE), (MSG_X, 8, WIDE)],
    )
    from_x = on_chip(msg_x)
    g_own, h_own, k_own, packed = call(
        material_kernel,
        (c_own, s_own, table),
        [(NZ, ROWS, WIDE)] * 3 + [(M_TILES, 8, COLS)],
        [(M_TILES, 8, WIDE), BUFFER],
        place=False,
    )
    corner_tiles = call(corner_kernel, (from_o, packed), [(MSG_X // 2, 8, COLS)] * 2, place=False, far={1: pl.ANY})
    wide = call(widen_kernel, (from_o, *both_sides(*corner_tiles)), [(MSG_X, 8, WIDE)], place=False)[0]
    packed_partner = on_chip(packed)
    packed_odd = across_chips(jnp.concatenate([packed, packed_partner], axis=0))
    r, g, h, d, inverse, xp, r1 = call(
        down_kernel,
        (place, r_own, g_own, h_own, k_own, from_x, wide, table),
        [FIELD0, (NZ, EXT0, WIDE), (NZ + 2, EXT0, WIDE), (NZ, EXT0, WIDE), (NZ, EXT0, WIDE), PADDED0, (R_TILES, 8, COLS)],
        [PADDED0, (NZ, EXT0, WIDE), (2, NZ, WIDE), SUMS, BUFFER],
    )
    rows = rows_of(r1, on_chip(r1))
    packed_near = call(
        after_kernel, (packed_odd, rows[1]), [packed.shape], place=False, far={1: pl.ANY}
    )[0]
    material = (packed, packed_partner, packed_odd, on_chip(packed_near))
    one = [(8, EXT1, COLS), (10, EXT1, COLS), (8, EXT1, COLS), (8, EXT1, COLS)]
    two = [(4, EXT2, COLS), (6, EXT2, COLS), (4, EXT2, COLS)]
    coarse = call(
        coarse_kernel, (place, *material), [*one, *two], [one[0], one[0], one[0], two[0], BUFFER]
    )
    r, xp, r1 = call(
        middle_kernel,
        (place, r, g, h, d, inverse, xp, *rows, *coarse),
        [FIELD0, PADDED0, (R_TILES, 8, COLS)],
        [PADDED0, PADDED0, *COARSE_SCRATCH, SUMS, BUFFER],
    )
    count = count_x * count_y
    direction, image, sums = call(
        last_kernel,
        (place, fields, r, g, h, d, inverse, xp, *rows_of(r1, on_chip(r1)), *coarse),
        [(2, NZ, ROWS, COLS)] * 2 + [(count, COLS)],
        [PADDED0, PADDED0, *COARSE_SCRATCH, (4, ROWS, COLS), BUFFER],
    )
    sums = lax.all_to_all(sums.reshape(count, 1, COLS), ("gx", "gy"), 0, 0).reshape(count, COLS)
    return tuple(
        call(
            scale_kernel,
            (fields, direction, image, sums),
            [(2, NZ, ROWS, COLS)] * 2,
            place=False,
        )
    )


def solution(mesh):
    return jax.shard_map(
        functools.partial(shards, mesh.shape["gx"], mesh.shape["gy"]),
        mesh=mesh,
        in_specs=(
            P(None, None, "gx", "gy"),
            P(None, "gx", "gy"),
            P(None, "gx", "gy"),
            P(),
            P(),
            P(),
        ),
        out_specs=(P(None, None, "gx", "gy"), P(None, None, "gx", "gy")),
        check_vma=False,
    )
```

```python
import functools
import math

import jax
import jax.numpy as jnp
from jax import lax
from jax.experimental import pallas as pl
from jax.experimental.pallas import tpu as pltpu
from jax.sharding import PartitionSpec as P

F32 = jnp.float32
NZ = 16
ROWS = 16
COLS = 128
WIDE = 256
HALF = 64
UNROLL = 8
EXT0 = 32
EXT1 = 40
EXT2 = 24


def cheb_weights(degree, lower_end, upper_end):
    middle = 0.5 * (upper_end + lower_end)
    radius = 0.5 * (upper_end - lower_end)
    return [
        1.0 / (middle + radius * math.cos(math.pi * (2 * index_k + 1) / (2 * degree)))
        for index_k in range(degree)
    ]


FINE = cheb_weights(2, 0.3, 2.0)
COARSE = cheb_weights(4, 0.1, 2.0)


def loop(count, body):
    def step(index, carry):
        body(index)
        return carry

    lax.fori_loop(0, count, step, 0, unroll=min(count, UNROLL))


def lanes(rows, width):
    return lax.broadcasted_iota(jnp.int32, (rows, width), 1)


def sublanes(rows, width):
    return lax.broadcasted_iota(jnp.int32, (rows, width), 0)


def lane_sum(value, step):
    width = value.shape[1]
    first = (lanes(*value.shape) // step) % 2 == 0
    return value + jnp.where(first, pltpu.roll(value, width - step, 1), pltpu.roll(value, step, 1))


def across(value, step):
    rows, width = value.shape
    return (
        pltpu.roll(value, 1, 0)
        + pltpu.roll(value, rows - 1, 0)
        + pltpu.roll(value, step, 1)
        + pltpu.roll(value, width - step, 1)
    )


def row_pairs(buffer, value):
    rows, width = value.shape
    parts = []
    for half in range(width // COLS):
        buffer[half, 0:rows, :] = value[:, half * COLS : (half + 1) * COLS]
        parts.append(
            buffer[half, pl.ds(0, rows // 2, stride=2), :] + buffer[half, pl.ds(1, rows // 2, stride=2), :]
        )
    return parts[0] if len(parts) == 1 else jnp.concatenate(parts, axis=1)


def row_repeat(buffer, value):
    rows, width = value.shape
    parts = []
    for half in range(width // COLS):
        part = value[:, half * COLS : (half + 1) * COLS]
        buffer[half, pl.ds(0, rows, stride=2), :] = part
        buffer[half, pl.ds(1, rows, stride=2), :] = part
        parts.append(buffer[half, 0 : 2 * rows, :])
    return parts[0] if len(parts) == 1 else jnp.concatenate(parts, axis=1)


def column_pairs(value):
    row = lax.broadcasted_iota(jnp.int32, (WIDE, COLS), 0)
    column = lax.broadcasted_iota(jnp.int32, (WIDE, COLS), 1)
    matrix = jnp.where(row // 2 == column, 1.0, 0.0)
    return jnp.dot(value, matrix, precision=lax.Precision.HIGHEST, preferred_element_type=F32)


def column_repeat(value):
    row = lax.broadcasted_iota(jnp.int32, (COLS, WIDE), 0)
    column = lax.broadcasted_iota(jnp.int32, (COLS, WIDE), 1)
    matrix = jnp.where(column // 2 == row, 1.0, 0.0)
    return jnp.dot(value, matrix, precision=lax.Precision.HIGHEST, preferred_element_type=F32)


def half_rows(first, second, lower):
    row = sublanes(*first.shape)
    low = jnp.where(row < 4, first, pltpu.roll(second, 4, 0))
    high = jnp.where(row < 4, pltpu.roll(first, 4, 0), second)
    return jnp.where(lower, low, high)


def pick(table_row, index):
    rows, width = index.shape
    table = jnp.broadcast_to(table_row, (rows, COLS))
    parts = [
        jnp.take_along_axis(table, index[:, start : start + COLS], axis=1)
        for start in range(0, width, COLS)
    ]
    return parts[0] if len(parts) == 1 else jnp.concatenate(parts, axis=1)


def pack_halves(first, second):
    left = lanes(*first.shape) < HALF
    low = jnp.where(left, first, pltpu.roll(second, HALF, 1))
    high = jnp.where(left, pltpu.roll(first, HALF, 1), second)
    return low, high


def unpack_halves(from_right, from_left):
    left = lanes(*from_right.shape) < HALF
    first = jnp.where(left, from_right, pltpu.roll(from_left, HALF, 1))
    second = jnp.where(left, pltpu.roll(from_right, HALF, 1), from_left)
    return first, second


def pack_sea(fields):
    rows, width = fields[0].shape
    even_lane = lanes(rows, width) % 2 == 0
    even_row = sublanes(rows, width) % 2 == 0
    pairs = [
        jnp.where(even_lane, fields[i], pltpu.roll(fields[i + 1], 1, 1)) for i in (0, 2)
    ]
    return jnp.where(even_row, pairs[0], pltpu.roll(pairs[1], 1, 0))


def unpack_sea(packed):
    rows, width = packed.shape
    spot = (lanes(rows, width) % 2 == 0) & (sublanes(rows, width) % 2 == 0)
    fields = []
    for pair in (packed, pltpu.roll(packed, rows - 1, 0)):
        for field in (pair, pltpu.roll(pair, width - 1, 1)):
            fields.append(jnp.where(spot, field, 1.0))
    return fields


def fill_message(message, rhs, classes, sea, start, edge):
    def fields(z):
        for i in range(2):
            message[2 * z + i] = rhs(z, i)[pl.ds(start, 8), :]
        message[32 + z] = classes.at[z][pl.ds(start, 8), :]
        message.at[52 + z // 8][pl.ds(z % 8, 1), :] = classes.at[z][pl.ds(edge, 1), :]
        message.at[54 + z // 8][pl.ds(z % 8, 1), :] = sea.at[z][pl.ds(edge, 1), :]

    loop(NZ, fields)

    def quads(j):
        message[48 + j] = pack_sea([sea[4 * j + i, pl.ds(start, 8), :] for i in range(4)])

    loop(4, quads)


MSG_Y = 26
MSG_X = 56
R_TILES = 16
M_TILES = 24


def start_kernel(place, fields, to_left, to_right, message):
    core = place[0]
    classes, sea = fields.at[2], fields.at[3]

    def convert(pair):
        to_left[16 + pair], to_right[16 + pair] = pack_halves(classes[2 * pair], classes[2 * pair + 1])

    loop(8, convert)
    for j in range(2):
        quads = [pack_sea([sea[8 * j + 4 * q + i] for i in range(4)]) for q in range(2)]
        to_left[24 + j], to_right[24 + j] = pack_halves(quads[0], quads[1])

    def pair(z):
        to_left[z], to_right[z] = pack_halves(fields[0, z], fields[1, z])

    loop(NZ, pair)
    start = pl.multiple_of(8 * core, 8)
    fill_message(message, lambda z, i: fields.at[i, z], classes, sea, start, 8 - core)


def corner_kernel(message, after, to_left, to_right):
    def pair(p):
        to_left[p], to_right[p] = pack_halves(message[2 * p], message[2 * p + 1])

    loop(MSG_X // 2, pair)


def widen_kernel(message, corner_left, corner_right, wide):
    def pair(p):
        for i, halo in enumerate(unpack_halves(corner_right[p], corner_left[p])):
            wide[2 * p + i] = jnp.concatenate([message[2 * p + i], halo], axis=1)

    loop(MSG_X // 2, pair)


def rows_kernel(place, fields, from_left, from_right, r_out, c_out, s_out, message):
    core = place[0]
    gy = place[2]
    left = lanes(ROWS, COLS) < HALF
    inside = jnp.where(
        left,
        jnp.where(gy < place[4] - 1, 1.0, 0.0),
        jnp.where(gy > 0, 1.0, 0.0),
    )

    def rhs_step(z):
        halo = unpack_halves(from_right[z], from_left[z])
        for i in range(2):
            r_out[z, i] = jnp.concatenate([fields[i, z], halo[i]], axis=1)

    loop(NZ, rhs_step)

    def class_step(pair):
        for i, halo in enumerate(unpack_halves(from_right[16 + pair], from_left[16 + pair])):
            c_out[2 * pair + i] = jnp.concatenate([fields[2, 2 * pair + i], halo], axis=1)

    loop(8, class_step)
    for j in range(2):
        quads = unpack_halves(from_right[24 + j], from_left[24 + j])
        for q in range(2):
            for i, field in enumerate(unpack_sea(quads[q])):
                z = 8 * j + 4 * q + i
                s_out[z] = jnp.concatenate([fields[3, z], field * inside], axis=1)
    start = pl.multiple_of(8 * (1 - core), 8)
    fill_message(message, lambda z, i: r_out.at[z, i], c_out, s_out, start, 7 + core)


def material_kernel(c_in, s_in, table, g_out, h_out, k_out, coarse, sums, buffer):
    def fields(z):
        index = c_in[z].astype(jnp.int32)
        sea = s_in[z]
        g = pick(table[0:1], index) * sea
        h = pick(table[1:2], index) * sea
        k = pick(table[2:3], index) * sea + (1.0 - sea)
        g_out[z] = g
        h_out[z] = h
        k_out[z] = k
        return 0.125 * g * g, 0.125 * h * h, k

    def step(pair):
        first = fields(2 * pair)
        second = fields(2 * pair + 1)
        for i in range(3):
            sums[8 * i + pair] = row_pairs(buffer.at[i], first[i] + second[i])

    loop(8, step)
    coarse[...] = column_pairs(sums[...].reshape(M_TILES * 8, WIDE)).reshape(M_TILES, 8, COLS)


class Level:
    def __init__(self, depth, step, g, h, inverse, diagonal=None):
        self.depth, self.step = depth, step
        self.g, self.h, self.inverse, self.diagonal = g, h, inverse, diagonal

    def couple(self, x, z, i):
        horizontal = self.g[z] * across(self.g[z] * x[z + 1, i], self.step)
        vertical = self.h[z + 1] * (self.h[z] * x[z, i] + self.h[z + 2] * x[z + 2, i])
        return horizontal + vertical

    def first(self, x, r, weight):
        def body(z):
            scaled = weight * self.inverse[z]
            for i in range(2):
                x[z + 1, i] = scaled * r[z, i]

        loop(self.depth, body)

    def update(self, new, x, r, weight):
        def body(z):
            scaled = weight * self.inverse[z]
            for i in range(2):
                new[z + 1, i] = (1.0 - weight) * x[z + 1, i] + scaled * (r[z, i] + self.couple(x, z, i))

        loop(self.depth, body)

    def defect(self, x, r, z, i):
        return r[z, i] - self.diagonal[z] * x[z + 1, i] + self.couple(x, z, i)

    def diagonal_of(self, k, z):
        horizontal = self.g[z] * across(self.g[z], self.step)
        vertical = self.h[z + 1] * (self.h[z] + self.h[z + 2])
        return k + horizontal + vertical


def clear_ends(*refs):
    for ref in refs:
        ref[0] = jnp.zeros(ref.shape[1:], ref.dtype)
        ref[ref.shape[0] - 1] = jnp.zeros(ref.shape[1:], ref.dtype)


def fine_restrict(level, x, r, sums, buffer, out):
    def body(pair):
        for i in range(2):
            total = level.defect(x, r, 2 * pair, i) + level.defect(x, r, 2 * pair + 1, i)
            sums[2 * pair + i] = row_pairs(buffer.at[i], total[8:24])

    loop(NZ // 2, body)
    out[...] = column_pairs(sums[...].reshape(R_TILES * 8, WIDE)).reshape(R_TILES, 8, COLS)


def down_kernel(
    place, r_own, g_own, h_own, k_own, from_x, wide, table,
    r, g, h, d, inverse, xp, r1, xa, ka, edges, sums, buffer,
):
    core = place[0]
    gx = place[1]
    gy = place[2]
    open_side = jnp.where((gx > 0) & (gx < place[3] - 1), 1.0, 0.0)
    lane = lanes(8, WIDE)
    ends = jnp.where(
        lane < COLS,
        1.0,
        jnp.where(lane < COLS + HALF, jnp.where(gy < place[4] - 1, 1.0, 0.0), jnp.where(gy > 0, 1.0, 0.0)),
    )
    clear_ends(h, xp, xa)

    def own(z):
        for i in range(2):
            r[z, i, 8:24, :] = r_own[z, i]
        g[z, 8:24, :] = g_own[z]
        h[z + 1, 8:24, :] = h_own[z]
        ka[z, 8:24, :] = k_own[z]

    loop(NZ, own)

    for message, start, scale, slot in ((from_x, 24 * (1 - core), 1.0, 1 - core), (wide, 24 * core, open_side, core)):
        start = pl.multiple_of(start, 8)
        valid = scale * ends

        def halo(j, message=message, start=start, valid=valid):
            for q, sea in enumerate(unpack_sea(message[48 + j])):
                z = 4 * j + q
                sea = sea * valid
                index = message[32 + z].astype(jnp.int32)
                g[z, pl.ds(start, 8), :] = pick(table[0:1], index) * sea
                h[z + 1, pl.ds(start, 8), :] = pick(table[1:2], index) * sea
                ka[z, pl.ds(start, 8), :] = pick(table[2:3], index) * sea + (1.0 - sea)
                for i in range(2):
                    r[z, i, pl.ds(start, 8), :] = message[2 * z + i]

        loop(4, halo)
        for j in range(2):
            index = message[52 + j].astype(jnp.int32)
            edges[slot, 8 * j : 8 * j + 8, :] = pick(table[0:1], index) * (message[54 + j] * valid)

    level = Level(NZ, 1, g, h, inverse, d)
    row = sublanes(EXT0, WIDE)

    def diagonals(z):
        here = g[z]
        below = jnp.where(row == 0, edges[0, pl.ds(z, 1), :], pltpu.roll(here, 1, 0))
        above = jnp.where(row == EXT0 - 1, edges[1, pl.ds(z, 1), :], pltpu.roll(here, EXT0 - 1, 0))
        beside = pltpu.roll(here, 1, 1) + pltpu.roll(here, WIDE - 1, 1)
        total = ka[z] + here * (below + above + beside) + h[z + 1] * (h[z] + h[z + 2])
        d[z] = total
        reciprocal = 1.0 / total
        inverse[z] = reciprocal
        for i in range(2):
            xa[z + 1, i] = (FINE[0] * reciprocal) * r[z, i]

    loop(NZ, diagonals)
    level.update(xp, xa, r, FINE[1])
    fine_restrict(level, xp, r, sums, buffer, r1)


def coarse_coefficients(place, pieces, g1, h1, d1, i1, g2, h2, i2, w1, k1, u1, k2, buffer):
    core = place[0]
    clear_ends(h1, h2)
    own, partner, odd, far = pieces
    low = jnp.where(place[1] >= 2, 1.0, 0.0)
    high = jnp.where(place[1] < place[3] - 2, 1.0, 0.0)
    near_side = jnp.where(core == 0, low, high)
    far_side = jnp.where(core == 0, high, low)
    scales = (1.0, 1.0, near_side, near_side, far_side)
    starts = (16, 24 - 16 * core, 8 + 16 * core, 32 * core, 32 - 32 * core)
    starts = [s if isinstance(s, int) else pl.multiple_of(s, 8) for s in starts]

    def assemble(z):
        for i, field in enumerate((w1, u1, k1)):
            j = 8 * i + z
            tiles = (own[j], partner[j], odd[j], odd[M_TILES + j], far[j])
            for start, tile, scale in zip(starts, tiles, scales):
                field[z, pl.ds(start, 8), :] = tile * scale if i < 2 else tile

    loop(8, assemble)

    def roots(z):
        g1[z] = 2.0 * jnp.sqrt(w1[z])
        h1[z + 1] = 2.0 * jnp.sqrt(u1[z])

    loop(8, roots)
    one = Level(8, 1, g1, h1, i1, d1)

    def diagonals(z):
        total = one.diagonal_of(k1[z], z)
        d1[z] = total
        i1[z] = 1.0 / total

    loop(8, diagonals)

    def coarser(z):
        sums = [
            lane_sum(row_pairs(buffer.at[i], field[2 * z] + field[2 * z + 1]), 1)
            for i, field in enumerate((w1, u1, k1))
        ]
        blank = jnp.zeros((4, COLS), F32)
        g2[z] = jnp.concatenate([2.0 * jnp.sqrt(0.125 * sums[0]), blank], axis=0)
        h2[z + 1] = jnp.concatenate([2.0 * jnp.sqrt(0.125 * sums[1]), blank], axis=0)
        k2[z] = jnp.concatenate([sums[2], blank + 1.0], axis=0)

    loop(4, coarser)
    two = Level(4, 2, g2, h2, i2)

    def diagonals_two(z):
        i2[z] = 1.0 / two.diagonal_of(k2[z], z)

    loop(4, diagonals_two)


def coarse_solve(core, one, two, pieces, far_tile, r1, xa1, xb1, r2, xa2, xb2, buffer):
    own, partner, odd, second = pieces
    clear_ends(xa1, xb1, xa2, xb2)
    starts = (16, 24 - 16 * core, 8 + 16 * core, 32 * core, 32 - 32 * core)
    starts = [s if isinstance(s, int) else pl.multiple_of(s, 8) for s in starts]

    def assemble(z):
        for i in range(2):
            j = 2 * z + i
            tiles = (own[j], partner[j], odd[j], far_tile(z, i), second[j])
            for start, tile in zip(starts, tiles):
                r1[z, i, pl.ds(start, 8), :] = tile

    loop(8, assemble)
    one.first(xa1, r1, FINE[0])
    one.update(xb1, xa1, r1, FINE[1])

    def restrict(z):
        for i in range(2):
            total = one.defect(xb1, r1, 2 * z, i) + one.defect(xb1, r1, 2 * z + 1, i)
            sums = lane_sum(row_pairs(buffer.at[i], total), 1)
            r2[z, i] = jnp.concatenate([sums, jnp.zeros((4, COLS), F32)], axis=0)

    loop(4, restrict)
    two.first(xa2, r2, COARSE[0])
    two.update(xb2, xa2, r2, COARSE[1])
    two.update(xa2, xb2, r2, COARSE[2])
    two.update(xb2, xa2, r2, COARSE[3])

    inner = [ref.at[:, :, 8:32, :] for ref in (xa1, xb1, r1)]
    inner_one = Level(8, 1, *(ref.at[:, 8:32, :] for ref in (one.g, one.h, one.inverse)))

    def prolong(z):
        for i in range(2):
            fine = row_repeat(buffer.at[i], xb2[z + 1, i, 4:16, :])
            for half in range(2):
                inner[0][2 * z + half + 1, i] = inner[1][2 * z + half + 1, i] + fine

    loop(4, prolong)
    inner_one.update(inner[1], inner[0], inner[2], FINE[0])
    inner_one.update(inner[0], inner[1], inner[2], FINE[1])


def fine_correct(level, out, xp, c1, wide, buffer):
    rows = c1[1:9, :, 12:28, :].reshape(R_TILES * 16, COLS)
    wide[...] = column_repeat(rows).reshape(R_TILES, 16, WIDE)

    def body(pair):
        for i in range(2):
            fine = row_repeat(buffer.at[i], wide[2 * pair + i])
            for half in range(2):
                out[2 * pair + half + 1, i] = xp[2 * pair + half + 1, i] + fine

    loop(NZ // 2, body)


def near_kernel(odd, near):
    near[...] = odd[0:R_TILES]


def far_half_kernel(place, own, partner, message):
    message[0:R_TILES] = own[...]

    def pair(p):
        message[R_TILES + p] = half_rows(partner[2 * p], partner[2 * p + 1], place[0] == 0)

    loop(R_TILES // 2, pair)


def after_kernel(odd, after, near):
    near[...] = odd[0:M_TILES]


def coarse_kernel(
    place, own, partner, odd, far, g1, h1, d1, i1, g2, h2, i2, w1, k1, u1, k2, buffer
):
    coarse_coefficients(
        place, (own, partner, odd, far), g1, h1, d1, i1, g2, h2, i2, w1, k1, u1, k2, buffer
    )


def middle_kernel(
    place, r, g, h, d, inverse, xp, own, partner, odd, far, g1, h1, d1, i1, g2, h2, i2,
    z_out, xp_out, r1_out,
    xa, xb, r1, xa1, xb1, r2, xa2, xb2, wide, sums, buffer,
):
    core = place[0]
    zero = Level(NZ, 1, g, h, inverse, d)
    one = Level(8, 1, g1, h1, i1, d1)
    two = Level(4, 2, g2, h2, i2)
    coarse_solve(core, one, two, (own, partner, odd, far), lambda z, i: odd[R_TILES + 2 * z + i], r1, xa1, xb1, r2, xa2, xb2, buffer)
    clear_ends(xa, xb, xp_out)
    fine_correct(zero, xa, xp, xa1, wide, buffer)
    zero.update(xb, xa, r, FINE[0])

    def last(z):
        scaled = FINE[1] * inverse[z]
        first = FINE[0] * inverse[z]
        for i in range(2):
            value = (1.0 - FINE[1]) * xb[z + 1, i] + scaled * (r[z, i] + zero.couple(xb, z, i))
            z_out[z, i] = value
            xa[z + 1, i] = first * value

    loop(NZ, last)
    zero.update(xp_out, xa, z_out, FINE[1])
    fine_restrict(zero, xp_out, z_out, sums, buffer, r1_out)


def last_kernel(
    place, rhs, r, g, h, d, inverse, xp, own, partner, odd, far, g1, h1, d1, i1, g2, h2, i2,
    direction, image, sums,
    xa, xb, r1, xa1, xb1, r2, xa2, xb2, wide, totals, buffer,
):
    core = place[0]
    zero = Level(NZ, 1, g, h, inverse, d)
    one = Level(8, 1, g1, h1, i1, d1)
    two = Level(4, 2, g2, h2, i2)

    def far_tile(z, i):
        tile = odd[R_TILES + z]
        return jnp.where((core == 0) == (i == 0), pltpu.roll(tile, 4, 0), tile)

    coarse_solve(core, one, two, (own, partner, odd, far), far_tile, r1, xa1, xb1, r2, xa2, xb2, buffer)
    clear_ends(xa, xb)
    fine_correct(zero, xa, xp, xa1, wide, buffer)
    zero.update(xb, xa, r, FINE[0])
    zero.update(xa, xb, r, FINE[1])

    def first_image(z):
        for i in range(2):
            xb[z + 1, i] = d[z] * xa[z + 1, i] - zero.couple(xa, z, i)

    loop(NZ, first_image)
    totals[...] = jnp.zeros(totals.shape, F32)

    def second_image(z):
        for i in range(2):
            field = xa[z + 1, i, 8:24, 0:COLS]
            value = (d[z] * xb[z + 1, i] - zero.couple(xb, z, i))[8:24, 0:COLS]
            direction[i, z] = field
            image[i, z] = value
            totals[i] += rhs[i, z] * field
            totals[2 + i] += field * value

    loop(NZ, second_image)
    row = sublanes(8, COLS)
    lane = lanes(8, COLS)
    line = jnp.zeros((8, COLS), F32)
    for i in range(4):
        line = jnp.where(lane == i, jnp.sum(totals[i]), line)

    def spread(j):
        sums[pl.ds(pl.multiple_of(8 * j, 8), 8), :] = line

    loop(sums.shape[0] // 8, spread)


def scale_kernel(rhs, direction, image, sums, solution_field, residual):
    total = jnp.sum(sums[...], axis=0, keepdims=True)
    lane = lanes(1, COLS)
    parts = [jnp.sum(jnp.where(lane == i, total, 0.0), axis=1, keepdims=True) for i in range(4)]
    for i in range(2):
        alpha = parts[i] / parts[2 + i]

        def body(z, i=i, alpha=alpha):
            solution_field[i, z] = alpha * direction[i, z]
            residual[i, z] = rhs[i, z] - alpha * image[i, z]

        loop(NZ, body)


COSTS = {
    "start_kernel": 1,
    "corner_kernel": 1,
    "widen_kernel": 30,
    "rows_kernel": 1,
    "material_kernel": 1,
    "down_kernel": 4,
    "near_kernel": 30,
    "far_half_kernel": 1,
    "after_kernel": 30,
    "coarse_kernel": 1,
    "middle_kernel": 6,
    "last_kernel": 6,
    "scale_kernel": 1,
}


def call(kernel, operands, outs, scratch=(), place=True, far=None):
    far = far or {}
    vmem = pl.BlockSpec(memory_space=pltpu.VMEM)
    specs = [pl.BlockSpec(memory_space=far[i]) if i in far else vmem for i in range(len(operands))]
    if place:
        specs[0] = pl.BlockSpec(memory_space=pltpu.SMEM)
    return pl.pallas_call(
        kernel,
        out_shape=[jax.ShapeDtypeStruct(shape, F32) for shape in outs],
        in_specs=specs,
        out_specs=[vmem] * len(outs),
        scratch_shapes=[pltpu.VMEM(shape, F32) if isinstance(shape, tuple) else shape for shape in scratch],
        cost_estimate=pl.CostEstimate(
            flops=COSTS[kernel.__name__] * 1_000_000_000, bytes_accessed=COSTS[kernel.__name__] * 3_000_000, transcendentals=0
        ),
        compiler_params=pltpu.CompilerParams(vmem_limit_bytes=16 * 1024 * 1024),
    )(*operands)


FIELD0 = (NZ, 2, EXT0, WIDE)
PADDED0 = (NZ + 2, 2, EXT0, WIDE)
PADDED1 = (10, 2, EXT1, COLS)
PADDED2 = (6, 2, EXT2, COLS)
BUFFER = (3, 2, EXT1, COLS)
SUMS = (R_TILES, 8, WIDE)
SPREAD = (R_TILES, 16, WIDE)
COARSE_SCRATCH = [(8, 2, EXT1, COLS), PADDED1, PADDED1, (4, 2, EXT2, COLS), PADDED2, PADDED2, SPREAD]


def shards(count_x, count_y, right_side, classes, sea_mask, kappa_table, cross_table, vertical_table):
    gx = lax.axis_index("gx")
    gy = lax.axis_index("gy")
    place = jnp.stack([gx % 2, gx, gy, jnp.int32(count_x), jnp.int32(count_y)]).astype(jnp.int32)
    table = jnp.stack([jnp.sqrt(cross_table), jnp.sqrt(vertical_table), kappa_table])
    table = jnp.pad(table, ((0, 5), (0, COLS - table.shape[1])))

    pairs_on_chip = [(i, i ^ 1) for i in range(count_x)]
    pairs_across = [(i, (i + 1 if i % 2 else i - 1) % count_x) for i in range(count_x)]

    def on_chip(value):
        return lax.ppermute(value, "gx", pairs_on_chip)

    def across_chips(value):
        return lax.ppermute(value, "gx", pairs_across)

    def rows_of(own, partner, message):
        odd = across_chips(message)
        near = call(near_kernel, (odd,), [own.shape], place=False)[0]
        return own, partner, odd, on_chip(near)

    forward = [(i, (i + 1) % count_y) for i in range(count_y)]
    backward = [(target, source) for source, target in forward]

    def both_sides(to_left, to_right):
        return lax.ppermute(to_right, "gy", forward), lax.ppermute(to_left, "gy", backward)

    part = lax.broadcasted_iota(jnp.int32, (4, *classes.shape), 0)
    materials = jnp.where(part == 2, classes[None], sea_mask[None]).astype(F32)
    twice = jnp.broadcast_to(right_side[None], (2, *right_side.shape)).reshape(part.shape)
    fields = jnp.where(part < 2, twice, materials)
    to_left, to_right, msg_o = call(
        start_kernel, (place, fields), [(MSG_Y, ROWS, COLS), (MSG_Y, ROWS, COLS), (MSG_X, 8, COLS)]
    )
    from_o = across_chips(msg_o)
    from_left, from_right = both_sides(to_left, to_right)
    r_own, c_own, s_own, msg_x = call(
        rows_kernel,
        (place, fields, from_left, from_right),
        [(NZ, 2, ROWS, WIDE), (NZ, ROWS, WIDE), (NZ, ROWS, WIDE), (MSG_X, 8, WIDE)],
    )
    from_x = on_chip(msg_x)
    g_own, h_own, k_own, packed = call(
        material_kernel,
        (c_own, s_own, table),
        [(NZ, ROWS, WIDE)] * 3 + [(M_TILES, 8, COLS)],
        [(M_TILES, 8, WIDE), BUFFER],
        place=False,
    )
    corner_tiles = call(corner_kernel, (from_o, packed), [(MSG_X // 2, 8, COLS)] * 2, place=False, far={1: pl.ANY})
    wide = call(widen_kernel, (from_o, *both_sides(*corner_tiles)), [(MSG_X, 8, WIDE)], place=False)[0]
    packed_partner = on_chip(packed)
    packed_odd = across_chips(jnp.concatenate([packed, packed_partner], axis=0))
    r, g, h, d, inverse, xp, r1 = call(
        down_kernel,
        (place, r_own, g_own, h_own, k_own, from_x, wide, table),
        [FIELD0, (NZ, EXT0, WIDE), (NZ + 2, EXT0, WIDE), (NZ, EXT0, WIDE), (NZ, EXT0, WIDE), PADDED0, (R_TILES, 8, COLS)],
        [PADDED0, (NZ, EXT0, WIDE), (2, NZ, WIDE), SUMS, BUFFER],
    )
    partner = on_chip(r1)
    rows = rows_of(r1, partner, jnp.concatenate([r1, partner], axis=0))
    packed_near = call(
        after_kernel, (packed_odd, rows[1]), [packed.shape], place=False, far={1: pl.ANY}
    )[0]
    material = (packed, packed_partner, packed_odd, on_chip(packed_near))
    one = [(8, EXT1, COLS), (10, EXT1, COLS), (8, EXT1, COLS), (8, EXT1, COLS)]
    two = [(4, EXT2, COLS), (6, EXT2, COLS), (4, EXT2, COLS)]
    coarse = call(
        coarse_kernel, (place, *material), [*one, *two], [one[0], one[0], one[0], two[0], BUFFER]
    )
    r, xp, r1 = call(
        middle_kernel,
        (place, r, g, h, d, inverse, xp, *rows, *coarse),
        [FIELD0, PADDED0, (R_TILES, 8, COLS)],
        [PADDED0, PADDED0, *COARSE_SCRATCH, SUMS, BUFFER],
    )
    partner = on_chip(r1)
    message = call(far_half_kernel, (place, r1, partner), [(R_TILES * 3 // 2, 8, COLS)])[0]
    count = count_x * count_y
    direction, image, sums = call(
        last_kernel,
        (place, fields, r, g, h, d, inverse, xp, *rows_of(r1, partner, message), *coarse),
        [(2, NZ, ROWS, COLS)] * 2 + [(count, COLS)],
        [PADDED0, PADDED0, *COARSE_SCRATCH, (4, ROWS, COLS), BUFFER],
    )
    sums = lax.all_to_all(sums.reshape(count, 1, COLS), ("gx", "gy"), 0, 0).reshape(count, COLS)
    return tuple(
        call(
            scale_kernel,
            (fields, direction, image, sums),
            [(2, NZ, ROWS, COLS)] * 2,
            place=False,
        )
    )


def solution(mesh):
    return jax.shard_map(
        functools.partial(shards, mesh.shape["gx"], mesh.shape["gy"]),
        mesh=mesh,
        in_specs=(
            P(None, None, "gx", "gy"),
            P(None, "gx", "gy"),
            P(None, "gx", "gy"),
            P(),
            P(),
            P(),
        ),
        out_specs=(P(None, None, "gx", "gy"), P(None, None, "gx", "gy")),
        check_vma=False,
    )
```

```python
import functools
import math

import jax
import jax.numpy as jnp
from jax import lax
from jax.experimental import pallas as pl
from jax.experimental.pallas import tpu as pltpu
from jax.sharding import PartitionSpec as P

F32 = jnp.float32
NZ = 16
ROWS = 16
COLS = 128
WIDE = 256
HALF = 64
UNROLL = 8
EXT0 = 32
EXT1 = 40
EXT2 = 24


def cheb_weights(degree, lower_end, upper_end):
    middle = 0.5 * (upper_end + lower_end)
    radius = 0.5 * (upper_end - lower_end)
    return [
        1.0 / (middle + radius * math.cos(math.pi * (2 * index_k + 1) / (2 * degree)))
        for index_k in range(degree)
    ]


FINE = cheb_weights(2, 0.3, 2.0)
COARSE = cheb_weights(4, 0.1, 2.0)


def loop(count, body):
    def step(index, carry):
        body(index)
        return carry

    lax.fori_loop(0, count, step, 0, unroll=min(count, UNROLL))


def lanes(rows, width):
    return lax.broadcasted_iota(jnp.int32, (rows, width), 1)


def sublanes(rows, width):
    return lax.broadcasted_iota(jnp.int32, (rows, width), 0)


def lane_sum(value, step):
    width = value.shape[1]
    first = (lanes(*value.shape) // step) % 2 == 0
    return value + jnp.where(first, pltpu.roll(value, width - step, 1), pltpu.roll(value, step, 1))


def across(value, step):
    rows, width = value.shape
    return (
        pltpu.roll(value, 1, 0)
        + pltpu.roll(value, rows - 1, 0)
        + pltpu.roll(value, step, 1)
        + pltpu.roll(value, width - step, 1)
    )


def row_pairs(buffer, value):
    rows, width = value.shape
    parts = []
    for half in range(width // COLS):
        buffer[half, 0:rows, :] = value[:, half * COLS : (half + 1) * COLS]
        parts.append(
            buffer[half, pl.ds(0, rows // 2, stride=2), :] + buffer[half, pl.ds(1, rows // 2, stride=2), :]
        )
    return parts[0] if len(parts) == 1 else jnp.concatenate(parts, axis=1)


def row_repeat(buffer, value):
    rows, width = value.shape
    parts = []
    for half in range(width // COLS):
        part = value[:, half * COLS : (half + 1) * COLS]
        buffer[half, pl.ds(0, rows, stride=2), :] = part
        buffer[half, pl.ds(1, rows, stride=2), :] = part
        parts.append(buffer[half, 0 : 2 * rows, :])
    return parts[0] if len(parts) == 1 else jnp.concatenate(parts, axis=1)


def column_pairs(value):
    row = lax.broadcasted_iota(jnp.int32, (WIDE, COLS), 0)
    column = lax.broadcasted_iota(jnp.int32, (WIDE, COLS), 1)
    matrix = jnp.where(row // 2 == column, 1.0, 0.0)
    return jnp.dot(value, matrix, precision=lax.Precision.HIGHEST, preferred_element_type=F32)


def column_repeat(value):
    row = lax.broadcasted_iota(jnp.int32, (COLS, WIDE), 0)
    column = lax.broadcasted_iota(jnp.int32, (COLS, WIDE), 1)
    matrix = jnp.where(column // 2 == row, 1.0, 0.0)
    return jnp.dot(value, matrix, precision=lax.Precision.HIGHEST, preferred_element_type=F32)


def half_rows(first, second, lower):
    row = sublanes(*first.shape)
    low = jnp.where(row < 4, first, pltpu.roll(second, 4, 0))
    high = jnp.where(row < 4, pltpu.roll(first, 4, 0), second)
    return jnp.where(lower, low, high)


def pick(table_row, index):
    rows, width = index.shape
    table = jnp.broadcast_to(table_row, (rows, COLS))
    parts = [
        jnp.take_along_axis(table, index[:, start : start + COLS], axis=1)
        for start in range(0, width, COLS)
    ]
    return parts[0] if len(parts) == 1 else jnp.concatenate(parts, axis=1)


def pack_halves(first, second):
    left = lanes(*first.shape) < HALF
    low = jnp.where(left, first, pltpu.roll(second, HALF, 1))
    high = jnp.where(left, pltpu.roll(first, HALF, 1), second)
    return low, high


def unpack_halves(from_right, from_left):
    left = lanes(*from_right.shape) < HALF
    first = jnp.where(left, from_right, pltpu.roll(from_left, HALF, 1))
    second = jnp.where(left, pltpu.roll(from_right, HALF, 1), from_left)
    return first, second


SPAN = 51
QUINTS = 6


def pack_quint(a, b, c, d, e):
    lane = lanes(*a.shape)
    lows = [
        jnp.where(lane < SPAN, x, jnp.where(lane < 2 * SPAN, pltpu.roll(y, SPAN, 1), pltpu.roll(e, shift, 1)))
        for x, y, shift in ((a, b, 102), (c, d, 76))
    ]
    highs = [
        jnp.where(
            lane >= COLS - SPAN,
            x,
            jnp.where(lane >= COLS - 2 * SPAN, pltpu.roll(y, COLS - SPAN, 1), pltpu.roll(e, COLS - shift, 1)),
        )
        for x, y, shift in ((a, b, 102), (c, d, 76))
    ]
    return lows, highs


def unpack_quint(from_right, from_left):
    lane = lanes(*from_right[0].shape)
    left = lane < HALF
    fields = []
    for right, other in zip(from_right, from_left):
        fields.append(jnp.where(left, right, other))
        fields.append(jnp.where(left, pltpu.roll(right, COLS - SPAN, 1), pltpu.roll(other, SPAN, 1)))
    parts = [
        jnp.where(left, pltpu.roll(right, COLS - shift, 1), pltpu.roll(other, shift, 1))
        for right, other, shift in zip(from_right, from_left, (102, 76))
    ]
    outer = (lane < COLS - 102) | (lane >= 102)
    fields.append(jnp.where(outer, parts[0], parts[1]))
    return fields


def pack_sea(fields):
    rows, width = fields[0].shape
    even_lane = lanes(rows, width) % 2 == 0
    even_row = sublanes(rows, width) % 2 == 0
    pairs = [
        jnp.where(even_lane, fields[i], pltpu.roll(fields[i + 1], 1, 1)) for i in (0, 2)
    ]
    return jnp.where(even_row, pairs[0], pltpu.roll(pairs[1], 1, 0))


def unpack_sea(packed):
    rows, width = packed.shape
    spot = (lanes(rows, width) % 2 == 0) & (sublanes(rows, width) % 2 == 0)
    fields = []
    for pair in (packed, pltpu.roll(packed, rows - 1, 0)):
        for field in (pair, pltpu.roll(pair, width - 1, 1)):
            fields.append(jnp.where(spot, field, 1.0))
    return fields


def fill_message(message, rhs, classes, sea, start, edge):
    def fields(z):
        for i in range(2):
            message[2 * z + i] = rhs(z, i)[pl.ds(start, 8), :]
        message[32 + z] = classes.at[z][pl.ds(start, 8), :]
        message.at[52 + z // 8][pl.ds(z % 8, 1), :] = classes.at[z][pl.ds(edge, 1), :]
        message.at[54 + z // 8][pl.ds(z % 8, 1), :] = sea.at[z][pl.ds(edge, 1), :]

    loop(NZ, fields)

    def quads(j):
        message[48 + j] = pack_sea([sea[4 * j + i, pl.ds(start, 8), :] for i in range(4)])

    loop(4, quads)


MSG_Y = 23
CORNER = 25
MSG_X = 56
R_TILES = 16
M_TILES = 24


def start_kernel(place, fields, to_left, to_right, message):
    core = place[0]
    classes, sea = fields.at[2], fields.at[3]

    def convert(pair):
        to_left[13 + pair], to_right[13 + pair] = pack_halves(classes[2 * pair], classes[2 * pair + 1])

    loop(8, convert)
    for j in range(2):
        quads = [pack_sea([sea[8 * j + 4 * q + i] for i in range(4)]) for q in range(2)]
        to_left[21 + j], to_right[21 + j] = pack_halves(quads[0], quads[1])

    def quint(k):
        group = [fields[(5 * k + t) // NZ, (5 * k + t) % NZ] for t in range(5)]
        lows, highs = pack_quint(*group)
        for t in range(2):
            to_left[2 * k + t] = lows[t]
            to_right[2 * k + t] = highs[t]

    loop(QUINTS, quint)
    to_left[12], to_right[12] = pack_halves(fields[1, 14], fields[1, 15])
    start = pl.multiple_of(8 * core, 8)
    fill_message(message, lambda z, i: fields.at[i, z], classes, sea, start, 8 - core)


def corner_kernel(message, after, to_left, to_right):
    def quint(k):
        lows, highs = pack_quint(*(message[5 * k + t] for t in range(5)))
        for t in range(2):
            to_left[2 * k + t] = lows[t]
            to_right[2 * k + t] = highs[t]

    loop(QUINTS, quint)

    def pair(p):
        to_left[12 + p], to_right[12 + p] = pack_halves(message[30 + 2 * p], message[31 + 2 * p])

    loop(CORNER - 12, pair)


def widen_kernel(message, corner_left, corner_right, wide):
    def quint(k):
        halos = unpack_quint(
            [corner_right[2 * k + t] for t in range(2)], [corner_left[2 * k + t] for t in range(2)]
        )
        for t, halo in enumerate(halos):
            wide[5 * k + t] = jnp.concatenate([message[5 * k + t], halo], axis=1)

    loop(QUINTS, quint)

    def pair(p):
        for i, halo in enumerate(unpack_halves(corner_right[12 + p], corner_left[12 + p])):
            wide[30 + 2 * p + i] = jnp.concatenate([message[30 + 2 * p + i], halo], axis=1)

    loop(CORNER - 12, pair)


def rows_kernel(place, fields, from_left, from_right, r_out, c_out, s_out, message):
    core = place[0]
    gy = place[2]
    left = lanes(ROWS, COLS) < HALF
    inside = jnp.where(
        left,
        jnp.where(gy < place[4] - 1, 1.0, 0.0),
        jnp.where(gy > 0, 1.0, 0.0),
    )

    def rhs_step(k):
        halos = unpack_quint(
            [from_right[2 * k + t] for t in range(2)], [from_left[2 * k + t] for t in range(2)]
        )
        for t, halo in enumerate(halos):
            i, z = (5 * k + t) // NZ, (5 * k + t) % NZ
            r_out[z, i] = jnp.concatenate([fields[i, z], halo], axis=1)

    loop(QUINTS, rhs_step)
    for t, halo in enumerate(unpack_halves(from_right[12], from_left[12])):
        r_out[14 + t, 1] = jnp.concatenate([fields[1, 14 + t], halo], axis=1)

    def class_step(pair):
        for i, halo in enumerate(unpack_halves(from_right[13 + pair], from_left[13 + pair])):
            c_out[2 * pair + i] = jnp.concatenate([fields[2, 2 * pair + i], halo], axis=1)

    loop(8, class_step)
    for j in range(2):
        quads = unpack_halves(from_right[21 + j], from_left[21 + j])
        for q in range(2):
            for i, field in enumerate(unpack_sea(quads[q])):
                z = 8 * j + 4 * q + i
                s_out[z] = jnp.concatenate([fields[3, z], field * inside], axis=1)
    start = pl.multiple_of(8 * (1 - core), 8)
    fill_message(message, lambda z, i: r_out.at[z, i], c_out, s_out, start, 7 + core)


def material_kernel(c_in, s_in, table, g_out, h_out, k_out, coarse, sums, buffer):
    def fields(z):
        index = c_in[z].astype(jnp.int32)
        sea = s_in[z]
        g = pick(table[0:1], index) * sea
        h = pick(table[1:2], index) * sea
        k = pick(table[2:3], index) * sea + (1.0 - sea)
        g_out[z] = g
        h_out[z] = h
        k_out[z] = k
        return 0.125 * g * g, 0.125 * h * h, k

    def step(pair):
        first = fields(2 * pair)
        second = fields(2 * pair + 1)
        for i in range(3):
            sums[8 * i + pair] = row_pairs(buffer.at[i], first[i] + second[i])

    loop(8, step)
    coarse[...] = column_pairs(sums[...].reshape(M_TILES * 8, WIDE)).reshape(M_TILES, 8, COLS)


class Level:
    def __init__(self, depth, step, g, h, inverse, diagonal=None):
        self.depth, self.step = depth, step
        self.g, self.h, self.inverse, self.diagonal = g, h, inverse, diagonal

    def couple(self, x, z, i):
        horizontal = self.g[z] * across(self.g[z] * x[z + 1, i], self.step)
        vertical = self.h[z + 1] * (self.h[z] * x[z, i] + self.h[z + 2] * x[z + 2, i])
        return horizontal + vertical

    def first(self, x, r, weight):
        def body(z):
            scaled = weight * self.inverse[z]
            for i in range(2):
                x[z + 1, i] = scaled * r[z, i]

        loop(self.depth, body)

    def update(self, new, x, r, weight):
        def body(z):
            scaled = weight * self.inverse[z]
            for i in range(2):
                new[z + 1, i] = (1.0 - weight) * x[z + 1, i] + scaled * (r[z, i] + self.couple(x, z, i))

        loop(self.depth, body)

    def defect(self, x, r, z, i):
        return r[z, i] - self.diagonal[z] * x[z + 1, i] + self.couple(x, z, i)

    def diagonal_of(self, k, z):
        horizontal = self.g[z] * across(self.g[z], self.step)
        vertical = self.h[z + 1] * (self.h[z] + self.h[z + 2])
        return k + horizontal + vertical


def clear_ends(*refs):
    for ref in refs:
        ref[0] = jnp.zeros(ref.shape[1:], ref.dtype)
        ref[ref.shape[0] - 1] = jnp.zeros(ref.shape[1:], ref.dtype)


def fine_restrict(level, x, r, sums, buffer, out):
    def body(pair):
        for i in range(2):
            total = level.defect(x, r, 2 * pair, i) + level.defect(x, r, 2 * pair + 1, i)
            sums[2 * pair + i] = row_pairs(buffer.at[i], total[8:24])

    loop(NZ // 2, body)
    out[...] = column_pairs(sums[...].reshape(R_TILES * 8, WIDE)).reshape(R_TILES, 8, COLS)


def down_kernel(
    place, r_own, g_own, h_own, k_own, from_x, wide, table,
    r, g, h, d, inverse, xp, r1, xa, ka, edges, sums, buffer,
):
    core = place[0]
    gx = place[1]
    gy = place[2]
    open_side = jnp.where((gx > 0) & (gx < place[3] - 1), 1.0, 0.0)
    lane = lanes(8, WIDE)
    ends = jnp.where(
        lane < COLS,
        1.0,
        jnp.where(lane < COLS + HALF, jnp.where(gy < place[4] - 1, 1.0, 0.0), jnp.where(gy > 0, 1.0, 0.0)),
    )
    clear_ends(h, xp, xa)

    def own(z):
        for i in range(2):
            r[z, i, 8:24, :] = r_own[z, i]
        g[z, 8:24, :] = g_own[z]
        h[z + 1, 8:24, :] = h_own[z]
        ka[z, 8:24, :] = k_own[z]

    loop(NZ, own)

    for message, start, scale, slot in ((from_x, 24 * (1 - core), 1.0, 1 - core), (wide, 24 * core, open_side, core)):
        start = pl.multiple_of(start, 8)
        valid = scale * ends

        def halo(j, message=message, start=start, valid=valid):
            for q, sea in enumerate(unpack_sea(message[48 + j])):
                z = 4 * j + q
                sea = sea * valid
                index = message[32 + z].astype(jnp.int32)
                g[z, pl.ds(start, 8), :] = pick(table[0:1], index) * sea
                h[z + 1, pl.ds(start, 8), :] = pick(table[1:2], index) * sea
                ka[z, pl.ds(start, 8), :] = pick(table[2:3], index) * sea + (1.0 - sea)
                for i in range(2):
                    r[z, i, pl.ds(start, 8), :] = message[2 * z + i]

        loop(4, halo)
        for j in range(2):
            index = message[52 + j].astype(jnp.int32)
            edges[slot, 8 * j : 8 * j + 8, :] = pick(table[0:1], index) * (message[54 + j] * valid)

    level = Level(NZ, 1, g, h, inverse, d)
    row = sublanes(EXT0, WIDE)

    def diagonals(z):
        here = g[z]
        below = jnp.where(row == 0, edges[0, pl.ds(z, 1), :], pltpu.roll(here, 1, 0))
        above = jnp.where(row == EXT0 - 1, edges[1, pl.ds(z, 1), :], pltpu.roll(here, EXT0 - 1, 0))
        beside = pltpu.roll(here, 1, 1) + pltpu.roll(here, WIDE - 1, 1)
        total = ka[z] + here * (below + above + beside) + h[z + 1] * (h[z] + h[z + 2])
        d[z] = total
        reciprocal = 1.0 / total
        inverse[z] = reciprocal
        for i in range(2):
            xa[z + 1, i] = (FINE[0] * reciprocal) * r[z, i]

    loop(NZ, diagonals)
    level.update(xp, xa, r, FINE[1])
    fine_restrict(level, xp, r, sums, buffer, r1)


def coarse_coefficients(place, pieces, g1, h1, d1, i1, g2, h2, i2, w1, k1, u1, k2, buffer):
    core = place[0]
    clear_ends(h1, h2)
    own, partner, odd, far = pieces
    low = jnp.where(place[1] >= 2, 1.0, 0.0)
    high = jnp.where(place[1] < place[3] - 2, 1.0, 0.0)
    near_side = jnp.where(core == 0, low, high)
    far_side = jnp.where(core == 0, high, low)
    scales = (1.0, 1.0, near_side, near_side, far_side)
    starts = (16, 24 - 16 * core, 8 + 16 * core, 32 * core, 32 - 32 * core)
    starts = [s if isinstance(s, int) else pl.multiple_of(s, 8) for s in starts]

    def assemble(z):
        for i, field in enumerate((w1, u1, k1)):
            j = 8 * i + z
            tiles = (own[j], partner[j], odd[j], odd[M_TILES + j], far[j])
            for start, tile, scale in zip(starts, tiles, scales):
                field[z, pl.ds(start, 8), :] = tile * scale if i < 2 else tile

    loop(8, assemble)

    def roots(z):
        g1[z] = 2.0 * jnp.sqrt(w1[z])
        h1[z + 1] = 2.0 * jnp.sqrt(u1[z])

    loop(8, roots)
    one = Level(8, 1, g1, h1, i1, d1)

    def diagonals(z):
        total = one.diagonal_of(k1[z], z)
        d1[z] = total
        i1[z] = 1.0 / total

    loop(8, diagonals)

    def coarser(z):
        sums = [
            lane_sum(row_pairs(buffer.at[i], field[2 * z] + field[2 * z + 1]), 1)
            for i, field in enumerate((w1, u1, k1))
        ]
        blank = jnp.zeros((4, COLS), F32)
        g2[z] = jnp.concatenate([2.0 * jnp.sqrt(0.125 * sums[0]), blank], axis=0)
        h2[z + 1] = jnp.concatenate([2.0 * jnp.sqrt(0.125 * sums[1]), blank], axis=0)
        k2[z] = jnp.concatenate([sums[2], blank + 1.0], axis=0)

    loop(4, coarser)
    two = Level(4, 2, g2, h2, i2)

    def diagonals_two(z):
        i2[z] = 1.0 / two.diagonal_of(k2[z], z)

    loop(4, diagonals_two)


def coarse_solve(core, one, two, pieces, far_tile, r1, xa1, xb1, r2, xa2, xb2, buffer):
    own, partner, odd, second = pieces
    clear_ends(xa1, xb1, xa2, xb2)
    starts = (16, 24 - 16 * core, 8 + 16 * core, 32 * core, 32 - 32 * core)
    starts = [s if isinstance(s, int) else pl.multiple_of(s, 8) for s in starts]

    def assemble(z):
        for i in range(2):
            j = 2 * z + i
            tiles = (own[j], partner[j], odd[j], far_tile(z, i), second[j])
            for start, tile in zip(starts, tiles):
                r1[z, i, pl.ds(start, 8), :] = tile

    loop(8, assemble)
    one.first(xa1, r1, FINE[0])
    one.update(xb1, xa1, r1, FINE[1])

    def restrict(z):
        for i in range(2):
            total = one.defect(xb1, r1, 2 * z, i) + one.defect(xb1, r1, 2 * z + 1, i)
            sums = lane_sum(row_pairs(buffer.at[i], total), 1)
            r2[z, i] = jnp.concatenate([sums, jnp.zeros((4, COLS), F32)], axis=0)

    loop(4, restrict)
    two.first(xa2, r2, COARSE[0])
    two.update(xb2, xa2, r2, COARSE[1])
    two.update(xa2, xb2, r2, COARSE[2])
    two.update(xb2, xa2, r2, COARSE[3])

    inner = [ref.at[:, :, 8:32, :] for ref in (xa1, xb1, r1)]
    inner_one = Level(8, 1, *(ref.at[:, 8:32, :] for ref in (one.g, one.h, one.inverse)))

    def prolong(z):
        for i in range(2):
            fine = row_repeat(buffer.at[i], xb2[z + 1, i, 4:16, :])
            for half in range(2):
                inner[0][2 * z + half + 1, i] = inner[1][2 * z + half + 1, i] + fine

    loop(4, prolong)
    inner_one.update(inner[1], inner[0], inner[2], FINE[0])
    inner_one.update(inner[0], inner[1], inner[2], FINE[1])


def fine_correct(level, out, xp, c1, wide, buffer):
    rows = c1[1:9, :, 12:28, :].reshape(R_TILES * 16, COLS)
    wide[...] = column_repeat(rows).reshape(R_TILES, 16, WIDE)

    def body(pair):
        for i in range(2):
            fine = row_repeat(buffer.at[i], wide[2 * pair + i])
            for half in range(2):
                out[2 * pair + half + 1, i] = xp[2 * pair + half + 1, i] + fine

    loop(NZ // 2, body)


def near_kernel(odd, near):
    near[...] = odd[0:R_TILES]


def far_half_kernel(place, own, partner, message):
    message[0:R_TILES] = own[...]

    def pair(p):
        message[R_TILES + p] = half_rows(partner[2 * p], partner[2 * p + 1], place[0] == 0)

    loop(R_TILES // 2, pair)


def after_kernel(odd, after, near):
    near[...] = odd[0:M_TILES]


def coarse_kernel(
    place, own, partner, odd, far, g1, h1, d1, i1, g2, h2, i2, w1, k1, u1, k2, buffer
):
    coarse_coefficients(
        place, (own, partner, odd, far), g1, h1, d1, i1, g2, h2, i2, w1, k1, u1, k2, buffer
    )


def middle_kernel(
    place, r, g, h, d, inverse, xp, own, partner, odd, far, g1, h1, d1, i1, g2, h2, i2,
    z_out, xp_out, r1_out,
    xa, xb, r1, xa1, xb1, r2, xa2, xb2, wide, sums, buffer,
):
    core = place[0]
    zero = Level(NZ, 1, g, h, inverse, d)
    one = Level(8, 1, g1, h1, i1, d1)
    two = Level(4, 2, g2, h2, i2)
    coarse_solve(core, one, two, (own, partner, odd, far), lambda z, i: odd[R_TILES + 2 * z + i], r1, xa1, xb1, r2, xa2, xb2, buffer)
    clear_ends(xa, xb, xp_out)
    fine_correct(zero, xa, xp, xa1, wide, buffer)
    zero.update(xb, xa, r, FINE[0])

    def last(z):
        scaled = FINE[1] * inverse[z]
        first = FINE[0] * inverse[z]
        for i in range(2):
            value = (1.0 - FINE[1]) * xb[z + 1, i] + scaled * (r[z, i] + zero.couple(xb, z, i))
            z_out[z, i] = value
            xa[z + 1, i] = first * value

    loop(NZ, last)
    zero.update(xp_out, xa, z_out, FINE[1])
    fine_restrict(zero, xp_out, z_out, sums, buffer, r1_out)


def last_kernel(
    place, rhs, r, g, h, d, inverse, xp, own, partner, odd, far, g1, h1, d1, i1, g2, h2, i2,
    direction, image, sums,
    xa, xb, r1, xa1, xb1, r2, xa2, xb2, wide, totals, buffer,
):
    core = place[0]
    zero = Level(NZ, 1, g, h, inverse, d)
    one = Level(8, 1, g1, h1, i1, d1)
    two = Level(4, 2, g2, h2, i2)

    def far_tile(z, i):
        tile = odd[R_TILES + z]
        return jnp.where((core == 0) == (i == 0), pltpu.roll(tile, 4, 0), tile)

    coarse_solve(core, one, two, (own, partner, odd, far), far_tile, r1, xa1, xb1, r2, xa2, xb2, buffer)
    clear_ends(xa, xb)
    fine_correct(zero, xa, xp, xa1, wide, buffer)
    zero.update(xb, xa, r, FINE[0])
    zero.update(xa, xb, r, FINE[1])

    def first_image(z):
        for i in range(2):
            xb[z + 1, i] = d[z] * xa[z + 1, i] - zero.couple(xa, z, i)

    loop(NZ, first_image)
    totals[...] = jnp.zeros(totals.shape, F32)

    def second_image(z):
        for i in range(2):
            field = xa[z + 1, i, 8:24, 0:COLS]
            value = (d[z] * xb[z + 1, i] - zero.couple(xb, z, i))[8:24, 0:COLS]
            direction[i, z] = field
            image[i, z] = value
            totals[i] += rhs[i, z] * field
            totals[2 + i] += field * value

    loop(NZ, second_image)
    row = sublanes(8, COLS)
    lane = lanes(8, COLS)
    line = jnp.zeros((8, COLS), F32)
    for i in range(4):
        line = jnp.where(lane == i, jnp.sum(totals[i]), line)

    def spread(j):
        sums[pl.ds(pl.multiple_of(8 * j, 8), 8), :] = line

    loop(sums.shape[0] // 8, spread)


def scale_kernel(rhs, direction, image, sums, solution_field, residual):
    total = jnp.sum(sums[...], axis=0, keepdims=True)
    lane = lanes(1, COLS)
    parts = [jnp.sum(jnp.where(lane == i, total, 0.0), axis=1, keepdims=True) for i in range(4)]
    for i in range(2):
        alpha = parts[i] / parts[2 + i]

        def body(z, i=i, alpha=alpha):
            solution_field[i, z] = alpha * direction[i, z]
            residual[i, z] = rhs[i, z] - alpha * image[i, z]

        loop(NZ, body)


COSTS = {
    "start_kernel": 1,
    "corner_kernel": 1,
    "widen_kernel": 30,
    "rows_kernel": 1,
    "material_kernel": 1,
    "down_kernel": 4,
    "near_kernel": 30,
    "far_half_kernel": 1,
    "after_kernel": 30,
    "coarse_kernel": 1,
    "middle_kernel": 6,
    "last_kernel": 6,
    "scale_kernel": 1,
}


def call(kernel, operands, outs, scratch=(), place=True, far=None):
    far = far or {}
    vmem = pl.BlockSpec(memory_space=pltpu.VMEM)
    specs = [pl.BlockSpec(memory_space=far[i]) if i in far else vmem for i in range(len(operands))]
    if place:
        specs[0] = pl.BlockSpec(memory_space=pltpu.SMEM)
    return pl.pallas_call(
        kernel,
        out_shape=[jax.ShapeDtypeStruct(shape, F32) for shape in outs],
        in_specs=specs,
        out_specs=[vmem] * len(outs),
        scratch_shapes=[pltpu.VMEM(shape, F32) if isinstance(shape, tuple) else shape for shape in scratch],
        cost_estimate=pl.CostEstimate(
            flops=COSTS[kernel.__name__] * 1_000_000_000, bytes_accessed=COSTS[kernel.__name__] * 3_000_000, transcendentals=0
        ),
        compiler_params=pltpu.CompilerParams(vmem_limit_bytes=16 * 1024 * 1024),
    )(*operands)


FIELD0 = (NZ, 2, EXT0, WIDE)
PADDED0 = (NZ + 2, 2, EXT0, WIDE)
PADDED1 = (10, 2, EXT1, COLS)
PADDED2 = (6, 2, EXT2, COLS)
BUFFER = (3, 2, EXT1, COLS)
SUMS = (R_TILES, 8, WIDE)
SPREAD = (R_TILES, 16, WIDE)
COARSE_SCRATCH = [(8, 2, EXT1, COLS), PADDED1, PADDED1, (4, 2, EXT2, COLS), PADDED2, PADDED2, SPREAD]


def shards(count_x, count_y, right_side, classes, sea_mask, kappa_table, cross_table, vertical_table):
    gx = lax.axis_index("gx")
    gy = lax.axis_index("gy")
    place = jnp.stack([gx % 2, gx, gy, jnp.int32(count_x), jnp.int32(count_y)]).astype(jnp.int32)
    table = jnp.stack([jnp.sqrt(cross_table), jnp.sqrt(vertical_table), kappa_table])
    table = jnp.pad(table, ((0, 5), (0, COLS - table.shape[1])))

    pairs_on_chip = [(i, i ^ 1) for i in range(count_x)]
    pairs_across = [(i, (i + 1 if i % 2 else i - 1) % count_x) for i in range(count_x)]

    def on_chip(value):
        return lax.ppermute(value, "gx", pairs_on_chip)

    def across_chips(value):
        return lax.ppermute(value, "gx", pairs_across)

    def rows_of(own, partner, message):
        odd = across_chips(message)
        near = call(near_kernel, (odd,), [own.shape], place=False)[0]
        return own, partner, odd, on_chip(near)

    forward = [(i, (i + 1) % count_y) for i in range(count_y)]
    backward = [(target, source) for source, target in forward]

    def both_sides(to_left, to_right):
        return lax.ppermute(to_right, "gy", forward), lax.ppermute(to_left, "gy", backward)

    part = lax.broadcasted_iota(jnp.int32, (4, *classes.shape), 0)
    materials = jnp.where(part == 2, classes[None], sea_mask[None]).astype(F32)
    twice = jnp.broadcast_to(right_side[None], (2, *right_side.shape)).reshape(part.shape)
    fields = jnp.where(part < 2, twice, materials)
    to_left, to_right, msg_o = call(
        start_kernel, (place, fields), [(MSG_Y, ROWS, COLS), (MSG_Y, ROWS, COLS), (MSG_X, 8, COLS)]
    )
    from_o = across_chips(msg_o)
    from_left, from_right = both_sides(to_left, to_right)
    r_own, c_own, s_own, msg_x = call(
        rows_kernel,
        (place, fields, from_left, from_right),
        [(NZ, 2, ROWS, WIDE), (NZ, ROWS, WIDE), (NZ, ROWS, WIDE), (MSG_X, 8, WIDE)],
    )
    from_x = on_chip(msg_x)
    g_own, h_own, k_own, packed = call(
        material_kernel,
        (c_own, s_own, table),
        [(NZ, ROWS, WIDE)] * 3 + [(M_TILES, 8, COLS)],
        [(M_TILES, 8, WIDE), BUFFER],
        place=False,
    )
    corner_tiles = call(corner_kernel, (from_o, packed), [(CORNER, 8, COLS)] * 2, place=False, far={1: pl.ANY})
    wide = call(widen_kernel, (from_o, *both_sides(*corner_tiles)), [(MSG_X, 8, WIDE)], place=False)[0]
    packed_partner = on_chip(packed)
    packed_odd = across_chips(jnp.concatenate([packed, packed_partner], axis=0))
    r, g, h, d, inverse, xp, r1 = call(
        down_kernel,
        (place, r_own, g_own, h_own, k_own, from_x, wide, table),
        [FIELD0, (NZ, EXT0, WIDE), (NZ + 2, EXT0, WIDE), (NZ, EXT0, WIDE), (NZ, EXT0, WIDE), PADDED0, (R_TILES, 8, COLS)],
        [PADDED0, (NZ, EXT0, WIDE), (2, NZ, WIDE), SUMS, BUFFER],
    )
    partner = on_chip(r1)
    rows = rows_of(r1, partner, jnp.concatenate([r1, partner], axis=0))
    packed_near = call(
        after_kernel, (packed_odd, rows[1]), [packed.shape], place=False, far={1: pl.ANY}
    )[0]
    material = (packed, packed_partner, packed_odd, on_chip(packed_near))
    one = [(8, EXT1, COLS), (10, EXT1, COLS), (8, EXT1, COLS), (8, EXT1, COLS)]
    two = [(4, EXT2, COLS), (6, EXT2, COLS), (4, EXT2, COLS)]
    coarse = call(
        coarse_kernel, (place, *material), [*one, *two], [one[0], one[0], one[0], two[0], BUFFER]
    )
    r, xp, r1 = call(
        middle_kernel,
        (place, r, g, h, d, inverse, xp, *rows, *coarse),
        [FIELD0, PADDED0, (R_TILES, 8, COLS)],
        [PADDED0, PADDED0, *COARSE_SCRATCH, SUMS, BUFFER],
    )
    partner = on_chip(r1)
    message = call(far_half_kernel, (place, r1, partner), [(R_TILES * 3 // 2, 8, COLS)])[0]
    count = count_x * count_y
    direction, image, sums = call(
        last_kernel,
        (place, fields, r, g, h, d, inverse, xp, *rows_of(r1, partner, message), *coarse),
        [(2, NZ, ROWS, COLS)] * 2 + [(count, COLS)],
        [PADDED0, PADDED0, *COARSE_SCRATCH, (4, ROWS, COLS), BUFFER],
    )
    sums = lax.all_to_all(sums.reshape(count, 1, COLS), ("gx", "gy"), 0, 0).reshape(count, COLS)
    return tuple(
        call(
            scale_kernel,
            (fields, direction, image, sums),
            [(2, NZ, ROWS, COLS)] * 2,
            place=False,
        )
    )


def solution(mesh):
    return jax.shard_map(
        functools.partial(shards, mesh.shape["gx"], mesh.shape["gy"]),
        mesh=mesh,
        in_specs=(
            P(None, None, "gx", "gy"),
            P(None, "gx", "gy"),
            P(None, "gx", "gy"),
            P(),
            P(),
            P(),
        ),
        out_specs=(P(None, None, "gx", "gy"), P(None, None, "gx", "gy")),
        check_vma=False,
    )
```

```python
import functools
import math

import jax
import jax.numpy as jnp
from jax import lax
from jax.experimental import pallas as pl
from jax.experimental.pallas import tpu as pltpu
from jax.sharding import PartitionSpec as P

F32 = jnp.float32
NZ = 16
ROWS = 16
COLS = 128
WIDE = 256
HALF = 64
UNROLL = 8
EXT0 = 32
EXT1 = 40
EXT2 = 24


def cheb_weights(degree, lower_end, upper_end):
    middle = 0.5 * (upper_end + lower_end)
    radius = 0.5 * (upper_end - lower_end)
    return [
        1.0 / (middle + radius * math.cos(math.pi * (2 * index_k + 1) / (2 * degree)))
        for index_k in range(degree)
    ]


FINE = cheb_weights(2, 0.3, 2.0)
COARSE = cheb_weights(4, 0.1, 2.0)


def loop(count, body):
    def step(index, carry):
        body(index)
        return carry

    lax.fori_loop(0, count, step, 0, unroll=min(count, UNROLL))


def lanes(rows, width):
    return lax.broadcasted_iota(jnp.int32, (rows, width), 1)


def sublanes(rows, width):
    return lax.broadcasted_iota(jnp.int32, (rows, width), 0)


def lane_sum(value, step):
    width = value.shape[1]
    first = (lanes(*value.shape) // step) % 2 == 0
    return value + jnp.where(first, pltpu.roll(value, width - step, 1), pltpu.roll(value, step, 1))


def across(value, step):
    rows, width = value.shape
    return (
        pltpu.roll(value, 1, 0)
        + pltpu.roll(value, rows - 1, 0)
        + pltpu.roll(value, step, 1)
        + pltpu.roll(value, width - step, 1)
    )


def row_pairs(buffer, value):
    rows, width = value.shape
    parts = []
    for half in range(width // COLS):
        buffer[half, 0:rows, :] = value[:, half * COLS : (half + 1) * COLS]
        parts.append(
            buffer[half, pl.ds(0, rows // 2, stride=2), :] + buffer[half, pl.ds(1, rows // 2, stride=2), :]
        )
    return parts[0] if len(parts) == 1 else jnp.concatenate(parts, axis=1)


def row_repeat(buffer, value):
    rows, width = value.shape
    parts = []
    for half in range(width // COLS):
        part = value[:, half * COLS : (half + 1) * COLS]
        buffer[half, pl.ds(0, rows, stride=2), :] = part
        buffer[half, pl.ds(1, rows, stride=2), :] = part
        parts.append(buffer[half, 0 : 2 * rows, :])
    return parts[0] if len(parts) == 1 else jnp.concatenate(parts, axis=1)


def column_pairs(value):
    row = lax.broadcasted_iota(jnp.int32, (WIDE, COLS), 0)
    column = lax.broadcasted_iota(jnp.int32, (WIDE, COLS), 1)
    matrix = jnp.where(row // 2 == column, 1.0, 0.0)
    return jnp.dot(value, matrix, precision=lax.Precision.HIGHEST, preferred_element_type=F32)


def column_repeat(value):
    row = lax.broadcasted_iota(jnp.int32, (COLS, WIDE), 0)
    column = lax.broadcasted_iota(jnp.int32, (COLS, WIDE), 1)
    matrix = jnp.where(column // 2 == row, 1.0, 0.0)
    return jnp.dot(value, matrix, precision=lax.Precision.HIGHEST, preferred_element_type=F32)


def half_rows(first, second, lower):
    row = sublanes(*first.shape)
    low = jnp.where(row < 4, first, pltpu.roll(second, 4, 0))
    high = jnp.where(row < 4, pltpu.roll(first, 4, 0), second)
    return jnp.where(lower, low, high)


def pick(table_row, index):
    rows, width = index.shape
    table = jnp.broadcast_to(table_row, (rows, COLS))
    parts = [
        jnp.take_along_axis(table, index[:, start : start + COLS], axis=1)
        for start in range(0, width, COLS)
    ]
    return parts[0] if len(parts) == 1 else jnp.concatenate(parts, axis=1)


def pack_halves(first, second):
    left = lanes(*first.shape) < HALF
    low = jnp.where(left, first, pltpu.roll(second, HALF, 1))
    high = jnp.where(left, pltpu.roll(first, HALF, 1), second)
    return low, high


def unpack_halves(from_right, from_left):
    left = lanes(*from_right.shape) < HALF
    first = jnp.where(left, from_right, pltpu.roll(from_left, HALF, 1))
    second = jnp.where(left, pltpu.roll(from_right, HALF, 1), from_left)
    return first, second


SPAN = 51
QUINTS = 9


def pack_quint(a, b, c, d, e):
    lane = lanes(*a.shape)
    lows = [
        jnp.where(lane < SPAN, x, jnp.where(lane < 2 * SPAN, pltpu.roll(y, SPAN, 1), pltpu.roll(e, shift, 1)))
        for x, y, shift in ((a, b, 102), (c, d, 76))
    ]
    highs = [
        jnp.where(
            lane >= COLS - SPAN,
            x,
            jnp.where(lane >= COLS - 2 * SPAN, pltpu.roll(y, COLS - SPAN, 1), pltpu.roll(e, COLS - shift, 1)),
        )
        for x, y, shift in ((a, b, 102), (c, d, 76))
    ]
    return lows, highs


def unpack_quint(from_right, from_left):
    lane = lanes(*from_right[0].shape)
    left = lane < HALF
    fields = []
    for right, other in zip(from_right, from_left):
        fields.append(jnp.where(left, right, other))
        fields.append(jnp.where(left, pltpu.roll(right, COLS - SPAN, 1), pltpu.roll(other, SPAN, 1)))
    parts = [
        jnp.where(left, pltpu.roll(right, COLS - shift, 1), pltpu.roll(other, shift, 1))
        for right, other, shift in zip(from_right, from_left, (102, 76))
    ]
    outer = (lane < COLS - 102) | (lane >= 102)
    fields.append(jnp.where(outer, parts[0], parts[1]))
    return fields


def pack_sea(fields):
    rows, width = fields[0].shape
    even_lane = lanes(rows, width) % 2 == 0
    even_row = sublanes(rows, width) % 2 == 0
    pairs = [
        jnp.where(even_lane, fields[i], pltpu.roll(fields[i + 1], 1, 1)) for i in (0, 2)
    ]
    return jnp.where(even_row, pairs[0], pltpu.roll(pairs[1], 1, 0))


def unpack_sea(packed):
    rows, width = packed.shape
    spot = (lanes(rows, width) % 2 == 0) & (sublanes(rows, width) % 2 == 0)
    fields = []
    for pair in (packed, pltpu.roll(packed, rows - 1, 0)):
        for field in (pair, pltpu.roll(pair, width - 1, 1)):
            fields.append(jnp.where(spot, field, 1.0))
    return fields


def fill_message(message, rhs, classes, sea, start, edge):
    def fields(z):
        for i in range(2):
            message[2 * z + i] = rhs(z, i)[pl.ds(start, 8), :]
        message[32 + z] = classes.at[z][pl.ds(start, 8), :]
        message.at[52 + z // 8][pl.ds(z % 8, 1), :] = classes.at[z][pl.ds(edge, 1), :]
        message.at[54 + z // 8][pl.ds(z % 8, 1), :] = sea.at[z][pl.ds(edge, 1), :]

    loop(NZ, fields)

    def quads(j):
        message[48 + j] = pack_sea([sea[4 * j + i, pl.ds(start, 8), :] for i in range(4)])

    loop(4, quads)


MSG_Y = 22
CORNER = 24
MSG_X = 56
R_TILES = 16
M_TILES = 24


def start_kernel(place, fields, to_left, to_right, message):
    core = place[0]
    classes, sea = fields.at[2], fields.at[3]

    def quint(k):
        lows, highs = pack_quint(*(fields[(5 * k + t) // NZ, (5 * k + t) % NZ] for t in range(5)))
        for t in range(2):
            to_left[2 * k + t] = lows[t]
            to_right[2 * k + t] = highs[t]

    loop(QUINTS, quint)
    rest = [classes[13], classes[14], classes[15]]
    rest += [pack_sea([sea[4 * q + i] for i in range(4)]) for q in range(4)]
    rest.append(rest[-1])
    for j in range(4):
        to_left[18 + j], to_right[18 + j] = pack_halves(rest[2 * j], rest[2 * j + 1])
    start = pl.multiple_of(8 * core, 8)
    fill_message(message, lambda z, i: fields.at[i, z], classes, sea, start, 8 - core)


def corner_kernel(message, after, to_left, to_right):
    def quint(k):
        lows, highs = pack_quint(*(message[5 * k + t] for t in range(5)))
        for t in range(2):
            to_left[2 * k + t] = lows[t]
            to_right[2 * k + t] = highs[t]

    loop(QUINTS, quint)
    for p in range(6):
        first = 45 + 2 * p
        to_left[18 + p], to_right[18 + p] = pack_halves(message[first], message[min(first + 1, MSG_X - 1)])


def valid_class(halo):
    return jnp.clip(halo, 0.0, 15.0)


def widen_kernel(message, corner_left, corner_right, wide):
    def quint(k):
        halos = unpack_quint(
            [corner_right[2 * k + t] for t in range(2)], [corner_left[2 * k + t] for t in range(2)]
        )
        for t, halo in enumerate(halos):
            wide[5 * k + t] = jnp.concatenate([message[5 * k + t], halo], axis=1)

    loop(QUINTS, quint)
    for j in range(32, 35):
        wide[j, :, COLS:] = valid_class(wide[j, :, COLS:])
    for p in range(6):
        first = 45 + 2 * p
        for i, halo in enumerate(unpack_halves(corner_right[18 + p], corner_left[18 + p])):
            if first + i < MSG_X:
                wide[first + i] = jnp.concatenate([message[first + i], halo], axis=1)


def rows_kernel(place, fields, from_left, from_right, r_out, c_out, s_out, message):
    core = place[0]
    gy = place[2]
    left = lanes(ROWS, COLS) < HALF
    inside = jnp.where(
        left,
        jnp.where(gy < place[4] - 1, 1.0, 0.0),
        jnp.where(gy > 0, 1.0, 0.0),
    )

    def group(k):
        return unpack_quint(
            [from_right[2 * k + t] for t in range(2)], [from_left[2 * k + t] for t in range(2)]
        )

    def put_rhs(f, halo):
        r_out[f % NZ, f // NZ] = jnp.concatenate([fields[f // NZ, f % NZ], halo], axis=1)

    def put_class(z, halo):
        c_out[z] = jnp.concatenate([fields[2, z], halo], axis=1)

    def rhs_step(k):
        for t, halo in enumerate(group(k)):
            put_rhs(5 * k + t, halo)

    loop(6, rhs_step)
    mixed = group(6)
    for t in range(2):
        put_rhs(30 + t, mixed[t])
    for t in range(3):
        put_class(t, valid_class(mixed[2 + t]))
    for k in (7, 8):
        for t, halo in enumerate(group(k)):
            put_class(5 * k + t - 32, halo)
    rest = []
    for j in range(4):
        rest += unpack_halves(from_right[18 + j], from_left[18 + j])
    for t in range(3):
        put_class(13 + t, rest[t])
    for q in range(4):
        for i, field in enumerate(unpack_sea(rest[3 + q])):
            s_out[4 * q + i] = jnp.concatenate([fields[3, 4 * q + i], field * inside], axis=1)
    start = pl.multiple_of(8 * (1 - core), 8)
    fill_message(message, lambda z, i: r_out.at[z, i], c_out, s_out, start, 7 + core)


def material_kernel(c_in, s_in, table, g_out, h_out, k_out, coarse, sums, buffer):
    def fields(z):
        index = c_in[z].astype(jnp.int32)
        sea = s_in[z]
        g = pick(table[0:1], index) * sea
        h = pick(table[1:2], index) * sea
        k = pick(table[2:3], index) * sea + (1.0 - sea)
        g_out[z] = g
        h_out[z] = h
        k_out[z] = k
        return 0.125 * g * g, 0.125 * h * h, k

    def step(pair):
        first = fields(2 * pair)
        second = fields(2 * pair + 1)
        for i in range(3):
            sums[8 * i + pair] = row_pairs(buffer.at[i], first[i] + second[i])

    loop(8, step)
    coarse[...] = column_pairs(sums[...].reshape(M_TILES * 8, WIDE)).reshape(M_TILES, 8, COLS)


class Level:
    def __init__(self, depth, step, g, h, inverse, diagonal=None):
        self.depth, self.step = depth, step
        self.g, self.h, self.inverse, self.diagonal = g, h, inverse, diagonal

    def couple(self, x, z, i):
        horizontal = self.g[z] * across(self.g[z] * x[z + 1, i], self.step)
        vertical = self.h[z + 1] * (self.h[z] * x[z, i] + self.h[z + 2] * x[z + 2, i])
        return horizontal + vertical

    def first(self, x, r, weight):
        def body(z):
            scaled = weight * self.inverse[z]
            for i in range(2):
                x[z + 1, i] = scaled * r[z, i]

        loop(self.depth, body)

    def update(self, new, x, r, weight):
        def body(z):
            scaled = weight * self.inverse[z]
            for i in range(2):
                new[z + 1, i] = (1.0 - weight) * x[z + 1, i] + scaled * (r[z, i] + self.couple(x, z, i))

        loop(self.depth, body)

    def defect(self, x, r, z, i):
        return r[z, i] - self.diagonal[z] * x[z + 1, i] + self.couple(x, z, i)

    def diagonal_of(self, k, z):
        horizontal = self.g[z] * across(self.g[z], self.step)
        vertical = self.h[z + 1] * (self.h[z] + self.h[z + 2])
        return k + horizontal + vertical


def clear_ends(*refs):
    for ref in refs:
        ref[0] = jnp.zeros(ref.shape[1:], ref.dtype)
        ref[ref.shape[0] - 1] = jnp.zeros(ref.shape[1:], ref.dtype)


def fine_restrict(level, x, r, sums, buffer, out):
    def body(pair):
        for i in range(2):
            total = level.defect(x, r, 2 * pair, i) + level.defect(x, r, 2 * pair + 1, i)
            sums[2 * pair + i] = row_pairs(buffer.at[i], total[8:24])

    loop(NZ // 2, body)
    out[...] = column_pairs(sums[...].reshape(R_TILES * 8, WIDE)).reshape(R_TILES, 8, COLS)


def down_kernel(
    place, r_own, g_own, h_own, k_own, from_x, wide, table,
    r, g, h, d, inverse, xp, r1, xa, ka, edges, sums, buffer,
):
    core = place[0]
    gx = place[1]
    gy = place[2]
    open_side = jnp.where((gx > 0) & (gx < place[3] - 1), 1.0, 0.0)
    lane = lanes(8, WIDE)
    ends = jnp.where(
        lane < COLS,
        1.0,
        jnp.where(lane < COLS + HALF, jnp.where(gy < place[4] - 1, 1.0, 0.0), jnp.where(gy > 0, 1.0, 0.0)),
    )
    clear_ends(h, xp, xa)

    def own(z):
        for i in range(2):
            r[z, i, 8:24, :] = r_own[z, i]
        g[z, 8:24, :] = g_own[z]
        h[z + 1, 8:24, :] = h_own[z]
        ka[z, 8:24, :] = k_own[z]

    loop(NZ, own)

    for message, start, scale, slot in ((from_x, 24 * (1 - core), 1.0, 1 - core), (wide, 24 * core, open_side, core)):
        start = pl.multiple_of(start, 8)
        valid = scale * ends

        def halo(j, message=message, start=start, valid=valid):
            for q, sea in enumerate(unpack_sea(message[48 + j])):
                z = 4 * j + q
                sea = sea * valid
                index = message[32 + z].astype(jnp.int32)
                g[z, pl.ds(start, 8), :] = pick(table[0:1], index) * sea
                h[z + 1, pl.ds(start, 8), :] = pick(table[1:2], index) * sea
                ka[z, pl.ds(start, 8), :] = pick(table[2:3], index) * sea + (1.0 - sea)
                for i in range(2):
                    r[z, i, pl.ds(start, 8), :] = message[2 * z + i]

        loop(4, halo)
        for j in range(2):
            index = message[52 + j].astype(jnp.int32)
            edges[slot, 8 * j : 8 * j + 8, :] = pick(table[0:1], index) * (message[54 + j] * valid)

    level = Level(NZ, 1, g, h, inverse, d)
    row = sublanes(EXT0, WIDE)

    def diagonals(z):
        here = g[z]
        below = jnp.where(row == 0, edges[0, pl.ds(z, 1), :], pltpu.roll(here, 1, 0))
        above = jnp.where(row == EXT0 - 1, edges[1, pl.ds(z, 1), :], pltpu.roll(here, EXT0 - 1, 0))
        beside = pltpu.roll(here, 1, 1) + pltpu.roll(here, WIDE - 1, 1)
        total = ka[z] + here * (below + above + beside) + h[z + 1] * (h[z] + h[z + 2])
        d[z] = total
        reciprocal = 1.0 / total
        inverse[z] = reciprocal
        for i in range(2):
            xa[z + 1, i] = (FINE[0] * reciprocal) * r[z, i]

    loop(NZ, diagonals)
    level.update(xp, xa, r, FINE[1])
    fine_restrict(level, xp, r, sums, buffer, r1)


def coarse_coefficients(place, pieces, g1, h1, d1, i1, g2, h2, i2, w1, k1, u1, k2, buffer):
    core = place[0]
    clear_ends(h1, h2)
    own, partner, odd, far = pieces
    low = jnp.where(place[1] >= 2, 1.0, 0.0)
    high = jnp.where(place[1] < place[3] - 2, 1.0, 0.0)
    near_side = jnp.where(core == 0, low, high)
    far_side = jnp.where(core == 0, high, low)
    scales = (1.0, 1.0, near_side, near_side, far_side)
    starts = (16, 24 - 16 * core, 8 + 16 * core, 32 * core, 32 - 32 * core)
    starts = [s if isinstance(s, int) else pl.multiple_of(s, 8) for s in starts]

    def assemble(z):
        for i, field in enumerate((w1, u1, k1)):
            j = 8 * i + z
            tiles = (own[j], partner[j], odd[j], odd[M_TILES + j], far[j])
            for start, tile, scale in zip(starts, tiles, scales):
                field[z, pl.ds(start, 8), :] = tile * scale if i < 2 else tile

    loop(8, assemble)

    def roots(z):
        g1[z] = 2.0 * jnp.sqrt(w1[z])
        h1[z + 1] = 2.0 * jnp.sqrt(u1[z])

    loop(8, roots)
    one = Level(8, 1, g1, h1, i1, d1)

    def diagonals(z):
        total = one.diagonal_of(k1[z], z)
        d1[z] = total
        i1[z] = 1.0 / total

    loop(8, diagonals)

    def coarser(z):
        sums = [
            lane_sum(row_pairs(buffer.at[i], field[2 * z] + field[2 * z + 1]), 1)
            for i, field in enumerate((w1, u1, k1))
        ]
        blank = jnp.zeros((4, COLS), F32)
        g2[z] = jnp.concatenate([2.0 * jnp.sqrt(0.125 * sums[0]), blank], axis=0)
        h2[z + 1] = jnp.concatenate([2.0 * jnp.sqrt(0.125 * sums[1]), blank], axis=0)
        k2[z] = jnp.concatenate([sums[2], blank + 1.0], axis=0)

    loop(4, coarser)
    two = Level(4, 2, g2, h2, i2)

    def diagonals_two(z):
        i2[z] = 1.0 / two.diagonal_of(k2[z], z)

    loop(4, diagonals_two)


def coarse_solve(core, one, two, pieces, far_tile, r1, xa1, xb1, r2, xa2, xb2, buffer):
    own, partner, odd, second = pieces
    clear_ends(xa1, xb1, xa2, xb2)
    starts = (16, 24 - 16 * core, 8 + 16 * core, 32 * core, 32 - 32 * core)
    starts = [s if isinstance(s, int) else pl.multiple_of(s, 8) for s in starts]

    def assemble(z):
        for i in range(2):
            j = 2 * z + i
            tiles = (own[j], partner[j], odd[j], far_tile(z, i), second[j])
            for start, tile in zip(starts, tiles):
                r1[z, i, pl.ds(start, 8), :] = tile

    loop(8, assemble)
    one.first(xa1, r1, FINE[0])
    one.update(xb1, xa1, r1, FINE[1])

    def restrict(z):
        for i in range(2):
            total = one.defect(xb1, r1, 2 * z, i) + one.defect(xb1, r1, 2 * z + 1, i)
            sums = lane_sum(row_pairs(buffer.at[i], total), 1)
            r2[z, i] = jnp.concatenate([sums, jnp.zeros((4, COLS), F32)], axis=0)

    loop(4, restrict)
    two.first(xa2, r2, COARSE[0])
    two.update(xb2, xa2, r2, COARSE[1])
    two.update(xa2, xb2, r2, COARSE[2])
    two.update(xb2, xa2, r2, COARSE[3])

    inner = [ref.at[:, :, 8:32, :] for ref in (xa1, xb1, r1)]
    inner_one = Level(8, 1, *(ref.at[:, 8:32, :] for ref in (one.g, one.h, one.inverse)))

    def prolong(z):
        for i in range(2):
            fine = row_repeat(buffer.at[i], xb2[z + 1, i, 4:16, :])
            for half in range(2):
                inner[0][2 * z + half + 1, i] = inner[1][2 * z + half + 1, i] + fine

    loop(4, prolong)
    inner_one.update(inner[1], inner[0], inner[2], FINE[0])
    inner_one.update(inner[0], inner[1], inner[2], FINE[1])


def fine_correct(level, out, xp, c1, wide, buffer):
    rows = c1[1:9, :, 12:28, :].reshape(R_TILES * 16, COLS)
    wide[...] = column_repeat(rows).reshape(R_TILES, 16, WIDE)

    def body(pair):
        for i in range(2):
            fine = row_repeat(buffer.at[i], wide[2 * pair + i])
            for half in range(2):
                out[2 * pair + half + 1, i] = xp[2 * pair + half + 1, i] + fine

    loop(NZ // 2, body)


def near_kernel(odd, near):
    near[...] = odd[0:R_TILES]


def far_half_kernel(place, own, partner, message):
    message[0:R_TILES] = own[...]

    def pair(p):
        message[R_TILES + p] = half_rows(partner[2 * p], partner[2 * p + 1], place[0] == 0)

    loop(R_TILES // 2, pair)


def after_kernel(odd, after, near):
    near[...] = odd[0:M_TILES]


def coarse_kernel(
    place, own, partner, odd, far, g1, h1, d1, i1, g2, h2, i2, w1, k1, u1, k2, buffer
):
    coarse_coefficients(
        place, (own, partner, odd, far), g1, h1, d1, i1, g2, h2, i2, w1, k1, u1, k2, buffer
    )


def middle_kernel(
    place, r, g, h, d, inverse, xp, own, partner, odd, far, g1, h1, d1, i1, g2, h2, i2,
    z_out, xp_out, r1_out,
    xa, xb, r1, xa1, xb1, r2, xa2, xb2, wide, sums, buffer,
):
    core = place[0]
    zero = Level(NZ, 1, g, h, inverse, d)
    one = Level(8, 1, g1, h1, i1, d1)
    two = Level(4, 2, g2, h2, i2)
    coarse_solve(core, one, two, (own, partner, odd, far), lambda z, i: odd[R_TILES + 2 * z + i], r1, xa1, xb1, r2, xa2, xb2, buffer)
    clear_ends(xa, xb, xp_out)
    fine_correct(zero, xa, xp, xa1, wide, buffer)
    zero.update(xb, xa, r, FINE[0])

    def last(z):
        scaled = FINE[1] * inverse[z]
        first = FINE[0] * inverse[z]
        for i in range(2):
            value = (1.0 - FINE[1]) * xb[z + 1, i] + scaled * (r[z, i] + zero.couple(xb, z, i))
            z_out[z, i] = value
            xa[z + 1, i] = first * value

    loop(NZ, last)
    zero.update(xp_out, xa, z_out, FINE[1])
    fine_restrict(zero, xp_out, z_out, sums, buffer, r1_out)


def last_kernel(
    place, rhs, r, g, h, d, inverse, xp, own, partner, odd, far, g1, h1, d1, i1, g2, h2, i2,
    direction, image, sums,
    xa, xb, r1, xa1, xb1, r2, xa2, xb2, wide, totals, buffer,
):
    core = place[0]
    zero = Level(NZ, 1, g, h, inverse, d)
    one = Level(8, 1, g1, h1, i1, d1)
    two = Level(4, 2, g2, h2, i2)

    def far_tile(z, i):
        tile = odd[R_TILES + z]
        return jnp.where((core == 0) == (i == 0), pltpu.roll(tile, 4, 0), tile)

    coarse_solve(core, one, two, (own, partner, odd, far), far_tile, r1, xa1, xb1, r2, xa2, xb2, buffer)
    clear_ends(xa, xb)
    fine_correct(zero, xa, xp, xa1, wide, buffer)
    zero.update(xb, xa, r, FINE[0])
    zero.update(xa, xb, r, FINE[1])

    def first_image(z):
        for i in range(2):
            xb[z + 1, i] = d[z] * xa[z + 1, i] - zero.couple(xa, z, i)

    loop(NZ, first_image)
    totals[...] = jnp.zeros(totals.shape, F32)

    def second_image(z):
        for i in range(2):
            field = xa[z + 1, i, 8:24, 0:COLS]
            value = (d[z] * xb[z + 1, i] - zero.couple(xb, z, i))[8:24, 0:COLS]
            direction[i, z] = field
            image[i, z] = value
            totals[i] += rhs[i, z] * field
            totals[2 + i] += field * value

    loop(NZ, second_image)
    row = sublanes(8, COLS)
    lane = lanes(8, COLS)
    line = jnp.zeros((8, COLS), F32)
    for i in range(4):
        line = jnp.where(lane == i, jnp.sum(totals[i]), line)

    def spread(j):
        sums[pl.ds(pl.multiple_of(8 * j, 8), 8), :] = line

    loop(sums.shape[0] // 8, spread)


def scale_kernel(rhs, direction, image, sums, solution_field, residual):
    total = jnp.sum(sums[...], axis=0, keepdims=True)
    lane = lanes(1, COLS)
    parts = [jnp.sum(jnp.where(lane == i, total, 0.0), axis=1, keepdims=True) for i in range(4)]
    for i in range(2):
        alpha = parts[i] / parts[2 + i]

        def body(z, i=i, alpha=alpha):
            solution_field[i, z] = alpha * direction[i, z]
            residual[i, z] = rhs[i, z] - alpha * image[i, z]

        loop(NZ, body)


COSTS = {
    "start_kernel": 1,
    "corner_kernel": 1,
    "widen_kernel": 30,
    "rows_kernel": 1,
    "material_kernel": 1,
    "down_kernel": 4,
    "near_kernel": 30,
    "far_half_kernel": 1,
    "after_kernel": 30,
    "coarse_kernel": 1,
    "middle_kernel": 6,
    "last_kernel": 6,
    "scale_kernel": 1,
}


def call(kernel, operands, outs, scratch=(), place=True, far=None):
    far = far or {}
    vmem = pl.BlockSpec(memory_space=pltpu.VMEM)
    specs = [pl.BlockSpec(memory_space=far[i]) if i in far else vmem for i in range(len(operands))]
    if place:
        specs[0] = pl.BlockSpec(memory_space=pltpu.SMEM)
    return pl.pallas_call(
        kernel,
        out_shape=[jax.ShapeDtypeStruct(shape, F32) for shape in outs],
        in_specs=specs,
        out_specs=[vmem] * len(outs),
        scratch_shapes=[pltpu.VMEM(shape, F32) if isinstance(shape, tuple) else shape for shape in scratch],
        cost_estimate=pl.CostEstimate(
            flops=COSTS[kernel.__name__] * 1_000_000_000, bytes_accessed=COSTS[kernel.__name__] * 3_000_000, transcendentals=0
        ),
        compiler_params=pltpu.CompilerParams(vmem_limit_bytes=16 * 1024 * 1024),
    )(*operands)


FIELD0 = (NZ, 2, EXT0, WIDE)
PADDED0 = (NZ + 2, 2, EXT0, WIDE)
PADDED1 = (10, 2, EXT1, COLS)
PADDED2 = (6, 2, EXT2, COLS)
BUFFER = (3, 2, EXT1, COLS)
SUMS = (R_TILES, 8, WIDE)
SPREAD = (R_TILES, 16, WIDE)
COARSE_SCRATCH = [(8, 2, EXT1, COLS), PADDED1, PADDED1, (4, 2, EXT2, COLS), PADDED2, PADDED2, SPREAD]


def shards(count_x, count_y, right_side, classes, sea_mask, kappa_table, cross_table, vertical_table):
    gx = lax.axis_index("gx")
    gy = lax.axis_index("gy")
    place = jnp.stack([gx % 2, gx, gy, jnp.int32(count_x), jnp.int32(count_y)]).astype(jnp.int32)
    table = jnp.stack([jnp.sqrt(cross_table), jnp.sqrt(vertical_table), kappa_table])
    table = jnp.pad(table, ((0, 5), (0, COLS - table.shape[1])))

    pairs_on_chip = [(i, i ^ 1) for i in range(count_x)]
    pairs_across = [(i, (i + 1 if i % 2 else i - 1) % count_x) for i in range(count_x)]

    def on_chip(value):
        return lax.ppermute(value, "gx", pairs_on_chip)

    def across_chips(value):
        return lax.ppermute(value, "gx", pairs_across)

    def rows_of(own, partner, message):
        odd = across_chips(message)
        near = call(near_kernel, (odd,), [own.shape], place=False)[0]
        return own, partner, odd, on_chip(near)

    forward = [(i, (i + 1) % count_y) for i in range(count_y)]
    backward = [(target, source) for source, target in forward]

    def both_sides(to_left, to_right):
        return lax.ppermute(to_right, "gy", forward), lax.ppermute(to_left, "gy", backward)

    part = lax.broadcasted_iota(jnp.int32, (4, *classes.shape), 0)
    materials = jnp.where(part == 2, classes[None], sea_mask[None]).astype(F32)
    twice = jnp.broadcast_to(right_side[None], (2, *right_side.shape)).reshape(part.shape)
    fields = jnp.where(part < 2, twice, materials)
    to_left, to_right, msg_o = call(
        start_kernel, (place, fields), [(MSG_Y, ROWS, COLS), (MSG_Y, ROWS, COLS), (MSG_X, 8, COLS)]
    )
    from_o = across_chips(msg_o)
    from_left, from_right = both_sides(to_left, to_right)
    r_own, c_own, s_own, msg_x = call(
        rows_kernel,
        (place, fields, from_left, from_right),
        [(NZ, 2, ROWS, WIDE), (NZ, ROWS, WIDE), (NZ, ROWS, WIDE), (MSG_X, 8, WIDE)],
    )
    from_x = on_chip(msg_x)
    g_own, h_own, k_own, packed = call(
        material_kernel,
        (c_own, s_own, table),
        [(NZ, ROWS, WIDE)] * 3 + [(M_TILES, 8, COLS)],
        [(M_TILES, 8, WIDE), BUFFER],
        place=False,
    )
    corner_tiles = call(corner_kernel, (from_o, packed), [(CORNER, 8, COLS)] * 2, place=False, far={1: pl.ANY})
    wide = call(widen_kernel, (from_o, *both_sides(*corner_tiles)), [(MSG_X, 8, WIDE)], place=False)[0]
    packed_partner = on_chip(packed)
    packed_odd = across_chips(jnp.concatenate([packed, packed_partner], axis=0))
    r, g, h, d, inverse, xp, r1 = call(
        down_kernel,
        (place, r_own, g_own, h_own, k_own, from_x, wide, table),
        [FIELD0, (NZ, EXT0, WIDE), (NZ + 2, EXT0, WIDE), (NZ, EXT0, WIDE), (NZ, EXT0, WIDE), PADDED0, (R_TILES, 8, COLS)],
        [PADDED0, (NZ, EXT0, WIDE), (2, NZ, WIDE), SUMS, BUFFER],
    )
    partner = on_chip(r1)
    rows = rows_of(r1, partner, jnp.concatenate([r1, partner], axis=0))
    packed_near = call(
        after_kernel, (packed_odd, rows[1]), [packed.shape], place=False, far={1: pl.ANY}
    )[0]
    material = (packed, packed_partner, packed_odd, on_chip(packed_near))
    one = [(8, EXT1, COLS), (10, EXT1, COLS), (8, EXT1, COLS), (8, EXT1, COLS)]
    two = [(4, EXT2, COLS), (6, EXT2, COLS), (4, EXT2, COLS)]
    coarse = call(
        coarse_kernel, (place, *material), [*one, *two], [one[0], one[0], one[0], two[0], BUFFER]
    )
    r, xp, r1 = call(
        middle_kernel,
        (place, r, g, h, d, inverse, xp, *rows, *coarse),
        [FIELD0, PADDED0, (R_TILES, 8, COLS)],
        [PADDED0, PADDED0, *COARSE_SCRATCH, SUMS, BUFFER],
    )
    partner = on_chip(r1)
    message = call(far_half_kernel, (place, r1, partner), [(R_TILES * 3 // 2, 8, COLS)])[0]
    count = count_x * count_y
    direction, image, sums = call(
        last_kernel,
        (place, fields, r, g, h, d, inverse, xp, *rows_of(r1, partner, message), *coarse),
        [(2, NZ, ROWS, COLS)] * 2 + [(count, COLS)],
        [PADDED0, PADDED0, *COARSE_SCRATCH, (4, ROWS, COLS), BUFFER],
    )
    sums = lax.all_to_all(sums.reshape(count, 1, COLS), ("gx", "gy"), 0, 0).reshape(count, COLS)
    return tuple(
        call(
            scale_kernel,
            (fields, direction, image, sums),
            [(2, NZ, ROWS, COLS)] * 2,
            place=False,
        )
    )


def solution(mesh):
    return jax.shard_map(
        functools.partial(shards, mesh.shape["gx"], mesh.shape["gy"]),
        mesh=mesh,
        in_specs=(
            P(None, None, "gx", "gy"),
            P(None, "gx", "gy"),
            P(None, "gx", "gy"),
            P(),
            P(),
            P(),
        ),
        out_specs=(P(None, None, "gx", "gy"), P(None, None, "gx", "gy")),
        check_vma=False,
    )
```

```python
import functools
import math

import jax
import jax.numpy as jnp
from jax import lax
from jax.experimental import pallas as pl
from jax.experimental.pallas import tpu as pltpu
from jax.sharding import PartitionSpec as P

F32 = jnp.float32
NZ = 16
ROWS = 16
COLS = 128
WIDE = 256
HALF = 64
UNROLL = 8
EXT0 = 32
EXT1 = 40
EXT2 = 24


def cheb_weights(degree, lower_end, upper_end):
    middle = 0.5 * (upper_end + lower_end)
    radius = 0.5 * (upper_end - lower_end)
    return [
        1.0 / (middle + radius * math.cos(math.pi * (2 * index_k + 1) / (2 * degree)))
        for index_k in range(degree)
    ]


FINE = cheb_weights(2, 0.3, 2.0)
COARSE = cheb_weights(4, 0.1, 2.0)


def loop(count, body):
    def step(index, carry):
        body(index)
        return carry

    lax.fori_loop(0, count, step, 0, unroll=min(count, UNROLL))


def lanes(rows, width):
    return lax.broadcasted_iota(jnp.int32, (rows, width), 1)


def sublanes(rows, width):
    return lax.broadcasted_iota(jnp.int32, (rows, width), 0)


def lane_sum(value, step):
    width = value.shape[1]
    first = (lanes(*value.shape) // step) % 2 == 0
    return value + jnp.where(first, pltpu.roll(value, width - step, 1), pltpu.roll(value, step, 1))


def across(value, step):
    rows, width = value.shape
    return (
        pltpu.roll(value, 1, 0)
        + pltpu.roll(value, rows - 1, 0)
        + pltpu.roll(value, step, 1)
        + pltpu.roll(value, width - step, 1)
    )


def row_pairs(buffer, value):
    rows, width = value.shape
    parts = []
    for half in range(width // COLS):
        buffer[half, 0:rows, :] = value[:, half * COLS : (half + 1) * COLS]
        parts.append(
            buffer[half, pl.ds(0, rows // 2, stride=2), :] + buffer[half, pl.ds(1, rows // 2, stride=2), :]
        )
    return parts[0] if len(parts) == 1 else jnp.concatenate(parts, axis=1)


def row_repeat(buffer, value):
    rows, width = value.shape
    parts = []
    for half in range(width // COLS):
        part = value[:, half * COLS : (half + 1) * COLS]
        buffer[half, pl.ds(0, rows, stride=2), :] = part
        buffer[half, pl.ds(1, rows, stride=2), :] = part
        parts.append(buffer[half, 0 : 2 * rows, :])
    return parts[0] if len(parts) == 1 else jnp.concatenate(parts, axis=1)


def column_pairs(value):
    row = lax.broadcasted_iota(jnp.int32, (WIDE, COLS), 0)
    column = lax.broadcasted_iota(jnp.int32, (WIDE, COLS), 1)
    matrix = jnp.where(row // 2 == column, 1.0, 0.0)
    return jnp.dot(value, matrix, precision=lax.Precision.HIGHEST, preferred_element_type=F32)


def column_repeat(value):
    row = lax.broadcasted_iota(jnp.int32, (COLS, WIDE), 0)
    column = lax.broadcasted_iota(jnp.int32, (COLS, WIDE), 1)
    matrix = jnp.where(column // 2 == row, 1.0, 0.0)
    return jnp.dot(value, matrix, precision=lax.Precision.HIGHEST, preferred_element_type=F32)


def half_rows(first, second, lower):
    row = sublanes(*first.shape)
    low = jnp.where(row < 4, first, pltpu.roll(second, 4, 0))
    high = jnp.where(row < 4, pltpu.roll(first, 4, 0), second)
    return jnp.where(lower, low, high)


def pick(table_row, index):
    rows, width = index.shape
    table = jnp.broadcast_to(table_row, (rows, COLS))
    parts = [
        jnp.take_along_axis(table, index[:, start : start + COLS], axis=1)
        for start in range(0, width, COLS)
    ]
    return parts[0] if len(parts) == 1 else jnp.concatenate(parts, axis=1)


def pack_halves(first, second):
    left = lanes(*first.shape) < HALF
    low = jnp.where(left, first, pltpu.roll(second, HALF, 1))
    high = jnp.where(left, pltpu.roll(first, HALF, 1), second)
    return low, high


def unpack_halves(from_right, from_left):
    left = lanes(*from_right.shape) < HALF
    first = jnp.where(left, from_right, pltpu.roll(from_left, HALF, 1))
    second = jnp.where(left, pltpu.roll(from_right, HALF, 1), from_left)
    return first, second


SPAN = 51
QUINTS = 9


def pack_quint(a, b, c, d, e):
    lane = lanes(*a.shape)
    lows = [
        jnp.where(lane < SPAN, x, jnp.where(lane < 2 * SPAN, pltpu.roll(y, SPAN, 1), pltpu.roll(e, shift, 1)))
        for x, y, shift in ((a, b, 102), (c, d, 76))
    ]
    highs = [
        jnp.where(
            lane >= COLS - SPAN,
            x,
            jnp.where(lane >= COLS - 2 * SPAN, pltpu.roll(y, COLS - SPAN, 1), pltpu.roll(e, COLS - shift, 1)),
        )
        for x, y, shift in ((a, b, 102), (c, d, 76))
    ]
    return lows, highs


def unpack_quint(from_right, from_left):
    lane = lanes(*from_right[0].shape)
    left = lane < HALF
    fields = []
    for right, other in zip(from_right, from_left):
        fields.append(jnp.where(left, right, other))
        fields.append(jnp.where(left, pltpu.roll(right, COLS - SPAN, 1), pltpu.roll(other, SPAN, 1)))
    parts = [
        jnp.where(left, pltpu.roll(right, COLS - shift, 1), pltpu.roll(other, shift, 1))
        for right, other, shift in zip(from_right, from_left, (102, 76))
    ]
    outer = (lane < COLS - 102) | (lane >= 102)
    fields.append(jnp.where(outer, parts[0], parts[1]))
    return fields


def pack_sea(fields):
    rows, width = fields[0].shape
    even_lane = lanes(rows, width) % 2 == 0
    even_row = sublanes(rows, width) % 2 == 0
    pairs = [
        jnp.where(even_lane, fields[i], pltpu.roll(fields[i + 1], 1, 1)) for i in (0, 2)
    ]
    return jnp.where(even_row, pairs[0], pltpu.roll(pairs[1], 1, 0))


def unpack_sea(packed):
    rows, width = packed.shape
    spot = (lanes(rows, width) % 2 == 0) & (sublanes(rows, width) % 2 == 0)
    fields = []
    for pair in (packed, pltpu.roll(packed, rows - 1, 0)):
        for field in (pair, pltpu.roll(pair, width - 1, 1)):
            fields.append(jnp.where(spot, field, 1.0))
    return fields


def fill_message(message, rhs, classes, sea, start, edge):
    def fields(z):
        for i in range(2):
            message[2 * z + i] = rhs(z, i)[pl.ds(start, 8), :]
        message[32 + z] = classes.at[z][pl.ds(start, 8), :]
        message.at[52 + z // 8][pl.ds(z % 8, 1), :] = classes.at[z][pl.ds(edge, 1), :]
        message.at[54 + z // 8][pl.ds(z % 8, 1), :] = sea.at[z][pl.ds(edge, 1), :]

    loop(NZ, fields)

    def quads(j):
        message[48 + j] = pack_sea([sea[4 * j + i, pl.ds(start, 8), :] for i in range(4)])

    loop(4, quads)


MSG_Y = 22
CORNER = 24
MSG_X = 56
R_TILES = 16
M_TILES = 24


def start_kernel(place, fields, to_left, to_right, message):
    core = place[0]
    classes, sea = fields.at[2], fields.at[3]

    def quint(k):
        lows, highs = pack_quint(*(fields[(5 * k + t) // NZ, (5 * k + t) % NZ] for t in range(5)))
        for t in range(2):
            to_left[2 * k + t] = lows[t]
            to_right[2 * k + t] = highs[t]

    loop(QUINTS, quint)
    rest = [classes[13], classes[14], classes[15]]
    rest += [pack_sea([sea[4 * q + i] for i in range(4)]) for q in range(4)]
    rest.append(rest[-1])
    for j in range(4):
        to_left[18 + j], to_right[18 + j] = pack_halves(rest[2 * j], rest[2 * j + 1])
    start = pl.multiple_of(8 * core, 8)
    fill_message(message, lambda z, i: fields.at[i, z], classes, sea, start, 8 - core)


def corner_kernel(message, after, to_left, to_right):
    def quint(k):
        lows, highs = pack_quint(*(message[5 * k + t] for t in range(5)))
        for t in range(2):
            to_left[2 * k + t] = lows[t]
            to_right[2 * k + t] = highs[t]

    loop(QUINTS, quint)
    for p in range(6):
        first = 45 + 2 * p
        to_left[18 + p], to_right[18 + p] = pack_halves(message[first], message[min(first + 1, MSG_X - 1)])


def valid_class(halo):
    return jnp.clip(halo, 0.0, 15.0)


def widen_kernel(message, corner_left, corner_right, wide):
    def quint(k):
        halos = unpack_quint(
            [corner_right[2 * k + t] for t in range(2)], [corner_left[2 * k + t] for t in range(2)]
        )
        for t, halo in enumerate(halos):
            wide[5 * k + t] = jnp.concatenate([message[5 * k + t], halo], axis=1)

    loop(QUINTS, quint)
    for j in range(32, 35):
        wide[j, :, COLS:] = valid_class(wide[j, :, COLS:])
    for p in range(6):
        first = 45 + 2 * p
        for i, halo in enumerate(unpack_halves(corner_right[18 + p], corner_left[18 + p])):
            if first + i < MSG_X:
                wide[first + i] = jnp.concatenate([message[first + i], halo], axis=1)


def rows_kernel(place, fields, from_left, from_right, r_out, c_out, s_out, message):
    core = place[0]
    gy = place[2]
    left = lanes(ROWS, COLS) < HALF
    inside = jnp.where(
        left,
        jnp.where(gy < place[4] - 1, 1.0, 0.0),
        jnp.where(gy > 0, 1.0, 0.0),
    )

    def group(k):
        return unpack_quint(
            [from_right[2 * k + t] for t in range(2)], [from_left[2 * k + t] for t in range(2)]
        )

    def put_rhs(f, halo):
        r_out[f % NZ, f // NZ] = jnp.concatenate([fields[f // NZ, f % NZ], halo], axis=1)

    def put_class(z, halo):
        c_out[z] = jnp.concatenate([fields[2, z], halo], axis=1)

    def rhs_step(k):
        for t, halo in enumerate(group(k)):
            put_rhs(5 * k + t, halo)

    loop(6, rhs_step)
    mixed = group(6)
    for t in range(2):
        put_rhs(30 + t, mixed[t])
    for t in range(3):
        put_class(t, valid_class(mixed[2 + t]))
    for k in (7, 8):
        for t, halo in enumerate(group(k)):
            put_class(5 * k + t - 32, halo)
    rest = []
    for j in range(4):
        rest += unpack_halves(from_right[18 + j], from_left[18 + j])
    for t in range(3):
        put_class(13 + t, rest[t])
    for q in range(4):
        for i, field in enumerate(unpack_sea(rest[3 + q])):
            s_out[4 * q + i] = jnp.concatenate([fields[3, 4 * q + i], field * inside], axis=1)
    start = pl.multiple_of(8 * (1 - core), 8)
    fill_message(message, lambda z, i: r_out.at[z, i], c_out, s_out, start, 7 + core)


def material_kernel(c_in, s_in, table, g_out, h_out, k_out, coarse, sums, buffer):
    def fields(z):
        index = c_in[z].astype(jnp.int32)
        sea = s_in[z]
        g = pick(table[0:1], index) * sea
        h = pick(table[1:2], index) * sea
        k = pick(table[2:3], index) * sea + (1.0 - sea)
        g_out[z] = g
        h_out[z] = h
        k_out[z] = k
        return 0.125 * g * g, 0.125 * h * h, k

    def step(pair):
        first = fields(2 * pair)
        second = fields(2 * pair + 1)
        for i in range(3):
            sums[8 * i + pair] = row_pairs(buffer.at[i], first[i] + second[i])

    loop(8, step)
    coarse[...] = column_pairs(sums[...].reshape(M_TILES * 8, WIDE)).reshape(M_TILES, 8, COLS)


class Level:
    def __init__(self, depth, step, g, h, inverse, diagonal=None):
        self.depth, self.step = depth, step
        self.g, self.h, self.inverse, self.diagonal = g, h, inverse, diagonal

    def couple(self, x, z, i):
        horizontal = self.g[z] * across(self.g[z] * x[z + 1, i], self.step)
        vertical = self.h[z + 1] * (self.h[z] * x[z, i] + self.h[z + 2] * x[z + 2, i])
        return horizontal + vertical

    def first(self, x, r, weight):
        def body(z):
            scaled = weight * self.inverse[z]
            for i in range(2):
                x[z + 1, i] = scaled * r[z, i]

        loop(self.depth, body)

    def update(self, new, x, r, weight):
        def body(z):
            scaled = weight * self.inverse[z]
            for i in range(2):
                new[z + 1, i] = (1.0 - weight) * x[z + 1, i] + scaled * (r[z, i] + self.couple(x, z, i))

        loop(self.depth, body)

    def defect(self, x, r, z, i):
        return r[z, i] - self.diagonal[z] * x[z + 1, i] + self.couple(x, z, i)

    def diagonal_of(self, k, z):
        horizontal = self.g[z] * across(self.g[z], self.step)
        vertical = self.h[z + 1] * (self.h[z] + self.h[z + 2])
        return k + horizontal + vertical


def clear_ends(*refs):
    for ref in refs:
        ref[0] = jnp.zeros(ref.shape[1:], ref.dtype)
        ref[ref.shape[0] - 1] = jnp.zeros(ref.shape[1:], ref.dtype)


def fine_restrict(level, x, r, sums, buffer, out):
    def body(pair):
        for i in range(2):
            total = level.defect(x, r, 2 * pair, i) + level.defect(x, r, 2 * pair + 1, i)
            sums[2 * pair + i] = row_pairs(buffer.at[i], total[8:24])

    loop(NZ // 2, body)
    out[...] = column_pairs(sums[...].reshape(R_TILES * 8, WIDE)).reshape(R_TILES, 8, COLS)


def down_kernel(
    place, r_own, g_own, h_own, k_own, from_x, wide, table,
    r, g, h, d, inverse, xp, r1, xa, ka, edges, sums, buffer,
):
    core = place[0]
    gx = place[1]
    gy = place[2]
    open_side = jnp.where((gx > 0) & (gx < place[3] - 1), 1.0, 0.0)
    lane = lanes(8, WIDE)
    ends = jnp.where(
        lane < COLS,
        1.0,
        jnp.where(lane < COLS + HALF, jnp.where(gy < place[4] - 1, 1.0, 0.0), jnp.where(gy > 0, 1.0, 0.0)),
    )
    clear_ends(h, xp, xa)

    def own(z):
        for i in range(2):
            r[z, i, 8:24, :] = r_own[z, i]
        g[z, 8:24, :] = g_own[z]
        h[z + 1, 8:24, :] = h_own[z]
        ka[z, 8:24, :] = k_own[z]

    loop(NZ, own)

    for message, start, scale, slot in ((from_x, 24 * (1 - core), 1.0, 1 - core), (wide, 24 * core, open_side, core)):
        start = pl.multiple_of(start, 8)
        valid = scale * ends

        def halo(j, message=message, start=start, valid=valid):
            for q, sea in enumerate(unpack_sea(message[48 + j])):
                z = 4 * j + q
                sea = sea * valid
                index = message[32 + z].astype(jnp.int32)
                g[z, pl.ds(start, 8), :] = pick(table[0:1], index) * sea
                h[z + 1, pl.ds(start, 8), :] = pick(table[1:2], index) * sea
                ka[z, pl.ds(start, 8), :] = pick(table[2:3], index) * sea + (1.0 - sea)
                for i in range(2):
                    r[z, i, pl.ds(start, 8), :] = message[2 * z + i]

        loop(4, halo)
        for j in range(2):
            index = message[52 + j].astype(jnp.int32)
            edges[slot, 8 * j : 8 * j + 8, :] = pick(table[0:1], index) * (message[54 + j] * valid)

    level = Level(NZ, 1, g, h, inverse, d)
    row = sublanes(EXT0, WIDE)

    def diagonals(z):
        here = g[z]
        below = jnp.where(row == 0, edges[0, pl.ds(z, 1), :], pltpu.roll(here, 1, 0))
        above = jnp.where(row == EXT0 - 1, edges[1, pl.ds(z, 1), :], pltpu.roll(here, EXT0 - 1, 0))
        beside = pltpu.roll(here, 1, 1) + pltpu.roll(here, WIDE - 1, 1)
        total = ka[z] + here * (below + above + beside) + h[z + 1] * (h[z] + h[z + 2])
        d[z] = total
        reciprocal = 1.0 / total
        inverse[z] = reciprocal
        for i in range(2):
            xa[z + 1, i] = (FINE[0] * reciprocal) * r[z, i]

    loop(NZ, diagonals)
    level.update(xp, xa, r, FINE[1])
    fine_restrict(level, xp, r, sums, buffer, r1)


def coarse_coefficients(place, pieces, g1, h1, d1, i1, g2, h2, i2, w1, k1, u1, k2, buffer):
    core = place[0]
    clear_ends(h1, h2)
    own, partner, odd, far = pieces
    low = jnp.where(place[1] >= 2, 1.0, 0.0)
    high = jnp.where(place[1] < place[3] - 2, 1.0, 0.0)
    near_side = jnp.where(core == 0, low, high)
    far_side = jnp.where(core == 0, high, low)
    scales = (1.0, 1.0, near_side, near_side, far_side)
    starts = (16, 24 - 16 * core, 8 + 16 * core, 32 * core, 32 - 32 * core)
    starts = [s if isinstance(s, int) else pl.multiple_of(s, 8) for s in starts]

    def assemble(z):
        for i, field in enumerate((w1, u1, k1)):
            j = 8 * i + z
            tiles = (own[j], partner[j], odd[j], odd[M_TILES + j], far[j])
            for start, tile, scale in zip(starts, tiles, scales):
                field[z, pl.ds(start, 8), :] = tile * scale if i < 2 else tile

    loop(8, assemble)

    def roots(z):
        g1[z] = 2.0 * jnp.sqrt(w1[z])
        h1[z + 1] = 2.0 * jnp.sqrt(u1[z])

    loop(8, roots)
    one = Level(8, 1, g1, h1, i1, d1)

    def diagonals(z):
        total = one.diagonal_of(k1[z], z)
        d1[z] = total
        i1[z] = 1.0 / total

    loop(8, diagonals)

    def coarser(z):
        sums = [
            lane_sum(row_pairs(buffer.at[i], field[2 * z] + field[2 * z + 1]), 1)
            for i, field in enumerate((w1, u1, k1))
        ]
        blank = jnp.zeros((4, COLS), F32)
        g2[z] = jnp.concatenate([2.0 * jnp.sqrt(0.125 * sums[0]), blank], axis=0)
        h2[z + 1] = jnp.concatenate([2.0 * jnp.sqrt(0.125 * sums[1]), blank], axis=0)
        k2[z] = jnp.concatenate([sums[2], blank + 1.0], axis=0)

    loop(4, coarser)
    two = Level(4, 2, g2, h2, i2)

    def diagonals_two(z):
        i2[z] = 1.0 / two.diagonal_of(k2[z], z)

    loop(4, diagonals_two)


def coarse_solve(core, one, two, pieces, far_tile, r1, xa1, xb1, r2, xa2, xb2, buffer):
    own, partner, odd, second = pieces
    clear_ends(xa1, xb1, xa2, xb2)
    starts = (16, 24 - 16 * core, 8 + 16 * core, 32 * core, 32 - 32 * core)
    starts = [s if isinstance(s, int) else pl.multiple_of(s, 8) for s in starts]

    def assemble(z):
        for i in range(2):
            j = 2 * z + i
            tiles = (own[j], partner[j], odd[j], far_tile(z, i), second[j])
            for start, tile in zip(starts, tiles):
                r1[z, i, pl.ds(start, 8), :] = tile

    loop(8, assemble)
    one.first(xa1, r1, FINE[0])
    one.update(xb1, xa1, r1, FINE[1])

    def restrict(z):
        for i in range(2):
            total = one.defect(xb1, r1, 2 * z, i) + one.defect(xb1, r1, 2 * z + 1, i)
            sums = lane_sum(row_pairs(buffer.at[i], total), 1)
            r2[z, i] = jnp.concatenate([sums, jnp.zeros((4, COLS), F32)], axis=0)

    loop(4, restrict)
    two.first(xa2, r2, COARSE[0])
    two.update(xb2, xa2, r2, COARSE[1])
    two.update(xa2, xb2, r2, COARSE[2])
    two.update(xb2, xa2, r2, COARSE[3])

    inner = [ref.at[:, :, 8:32, :] for ref in (xa1, xb1, r1)]
    inner_one = Level(8, 1, *(ref.at[:, 8:32, :] for ref in (one.g, one.h, one.inverse)))

    def prolong(z):
        for i in range(2):
            fine = row_repeat(buffer.at[i], xb2[z + 1, i, 4:16, :])
            for half in range(2):
                inner[0][2 * z + half + 1, i] = inner[1][2 * z + half + 1, i] + fine

    loop(4, prolong)
    inner_one.update(inner[1], inner[0], inner[2], FINE[0])
    inner_one.update(inner[0], inner[1], inner[2], FINE[1])


def fine_correct(level, out, xp, c1, wide, buffer):
    rows = c1[1:9, :, 12:28, :].reshape(R_TILES * 16, COLS)
    wide[...] = column_repeat(rows).reshape(R_TILES, 16, WIDE)

    def body(pair):
        for i in range(2):
            fine = row_repeat(buffer.at[i], wide[2 * pair + i])
            for half in range(2):
                out[2 * pair + half + 1, i] = xp[2 * pair + half + 1, i] + fine

    loop(NZ // 2, body)


def near_kernel(odd, near):
    near[...] = odd[0:R_TILES]


def far_half_kernel(place, own, partner, message):
    message[0:R_TILES] = own[...]

    def pair(p):
        message[R_TILES + p] = half_rows(partner[2 * p], partner[2 * p + 1], place[0] == 0)

    loop(R_TILES // 2, pair)


def join_kernel(own, partner, after, message):
    message[0:M_TILES] = own[...]
    message[M_TILES:] = partner[...]


def after_kernel(odd, after, near):
    near[...] = odd[0:M_TILES]


def coarse_kernel(
    place, own, partner, odd, far, g1, h1, d1, i1, g2, h2, i2, w1, k1, u1, k2, buffer
):
    coarse_coefficients(
        place, (own, partner, odd, far), g1, h1, d1, i1, g2, h2, i2, w1, k1, u1, k2, buffer
    )


def middle_kernel(
    place, r, g, h, d, inverse, xp, own, partner, odd, far, g1, h1, d1, i1, g2, h2, i2,
    z_out, xp_out, r1_out,
    xa, xb, r1, xa1, xb1, r2, xa2, xb2, wide, sums, buffer,
):
    core = place[0]
    zero = Level(NZ, 1, g, h, inverse, d)
    one = Level(8, 1, g1, h1, i1, d1)
    two = Level(4, 2, g2, h2, i2)
    coarse_solve(core, one, two, (own, partner, odd, far), lambda z, i: odd[R_TILES + 2 * z + i], r1, xa1, xb1, r2, xa2, xb2, buffer)
    clear_ends(xa, xb, xp_out)
    fine_correct(zero, xa, xp, xa1, wide, buffer)
    zero.update(xb, xa, r, FINE[0])

    def last(z):
        scaled = FINE[1] * inverse[z]
        first = FINE[0] * inverse[z]
        for i in range(2):
            value = (1.0 - FINE[1]) * xb[z + 1, i] + scaled * (r[z, i] + zero.couple(xb, z, i))
            z_out[z, i] = value
            xa[z + 1, i] = first * value

    loop(NZ, last)
    zero.update(xp_out, xa, z_out, FINE[1])
    fine_restrict(zero, xp_out, z_out, sums, buffer, r1_out)


def last_kernel(
    place, rhs, r, g, h, d, inverse, xp, own, partner, odd, far, g1, h1, d1, i1, g2, h2, i2,
    direction, image, sums,
    xa, xb, r1, xa1, xb1, r2, xa2, xb2, wide, totals, buffer,
):
    core = place[0]
    zero = Level(NZ, 1, g, h, inverse, d)
    one = Level(8, 1, g1, h1, i1, d1)
    two = Level(4, 2, g2, h2, i2)

    def far_tile(z, i):
        tile = odd[R_TILES + z]
        return jnp.where((core == 0) == (i == 0), pltpu.roll(tile, 4, 0), tile)

    coarse_solve(core, one, two, (own, partner, odd, far), far_tile, r1, xa1, xb1, r2, xa2, xb2, buffer)
    clear_ends(xa, xb)
    fine_correct(zero, xa, xp, xa1, wide, buffer)
    zero.update(xb, xa, r, FINE[0])
    zero.update(xa, xb, r, FINE[1])

    def first_image(z):
        for i in range(2):
            xb[z + 1, i] = d[z] * xa[z + 1, i] - zero.couple(xa, z, i)

    loop(NZ, first_image)
    totals[...] = jnp.zeros(totals.shape, F32)

    def second_image(z):
        for i in range(2):
            field = xa[z + 1, i, 8:24, 0:COLS]
            value = (d[z] * xb[z + 1, i] - zero.couple(xb, z, i))[8:24, 0:COLS]
            direction[i, z] = field
            image[i, z] = value
            totals[i] += rhs[i, z] * field
            totals[2 + i] += field * value

    loop(NZ, second_image)
    row = sublanes(8, COLS)
    lane = lanes(8, COLS)
    line = jnp.zeros((8, COLS), F32)
    for i in range(4):
        line = jnp.where(lane == i, jnp.sum(totals[i]), line)

    def spread(j):
        sums[pl.ds(pl.multiple_of(8 * j, 8), 8), :] = line

    loop(sums.shape[0] // 8, spread)


def scale_kernel(rhs, direction, image, sums, solution_field, residual):
    total = jnp.sum(sums[...], axis=0, keepdims=True)
    lane = lanes(1, COLS)
    parts = [jnp.sum(jnp.where(lane == i, total, 0.0), axis=1, keepdims=True) for i in range(4)]
    for i in range(2):
        alpha = parts[i] / parts[2 + i]

        def body(z, i=i, alpha=alpha):
            solution_field[i, z] = alpha * direction[i, z]
            residual[i, z] = rhs[i, z] - alpha * image[i, z]

        loop(NZ, body)


COSTS = {
    "start_kernel": 1,
    "corner_kernel": 1,
    "widen_kernel": 30,
    "rows_kernel": 1,
    "material_kernel": 1,
    "down_kernel": 4,
    "near_kernel": 30,
    "far_half_kernel": 1,
    "join_kernel": 1,
    "after_kernel": 30,
    "coarse_kernel": 1,
    "middle_kernel": 6,
    "last_kernel": 6,
    "scale_kernel": 1,
}


def call(kernel, operands, outs, scratch=(), place=True, far=None):
    far = far or {}
    vmem = pl.BlockSpec(memory_space=pltpu.VMEM)
    specs = [pl.BlockSpec(memory_space=far[i]) if i in far else vmem for i in range(len(operands))]
    if place:
        specs[0] = pl.BlockSpec(memory_space=pltpu.SMEM)
    return pl.pallas_call(
        kernel,
        out_shape=[jax.ShapeDtypeStruct(shape, F32) for shape in outs],
        in_specs=specs,
        out_specs=[vmem] * len(outs),
        scratch_shapes=[pltpu.VMEM(shape, F32) if isinstance(shape, tuple) else shape for shape in scratch],
        cost_estimate=pl.CostEstimate(
            flops=COSTS[kernel.__name__] * 1_000_000_000, bytes_accessed=COSTS[kernel.__name__] * 3_000_000, transcendentals=0
        ),
        compiler_params=pltpu.CompilerParams(vmem_limit_bytes=16 * 1024 * 1024),
    )(*operands)


FIELD0 = (NZ, 2, EXT0, WIDE)
PADDED0 = (NZ + 2, 2, EXT0, WIDE)
PADDED1 = (10, 2, EXT1, COLS)
PADDED2 = (6, 2, EXT2, COLS)
BUFFER = (3, 2, EXT1, COLS)
SUMS = (R_TILES, 8, WIDE)
SPREAD = (R_TILES, 16, WIDE)
COARSE_SCRATCH = [(8, 2, EXT1, COLS), PADDED1, PADDED1, (4, 2, EXT2, COLS), PADDED2, PADDED2, SPREAD]


def shards(count_x, count_y, right_side, classes, sea_mask, kappa_table, cross_table, vertical_table):
    gx = lax.axis_index("gx")
    gy = lax.axis_index("gy")
    place = jnp.stack([gx % 2, gx, gy, jnp.int32(count_x), jnp.int32(count_y)]).astype(jnp.int32)
    table = jnp.stack([jnp.sqrt(cross_table), jnp.sqrt(vertical_table), kappa_table])
    table = jnp.pad(table, ((0, 5), (0, COLS - table.shape[1])))

    pairs_on_chip = [(i, i ^ 1) for i in range(count_x)]
    pairs_across = [(i, (i + 1 if i % 2 else i - 1) % count_x) for i in range(count_x)]

    def on_chip(value):
        return lax.ppermute(value, "gx", pairs_on_chip)

    def across_chips(value):
        return lax.ppermute(value, "gx", pairs_across)

    def rows_of(own, partner, message):
        odd = across_chips(message)
        near = call(near_kernel, (odd,), [own.shape], place=False)[0]
        return own, partner, odd, on_chip(near)

    forward = [(i, (i + 1) % count_y) for i in range(count_y)]
    backward = [(target, source) for source, target in forward]

    def both_sides(to_left, to_right):
        return lax.ppermute(to_right, "gy", forward), lax.ppermute(to_left, "gy", backward)

    part = lax.broadcasted_iota(jnp.int32, (4, *classes.shape), 0)
    materials = jnp.where(part == 2, classes[None], sea_mask[None]).astype(F32)
    twice = jnp.broadcast_to(right_side[None], (2, *right_side.shape)).reshape(part.shape)
    fields = jnp.where(part < 2, twice, materials)
    to_left, to_right, msg_o = call(
        start_kernel, (place, fields), [(MSG_Y, ROWS, COLS), (MSG_Y, ROWS, COLS), (MSG_X, 8, COLS)]
    )
    from_o = across_chips(msg_o)
    from_left, from_right = both_sides(to_left, to_right)
    r_own, c_own, s_own, msg_x = call(
        rows_kernel,
        (place, fields, from_left, from_right),
        [(NZ, 2, ROWS, WIDE), (NZ, ROWS, WIDE), (NZ, ROWS, WIDE), (MSG_X, 8, WIDE)],
    )
    from_x = on_chip(msg_x)
    g_own, h_own, k_own, packed = call(
        material_kernel,
        (c_own, s_own, table),
        [(NZ, ROWS, WIDE)] * 3 + [(M_TILES, 8, COLS)],
        [(M_TILES, 8, WIDE), BUFFER],
        place=False,
    )
    corner_tiles = call(corner_kernel, (from_o, packed), [(CORNER, 8, COLS)] * 2, place=False, far={1: pl.ANY})
    corners = both_sides(*corner_tiles)
    wide = call(widen_kernel, (from_o, *corners), [(MSG_X, 8, WIDE)], place=False)[0]
    packed_partner = on_chip(packed)
    both = call(
        join_kernel, (packed, packed_partner, corners[0]), [(2 * M_TILES, 8, COLS)], place=False, far={2: pl.ANY}
    )[0]
    packed_odd = across_chips(both)
    r, g, h, d, inverse, xp, r1 = call(
        down_kernel,
        (place, r_own, g_own, h_own, k_own, from_x, wide, table),
        [FIELD0, (NZ, EXT0, WIDE), (NZ + 2, EXT0, WIDE), (NZ, EXT0, WIDE), (NZ, EXT0, WIDE), PADDED0, (R_TILES, 8, COLS)],
        [PADDED0, (NZ, EXT0, WIDE), (2, NZ, WIDE), SUMS, BUFFER],
    )
    partner = on_chip(r1)
    rows = rows_of(r1, partner, jnp.concatenate([r1, partner], axis=0))
    packed_near = call(
        after_kernel, (packed_odd, rows[1]), [packed.shape], place=False, far={1: pl.ANY}
    )[0]
    material = (packed, packed_partner, packed_odd, on_chip(packed_near))
    one = [(8, EXT1, COLS), (10, EXT1, COLS), (8, EXT1, COLS), (8, EXT1, COLS)]
    two = [(4, EXT2, COLS), (6, EXT2, COLS), (4, EXT2, COLS)]
    coarse = call(
        coarse_kernel, (place, *material), [*one, *two], [one[0], one[0], one[0], two[0], BUFFER]
    )
    r, xp, r1 = call(
        middle_kernel,
        (place, r, g, h, d, inverse, xp, *rows, *coarse),
        [FIELD0, PADDED0, (R_TILES, 8, COLS)],
        [PADDED0, PADDED0, *COARSE_SCRATCH, SUMS, BUFFER],
    )
    partner = on_chip(r1)
    message = call(far_half_kernel, (place, r1, partner), [(R_TILES * 3 // 2, 8, COLS)])[0]
    count = count_x * count_y
    direction, image, sums = call(
        last_kernel,
        (place, fields, r, g, h, d, inverse, xp, *rows_of(r1, partner, message), *coarse),
        [(2, NZ, ROWS, COLS)] * 2 + [(count, COLS)],
        [PADDED0, PADDED0, *COARSE_SCRATCH, (4, ROWS, COLS), BUFFER],
    )
    sums = lax.all_to_all(sums.reshape(count, 1, COLS), ("gx", "gy"), 0, 0).reshape(count, COLS)
    return tuple(
        call(
            scale_kernel,
            (fields, direction, image, sums),
            [(2, NZ, ROWS, COLS)] * 2,
            place=False,
        )
    )


def solution(mesh):
    return jax.shard_map(
        functools.partial(shards, mesh.shape["gx"], mesh.shape["gy"]),
        mesh=mesh,
        in_specs=(
            P(None, None, "gx", "gy"),
            P(None, "gx", "gy"),
            P(None, "gx", "gy"),
            P(),
            P(),
            P(),
        ),
        out_specs=(P(None, None, "gx", "gy"), P(None, None, "gx", "gy")),
        check_vma=False,
    )
```

```python
import functools
import math

import jax
import jax.numpy as jnp
from jax import lax
from jax.experimental import pallas as pl
from jax.experimental.pallas import tpu as pltpu
from jax.sharding import PartitionSpec as P

F32 = jnp.float32
NZ = 16
ROWS = 16
COLS = 128
WIDE = 256
HALF = 64
UNROLL = 8
EXT0 = 32
EXT1 = 40
EXT2 = 24


def cheb_weights(degree, lower_end, upper_end):
    middle = 0.5 * (upper_end + lower_end)
    radius = 0.5 * (upper_end - lower_end)
    return [
        1.0 / (middle + radius * math.cos(math.pi * (2 * index_k + 1) / (2 * degree)))
        for index_k in range(degree)
    ]


FINE = cheb_weights(2, 0.3, 2.0)
COARSE = cheb_weights(4, 0.1, 2.0)


def loop(count, body):
    def step(index, carry):
        body(index)
        return carry

    lax.fori_loop(0, count, step, 0, unroll=min(count, UNROLL))


def lanes(rows, width):
    return lax.broadcasted_iota(jnp.int32, (rows, width), 1)


def sublanes(rows, width):
    return lax.broadcasted_iota(jnp.int32, (rows, width), 0)


def lane_sum(value, step):
    width = value.shape[1]
    first = (lanes(*value.shape) // step) % 2 == 0
    return value + jnp.where(first, pltpu.roll(value, width - step, 1), pltpu.roll(value, step, 1))


def across(value, step):
    rows, width = value.shape
    return (
        pltpu.roll(value, 1, 0)
        + pltpu.roll(value, rows - 1, 0)
        + pltpu.roll(value, step, 1)
        + pltpu.roll(value, width - step, 1)
    )


def row_pairs(buffer, value):
    rows, width = value.shape
    parts = []
    for half in range(width // COLS):
        buffer[half, 0:rows, :] = value[:, half * COLS : (half + 1) * COLS]
        parts.append(
            buffer[half, pl.ds(0, rows // 2, stride=2), :] + buffer[half, pl.ds(1, rows // 2, stride=2), :]
        )
    return parts[0] if len(parts) == 1 else jnp.concatenate(parts, axis=1)


def row_repeat(buffer, value):
    rows, width = value.shape
    parts = []
    for half in range(width // COLS):
        part = value[:, half * COLS : (half + 1) * COLS]
        buffer[half, pl.ds(0, rows, stride=2), :] = part
        buffer[half, pl.ds(1, rows, stride=2), :] = part
        parts.append(buffer[half, 0 : 2 * rows, :])
    return parts[0] if len(parts) == 1 else jnp.concatenate(parts, axis=1)


def column_pairs(value):
    row = lax.broadcasted_iota(jnp.int32, (WIDE, COLS), 0)
    column = lax.broadcasted_iota(jnp.int32, (WIDE, COLS), 1)
    matrix = jnp.where(row // 2 == column, 1.0, 0.0)
    return jnp.dot(value, matrix, precision=lax.Precision.HIGHEST, preferred_element_type=F32)


def column_repeat(value):
    row = lax.broadcasted_iota(jnp.int32, (COLS, WIDE), 0)
    column = lax.broadcasted_iota(jnp.int32, (COLS, WIDE), 1)
    matrix = jnp.where(column // 2 == row, 1.0, 0.0)
    return jnp.dot(value, matrix, precision=lax.Precision.HIGHEST, preferred_element_type=F32)


def half_rows(first, second, lower):
    row = sublanes(*first.shape)
    low = jnp.where(row < 4, first, pltpu.roll(second, 4, 0))
    high = jnp.where(row < 4, pltpu.roll(first, 4, 0), second)
    return jnp.where(lower, low, high)


def pick(table_row, index):
    rows, width = index.shape
    table = jnp.broadcast_to(table_row, (rows, COLS))
    parts = [
        jnp.take_along_axis(table, index[:, start : start + COLS], axis=1)
        for start in range(0, width, COLS)
    ]
    return parts[0] if len(parts) == 1 else jnp.concatenate(parts, axis=1)


def pack_halves(first, second):
    left = lanes(*first.shape) < HALF
    low = jnp.where(left, first, pltpu.roll(second, HALF, 1))
    high = jnp.where(left, pltpu.roll(first, HALF, 1), second)
    return low, high


def unpack_halves(from_right, from_left):
    left = lanes(*from_right.shape) < HALF
    first = jnp.where(left, from_right, pltpu.roll(from_left, HALF, 1))
    second = jnp.where(left, pltpu.roll(from_right, HALF, 1), from_left)
    return first, second


SPAN = 51
QUINTS = 9


def pack_quint(a, b, c, d, e):
    lane = lanes(*a.shape)
    lows = [
        jnp.where(lane < SPAN, x, jnp.where(lane < 2 * SPAN, pltpu.roll(y, SPAN, 1), pltpu.roll(e, shift, 1)))
        for x, y, shift in ((a, b, 102), (c, d, 76))
    ]
    highs = [
        jnp.where(
            lane >= COLS - SPAN,
            x,
            jnp.where(lane >= COLS - 2 * SPAN, pltpu.roll(y, COLS - SPAN, 1), pltpu.roll(e, COLS - shift, 1)),
        )
        for x, y, shift in ((a, b, 102), (c, d, 76))
    ]
    return lows, highs


def unpack_quint(from_right, from_left):
    lane = lanes(*from_right[0].shape)
    left = lane < HALF
    fields = []
    for right, other in zip(from_right, from_left):
        fields.append(jnp.where(left, right, other))
        fields.append(jnp.where(left, pltpu.roll(right, COLS - SPAN, 1), pltpu.roll(other, SPAN, 1)))
    parts = [
        jnp.where(left, pltpu.roll(right, COLS - shift, 1), pltpu.roll(other, shift, 1))
        for right, other, shift in zip(from_right, from_left, (102, 76))
    ]
    outer = (lane < COLS - 102) | (lane >= 102)
    fields.append(jnp.where(outer, parts[0], parts[1]))
    return fields


def pack_sea(fields):
    rows, width = fields[0].shape
    even_lane = lanes(rows, width) % 2 == 0
    even_row = sublanes(rows, width) % 2 == 0
    pairs = [
        jnp.where(even_lane, fields[i], pltpu.roll(fields[i + 1], 1, 1)) for i in (0, 2)
    ]
    return jnp.where(even_row, pairs[0], pltpu.roll(pairs[1], 1, 0))


def unpack_sea(packed):
    rows, width = packed.shape
    spot = (lanes(rows, width) % 2 == 0) & (sublanes(rows, width) % 2 == 0)
    fields = []
    for pair in (packed, pltpu.roll(packed, rows - 1, 0)):
        for field in (pair, pltpu.roll(pair, width - 1, 1)):
            fields.append(jnp.where(spot, field, 1.0))
    return fields


def fill_message(message, rhs, classes, sea, start, edge):
    def fields(z):
        for i in range(2):
            message[2 * z + i] = rhs(z, i)[pl.ds(start, 8), :]
        message[32 + z] = classes.at[z][pl.ds(start, 8), :]
        message.at[52 + z // 8][pl.ds(z % 8, 1), :] = classes.at[z][pl.ds(edge, 1), :]
        message.at[54 + z // 8][pl.ds(z % 8, 1), :] = sea.at[z][pl.ds(edge, 1), :]

    loop(NZ, fields)

    def quads(j):
        message[48 + j] = pack_sea([sea[4 * j + i, pl.ds(start, 8), :] for i in range(4)])

    loop(4, quads)


MSG_Y = 22
CORNER = 24
MSG_X = 56
R_TILES = 16
M_TILES = 24


def start_kernel(place, fields, to_left, to_right, message):
    core = place[0]
    classes, sea = fields.at[2], fields.at[3]

    def quint(k):
        lows, highs = pack_quint(*(fields[(5 * k + t) // NZ, (5 * k + t) % NZ] for t in range(5)))
        for t in range(2):
            to_left[2 * k + t] = lows[t]
            to_right[2 * k + t] = highs[t]

    loop(QUINTS, quint)
    rest = [classes[13], classes[14], classes[15]]
    rest += [pack_sea([sea[4 * q + i] for i in range(4)]) for q in range(4)]
    rest.append(rest[-1])
    for j in range(4):
        to_left[18 + j], to_right[18 + j] = pack_halves(rest[2 * j], rest[2 * j + 1])
    start = pl.multiple_of(8 * core, 8)
    fill_message(message, lambda z, i: fields.at[i, z], classes, sea, start, 8 - core)


def corner_kernel(message, after, to_left, to_right):
    def quint(k):
        lows, highs = pack_quint(*(message[5 * k + t] for t in range(5)))
        for t in range(2):
            to_left[2 * k + t] = lows[t]
            to_right[2 * k + t] = highs[t]

    loop(QUINTS, quint)
    for p in range(6):
        first = 45 + 2 * p
        to_left[18 + p], to_right[18 + p] = pack_halves(message[first], message[min(first + 1, MSG_X - 1)])


def valid_class(halo):
    return jnp.clip(halo, 0.0, 15.0)


def widen_kernel(message, corner_left, corner_right, wide):
    def quint(k):
        halos = unpack_quint(
            [corner_right[2 * k + t] for t in range(2)], [corner_left[2 * k + t] for t in range(2)]
        )
        for t, halo in enumerate(halos):
            wide[5 * k + t] = jnp.concatenate([message[5 * k + t], halo], axis=1)

    loop(QUINTS, quint)
    for j in range(32, 35):
        wide[j, :, COLS:] = valid_class(wide[j, :, COLS:])
    for p in range(6):
        first = 45 + 2 * p
        for i, halo in enumerate(unpack_halves(corner_right[18 + p], corner_left[18 + p])):
            if first + i < MSG_X:
                wide[first + i] = jnp.concatenate([message[first + i], halo], axis=1)


def rows_kernel(place, fields, from_left, from_right, r_out, c_out, s_out, message):
    core = place[0]
    gy = place[2]
    left = lanes(ROWS, COLS) < HALF
    inside = jnp.where(
        left,
        jnp.where(gy < place[4] - 1, 1.0, 0.0),
        jnp.where(gy > 0, 1.0, 0.0),
    )

    def group(k):
        return unpack_quint(
            [from_right[2 * k + t] for t in range(2)], [from_left[2 * k + t] for t in range(2)]
        )

    def put_rhs(f, halo):
        r_out[f % NZ, f // NZ] = jnp.concatenate([fields[f // NZ, f % NZ], halo], axis=1)

    def put_class(z, halo):
        c_out[z] = jnp.concatenate([fields[2, z], halo], axis=1)

    def rhs_step(k):
        for t, halo in enumerate(group(k)):
            put_rhs(5 * k + t, halo)

    loop(6, rhs_step)
    mixed = group(6)
    for t in range(2):
        put_rhs(30 + t, mixed[t])
    for t in range(3):
        put_class(t, valid_class(mixed[2 + t]))
    for k in (7, 8):
        for t, halo in enumerate(group(k)):
            put_class(5 * k + t - 32, halo)
    rest = []
    for j in range(4):
        rest += unpack_halves(from_right[18 + j], from_left[18 + j])
    for t in range(3):
        put_class(13 + t, rest[t])
    for q in range(4):
        for i, field in enumerate(unpack_sea(rest[3 + q])):
            s_out[4 * q + i] = jnp.concatenate([fields[3, 4 * q + i], field * inside], axis=1)
    start = pl.multiple_of(8 * (1 - core), 8)
    fill_message(message, lambda z, i: r_out.at[z, i], c_out, s_out, start, 7 + core)


def material_kernel(c_in, s_in, table, g_out, h_out, k_out, coarse, sums, buffer):
    def fields(z):
        index = c_in[z].astype(jnp.int32)
        sea = s_in[z]
        g = pick(table[0:1], index) * sea
        h = pick(table[1:2], index) * sea
        k = pick(table[2:3], index) * sea + (1.0 - sea)
        g_out[z] = g
        h_out[z] = h
        k_out[z] = k
        return 0.125 * g * g, 0.125 * h * h, k

    def step(pair):
        first = fields(2 * pair)
        second = fields(2 * pair + 1)
        for i in range(3):
            sums[8 * i + pair] = row_pairs(buffer.at[i], first[i] + second[i])

    loop(8, step)
    coarse[...] = column_pairs(sums[...].reshape(M_TILES * 8, WIDE)).reshape(M_TILES, 8, COLS)


class Level:
    def __init__(self, depth, step, g, h, inverse, diagonal=None):
        self.depth, self.step = depth, step
        self.g, self.h, self.inverse, self.diagonal = g, h, inverse, diagonal

    def couple(self, x, z, i):
        horizontal = self.g[z] * across(self.g[z] * x[z + 1, i], self.step)
        vertical = self.h[z + 1] * (self.h[z] * x[z, i] + self.h[z + 2] * x[z + 2, i])
        return horizontal + vertical

    def first(self, x, r, weight):
        def body(z):
            scaled = weight * self.inverse[z]
            for i in range(2):
                x[z + 1, i] = scaled * r[z, i]

        loop(self.depth, body)

    def update(self, new, x, r, weight):
        def body(z):
            scaled = weight * self.inverse[z]
            for i in range(2):
                new[z + 1, i] = (1.0 - weight) * x[z + 1, i] + scaled * (r[z, i] + self.couple(x, z, i))

        loop(self.depth, body)

    def defect(self, x, r, z, i):
        return r[z, i] - self.diagonal[z] * x[z + 1, i] + self.couple(x, z, i)

    def diagonal_of(self, k, z):
        horizontal = self.g[z] * across(self.g[z], self.step)
        vertical = self.h[z + 1] * (self.h[z] + self.h[z + 2])
        return k + horizontal + vertical


def clear_ends(*refs):
    for ref in refs:
        ref[0] = jnp.zeros(ref.shape[1:], ref.dtype)
        ref[ref.shape[0] - 1] = jnp.zeros(ref.shape[1:], ref.dtype)


def fine_restrict(level, x, r, sums, buffer, out):
    def body(pair):
        for i in range(2):
            total = level.defect(x, r, 2 * pair, i) + level.defect(x, r, 2 * pair + 1, i)
            sums[2 * pair + i] = row_pairs(buffer.at[i], total[8:24])

    loop(NZ // 2, body)
    out[...] = column_pairs(sums[...].reshape(R_TILES * 8, WIDE)).reshape(R_TILES, 8, COLS)


def down_kernel(
    place, r_own, g_own, h_own, k_own, from_x, wide, table,
    r, g, h, d, inverse, xp, r1, xa, ka, edges, sums, buffer,
):
    core = place[0]
    gx = place[1]
    gy = place[2]
    open_side = jnp.where((gx > 0) & (gx < place[3] - 1), 1.0, 0.0)
    lane = lanes(8, WIDE)
    ends = jnp.where(
        lane < COLS,
        1.0,
        jnp.where(lane < COLS + HALF, jnp.where(gy < place[4] - 1, 1.0, 0.0), jnp.where(gy > 0, 1.0, 0.0)),
    )
    clear_ends(h, xp, xa)

    def own(z):
        for i in range(2):
            r[z, i, 8:24, :] = r_own[z, i]
        g[z, 8:24, :] = g_own[z]
        h[z + 1, 8:24, :] = h_own[z]
        ka[z, 8:24, :] = k_own[z]

    loop(NZ, own)

    for message, start, scale, slot in ((from_x, 24 * (1 - core), 1.0, 1 - core), (wide, 24 * core, open_side, core)):
        start = pl.multiple_of(start, 8)
        valid = scale * ends

        def halo(j, message=message, start=start, valid=valid):
            for q, sea in enumerate(unpack_sea(message[48 + j])):
                z = 4 * j + q
                sea = sea * valid
                index = message[32 + z].astype(jnp.int32)
                g[z, pl.ds(start, 8), :] = pick(table[0:1], index) * sea
                h[z + 1, pl.ds(start, 8), :] = pick(table[1:2], index) * sea
                ka[z, pl.ds(start, 8), :] = pick(table[2:3], index) * sea + (1.0 - sea)
                for i in range(2):
                    r[z, i, pl.ds(start, 8), :] = message[2 * z + i]

        loop(4, halo)
        for j in range(2):
            index = message[52 + j].astype(jnp.int32)
            edges[slot, 8 * j : 8 * j + 8, :] = pick(table[0:1], index) * (message[54 + j] * valid)

    level = Level(NZ, 1, g, h, inverse, d)
    row = sublanes(EXT0, WIDE)

    def diagonals(z):
        here = g[z]
        below = jnp.where(row == 0, edges[0, pl.ds(z, 1), :], pltpu.roll(here, 1, 0))
        above = jnp.where(row == EXT0 - 1, edges[1, pl.ds(z, 1), :], pltpu.roll(here, EXT0 - 1, 0))
        beside = pltpu.roll(here, 1, 1) + pltpu.roll(here, WIDE - 1, 1)
        total = ka[z] + here * (below + above + beside) + h[z + 1] * (h[z] + h[z + 2])
        d[z] = total
        reciprocal = 1.0 / total
        inverse[z] = reciprocal
        for i in range(2):
            xa[z + 1, i] = (FINE[0] * reciprocal) * r[z, i]

    loop(NZ, diagonals)
    level.update(xp, xa, r, FINE[1])
    fine_restrict(level, xp, r, sums, buffer, r1)


def coarse_coefficients(place, pieces, g1, h1, d1, i1, g2, h2, i2, w1, k1, u1, k2, buffer):
    core = place[0]
    clear_ends(h1, h2)
    own, partner, odd, far = pieces
    low = jnp.where(place[1] >= 2, 1.0, 0.0)
    high = jnp.where(place[1] < place[3] - 2, 1.0, 0.0)
    near_side = jnp.where(core == 0, low, high)
    far_side = jnp.where(core == 0, high, low)
    scales = (1.0, 1.0, near_side, near_side, far_side)
    starts = (16, 24 - 16 * core, 8 + 16 * core, 32 * core, 32 - 32 * core)
    starts = [s if isinstance(s, int) else pl.multiple_of(s, 8) for s in starts]

    def assemble(z):
        for i, field in enumerate((w1, u1, k1)):
            j = 8 * i + z
            tiles = (own[j], partner[j], odd[j], odd[M_TILES + j], far[j])
            for start, tile, scale in zip(starts, tiles, scales):
                field[z, pl.ds(start, 8), :] = tile * scale if i < 2 else tile

    loop(8, assemble)

    def roots(z):
        g1[z] = 2.0 * jnp.sqrt(w1[z])
        h1[z + 1] = 2.0 * jnp.sqrt(u1[z])

    loop(8, roots)
    one = Level(8, 1, g1, h1, i1, d1)

    def diagonals(z):
        total = one.diagonal_of(k1[z], z)
        d1[z] = total
        i1[z] = 1.0 / total

    loop(8, diagonals)

    def coarser(z):
        sums = [
            lane_sum(row_pairs(buffer.at[i], field[2 * z] + field[2 * z + 1]), 1)
            for i, field in enumerate((w1, u1, k1))
        ]
        blank = jnp.zeros((4, COLS), F32)
        g2[z] = jnp.concatenate([2.0 * jnp.sqrt(0.125 * sums[0]), blank], axis=0)
        h2[z + 1] = jnp.concatenate([2.0 * jnp.sqrt(0.125 * sums[1]), blank], axis=0)
        k2[z] = jnp.concatenate([sums[2], blank + 1.0], axis=0)

    loop(4, coarser)
    two = Level(4, 2, g2, h2, i2)

    def diagonals_two(z):
        i2[z] = 1.0 / two.diagonal_of(k2[z], z)

    loop(4, diagonals_two)


def coarse_solve(core, one, two, pieces, far_tile, r1, xa1, xb1, r2, xa2, xb2, buffer):
    own, partner, odd, second = pieces
    clear_ends(xa1, xb1, xa2, xb2)
    starts = (16, 24 - 16 * core, 8 + 16 * core, 32 * core, 32 - 32 * core)
    starts = [s if isinstance(s, int) else pl.multiple_of(s, 8) for s in starts]

    def assemble(z):
        for i in range(2):
            j = 2 * z + i
            tiles = (own[j], partner[j], odd[j], far_tile(z, i), second[j])
            for start, tile in zip(starts, tiles):
                r1[z, i, pl.ds(start, 8), :] = tile

    loop(8, assemble)
    one.first(xa1, r1, FINE[0])
    one.update(xb1, xa1, r1, FINE[1])

    def restrict(z):
        for i in range(2):
            total = one.defect(xb1, r1, 2 * z, i) + one.defect(xb1, r1, 2 * z + 1, i)
            sums = lane_sum(row_pairs(buffer.at[i], total), 1)
            r2[z, i] = jnp.concatenate([sums, jnp.zeros((4, COLS), F32)], axis=0)

    loop(4, restrict)
    two.first(xa2, r2, COARSE[0])
    two.update(xb2, xa2, r2, COARSE[1])
    two.update(xa2, xb2, r2, COARSE[2])
    two.update(xb2, xa2, r2, COARSE[3])

    inner = [ref.at[:, :, 8:32, :] for ref in (xa1, xb1, r1)]
    inner_one = Level(8, 1, *(ref.at[:, 8:32, :] for ref in (one.g, one.h, one.inverse)))

    def prolong(z):
        for i in range(2):
            fine = row_repeat(buffer.at[i], xb2[z + 1, i, 4:16, :])
            for half in range(2):
                inner[0][2 * z + half + 1, i] = inner[1][2 * z + half + 1, i] + fine

    loop(4, prolong)
    inner_one.update(inner[1], inner[0], inner[2], FINE[0])
    inner_one.update(inner[0], inner[1], inner[2], FINE[1])


def fine_correct(level, out, xp, c1, wide, buffer):
    rows = c1[1:9, :, 12:28, :].reshape(R_TILES * 16, COLS)
    wide[...] = column_repeat(rows).reshape(R_TILES, 16, WIDE)

    def body(pair):
        for i in range(2):
            fine = row_repeat(buffer.at[i], wide[2 * pair + i])
            for half in range(2):
                out[2 * pair + half + 1, i] = xp[2 * pair + half + 1, i] + fine

    loop(NZ // 2, body)


def near_kernel(odd, near):
    near[...] = odd[0:R_TILES]


def far_half_kernel(place, partner, message):
    def pair(p):
        message[p] = half_rows(partner[2 * p], partner[2 * p + 1], place[0] == 0)

    loop(R_TILES // 2, pair)


def after_kernel(odd, after, near):
    near[...] = odd[0:M_TILES]


def coarse_kernel(
    place, own, partner, odd, far, g1, h1, d1, i1, g2, h2, i2, w1, k1, u1, k2, buffer
):
    coarse_coefficients(
        place, (own, partner, odd, far), g1, h1, d1, i1, g2, h2, i2, w1, k1, u1, k2, buffer
    )


def middle_kernel(
    place, r, g, h, d, inverse, xp, own, partner, odd, far, g1, h1, d1, i1, g2, h2, i2,
    z_out, xp_out, r1_out,
    xa, xb, r1, xa1, xb1, r2, xa2, xb2, wide, sums, buffer,
):
    core = place[0]
    zero = Level(NZ, 1, g, h, inverse, d)
    one = Level(8, 1, g1, h1, i1, d1)
    two = Level(4, 2, g2, h2, i2)
    coarse_solve(core, one, two, (own, partner, odd, far), lambda z, i: odd[R_TILES + 2 * z + i], r1, xa1, xb1, r2, xa2, xb2, buffer)
    clear_ends(xa, xb, xp_out)
    fine_correct(zero, xa, xp, xa1, wide, buffer)
    zero.update(xb, xa, r, FINE[0])

    def last(z):
        scaled = FINE[1] * inverse[z]
        first = FINE[0] * inverse[z]
        for i in range(2):
            value = (1.0 - FINE[1]) * xb[z + 1, i] + scaled * (r[z, i] + zero.couple(xb, z, i))
            z_out[z, i] = value
            xa[z + 1, i] = first * value

    loop(NZ, last)
    zero.update(xp_out, xa, z_out, FINE[1])
    fine_restrict(zero, xp_out, z_out, sums, buffer, r1_out)


def last_kernel(
    place, rhs, r, g, h, d, inverse, xp, own, partner, odd, far, g1, h1, d1, i1, g2, h2, i2,
    direction, image, sums,
    xa, xb, r1, xa1, xb1, r2, xa2, xb2, wide, totals, buffer,
):
    core = place[0]
    zero = Level(NZ, 1, g, h, inverse, d)
    one = Level(8, 1, g1, h1, i1, d1)
    two = Level(4, 2, g2, h2, i2)

    def far_tile(z, i):
        tile = odd[R_TILES + z]
        return jnp.where((core == 0) == (i == 0), pltpu.roll(tile, 4, 0), tile)

    coarse_solve(core, one, two, (own, partner, odd, far), far_tile, r1, xa1, xb1, r2, xa2, xb2, buffer)
    clear_ends(xa, xb)
    fine_correct(zero, xa, xp, xa1, wide, buffer)
    zero.update(xb, xa, r, FINE[0])
    zero.update(xa, xb, r, FINE[1])

    def first_image(z):
        for i in range(2):
            xb[z + 1, i] = d[z] * xa[z + 1, i] - zero.couple(xa, z, i)

    loop(NZ, first_image)
    totals[...] = jnp.zeros(totals.shape, F32)

    def second_image(z):
        for i in range(2):
            field = xa[z + 1, i, 8:24, 0:COLS]
            value = (d[z] * xb[z + 1, i] - zero.couple(xb, z, i))[8:24, 0:COLS]
            direction[i, z] = field
            image[i, z] = value
            totals[i] += rhs[i, z] * field
            totals[2 + i] += field * value

    loop(NZ, second_image)
    row = sublanes(8, COLS)
    lane = lanes(8, COLS)
    line = jnp.zeros((8, COLS), F32)
    for i in range(4):
        line = jnp.where(lane == i, jnp.sum(totals[i]), line)

    def spread(j):
        sums[pl.ds(pl.multiple_of(8 * j, 8), 8), :] = line

    loop(sums.shape[0] // 8, spread)


def scale_kernel(rhs, direction, image, sums, solution_field, residual):
    total = jnp.sum(sums[...], axis=0, keepdims=True)
    lane = lanes(1, COLS)
    parts = [jnp.sum(jnp.where(lane == i, total, 0.0), axis=1, keepdims=True) for i in range(4)]
    for i in range(2):
        alpha = parts[i] / parts[2 + i]

        def body(z, i=i, alpha=alpha):
            solution_field[i, z] = alpha * direction[i, z]
            residual[i, z] = rhs[i, z] - alpha * image[i, z]

        loop(NZ, body)


COSTS = {
    "start_kernel": 1,
    "corner_kernel": 1,
    "widen_kernel": 30,
    "rows_kernel": 1,
    "material_kernel": 1,
    "down_kernel": 4,
    "near_kernel": 30,
    "far_half_kernel": 1,
    "after_kernel": 30,
    "coarse_kernel": 1,
    "middle_kernel": 6,
    "last_kernel": 6,
    "scale_kernel": 1,
}


def call(kernel, operands, outs, scratch=(), place=True, far=None):
    far = far or {}
    vmem = pl.BlockSpec(memory_space=pltpu.VMEM)
    specs = [pl.BlockSpec(memory_space=far[i]) if i in far else vmem for i in range(len(operands))]
    if place:
        specs[0] = pl.BlockSpec(memory_space=pltpu.SMEM)
    return pl.pallas_call(
        kernel,
        out_shape=[jax.ShapeDtypeStruct(shape, F32) for shape in outs],
        in_specs=specs,
        out_specs=[vmem] * len(outs),
        scratch_shapes=[pltpu.VMEM(shape, F32) if isinstance(shape, tuple) else shape for shape in scratch],
        cost_estimate=pl.CostEstimate(
            flops=COSTS[kernel.__name__] * 1_000_000_000, bytes_accessed=COSTS[kernel.__name__] * 3_000_000, transcendentals=0
        ),
        compiler_params=pltpu.CompilerParams(vmem_limit_bytes=16 * 1024 * 1024),
    )(*operands)


FIELD0 = (NZ, 2, EXT0, WIDE)
PADDED0 = (NZ + 2, 2, EXT0, WIDE)
PADDED1 = (10, 2, EXT1, COLS)
PADDED2 = (6, 2, EXT2, COLS)
BUFFER = (3, 2, EXT1, COLS)
SUMS = (R_TILES, 8, WIDE)
SPREAD = (R_TILES, 16, WIDE)
COARSE_SCRATCH = [(8, 2, EXT1, COLS), PADDED1, PADDED1, (4, 2, EXT2, COLS), PADDED2, PADDED2, SPREAD]


def shards(count_x, count_y, right_side, classes, sea_mask, kappa_table, cross_table, vertical_table):
    gx = lax.axis_index("gx")
    gy = lax.axis_index("gy")
    place = jnp.stack([gx % 2, gx, gy, jnp.int32(count_x), jnp.int32(count_y)]).astype(jnp.int32)
    table = jnp.stack([jnp.sqrt(cross_table), jnp.sqrt(vertical_table), kappa_table])
    table = jnp.pad(table, ((0, 5), (0, COLS - table.shape[1])))

    pairs_on_chip = [(i, i ^ 1) for i in range(count_x)]
    pairs_across = [(i, (i + 1 if i % 2 else i - 1) % count_x) for i in range(count_x)]

    def on_chip(value):
        return lax.ppermute(value, "gx", pairs_on_chip)

    def across_chips(value):
        return lax.ppermute(value, "gx", pairs_across)

    def rows_of(own, partner, message):
        odd = across_chips(message)
        near = call(near_kernel, (odd,), [own.shape], place=False)[0]
        return own, partner, odd, on_chip(near)

    forward = [(i, (i + 1) % count_y) for i in range(count_y)]
    backward = [(target, source) for source, target in forward]

    def both_sides(to_left, to_right):
        return lax.ppermute(to_right, "gy", forward), lax.ppermute(to_left, "gy", backward)

    part = lax.broadcasted_iota(jnp.int32, (4, *classes.shape), 0)
    materials = jnp.where(part == 2, classes[None], sea_mask[None]).astype(F32)
    twice = jnp.broadcast_to(right_side[None], (2, *right_side.shape)).reshape(part.shape)
    fields = jnp.where(part < 2, twice, materials)
    to_left, to_right, msg_o = call(
        start_kernel, (place, fields), [(MSG_Y, ROWS, COLS), (MSG_Y, ROWS, COLS), (MSG_X, 8, COLS)]
    )
    from_o = across_chips(msg_o)
    from_left, from_right = both_sides(to_left, to_right)
    r_own, c_own, s_own, msg_x = call(
        rows_kernel,
        (place, fields, from_left, from_right),
        [(NZ, 2, ROWS, WIDE), (NZ, ROWS, WIDE), (NZ, ROWS, WIDE), (MSG_X, 8, WIDE)],
    )
    from_x = on_chip(msg_x)
    g_own, h_own, k_own, packed = call(
        material_kernel,
        (c_own, s_own, table),
        [(NZ, ROWS, WIDE)] * 3 + [(M_TILES, 8, COLS)],
        [(M_TILES, 8, WIDE), BUFFER],
        place=False,
    )
    corner_tiles = call(corner_kernel, (from_o, packed), [(CORNER, 8, COLS)] * 2, place=False, far={1: pl.ANY})
    wide = call(widen_kernel, (from_o, *both_sides(*corner_tiles)), [(MSG_X, 8, WIDE)], place=False)[0]
    packed_partner = on_chip(packed)
    packed_odd = across_chips(jnp.concatenate([packed, packed_partner], axis=0))
    r, g, h, d, inverse, xp, r1 = call(
        down_kernel,
        (place, r_own, g_own, h_own, k_own, from_x, wide, table),
        [FIELD0, (NZ, EXT0, WIDE), (NZ + 2, EXT0, WIDE), (NZ, EXT0, WIDE), (NZ, EXT0, WIDE), PADDED0, (R_TILES, 8, COLS)],
        [PADDED0, (NZ, EXT0, WIDE), (2, NZ, WIDE), SUMS, BUFFER],
    )
    partner = on_chip(r1)
    rows = rows_of(r1, partner, jnp.concatenate([r1, partner], axis=0))
    packed_near = call(
        after_kernel, (packed_odd, rows[1]), [packed.shape], place=False, far={1: pl.ANY}
    )[0]
    material = (packed, packed_partner, packed_odd, on_chip(packed_near))
    one = [(8, EXT1, COLS), (10, EXT1, COLS), (8, EXT1, COLS), (8, EXT1, COLS)]
    two = [(4, EXT2, COLS), (6, EXT2, COLS), (4, EXT2, COLS)]
    coarse = call(
        coarse_kernel, (place, *material), [*one, *two], [one[0], one[0], one[0], two[0], BUFFER]
    )
    r, xp, r1 = call(
        middle_kernel,
        (place, r, g, h, d, inverse, xp, *rows, *coarse),
        [FIELD0, PADDED0, (R_TILES, 8, COLS)],
        [PADDED0, PADDED0, *COARSE_SCRATCH, SUMS, BUFFER],
    )
    partner = on_chip(r1)
    halves = call(far_half_kernel, (place, partner), [(R_TILES // 2, 8, COLS)])[0]
    message = jnp.concatenate([r1, halves], axis=0)
    count = count_x * count_y
    direction, image, sums = call(
        last_kernel,
        (place, fields, r, g, h, d, inverse, xp, *rows_of(r1, partner, message), *coarse),
        [(2, NZ, ROWS, COLS)] * 2 + [(count, COLS)],
        [PADDED0, PADDED0, *COARSE_SCRATCH, (4, ROWS, COLS), BUFFER],
    )
    sums = lax.all_to_all(sums.reshape(count, 1, COLS), ("gx", "gy"), 0, 0).reshape(count, COLS)
    return tuple(
        call(
            scale_kernel,
            (fields, direction, image, sums),
            [(2, NZ, ROWS, COLS)] * 2,
            place=False,
        )
    )


def solution(mesh):
    return jax.shard_map(
        functools.partial(shards, mesh.shape["gx"], mesh.shape["gy"]),
        mesh=mesh,
        in_specs=(
            P(None, None, "gx", "gy"),
            P(None, "gx", "gy"),
            P(None, "gx", "gy"),
            P(),
            P(),
            P(),
        ),
        out_specs=(P(None, None, "gx", "gy"), P(None, None, "gx", "gy")),
        check_vma=False,
    )
```

```python
import functools
import math

import jax
import jax.numpy as jnp
from jax import lax
from jax.experimental import pallas as pl
from jax.experimental.pallas import tpu as pltpu
from jax.sharding import PartitionSpec as P

F32 = jnp.float32
NZ = 16
ROWS = 16
COLS = 128
WIDE = 256
HALF = 64
UNROLL = 8
EXT0 = 32
EXT1 = 40
EXT2 = 24


def cheb_weights(degree, lower_end, upper_end):
    middle = 0.5 * (upper_end + lower_end)
    radius = 0.5 * (upper_end - lower_end)
    return [
        1.0 / (middle + radius * math.cos(math.pi * (2 * index_k + 1) / (2 * degree)))
        for index_k in range(degree)
    ]


FINE = cheb_weights(2, 0.3, 2.0)
COARSE = cheb_weights(4, 0.1, 2.0)


def loop(count, body):
    def step(index, carry):
        body(index)
        return carry

    lax.fori_loop(0, count, step, 0, unroll=count if count < 2 * UNROLL else UNROLL)


def lanes(rows, width):
    return lax.broadcasted_iota(jnp.int32, (rows, width), 1)


def sublanes(rows, width):
    return lax.broadcasted_iota(jnp.int32, (rows, width), 0)


def lane_sum(value, step):
    width = value.shape[1]
    first = (lanes(*value.shape) // step) % 2 == 0
    return value + jnp.where(first, pltpu.roll(value, width - step, 1), pltpu.roll(value, step, 1))


def across(value, step):
    rows, width = value.shape
    return (
        pltpu.roll(value, 1, 0)
        + pltpu.roll(value, rows - 1, 0)
        + pltpu.roll(value, step, 1)
        + pltpu.roll(value, width - step, 1)
    )


def row_pairs(buffer, value):
    rows, width = value.shape
    parts = []
    for half in range(width // COLS):
        buffer[half, 0:rows, :] = value[:, half * COLS : (half + 1) * COLS]
        parts.append(
            buffer[half, pl.ds(0, rows // 2, stride=2), :] + buffer[half, pl.ds(1, rows // 2, stride=2), :]
        )
    return parts[0] if len(parts) == 1 else jnp.concatenate(parts, axis=1)


def row_repeat(buffer, value):
    rows, width = value.shape
    parts = []
    for half in range(width // COLS):
        part = value[:, half * COLS : (half + 1) * COLS]
        buffer[half, pl.ds(0, rows, stride=2), :] = part
        buffer[half, pl.ds(1, rows, stride=2), :] = part
        parts.append(buffer[half, 0 : 2 * rows, :])
    return parts[0] if len(parts) == 1 else jnp.concatenate(parts, axis=1)


def column_pairs(value):
    row = lax.broadcasted_iota(jnp.int32, (WIDE, COLS), 0)
    column = lax.broadcasted_iota(jnp.int32, (WIDE, COLS), 1)
    matrix = jnp.where(row // 2 == column, 1.0, 0.0)
    return jnp.dot(value, matrix, precision=lax.Precision.HIGHEST, preferred_element_type=F32)


def column_repeat(value):
    row = lax.broadcasted_iota(jnp.int32, (COLS, WIDE), 0)
    column = lax.broadcasted_iota(jnp.int32, (COLS, WIDE), 1)
    matrix = jnp.where(column // 2 == row, 1.0, 0.0)
    return jnp.dot(value, matrix, precision=lax.Precision.HIGHEST, preferred_element_type=F32)


def half_rows(first, second, lower):
    row = sublanes(*first.shape)
    low = jnp.where(row < 4, first, pltpu.roll(second, 4, 0))
    high = jnp.where(row < 4, pltpu.roll(first, 4, 0), second)
    return jnp.where(lower, low, high)


def pick(table_row, index):
    rows, width = index.shape
    table = jnp.broadcast_to(table_row, (rows, COLS))
    parts = [
        jnp.take_along_axis(table, index[:, start : start + COLS], axis=1)
        for start in range(0, width, COLS)
    ]
    return parts[0] if len(parts) == 1 else jnp.concatenate(parts, axis=1)


def pack_halves(first, second):
    left = lanes(*first.shape) < HALF
    low = jnp.where(left, first, pltpu.roll(second, HALF, 1))
    high = jnp.where(left, pltpu.roll(first, HALF, 1), second)
    return low, high


def unpack_halves(from_right, from_left):
    left = lanes(*from_right.shape) < HALF
    first = jnp.where(left, from_right, pltpu.roll(from_left, HALF, 1))
    second = jnp.where(left, pltpu.roll(from_right, HALF, 1), from_left)
    return first, second


SPAN = 51
QUINTS = 9


def pack_quint(a, b, c, d, e):
    lane = lanes(*a.shape)
    lows = [
        jnp.where(lane < SPAN, x, jnp.where(lane < 2 * SPAN, pltpu.roll(y, SPAN, 1), pltpu.roll(e, shift, 1)))
        for x, y, shift in ((a, b, 102), (c, d, 76))
    ]
    highs = [
        jnp.where(
            lane >= COLS - SPAN,
            x,
            jnp.where(lane >= COLS - 2 * SPAN, pltpu.roll(y, COLS - SPAN, 1), pltpu.roll(e, COLS - shift, 1)),
        )
        for x, y, shift in ((a, b, 102), (c, d, 76))
    ]
    return lows, highs


def unpack_quint(from_right, from_left):
    lane = lanes(*from_right[0].shape)
    left = lane < HALF
    fields = []
    for right, other in zip(from_right, from_left):
        fields.append(jnp.where(left, right, other))
        fields.append(jnp.where(left, pltpu.roll(right, COLS - SPAN, 1), pltpu.roll(other, SPAN, 1)))
    parts = [
        jnp.where(left, pltpu.roll(right, COLS - shift, 1), pltpu.roll(other, shift, 1))
        for right, other, shift in zip(from_right, from_left, (102, 76))
    ]
    outer = (lane < COLS - 102) | (lane >= 102)
    fields.append(jnp.where(outer, parts[0], parts[1]))
    return fields


def pack_sea(fields):
    rows, width = fields[0].shape
    even_lane = lanes(rows, width) % 2 == 0
    even_row = sublanes(rows, width) % 2 == 0
    pairs = [
        jnp.where(even_lane, fields[i], pltpu.roll(fields[i + 1], 1, 1)) for i in (0, 2)
    ]
    return jnp.where(even_row, pairs[0], pltpu.roll(pairs[1], 1, 0))


def unpack_sea(packed):
    rows, width = packed.shape
    spot = (lanes(rows, width) % 2 == 0) & (sublanes(rows, width) % 2 == 0)
    fields = []
    for pair in (packed, pltpu.roll(packed, rows - 1, 0)):
        for field in (pair, pltpu.roll(pair, width - 1, 1)):
            fields.append(jnp.where(spot, field, 1.0))
    return fields


def fill_message(message, rhs, classes, sea, start, edge):
    def fields(z):
        for i in range(2):
            message[2 * z + i] = rhs(z, i)[pl.ds(start, 8), :]
        message[32 + z] = classes.at[z][pl.ds(start, 8), :]
        message.at[52 + z // 8][pl.ds(z % 8, 1), :] = classes.at[z][pl.ds(edge, 1), :]
        message.at[54 + z // 8][pl.ds(z % 8, 1), :] = sea.at[z][pl.ds(edge, 1), :]

    loop(NZ, fields)

    def quads(j):
        message[48 + j] = pack_sea([sea[4 * j + i, pl.ds(start, 8), :] for i in range(4)])

    loop(4, quads)


MSG_Y = 22
CORNER = 24
MSG_X = 56
R_TILES = 16
M_TILES = 24


def start_kernel(place, fields, to_left, to_right, message):
    core = place[0]
    classes, sea = fields.at[2], fields.at[3]

    def quint(k):
        lows, highs = pack_quint(*(fields[(5 * k + t) // NZ, (5 * k + t) % NZ] for t in range(5)))
        for t in range(2):
            to_left[2 * k + t] = lows[t]
            to_right[2 * k + t] = highs[t]

    loop(QUINTS, quint)
    rest = [classes[13], classes[14], classes[15]]
    rest += [pack_sea([sea[4 * q + i] for i in range(4)]) for q in range(4)]
    rest.append(rest[-1])
    for j in range(4):
        to_left[18 + j], to_right[18 + j] = pack_halves(rest[2 * j], rest[2 * j + 1])
    start = pl.multiple_of(8 * core, 8)
    fill_message(message, lambda z, i: fields.at[i, z], classes, sea, start, 8 - core)


def corner_kernel(message, after, to_left, to_right):
    def quint(k):
        lows, highs = pack_quint(*(message[5 * k + t] for t in range(5)))
        for t in range(2):
            to_left[2 * k + t] = lows[t]
            to_right[2 * k + t] = highs[t]

    loop(QUINTS, quint)
    for p in range(6):
        first = 45 + 2 * p
        to_left[18 + p], to_right[18 + p] = pack_halves(message[first], message[min(first + 1, MSG_X - 1)])


def valid_class(halo):
    return jnp.clip(halo, 0.0, 15.0)


def widen_kernel(message, corner_left, corner_right, wide):
    def quint(k):
        halos = unpack_quint(
            [corner_right[2 * k + t] for t in range(2)], [corner_left[2 * k + t] for t in range(2)]
        )
        for t, halo in enumerate(halos):
            wide[5 * k + t] = jnp.concatenate([message[5 * k + t], halo], axis=1)

    loop(QUINTS, quint)
    for j in range(32, 35):
        wide[j, :, COLS:] = valid_class(wide[j, :, COLS:])
    for p in range(6):
        first = 45 + 2 * p
        for i, halo in enumerate(unpack_halves(corner_right[18 + p], corner_left[18 + p])):
            if first + i < MSG_X:
                wide[first + i] = jnp.concatenate([message[first + i], halo], axis=1)


def rows_kernel(place, fields, from_left, from_right, r_out, c_out, s_out, message):
    core = place[0]
    gy = place[2]
    left = lanes(ROWS, COLS) < HALF
    inside = jnp.where(
        left,
        jnp.where(gy < place[4] - 1, 1.0, 0.0),
        jnp.where(gy > 0, 1.0, 0.0),
    )

    def group(k):
        return unpack_quint(
            [from_right[2 * k + t] for t in range(2)], [from_left[2 * k + t] for t in range(2)]
        )

    def put_rhs(f, halo):
        r_out[f % NZ, f // NZ] = jnp.concatenate([fields[f // NZ, f % NZ], halo], axis=1)

    def put_class(z, halo):
        c_out[z] = jnp.concatenate([fields[2, z], halo], axis=1)

    def rhs_step(k):
        for t, halo in enumerate(group(k)):
            put_rhs(5 * k + t, halo)

    loop(6, rhs_step)
    mixed = group(6)
    for t in range(2):
        put_rhs(30 + t, mixed[t])
    for t in range(3):
        put_class(t, valid_class(mixed[2 + t]))
    for k in (7, 8):
        for t, halo in enumerate(group(k)):
            put_class(5 * k + t - 32, halo)
    rest = []
    for j in range(4):
        rest += unpack_halves(from_right[18 + j], from_left[18 + j])
    for t in range(3):
        put_class(13 + t, rest[t])
    for q in range(4):
        for i, field in enumerate(unpack_sea(rest[3 + q])):
            s_out[4 * q + i] = jnp.concatenate([fields[3, 4 * q + i], field * inside], axis=1)
    start = pl.multiple_of(8 * (1 - core), 8)
    fill_message(message, lambda z, i: r_out.at[z, i], c_out, s_out, start, 7 + core)


def material_kernel(c_in, s_in, table, g_out, h_out, k_out, coarse, sums, buffer):
    def fields(z):
        index = c_in[z].astype(jnp.int32)
        sea = s_in[z]
        g = pick(table[0:1], index) * sea
        h = pick(table[1:2], index) * sea
        k = pick(table[2:3], index) * sea + (1.0 - sea)
        g_out[z] = g
        h_out[z] = h
        k_out[z] = k
        return 0.125 * g * g, 0.125 * h * h, k

    def step(pair):
        first = fields(2 * pair)
        second = fields(2 * pair + 1)
        for i in range(3):
            sums[8 * i + pair] = row_pairs(buffer.at[i], first[i] + second[i])

    loop(8, step)
    coarse[...] = column_pairs(sums[...].reshape(M_TILES * 8, WIDE)).reshape(M_TILES, 8, COLS)


class Level:
    def __init__(self, depth, step, g, h, inverse, diagonal=None):
        self.depth, self.step = depth, step
        self.g, self.h, self.inverse, self.diagonal = g, h, inverse, diagonal

    def couple(self, x, z, i):
        horizontal = self.g[z] * across(self.g[z] * x[z + 1, i], self.step)
        vertical = self.h[z + 1] * (self.h[z] * x[z, i] + self.h[z + 2] * x[z + 2, i])
        return horizontal + vertical

    def first(self, x, r, weight):
        def body(z):
            scaled = weight * self.inverse[z]
            for i in range(2):
                x[z + 1, i] = scaled * r[z, i]

        loop(self.depth, body)

    def update(self, new, x, r, weight):
        def body(z):
            scaled = weight * self.inverse[z]
            for i in range(2):
                new[z + 1, i] = (1.0 - weight) * x[z + 1, i] + scaled * (r[z, i] + self.couple(x, z, i))

        loop(self.depth, body)

    def defect(self, x, r, z, i):
        return r[z, i] - self.diagonal[z] * x[z + 1, i] + self.couple(x, z, i)

    def diagonal_of(self, k, z):
        horizontal = self.g[z] * across(self.g[z], self.step)
        vertical = self.h[z + 1] * (self.h[z] + self.h[z + 2])
        return k + horizontal + vertical


def clear_ends(*refs):
    for ref in refs:
        ref[0] = jnp.zeros(ref.shape[1:], ref.dtype)
        ref[ref.shape[0] - 1] = jnp.zeros(ref.shape[1:], ref.dtype)


def fine_restrict(level, x, r, sums, buffer, out):
    def body(pair):
        for i in range(2):
            total = level.defect(x, r, 2 * pair, i) + level.defect(x, r, 2 * pair + 1, i)
            sums[2 * pair + i] = row_pairs(buffer.at[i], total[8:24])

    loop(NZ // 2, body)
    out[...] = column_pairs(sums[...].reshape(R_TILES * 8, WIDE)).reshape(R_TILES, 8, COLS)


def down_kernel(
    place, r_own, g_own, h_own, k_own, from_x, wide, table,
    r, g, h, d, inverse, xp, r1, xa, ka, edges, sums, buffer,
):
    core = place[0]
    gx = place[1]
    gy = place[2]
    open_side = jnp.where((gx > 0) & (gx < place[3] - 1), 1.0, 0.0)
    lane = lanes(8, WIDE)
    ends = jnp.where(
        lane < COLS,
        1.0,
        jnp.where(lane < COLS + HALF, jnp.where(gy < place[4] - 1, 1.0, 0.0), jnp.where(gy > 0, 1.0, 0.0)),
    )
    clear_ends(h, xp, xa)

    def own(z):
        for i in range(2):
            r[z, i, 8:24, :] = r_own[z, i]
        g[z, 8:24, :] = g_own[z]
        h[z + 1, 8:24, :] = h_own[z]
        ka[z, 8:24, :] = k_own[z]

    loop(NZ, own)

    for message, start, scale, slot in ((from_x, 24 * (1 - core), 1.0, 1 - core), (wide, 24 * core, open_side, core)):
        start = pl.multiple_of(start, 8)
        valid = scale * ends

        def halo(j, message=message, start=start, valid=valid):
            for q, sea in enumerate(unpack_sea(message[48 + j])):
                z = 4 * j + q
                sea = sea * valid
                index = message[32 + z].astype(jnp.int32)
                g[z, pl.ds(start, 8), :] = pick(table[0:1], index) * sea
                h[z + 1, pl.ds(start, 8), :] = pick(table[1:2], index) * sea
                ka[z, pl.ds(start, 8), :] = pick(table[2:3], index) * sea + (1.0 - sea)
                for i in range(2):
                    r[z, i, pl.ds(start, 8), :] = message[2 * z + i]

        loop(4, halo)
        for j in range(2):
            index = message[52 + j].astype(jnp.int32)
            edges[slot, 8 * j : 8 * j + 8, :] = pick(table[0:1], index) * (message[54 + j] * valid)

    level = Level(NZ, 1, g, h, inverse, d)
    row = sublanes(EXT0, WIDE)

    def diagonals(z):
        here = g[z]
        below = jnp.where(row == 0, edges[0, pl.ds(z, 1), :], pltpu.roll(here, 1, 0))
        above = jnp.where(row == EXT0 - 1, edges[1, pl.ds(z, 1), :], pltpu.roll(here, EXT0 - 1, 0))
        beside = pltpu.roll(here, 1, 1) + pltpu.roll(here, WIDE - 1, 1)
        total = ka[z] + here * (below + above + beside) + h[z + 1] * (h[z] + h[z + 2])
        d[z] = total
        reciprocal = 1.0 / total
        inverse[z] = reciprocal
        for i in range(2):
            xa[z + 1, i] = (FINE[0] * reciprocal) * r[z, i]

    loop(NZ, diagonals)
    level.update(xp, xa, r, FINE[1])
    fine_restrict(level, xp, r, sums, buffer, r1)


def coarse_coefficients(place, pieces, g1, h1, d1, i1, g2, h2, i2, w1, k1, u1, k2, buffer):
    core = place[0]
    clear_ends(h1, h2)
    own, partner, odd, far = pieces
    low = jnp.where(place[1] >= 2, 1.0, 0.0)
    high = jnp.where(place[1] < place[3] - 2, 1.0, 0.0)
    near_side = jnp.where(core == 0, low, high)
    far_side = jnp.where(core == 0, high, low)
    scales = (1.0, 1.0, near_side, near_side, far_side)
    starts = (16, 24 - 16 * core, 8 + 16 * core, 32 * core, 32 - 32 * core)
    starts = [s if isinstance(s, int) else pl.multiple_of(s, 8) for s in starts]

    def assemble(z):
        for i, field in enumerate((w1, u1, k1)):
            j = 8 * i + z
            tiles = (own[j], partner[j], odd[j], odd[M_TILES + j], far[j])
            for start, tile, scale in zip(starts, tiles, scales):
                field[z, pl.ds(start, 8), :] = tile * scale if i < 2 else tile

    loop(8, assemble)

    def roots(z):
        g1[z] = 2.0 * jnp.sqrt(w1[z])
        h1[z + 1] = 2.0 * jnp.sqrt(u1[z])

    loop(8, roots)
    one = Level(8, 1, g1, h1, i1, d1)

    def diagonals(z):
        total = one.diagonal_of(k1[z], z)
        d1[z] = total
        i1[z] = 1.0 / total

    loop(8, diagonals)

    def coarser(z):
        sums = [
            lane_sum(row_pairs(buffer.at[i], field[2 * z] + field[2 * z + 1]), 1)
            for i, field in enumerate((w1, u1, k1))
        ]
        blank = jnp.zeros((4, COLS), F32)
        g2[z] = jnp.concatenate([2.0 * jnp.sqrt(0.125 * sums[0]), blank], axis=0)
        h2[z + 1] = jnp.concatenate([2.0 * jnp.sqrt(0.125 * sums[1]), blank], axis=0)
        k2[z] = jnp.concatenate([sums[2], blank + 1.0], axis=0)

    loop(4, coarser)
    two = Level(4, 2, g2, h2, i2)

    def diagonals_two(z):
        i2[z] = 1.0 / two.diagonal_of(k2[z], z)

    loop(4, diagonals_two)


def coarse_solve(core, one, two, pieces, far_tile, r1, xa1, xb1, r2, xa2, xb2, buffer):
    own, partner, odd, second = pieces
    clear_ends(xa1, xb1, xa2, xb2)
    starts = (16, 24 - 16 * core, 8 + 16 * core, 32 * core, 32 - 32 * core)
    starts = [s if isinstance(s, int) else pl.multiple_of(s, 8) for s in starts]

    def assemble(z):
        for i in range(2):
            j = 2 * z + i
            tiles = (own[j], partner[j], odd[j], far_tile(z, i), second[j])
            for start, tile in zip(starts, tiles):
                r1[z, i, pl.ds(start, 8), :] = tile

    loop(8, assemble)
    one.first(xa1, r1, FINE[0])
    one.update(xb1, xa1, r1, FINE[1])

    def restrict(z):
        for i in range(2):
            total = one.defect(xb1, r1, 2 * z, i) + one.defect(xb1, r1, 2 * z + 1, i)
            sums = lane_sum(row_pairs(buffer.at[i], total), 1)
            r2[z, i] = jnp.concatenate([sums, jnp.zeros((4, COLS), F32)], axis=0)

    loop(4, restrict)
    two.first(xa2, r2, COARSE[0])
    two.update(xb2, xa2, r2, COARSE[1])
    two.update(xa2, xb2, r2, COARSE[2])
    two.update(xb2, xa2, r2, COARSE[3])

    inner = [ref.at[:, :, 8:32, :] for ref in (xa1, xb1, r1)]
    inner_one = Level(8, 1, *(ref.at[:, 8:32, :] for ref in (one.g, one.h, one.inverse)))

    def prolong(z):
        for i in range(2):
            fine = row_repeat(buffer.at[i], xb2[z + 1, i, 4:16, :])
            for half in range(2):
                inner[0][2 * z + half + 1, i] = inner[1][2 * z + half + 1, i] + fine

    loop(4, prolong)
    inner_one.update(inner[1], inner[0], inner[2], FINE[0])
    inner_one.update(inner[0], inner[1], inner[2], FINE[1])


def fine_correct(level, out, xp, c1, wide, buffer):
    rows = c1[1:9, :, 12:28, :].reshape(R_TILES * 16, COLS)
    wide[...] = column_repeat(rows).reshape(R_TILES, 16, WIDE)

    def body(pair):
        for i in range(2):
            fine = row_repeat(buffer.at[i], wide[2 * pair + i])
            for half in range(2):
                out[2 * pair + half + 1, i] = xp[2 * pair + half + 1, i] + fine

    loop(NZ // 2, body)


def near_kernel(odd, near):
    near[...] = odd[0:R_TILES]


def far_half_kernel(place, partner, message):
    def pair(p):
        message[p] = half_rows(partner[2 * p], partner[2 * p + 1], place[0] == 0)

    loop(R_TILES // 2, pair)


def after_kernel(odd, after, near):
    near[...] = odd[0:M_TILES]


def coarse_kernel(
    place, own, partner, odd, far, g1, h1, d1, i1, g2, h2, i2, w1, k1, u1, k2, buffer
):
    coarse_coefficients(
        place, (own, partner, odd, far), g1, h1, d1, i1, g2, h2, i2, w1, k1, u1, k2, buffer
    )


def middle_kernel(
    place, r, g, h, d, inverse, xp, own, partner, odd, far, g1, h1, d1, i1, g2, h2, i2,
    z_out, xp_out, r1_out,
    xa, xb, r1, xa1, xb1, r2, xa2, xb2, wide, sums, buffer,
):
    core = place[0]
    zero = Level(NZ, 1, g, h, inverse, d)
    one = Level(8, 1, g1, h1, i1, d1)
    two = Level(4, 2, g2, h2, i2)
    coarse_solve(core, one, two, (own, partner, odd, far), lambda z, i: odd[R_TILES + 2 * z + i], r1, xa1, xb1, r2, xa2, xb2, buffer)
    clear_ends(xa, xb, xp_out)
    fine_correct(zero, xa, xp, xa1, wide, buffer)
    zero.update(xb, xa, r, FINE[0])

    def last(z):
        scaled = FINE[1] * inverse[z]
        first = FINE[0] * inverse[z]
        for i in range(2):
            value = (1.0 - FINE[1]) * xb[z + 1, i] + scaled * (r[z, i] + zero.couple(xb, z, i))
            z_out[z, i] = value
            xa[z + 1, i] = first * value

    loop(NZ, last)
    zero.update(xp_out, xa, z_out, FINE[1])
    fine_restrict(zero, xp_out, z_out, sums, buffer, r1_out)


def last_kernel(
    place, rhs, r, g, h, d, inverse, xp, own, partner, odd, far, g1, h1, d1, i1, g2, h2, i2,
    direction, image, sums,
    xa, xb, r1, xa1, xb1, r2, xa2, xb2, wide, totals, buffer,
):
    core = place[0]
    zero = Level(NZ, 1, g, h, inverse, d)
    one = Level(8, 1, g1, h1, i1, d1)
    two = Level(4, 2, g2, h2, i2)

    def far_tile(z, i):
        tile = odd[R_TILES + z]
        return jnp.where((core == 0) == (i == 0), pltpu.roll(tile, 4, 0), tile)

    coarse_solve(core, one, two, (own, partner, odd, far), far_tile, r1, xa1, xb1, r2, xa2, xb2, buffer)
    clear_ends(xa, xb)
    fine_correct(zero, xa, xp, xa1, wide, buffer)
    zero.update(xb, xa, r, FINE[0])
    zero.update(xa, xb, r, FINE[1])

    def first_image(z):
        for i in range(2):
            xb[z + 1, i] = d[z] * xa[z + 1, i] - zero.couple(xa, z, i)

    loop(NZ, first_image)
    totals[...] = jnp.zeros(totals.shape, F32)

    def second_image(z):
        for i in range(2):
            field = xa[z + 1, i, 8:24, 0:COLS]
            value = (d[z] * xb[z + 1, i] - zero.couple(xb, z, i))[8:24, 0:COLS]
            direction[i, z] = field
            image[i, z] = value
            totals[i] += rhs[i, z] * field
            totals[2 + i] += field * value

    loop(NZ, second_image)
    row = sublanes(8, COLS)
    lane = lanes(8, COLS)
    line = jnp.zeros((8, COLS), F32)
    for i in range(4):
        line = jnp.where(lane == i, jnp.sum(totals[i]), line)

    def spread(j):
        sums[pl.ds(pl.multiple_of(8 * j, 8), 8), :] = line

    loop(sums.shape[0] // 8, spread)


def scale_kernel(rhs, direction, image, sums, solution_field, residual):
    total = jnp.sum(sums[...], axis=0, keepdims=True)
    lane = lanes(1, COLS)
    parts = [jnp.sum(jnp.where(lane == i, total, 0.0), axis=1, keepdims=True) for i in range(4)]
    for i in range(2):
        alpha = parts[i] / parts[2 + i]

        def body(z, i=i, alpha=alpha):
            solution_field[i, z] = alpha * direction[i, z]
            residual[i, z] = rhs[i, z] - alpha * image[i, z]

        loop(NZ, body)


COSTS = {
    "start_kernel": 1,
    "corner_kernel": 1,
    "widen_kernel": 30,
    "rows_kernel": 1,
    "material_kernel": 1,
    "down_kernel": 4,
    "near_kernel": 30,
    "far_half_kernel": 1,
    "after_kernel": 30,
    "coarse_kernel": 1,
    "middle_kernel": 6,
    "last_kernel": 6,
    "scale_kernel": 1,
}


def call(kernel, operands, outs, scratch=(), place=True, far=None):
    far = far or {}
    vmem = pl.BlockSpec(memory_space=pltpu.VMEM)
    specs = [pl.BlockSpec(memory_space=far[i]) if i in far else vmem for i in range(len(operands))]
    if place:
        specs[0] = pl.BlockSpec(memory_space=pltpu.SMEM)
    return pl.pallas_call(
        kernel,
        out_shape=[jax.ShapeDtypeStruct(shape, F32) for shape in outs],
        in_specs=specs,
        out_specs=[vmem] * len(outs),
        scratch_shapes=[pltpu.VMEM(shape, F32) if isinstance(shape, tuple) else shape for shape in scratch],
        cost_estimate=pl.CostEstimate(
            flops=COSTS[kernel.__name__] * 1_000_000_000, bytes_accessed=COSTS[kernel.__name__] * 3_000_000, transcendentals=0
        ),
        compiler_params=pltpu.CompilerParams(vmem_limit_bytes=16 * 1024 * 1024),
    )(*operands)


FIELD0 = (NZ, 2, EXT0, WIDE)
PADDED0 = (NZ + 2, 2, EXT0, WIDE)
PADDED1 = (10, 2, EXT1, COLS)
PADDED2 = (6, 2, EXT2, COLS)
BUFFER = (3, 2, EXT1, COLS)
SUMS = (R_TILES, 8, WIDE)
SPREAD = (R_TILES, 16, WIDE)
COARSE_SCRATCH = [(8, 2, EXT1, COLS), PADDED1, PADDED1, (4, 2, EXT2, COLS), PADDED2, PADDED2, SPREAD]


def shards(count_x, count_y, right_side, classes, sea_mask, kappa_table, cross_table, vertical_table):
    gx = lax.axis_index("gx")
    gy = lax.axis_index("gy")
    place = jnp.stack([gx % 2, gx, gy, jnp.int32(count_x), jnp.int32(count_y)]).astype(jnp.int32)
    table = jnp.stack([jnp.sqrt(cross_table), jnp.sqrt(vertical_table), kappa_table])
    table = jnp.pad(table, ((0, 5), (0, COLS - table.shape[1])))

    pairs_on_chip = [(i, i ^ 1) for i in range(count_x)]
    pairs_across = [(i, (i + 1 if i % 2 else i - 1) % count_x) for i in range(count_x)]

    def on_chip(value):
        return lax.ppermute(value, "gx", pairs_on_chip)

    def across_chips(value):
        return lax.ppermute(value, "gx", pairs_across)

    def rows_of(own, partner, message):
        odd = across_chips(message)
        near = call(near_kernel, (odd,), [own.shape], place=False)[0]
        return own, partner, odd, on_chip(near)

    forward = [(i, (i + 1) % count_y) for i in range(count_y)]
    backward = [(target, source) for source, target in forward]

    def both_sides(to_left, to_right):
        return lax.ppermute(to_right, "gy", forward), lax.ppermute(to_left, "gy", backward)

    part = lax.broadcasted_iota(jnp.int32, (4, *classes.shape), 0)
    materials = jnp.where(part == 2, classes[None], sea_mask[None]).astype(F32)
    twice = jnp.broadcast_to(right_side[None], (2, *right_side.shape)).reshape(part.shape)
    fields = jnp.where(part < 2, twice, materials)
    to_left, to_right, msg_o = call(
        start_kernel, (place, fields), [(MSG_Y, ROWS, COLS), (MSG_Y, ROWS, COLS), (MSG_X, 8, COLS)]
    )
    from_o = across_chips(msg_o)
    from_left, from_right = both_sides(to_left, to_right)
    r_own, c_own, s_own, msg_x = call(
        rows_kernel,
        (place, fields, from_left, from_right),
        [(NZ, 2, ROWS, WIDE), (NZ, ROWS, WIDE), (NZ, ROWS, WIDE), (MSG_X, 8, WIDE)],
    )
    from_x = on_chip(msg_x)
    g_own, h_own, k_own, packed = call(
        material_kernel,
        (c_own, s_own, table),
        [(NZ, ROWS, WIDE)] * 3 + [(M_TILES, 8, COLS)],
        [(M_TILES, 8, WIDE), BUFFER],
        place=False,
    )
    corner_tiles = call(corner_kernel, (from_o, packed), [(CORNER, 8, COLS)] * 2, place=False, far={1: pl.ANY})
    wide = call(widen_kernel, (from_o, *both_sides(*corner_tiles)), [(MSG_X, 8, WIDE)], place=False)[0]
    packed_partner = on_chip(packed)
    packed_odd = across_chips(jnp.concatenate([packed, packed_partner], axis=0))
    r, g, h, d, inverse, xp, r1 = call(
        down_kernel,
        (place, r_own, g_own, h_own, k_own, from_x, wide, table),
        [FIELD0, (NZ, EXT0, WIDE), (NZ + 2, EXT0, WIDE), (NZ, EXT0, WIDE), (NZ, EXT0, WIDE), PADDED0, (R_TILES, 8, COLS)],
        [PADDED0, (NZ, EXT0, WIDE), (2, NZ, WIDE), SUMS, BUFFER],
    )
    partner = on_chip(r1)
    rows = rows_of(r1, partner, jnp.concatenate([r1, partner], axis=0))
    packed_near = call(
        after_kernel, (packed_odd, rows[1]), [packed.shape], place=False, far={1: pl.ANY}
    )[0]
    material = (packed, packed_partner, packed_odd, on_chip(packed_near))
    one = [(8, EXT1, COLS), (10, EXT1, COLS), (8, EXT1, COLS), (8, EXT1, COLS)]
    two = [(4, EXT2, COLS), (6, EXT2, COLS), (4, EXT2, COLS)]
    coarse = call(
        coarse_kernel, (place, *material), [*one, *two], [one[0], one[0], one[0], two[0], BUFFER]
    )
    r, xp, r1 = call(
        middle_kernel,
        (place, r, g, h, d, inverse, xp, *rows, *coarse),
        [FIELD0, PADDED0, (R_TILES, 8, COLS)],
        [PADDED0, PADDED0, *COARSE_SCRATCH, SUMS, BUFFER],
    )
    partner = on_chip(r1)
    halves = call(far_half_kernel, (place, partner), [(R_TILES // 2, 8, COLS)])[0]
    message = jnp.concatenate([r1, halves], axis=0)
    count = count_x * count_y
    direction, image, sums = call(
        last_kernel,
        (place, fields, r, g, h, d, inverse, xp, *rows_of(r1, partner, message), *coarse),
        [(2, NZ, ROWS, COLS)] * 2 + [(count, COLS)],
        [PADDED0, PADDED0, *COARSE_SCRATCH, (4, ROWS, COLS), BUFFER],
    )
    sums = lax.all_to_all(sums.reshape(count, 1, COLS), ("gx", "gy"), 0, 0).reshape(count, COLS)
    return tuple(
        call(
            scale_kernel,
            (fields, direction, image, sums),
            [(2, NZ, ROWS, COLS)] * 2,
            place=False,
        )
    )


def solution(mesh):
    return jax.shard_map(
        functools.partial(shards, mesh.shape["gx"], mesh.shape["gy"]),
        mesh=mesh,
        in_specs=(
            P(None, None, "gx", "gy"),
            P(None, "gx", "gy"),
            P(None, "gx", "gy"),
            P(),
            P(),
            P(),
        ),
        out_specs=(P(None, None, "gx", "gy"), P(None, None, "gx", "gy")),
        check_vma=False,
    )
```
